32 devices in a mesh: emb: 16 (over z, y, x), dp: 2 (over core).
Axes of the slice: x: 2, y: 2, z: 4, core: 2. Of those that a mesh axis runs over, the one named last changes fastest.
Arguments:
- hashed_ids: int32 [256, 128], P(('emb', 'dp')), may hold values from 0 to 8191
- owners: int32 [256, 128, 1], P(('emb', 'dp')), may hold values from 0 to 15; in each aligned block of 1024 rows (0 to 1023, 1024 to 2047, ..., all dimensions but the last counted through in order) at most 128 rows name the same one
- domain_tags: int32 [256], P(('emb', 'dp')), may hold values from 0 to 2
- user_counts: int32 [3], replicated, may hold values from 512 to 8192
- lengths: int32 [32, 8], P(('emb', 'dp')), may hold values from 1 to 128, 640 in all within a row
- buckets: int32 [128, 128], replicated, may hold values from 0 to 31
- table: bfloat16 [524288, 128], P('emb'), may hold values from -6 to 6
- gain_one: float32 [128], replicated, may hold values from 0.5 to 1.5
- query_weight_matrix: bfloat16 [128, 384], replicated, may hold values from -0.5 to 0.5
- key_weight_matrix: bfloat16 [128, 384], replicated, may hold values from -0.5 to 0.5
- value_weight_matrix: bfloat16 [128, 384], replicated, may hold values from -0.5 to 0.5
- attention_output_weight: bfloat16 [384, 128], replicated, may hold values from -0.875 to 0.875
- bias_table: float32 [32, 6], replicated, may hold values from -4 to 4
- gain_two: float32 [128], replicated, may hold values from 0.5 to 1.5
- feedforward_input_weight: bfloat16 [128, 1024], replicated, may hold values from -0.5 to 0.5
- feedforward_output_weight: bfloat16 [1024, 128], replicated, may hold values from -0.1875 to 0.1875
- cotangent: bfloat16 [256, 128, 128], P(('emb', 'dp')), may hold values from -6 to 6
Outputs:
- output: bfloat16 [256, 128, 128], P(('emb', 'dp'))
- input_grad: float32 [256, 128, 128], P(('emb', 'dp'))
- table_grad: float32 [524288, 128], P('emb')
- gain_one_grad: float32 [128], replicated
- w_query_grad: float32 [128, 384], replicated
- w_key_grad: float32 [128, 384], replicated
- w_value_grad: float32 [128, 384], replicated
- w_output_grad: float32 [384, 128], replicated
- bias_grad: float32 [32, 6], replicated
- gain_two_grad: float32 [128], replicated
- w_in_grad: float32 [128, 1024], replicated
- w_out_grad: float32 [1024, 128], replicated
The draws below stay inside these ranges and needn't reach their ends.
Inputs may be any that keep to these rules, and one draw needn't show every extreme that they name: `owners`: among the 1024 tokens of one device no shard is named more than 128 times, and in some device's tokens one shard is named exactly 128 times. The 8 lengths of each row sum to 640 and the largest of each row is 128.
All inputs are finite; a program needn't handle non-finite values.
Results may differ from the reference program's by a relative error of at most 0.012.
Values may be sent and summed in bfloat16 or wider, within the bound.
A program may use at most 128 MiB of HBM per device.

```python
import math
from functools import partial
import jax
import jax.numpy as jnp
import numpy as np
from jax import lax

D = 128
H = 6
DH = 64
FF = 1024
BUCKETS = 32
ROWS_DEV = 32768
L = 128
SEQ_DEV = 8
HD = 384
TOK_DEV = 1024
SEQS = 256
ROWS = 524288
DOMAIN_ROWS = 8192
CAP = 128
N_EMB = 16
N_DP = 2


def set_ends(drawn, key, smallest, top_value):
    extent = drawn.shape
    spot = [jax.random.randint(jax.random.fold_in(key, axis), (), 0, extent[axis]) for axis in range(len(extent))]
    drawn = drawn.at[tuple(spot)].set(smallest)
    longest = extent.index(max(extent))
    spot[longest] = (spot[longest] + 1) % extent[longest]
    return drawn.at[tuple(spot)].set(top_value)


def steps_of(stream_key, extent, split, low, high):
    loudness = 1.0
    for position, blocks in split:
        heights = jax.random.uniform(jax.random.fold_in(jax.random.fold_in(stream_key, 6), position), (blocks,), jnp.float32, low / len(split), high / len(split))
        loudness = loudness * jnp.repeat(jnp.exp(heights), extent[position] // blocks).reshape((-1,) + (1,) * (len(extent) - 1 - position))
    return loudness


def rank_bounds(count, lean):
    portions = [(1 << 20) // math.isqrt(standing ** lean) + 1 for standing in range(1, count + 1)]
    width = 1 + sum(portions) // (1 << 30)
    return np.cumsum(np.array([max(1, weight // width) for weight in portions]))


def skewed_ids(stream_key, dims, number_of, slope):
    grid = rank_bounds(number_of, slope)
    pick = jax.random.randint(jax.random.fold_in(stream_key, 1), dims, 0, int(grid[number_of - 1]))
    grade = jnp.searchsorted(jnp.asarray(grid, jnp.int32), pick, side="right")
    return jax.random.permutation(jax.random.fold_in(stream_key, 2), number_of)[grade].astype(jnp.int32)


def length_profile(count, total, most, skew):
    weights = [(1 << 20) // math.isqrt(standing ** skew) + 1 for standing in range(2, count + 1)]
    spare, given = total - most - (count - 1), [1] * (count - 1)
    while spare > 0:
        movable = [i for i in range(count - 1) if given[i] < most]
        mass, budget = sum([weights[i] for i in movable]), spare
        for i in movable:
            addition = min(most - given[i], max(1, budget * weights[i] // mass), spare)
            given[i] = given[i] + addition
            spare = spare - addition
    return np.array([most] + given)


def ragged_sizes(key, amount, total, limit, skew):
    if amount == 2:
        one = jax.random.randint(key, (), max(1, total - limit), min(limit, total - 1) + 1)
        return jnp.stack([one, total - one])
    tallies = jnp.asarray(length_profile(amount, total, limit, skew), jnp.int32)
    couples = (amount - 1) // 2
    donor, sink = tallies[1:1 + 2 * couples:2], tallies[2:2 + 2 * couples:2]
    margin = jnp.minimum(donor - 1, limit - sink)
    moved = jax.random.randint(jax.random.fold_in(key, 1), (couples,), 0, 1 << 20) % (margin + 1)
    tallies = tallies.at[1:1 + 2 * couples:2].set(donor - moved).at[2:2 + 2 * couples:2].set(sink + moved)
    return tallies[jax.random.permutation(jax.random.fold_in(key, 2), amount)]


def assign_block(rng, own, number, rows, count, top, bound, skew):
    order = jax.random.permutation(rng, count)
    crowded, ordinary = shares(count, rows * top, bound, skew, True), shares(count, rows * top, bound, skew, False)
    places = jnp.arange(count)

    def named(sizes, turn):
        used = int((sizes > 0).sum())
        fixed = max(1, used // 4)
        moved = fixed + (places - fixed + turn * (used - fixed)) % max(1, count - fixed)
        return jnp.zeros((count,), jnp.int32).at[order[jnp.where(places < fixed, places, moved)]].set(jnp.asarray(sizes, jnp.int32))

    sizes = jnp.where(number % 4 == 0, named(crowded, number // 4), named(ordinary, number - number // 4 - 1))
    mixed = jax.random.permutation(jax.random.fold_in(own, 3), count)
    donor, taker = mixed[0:count // 2 * 2:2], mixed[1:count // 2 * 2:2]
    room = jnp.minimum(sizes[donor] - 1, bound - sizes[taker]) // 2
    room = jnp.where((donor == order[0]) | (taker == order[0]) | (sizes[taker] == 0), 0, jnp.maximum(room, 0))
    moved = jax.random.randint(jax.random.fold_in(own, 4), (count // 2,), 0, 1 << 20) % (room + 1)
    sizes = sizes.at[donor].add(-moved).at[taker].add(moved)
    items = jnp.searchsorted(jnp.cumsum(sizes), jnp.arange(rows * top), side="right").astype(jnp.int32)
    table = items.reshape(top, rows).T
    table = table[jax.random.permutation(jax.random.fold_in(own, 1), rows)]
    turn = jax.random.randint(jax.random.fold_in(own, 2), (rows, 1), 0, top)
    return jnp.take_along_axis(table, (jnp.arange(top)[None, :] + turn) % top, axis=1)


def shares(count, total, most, slope, full):
    loads = [(1 << 20) // math.isqrt(standing ** slope) + 1 for standing in range(1, count + 1)]
    largest = most if full else min(most, max(-(-total // count), total * loads[0] // sum(loads)))
    least = 1 if total - largest >= count - 1 else 0
    given, spare = [largest] + [least] * (count - 1), total - largest - least * (count - 1)
    while spare > 0:
        free = [i for i in range(1, count) if given[i] < largest] or [i for i in range(1, count) if given[i] < most]
        mass, remaining = sum([loads[i] for i in free]), spare
        for i in free:
            extra = min(most - given[i], max(1, remaining * loads[i] // mass), spare)
            given[i] = given[i] + extra
            spare = spare - extra
    return np.array(given)


def bell_draw(key, dims, deviation, limit, pieces=(), kind=jnp.bfloat16):
    array = deviation * jax.random.normal(key, dims, jnp.float32)
    if pieces:
        array = array * steps_of(key, dims, pieces, -0.22, 0.18)
    return jnp.clip(array, -limit, limit).astype(kind)


def setup_inputs(seed: int = 0) -> dict:
    arg_keys = jax.random.split(jax.random.key(seed), 18)
    hashed_ids = set_ends(skewed_ids(arg_keys[0], (SEQS, L), DOMAIN_ROWS, 2), jax.random.fold_in(arg_keys[0], 3), 0, DOMAIN_ROWS - 1).astype(jnp.int32)
    owners_keys = jax.random.split(jax.random.fold_in(arg_keys[1], 1), SEQS * L // TOK_DEV)
    owners_turns = jax.random.permutation(jax.random.fold_in(arg_keys[1], 3), SEQS * L // TOK_DEV)
    owners = jax.vmap(lambda own, number: assign_block(jax.random.fold_in(arg_keys[1], 2), own, number, TOK_DEV, N_EMB, 1, CAP, 2))(owners_keys, owners_turns).reshape((SEQS, L, 1))
    domain_tags = set_ends(jax.random.randint(arg_keys[2], (SEQS,), 0, 3), jax.random.fold_in(arg_keys[2], 1), 0, 2).astype(jnp.int32)
    user_counts = jax.random.randint(arg_keys[3], (3,), max(1, DOMAIN_ROWS // 16), DOMAIN_ROWS + 1).astype(jnp.int32)
    lengths = jax.vmap(lambda own: ragged_sizes(own, SEQ_DEV, SEQ_DEV * L * 5 // 8, L, 1))(jax.random.split(arg_keys[4], (N_EMB * N_DP))).reshape((N_EMB * N_DP, SEQ_DEV)).astype(jnp.int32)
    buckets = set_ends(jax.random.randint(arg_keys[5], (L, L), 0, BUCKETS), jax.random.fold_in(arg_keys[5], 1), 0, BUCKETS - 1).astype(jnp.int32)
    table = bell_draw(arg_keys[6], (ROWS, D), 1.0, 6.0, ((0, 16),))
    gain_one = jnp.clip(1.0 + 0.1 * jax.random.normal(arg_keys[7], (D,), jnp.float32), 0.5, 1.5)
    query_weight_matrix = bell_draw(arg_keys[8], (D, HD), D ** -0.5, 0.5)
    key_weight_matrix = bell_draw(arg_keys[9], (D, HD), D ** -0.5, 0.5)
    value_weight_matrix = bell_draw(arg_keys[10], (D, HD), D ** -0.5, 0.5)
    attention_output_weight = bell_draw(arg_keys[11], (HD, D), (HD // 8) ** -0.5, 0.875)
    bias_table = bell_draw(arg_keys[12], (BUCKETS, H), 1.0, 4.0, (), jnp.float32)
    gain_two = jnp.clip(1.0 + 0.1 * jax.random.normal(arg_keys[13], (D,), jnp.float32), 0.5, 1.5)
    feedforward_input_weight = bell_draw(arg_keys[14], (D, FF), D ** -0.5, 0.5)
    feedforward_output_weight = bell_draw(arg_keys[15], (FF, D), FF ** -0.5, 0.1875)
    cotangent = bell_draw(arg_keys[16], (SEQS, L, D), 1.0, 6.0, ((0, 32),))
    return {"hashed_ids": hashed_ids, "owners": owners, "domain_tags": domain_tags, "user_counts": user_counts, "lengths": lengths, "buckets": buckets, "table": table, "gain_one": gain_one, "query_weight_matrix": query_weight_matrix, "key_weight_matrix": key_weight_matrix, "value_weight_matrix": value_weight_matrix, "attention_output_weight": attention_output_weight, "bias_table": bias_table, "gain_two": gain_two, "feedforward_input_weight": feedforward_input_weight, "feedforward_output_weight": feedforward_output_weight, "cotangent": cotangent}


@jax.custom_vjp
def reduced_precision(v):
    return lax.optimization_barrier(v.astype(jnp.bfloat16)).astype(jnp.float32)

@jax.custom_vjp
def reduced_backward(v):
    return v

def low_keep(v):
    return (reduced_precision(v), None)

def low_pass(kept, grad):
    return (grad,)

def back_keep(v):
    return (v, None)

def back_low(kept, grad):
    return (reduced_precision(grad),)
reduced_precision.defvjp(low_keep, low_pass)
reduced_backward.defvjp(back_keep, back_low)
epsilon = 1e-06
highest_precision = lax.Precision.HIGHEST

def rms_scaled(values, gain):
    return values * lax.rsqrt(lax.optimization_barrier(jnp.mean(values * values, axis=-1, keepdims=True)) + epsilon) * gain

def encoder_group(params, pair_bias, packed):
    hidden_state_rows, limits = packed
    gain_one, query_weight_matrix, key_weight_matrix, value_weight_matrix, attention_output_weight, gain_two, feedforward_input_weight, feedforward_output_weight = params
    groups = hidden_state_rows.shape[0]
    heads = query_weight_matrix.shape[1] // DH
    first_normalized = reduced_precision(rms_scaled(hidden_state_rows, gain_one))
    query_rows = reduced_precision(reduced_backward(jnp.einsum('rcf,fi->rci', first_normalized, query_weight_matrix, precision=highest_precision)))
    key_matrix_full = reduced_precision(reduced_backward(jnp.einsum('rcf,fi->rci', first_normalized, key_weight_matrix, precision=highest_precision)))
    value_matrix_full = reduced_precision(reduced_backward(jnp.einsum('rcf,fi->rci', first_normalized, value_weight_matrix, precision=highest_precision)))
    head_q = query_rows.reshape(groups, L, heads, DH)
    head_k = key_matrix_full.reshape(groups, L, heads, DH)
    head_v = value_matrix_full.reshape(groups, L, heads, DH)
    raw = jnp.einsum('sihd,sjhd->shij', head_q, head_k, precision=highest_precision) / math.sqrt(DH) + pair_bias[None]
    raw = reduced_backward(raw)
    visible = jnp.arange(L, dtype=jnp.int32)[None, :] < limits[:, None]
    scores = jnp.where(visible[:, None, None, :], raw, -1000000000.0)
    probs = reduced_precision(jax.nn.softmax(scores, axis=-1))
    attention_mixture = jnp.einsum('shij,sjhd->sihd', probs, head_v, precision=highest_precision).reshape(groups, L, heads * DH)
    attention_mixture = reduced_precision(reduced_backward(attention_mixture))
    residual_middle = hidden_state_rows + reduced_backward(jnp.einsum('oyn,nc->oyc', attention_mixture, attention_output_weight, precision=highest_precision))
    second_normalized = reduced_precision(rms_scaled(residual_middle, gain_two))
    hidden_preactivation = reduced_backward(jnp.einsum('rmk,kg->rmg', second_normalized, feedforward_input_weight, precision=highest_precision))
    activated_hidden = reduced_precision(jax.nn.gelu(hidden_preactivation))
    return residual_middle + jnp.einsum('uqj,jp->uqp', activated_hidden, feedforward_output_weight, precision=highest_precision)

def forward(table, offset, gain_one, query_weight_matrix, key_weight_matrix, value_weight_matrix, attention_output_weight, bias_table, gain_two, feedforward_input_weight, feedforward_output_weight, rows, limits, buckets):
    hidden_state_rows = table[rows] + offset
    pair_bias = jnp.transpose(bias_table[buckets], (2, 0, 1))
    block_seqs = math.gcd(SEQS, max(1, 4096 // L))
    params = (gain_one, query_weight_matrix, key_weight_matrix, value_weight_matrix, attention_output_weight, gain_two, feedforward_input_weight, feedforward_output_weight)
    grouped = (hidden_state_rows.reshape(SEQS // block_seqs, block_seqs, L, D), limits.reshape(SEQS // block_seqs, block_seqs))
    result = lax.map(jax.checkpoint(partial(encoder_group, params, pair_bias)), grouped)
    return result.reshape(SEQS, L, D)

def reference(hashed_ids, owners, domain_tags, user_counts, lengths, buckets, table, gain_one, query_weight_matrix, key_weight_matrix, value_weight_matrix, attention_output_weight, bias_table, gain_two, feedforward_input_weight, feedforward_output_weight, cotangent):
    counts = user_counts[domain_tags]
    local = domain_tags[:, None] * DOMAIN_ROWS + hashed_ids % counts[:, None]
    rows = (owners[:, :, 0] * ROWS_DEV + local).astype(jnp.int32)
    limits = lengths.reshape(-1).astype(jnp.int32)
    floats = (table.astype(jnp.float32), jnp.zeros((SEQS, L, D), jnp.float32), gain_one.astype(jnp.float32), query_weight_matrix.astype(jnp.float32), key_weight_matrix.astype(jnp.float32), value_weight_matrix.astype(jnp.float32), attention_output_weight.astype(jnp.float32), bias_table.astype(jnp.float32), gain_two.astype(jnp.float32), feedforward_input_weight.astype(jnp.float32), feedforward_output_weight.astype(jnp.float32))

    def closed(*values):
        return forward(*values, rows, limits, buckets)
    output, pullback = jax.vjp(closed, *floats)
    visible = (jnp.arange(L, dtype=jnp.int32)[None, :] < limits[:, None]).astype(jnp.float32)
    grads = pullback(cotangent.astype(jnp.float32) * visible[:, :, None])
    return (output.astype(jnp.bfloat16), grads[1], grads[0], grads[2], grads[3], grads[4], grads[5], grads[6], grads[7], grads[8], grads[9], grads[10])
```

```python
import functools
import math

import jax
import jax.numpy as jnp
from jax import lax
from jax.experimental import pallas as pl
from jax.experimental.pallas import tpu as pltpu
from jax.sharding import PartitionSpec as P

DH = 64
LANES = 128
EPSILON = 1e-06
LIVE = 32768
MESH = pl.DeviceIdType.MESH
F32 = jnp.float32
BF16 = jnp.bfloat16
VMEM_LIMIT = 56 * 1024 * 1024


def dot_nn(a, b):
    return lax.dot_general(a, b, (((1,), (0,)), ((), ())), preferred_element_type=F32)


def dot_nt(a, b):
    return lax.dot_general(a, b, (((1,), (1,)), ((), ())), preferred_element_type=F32)


def dot_tn(a, b):
    return lax.dot_general(a, b, (((0,), (0,)), ((), ())), preferred_element_type=F32)


def hot_slots(pos, first, count):
    rows = lax.broadcasted_iota(jnp.int32, (count, LANES), 0) + first
    parts = [
        jnp.where(rows == pos[s : s + 1, :], 1.0, 0.0).astype(BF16) for s in range(pos.shape[0])
    ]
    return jnp.concatenate(parts, axis=1)


def lookup_body(
    n, cap, used, ids, own, tags, counts, lens, table,
    x_t, pos_out, asked_out,
    req, asked_v, asked_s, tab_low, tab, gbuf, send, recv, x_acc,
    req_send, req_recv, row_send, row_recv, pair_send, pair_recv, tab_sem, smem_sem,
):
    me = lax.axis_index("emb")
    core = lax.axis_index("dp")
    seqs, length = ids.shape
    domain_rows = used // 3
    pieces = tab_sem.shape[0]
    piece = used // pieces

    barrier = pltpu.get_barrier_semaphore()

    def greet(k, carry):
        pl.semaphore_signal(
            barrier, inc=1, device_id={"emb": lax.rem(me + k, n)}, device_id_type=MESH
        )
        return carry

    lax.fori_loop(1, n, greet, 0)
    pl.semaphore_signal(barrier, inc=1, device_id={"dp": 1 - core}, device_id_type=MESH)

    def table_copy(c):
        part = pl.ds(c * piece, piece)
        return pltpu.make_async_copy(table.at[part], tab_low.at[part], tab_sem.at[c])

    for c in range(pieces):
        table_copy(c).start()

    row_id = lax.broadcasted_iota(jnp.int32, (seqs, length), 0)
    lane_id = lax.broadcasted_iota(jnp.int32, (seqs, length), 1)
    count_of = jnp.zeros((seqs, length), F32)
    tag_of = jnp.zeros((seqs, length), jnp.int32)
    len_of = jnp.zeros((seqs, length), jnp.int32)
    for s in range(seqs):
        tag = tags[s]
        count_of = jnp.where(row_id == s, counts[tag].astype(F32), count_of)
        tag_of = jnp.where(row_id == s, tag, tag_of)
        len_of = jnp.where(row_id == s, lens[0, s], len_of)
    code = ids[...].astype(F32)
    turns = jnp.floor((code + 0.5) / jnp.maximum(count_of, 1.0))
    local = tag_of * domain_rows + (code - turns * count_of).astype(jnp.int32)
    live = lane_id < len_of
    rel = own[...] - me
    rel = jnp.where(rel < 0, rel + n, rel)

    owner_id = lax.broadcasted_iota(jnp.int32, (n, length), 0)
    hot_live, hot_dead = [], []
    for s in range(seqs):
        hot = owner_id == rel[s : s + 1, :]
        alive = jnp.broadcast_to(live[s : s + 1, :].astype(F32), (n, length))
        hot_live.append(jnp.where(hot, alive, 0.0))
        hot_dead.append(jnp.where(hot, 1.0 - alive, 0.0))
    both = jnp.concatenate(hot_live + hot_dead, axis=0).astype(BF16)
    before = (
        lax.broadcasted_iota(jnp.int32, (length, length), 0)
        < lax.broadcasted_iota(jnp.int32, (length, length), 1)
    )
    prefix = dot_nn(both, jnp.where(before, 1.0, 0.0).astype(BF16))
    running = jnp.zeros((n, 1), F32)
    ranks = []
    for part, hots in enumerate((hot_live, hot_dead)):
        for s in range(seqs):
            at = (part * seqs + s) * n
            ranks.append(
                jnp.sum(hots[s] * (prefix[at : at + n] + running), axis=0, keepdims=True)
            )
            running = running + jnp.sum(hots[s], axis=1, keepdims=True)
    rank = jnp.concatenate([ranks[s] + ranks[seqs + s] for s in range(seqs)], axis=0)
    rank = rank.astype(jnp.int32)
    pos = rel * cap + rank
    pos_out[...] = pos

    low = (local & 255).astype(F32)
    high = (lax.shift_right_logical(local, 8) + jnp.where(live, LIVE // 256, 0)).astype(F32)
    slot_id = lax.broadcasted_iota(jnp.int32, (LANES, length), 0)
    asking = jnp.zeros((2 * n, LANES), F32)
    for s in range(seqs):
        hot = hot_live[s] + hot_dead[s]
        values = jnp.concatenate([hot * high[s : s + 1, :], hot * low[s : s + 1, :]], axis=0)
        slot_hot = jnp.where(slot_id == rank[s : s + 1, :], 1.0, 0.0).astype(BF16)
        asking = asking + dot_nt(values.astype(BF16), slot_hot)
    wanted = (asking[:n] * 256.0 + asking[n:]).astype(jnp.int32)
    for j in range(n):
        req[j] = wanted[j : j + 1, :]

    pl.semaphore_wait(barrier, n)

    def request(j):
        back = lax.rem(n - j, n)
        return pltpu.make_async_remote_copy(
            src_ref=req.at[j],
            dst_ref=asked_v.at[back],
            send_sem=req_send.at[j],
            recv_sem=req_recv.at[back],
            device_id={"emb": lax.rem(me + j, n)},
            device_id_type=MESH,
        )

    def arrived(j):
        return pltpu.make_async_remote_copy(
            src_ref=req.at[j],
            dst_ref=asked_v.at[j],
            send_sem=req_send.at[j],
            recv_sem=req_recv.at[j],
            device_id={"emb": lax.rem(me + j, n)},
            device_id_type=MESH,
        )

    def ask(j, carry):
        request(j).start()
        return carry

    lax.fori_loop(1, n, ask, 0)
    asked_v[0] = req[0]

    for c in range(pieces):
        table_copy(c).wait()

        def widen(r, carry):
            part = pl.ds(pl.multiple_of(c * piece + r * 256, 256), 256)
            tab[part, :] = tab_low[part, :].astype(F32)
            return carry

        lax.fori_loop(0, piece // 256, widen, 0)

    def all_asked(j, carry):
        arrived(j).wait_recv()
        return carry

    lax.fori_loop(1, n, all_asked, 0)
    to_scalar = pltpu.make_async_copy(asked_v, asked_s, smem_sem)
    to_scalar.start()

    def tally(j, carry):
        values = asked_v[j]
        asked_out[core, j, 0:1] = values
        number = jnp.sum(jnp.where(values >= LIVE, 1.0, 0.0), axis=1, keepdims=True)
        asked_out[core, j, 1:2] = jnp.broadcast_to(number.astype(jnp.int32), (1, LANES))
        return carry

    lax.fori_loop(0, n, tally, 0)
    share = pltpu.make_async_remote_copy(
        src_ref=asked_out.at[core],
        dst_ref=asked_out.at[core],
        send_sem=pair_send,
        recv_sem=pair_recv,
        device_id={"dp": 1 - core},
        device_id_type=MESH,
    )
    share.start()
    to_scalar.wait()

    def row_copy(j):
        back = lax.rem(n - j, n)
        return pltpu.make_async_remote_copy(
            src_ref=send.at[pl.ds(pl.multiple_of(j * cap, cap), cap)],
            dst_ref=recv.at[pl.ds(pl.multiple_of(back * cap, cap), cap)],
            send_sem=row_send.at[j],
            recv_sem=row_recv.at[back],
            device_id={"emb": lax.rem(me + j, n)},
            device_id_type=MESH,
        )

    def row_arrival(j):
        part = pl.ds(pl.multiple_of(j * cap, cap), cap)
        return pltpu.make_async_remote_copy(
            src_ref=send.at[part],
            dst_ref=recv.at[part],
            send_sem=row_send.at[j],
            recv_sem=row_recv.at[j],
            device_id={"emb": lax.rem(me + j, n)},
            device_id_type=MESH,
        )

    def gather(j):
        def eight(c, carry):
            for r in range(8):
                at = jnp.minimum(asked_s[j, 0, c * 8 + r] & (LIVE - 1), used - 1)
                gbuf[pl.ds(c * 8 + r, 1), :] = tab[pl.ds(at, 1), :]
            return carry

        lax.fori_loop(0, cap // 8, eight, 0)
        return gbuf[...].astype(BF16)

    def serve(j, carry):
        send[pl.ds(pl.multiple_of(j * cap, cap), cap), :] = gather(j)
        row_copy(j).start()
        return carry

    lax.fori_loop(1, n, serve, 0)
    recv[0:cap, :] = gather(0)

    def place(pair, carry):
        def ready(j, inner):
            row_arrival(j).wait_recv()
            return inner

        lax.fori_loop(jnp.maximum(2 * pair, 1), 2 * pair + 2, ready, 0)
        first = pl.multiple_of(pair * 2 * cap, 2 * cap)
        hot = hot_slots(pos_out[...], first, 2 * cap)
        got = dot_tn(recv[pl.ds(first, 2 * cap), :], hot)

        @pl.when(pair == 0)
        def _():
            x_acc[...] = got

        @pl.when(pair > 0)
        def _():
            x_acc[...] += got

        return carry

    lax.fori_loop(0, n // 2, place, 0)
    x_t[...] = x_acc[...].astype(BF16)

    def sent(j, carry):
        request(j).wait_send()
        row_copy(j).wait_send()
        return carry

    lax.fori_loop(1, n, sent, 0)
    share.wait()


def gelu_parts(u):
    k0 = math.sqrt(2.0 / math.pi)
    k1 = k0 * 0.044715
    square = u * u
    half = 0.5 * jnp.tanh(u * (k1 * square + k0)) + 0.5
    value = u * half
    slope = half + (2.0 * value) * (1.0 - half) * (3.0 * k1 * square + k0)
    return value, slope


def split_pair(both):
    zero = jnp.zeros((DH, LANES), both.dtype)
    left = jnp.concatenate([both[:DH], zero], axis=0)
    right = jnp.concatenate([zero, both[DH:]], axis=0)
    return jnp.concatenate([left, right], axis=1)


def block_body(
    cap2, lens, btab, buckets, x_t, cot, g1, wq, wk, wv, wo, g2, win, wout, pos,
    y_out, ig_out, slots_out, w_out, small_out,
    wqkv_t, wqkv, wo_t, win_t, wout_t, buck_t, bias, a_t, qkv_t, kv, p_s, o_t, c_t, act_t, du_t,
    dy_t, dm_t, dmb_t, do_t, dqkv_t, dsum, igb_t, g1_acc, g2_acc, b_acc,
):
    seqs, length, width = cot.shape
    tokens = seqs * length
    hd = wq.shape[1]
    ff = win.shape[1]
    heads = hd // DH
    pairs = heads // 2
    chunk = 256
    chunks = tokens // chunk
    bucket_count = btab.shape[1]

    for part, w in enumerate((wq, wk, wv)):
        wqkv[:, part * hd : (part + 1) * hd] = w[...]
        wqkv_t[part * hd : (part + 1) * hd, :] = w[...].T
    wo_t[...] = wo[...].T
    win_t[...] = win[...].T
    wout_t[...] = wout[...].T
    buck_t[...] = buckets[...].astype(F32).T
    g1_col = jnp.broadcast_to(g1[...], (8, width)).T[:, 0:1]
    g2_col = jnp.broadcast_to(g2[...], (8, width)).T[:, 0:1]
    g1_acc[...] = jnp.zeros_like(g1_acc)
    g2_acc[...] = jnp.zeros_like(g2_acc)
    dsum[...] = jnp.zeros_like(dsum)
    b_acc[...] = jnp.zeros_like(b_acc)

    def bias_rows(r, carry):
        part = pl.ds(pl.multiple_of(r * 8, 8), 8)
        bt = buck_t[part, :]
        rows = [jnp.zeros((8, length), F32) for _ in range(heads)]
        for b in range(bucket_count):
            here = bt == float(b)
            rows = [jnp.where(here, btab[h, b], rows[h]) for h in range(heads)]
        for p in range(pairs):
            bias[p, part, :] = jnp.concatenate(rows[2 * p : 2 * p + 2], axis=1)
        return carry

    lax.fori_loop(0, length // 8, bias_rows, 0)

    def norm_one(c):
        xf = x_t[:, pl.ds(pl.multiple_of(c * chunk, chunk), chunk)].astype(F32)
        scale = lax.rsqrt(jnp.mean(xf * xf, axis=0, keepdims=True) + EPSILON)
        return xf, scale

    def project(c, carry):
        part = pl.ds(pl.multiple_of(c * chunk, chunk), chunk)
        xf, scale = norm_one(c)
        a = (xf * scale * g1_col).astype(BF16)
        a_t[:, part] = a
        out = dot_nn(wqkv_t[...], a)
        qkv_t[0:hd, part] = out[:hd].astype(BF16) * jnp.array(1.0 / math.sqrt(DH), BF16)
        qkv_t[hd:, part] = out[hd:].astype(BF16)
        kv[part, :] = dot_nn(a.T, wqkv[:, hd:]).astype(BF16)
        return carry

    lax.fori_loop(0, chunks, project, 0)

    def attend(s, carry):
        part = pl.ds(pl.multiple_of(s * length, length), length)
        visible = lax.broadcasted_iota(jnp.int32, (length, 2 * length), 0) < lens[0, s]
        alive = lax.broadcasted_iota(jnp.int32, (width, length), 1) < lens[0, s]
        dy_t[:, part] = jnp.where(alive, cot[s].astype(F32).T, 0.0).astype(BF16)
        for p in range(pairs):
            rows = slice(p * 2 * DH, (p + 1) * 2 * DH)
            scores = dot_nn(kv[part, rows], split_pair(qkv_t[rows, part])) + bias[p]
            scores = jnp.where(visible, scores, -1000000000.0)
            expo = jnp.exp(scores - jnp.max(scores, axis=0, keepdims=True))
            prob = expo * (1.0 / jnp.sum(expo, axis=0, keepdims=True))
            p_s[s, p] = prob
            mixed = dot_nn(qkv_t[2 * hd + p * 2 * DH : 2 * hd + (p + 1) * 2 * DH, part], prob.astype(BF16))
            o_t[rows, part] = jnp.concatenate(
                [mixed[:DH, :length], mixed[DH:, length:]], axis=0
            ).astype(BF16)
        return carry

    lax.fori_loop(0, seqs, attend, 0)

    def feed(c, carry):
        part = pl.ds(pl.multiple_of(c * chunk, chunk), chunk)
        m = x_t[:, part].astype(F32) + dot_nn(wo_t[...], o_t[:, part])
        scale = lax.rsqrt(jnp.mean(m * m, axis=0, keepdims=True) + EPSILON)
        z = m * scale
        normed = (z * g2_col).astype(BF16)
        c_t[:, part] = normed
        dy = dy_t[:, part]
        u = dot_nn(win_t[...], normed)
        value, slope = gelu_parts(u)
        act = value.astype(BF16)
        act_t[:, part] = act
        du = (dot_nn(wout[...], dy) * slope).astype(BF16)
        du_t[:, part] = du
        y = m + dot_nn(wout_t[...], act)
        for k in range(chunk // length):
            y_out[c * (chunk // length) + k] = y[:, k * length : (k + 1) * length].T.astype(BF16)
        dc = dot_nn(win[...], du)
        gain = dc * z
        for k in range(chunk // length):
            g2_acc[...] += gain[:, k * length : (k + 1) * length]
        e = dc * g2_col
        dm = dy.astype(F32) + scale * (e - z * jnp.mean(e * z, axis=0, keepdims=True))
        dm_t[:, part] = dm
        low = dm.astype(BF16)
        dmb_t[:, part] = low
        do_t[:, part] = dot_nn(wo[...], low).astype(BF16)
        return carry

    lax.fori_loop(0, chunks, feed, 0)

    def attend_back(s, carry):
        part = pl.ds(pl.multiple_of(s * length, length), length)
        for p in range(pairs):
            rows = slice(p * 2 * DH, (p + 1) * 2 * DH)
            krows = slice(hd + p * 2 * DH, hd + (p + 1) * 2 * DH)
            vrows = slice(2 * hd + p * 2 * DH, 2 * hd + (p + 1) * 2 * DH)
            do2 = split_pair(do_t[rows, part])
            q2 = split_pair(qkv_t[rows, part])
            prob = p_s[s, p]
            dprob = dot_nn(kv[part, krows], do2)
            ds = prob * (dprob - jnp.sum(dprob * prob, axis=0, keepdims=True))
            dsum[p] += ds
            low = ds.astype(BF16)
            dqkv_t[vrows, part] = dot_nt(do2, prob.astype(BF16)).astype(BF16)
            dqkv_t[krows, part] = dot_nt(q2, low).astype(BF16)
            dq = dot_nn(qkv_t[krows, part], low) * (1.0 / math.sqrt(DH))
            dqkv_t[rows, part] = jnp.concatenate(
                [dq[:DH, :length], dq[DH:, length:]], axis=0
            ).astype(BF16)
        return carry

    lax.fori_loop(0, seqs, attend_back, 0)

    def inputs_back(c, carry):
        part = pl.ds(pl.multiple_of(c * chunk, chunk), chunk)
        xf, scale = norm_one(c)
        z = xf * scale
        da = dot_nn(wqkv[...], dqkv_t[:, part])
        gain = da * z
        for k in range(chunk // length):
            g1_acc[...] += gain[:, k * length : (k + 1) * length]
        e = da * g1_col
        ig = dm_t[:, part] + scale * (e - z * jnp.mean(e * z, axis=0, keepdims=True))
        igb_t[:, part] = ig.astype(BF16)
        for k in range(chunk // length):
            ig_out[c * (chunk // length) + k] = ig[:, k * length : (k + 1) * length].T
        return carry

    lax.fori_loop(0, chunks, inputs_back, 0)

    def to_slots(k, carry):
        first = pl.multiple_of(k * cap2, cap2)
        slots_out[pl.ds(first, cap2), :] = dot_nt(
            hot_slots(pos[...], first, cap2), igb_t[...]
        ).astype(BF16)
        return carry

    lax.fori_loop(0, slots_out.shape[0] // cap2, to_slots, 0)

    at = 0
    for k in range(3 * hd // width):
        block = slice(k * width, (k + 1) * width)
        w_out[at : at + width, :] = dot_nt(a_t[...], dqkv_t[block, :]).astype(BF16)
        at += width
    for k in range(ff // width):
        block = slice(k * width, (k + 1) * width)
        w_out[at : at + width, :] = dot_nt(c_t[...], du_t[block, :]).astype(BF16)
        at += width
    w_out[at : at + hd, :] = dot_nt(o_t[...], dmb_t[...]).astype(BF16)
    at += hd
    w_out[at : at + ff, :] = dot_nt(act_t[...], dy_t[...]).astype(BF16)
    at += ff
    if at < w_out.shape[0]:
        w_out[at:, :] = jnp.zeros((w_out.shape[0] - at, width), BF16)

    def bias_back(r, carry):
        part = pl.ds(pl.multiple_of(r * 8, 8), 8)
        bt = buck_t[part, :]
        grads = [dsum[h // 2, part, (h % 2) * length : (h % 2 + 1) * length] for h in range(heads)]
        for b in range(bucket_count):
            here = bt == float(b)
            for h in range(heads):
                b_acc[h, b] += jnp.where(here, grads[h], 0.0)
        return carry

    lax.fori_loop(0, length // 8, bias_back, 0)
    small_out[...] = jnp.zeros_like(small_out)
    small_out[0:1, :] = jnp.sum(g1_acc[...].T, axis=0, keepdims=True)
    small_out[1:2, :] = jnp.sum(g2_acc[...].T, axis=0, keepdims=True)
    for h in range(heads):
        by_bucket = jnp.sum(b_acc[h], axis=1)
        small_out[2 + h : 3 + h, 0:bucket_count] = jnp.sum(by_bucket.T, axis=0, keepdims=True)


def exchange_body(
    n, lo, cap, slots, w_in, small_in,
    inc, w_tot, small_tot,
    core_buf, half, lo_buf, quarter, hi_buf, small_a, small_b, small_c,
    row_send, row_recv, fwd_send, fwd_recv, core_sem, lo_send, lo_recv, hi_send, hi_recv,
    sa_sem, sb_send, sb_recv, sc_send, sc_recv, gh_send, gh_recv, gl_send, gl_recv, gc_send, gc_recv,
):
    me = lax.axis_index("emb")
    core = lax.axis_index("dp")
    hi = n // lo
    my_hi = me // lo
    my_lo = lax.rem(me, lo)
    half_rows, lo_rows, hi_rows = half.shape[0], quarter.shape[0], hi_buf.shape[1]

    barrier = pltpu.get_barrier_semaphore()

    def greet(k, carry):
        pl.semaphore_signal(
            barrier, inc=1, device_id={"emb": lax.rem(me + k, n)}, device_id_type=MESH
        )
        return carry

    lax.fori_loop(1, n, greet, 0)
    pl.semaphore_signal(barrier, inc=1, device_id={"dp": 1 - core}, device_id_type=MESH)
    pl.semaphore_wait(barrier, n)

    def block_at(j):
        return pl.ds(pl.multiple_of(j * cap, cap), cap)

    def remote(src, dst, send_sem, recv_sem, device):
        return pltpu.make_async_remote_copy(
            src_ref=src, dst_ref=dst, send_sem=send_sem, recv_sem=recv_sem,
            device_id=device, device_id_type=MESH,
        )

    def to_core(src, dst, send_sem, recv_sem):
        return remote(src, dst, send_sem, recv_sem, {"dp": 1 - core})

    theirs = pl.ds(pl.multiple_of((1 - core) * half_rows, half_rows), half_rows)
    mine = pl.ds(pl.multiple_of(core * half_rows, half_rows), half_rows)
    swap = to_core(w_in.at[theirs], core_buf, core_sem.at[0], core_sem.at[1])
    swap.start()
    small_a[core] = small_in[...]
    swap_small = to_core(small_a.at[core], small_a.at[core], sa_sem.at[0], sa_sem.at[1])
    swap_small.start()

    def row_copy(j):
        back = lax.rem(n - j, n)
        return remote(
            slots.at[block_at(j)], inc.at[core, block_at(back)],
            row_send.at[j], row_recv.at[back], {"emb": lax.rem(me + j, n)},
        )

    def row_arrival(j):
        return remote(
            slots.at[block_at(j)], inc.at[core, block_at(j)],
            row_send.at[j], row_recv.at[j], {"emb": lax.rem(me + j, n)},
        )

    def forward(j):
        return to_core(
            inc.at[core, block_at(j)], inc.at[core, block_at(j)], fwd_send.at[j], fwd_recv.at[j]
        )

    def forwarded(j):
        return to_core(
            inc.at[core, block_at(j)], inc.at[1 - core, block_at(j)], fwd_send.at[j], fwd_recv.at[j]
        )

    def row_start(j, carry):
        row_copy(j).start()
        return carry

    lax.fori_loop(1, n, row_start, 0)
    inc[core, 0:cap, :] = slots[0:cap, :]
    forward(0).start()

    swap.wait()
    swap_small.wait()

    def add_half(r, carry):
        at = pl.multiple_of(r * hi_rows, hi_rows)
        total = w_in[pl.ds(pl.multiple_of(core * half_rows + at, hi_rows), hi_rows), :].astype(F32)
        half[pl.ds(at, hi_rows), :] = (total + core_buf[pl.ds(at, hi_rows), :].astype(F32)).astype(
            BF16
        )
        return carry

    lax.fori_loop(0, half_rows // hi_rows, add_half, 0)
    small_b[my_lo] = small_a[0] + small_a[1]

    def lo_peer(k):
        return lax.rem(my_lo + k, lo)

    def lo_copy(k):
        peer = lo_peer(k)
        return remote(
            half.at[pl.ds(pl.multiple_of(peer * lo_rows, lo_rows), lo_rows)], lo_buf.at[lo - k],
            lo_send.at[k], lo_recv.at[lo - k], {"emb": my_hi * lo + peer},
        )

    def lo_arrival(k):
        return remote(
            quarter, lo_buf.at[k], lo_send.at[k], lo_recv.at[k], {"emb": my_hi * lo + lo_peer(k)}
        )

    def small_lo(k):
        return remote(
            small_b.at[my_lo], small_b.at[my_lo], sb_send.at[k], sb_recv.at[lo - k],
            {"emb": my_hi * lo + lo_peer(k)},
        )

    def small_lo_arrival(k):
        return remote(
            small_b.at[my_lo], small_b.at[lo_peer(k)], sb_send.at[k], sb_recv.at[k],
            {"emb": my_hi * lo + lo_peer(k)},
        )

    for k in range(1, lo):
        lo_copy(k).start()
        small_lo(k).start()
    for k in range(1, lo):
        lo_arrival(k).wait_recv()
        small_lo_arrival(k).wait_recv()

    def add_lo(r, carry):
        at = pl.multiple_of(r * hi_rows, hi_rows)
        total = half[pl.ds(pl.multiple_of(my_lo * lo_rows + at, hi_rows), hi_rows), :].astype(F32)
        for k in range(1, lo):
            total = total + lo_buf[k, pl.ds(at, hi_rows), :].astype(F32)
        quarter[pl.ds(at, hi_rows), :] = total.astype(BF16)
        return carry

    lax.fori_loop(0, lo_rows // hi_rows, add_lo, 0)
    total = small_b[0]
    for k in range(1, lo):
        total = total + small_b[k]
    small_c[my_hi] = total

    def hi_peer(k):
        return lax.rem(my_hi + k, hi)

    def hi_copy(k):
        peer = hi_peer(k)
        return remote(
            quarter.at[pl.ds(pl.multiple_of(peer * hi_rows, hi_rows), hi_rows)], hi_buf.at[hi - k],
            hi_send.at[k], hi_recv.at[hi - k], {"emb": peer * lo + my_lo},
        )

    def hi_arrival(k):
        return remote(
            hi_buf.at[k], hi_buf.at[k], hi_send.at[k], hi_recv.at[k], {"emb": hi_peer(k) * lo + my_lo}
        )

    def small_hi(k):
        return remote(
            small_c.at[my_hi], small_c.at[my_hi], sc_send.at[k], sc_recv.at[hi - k],
            {"emb": hi_peer(k) * lo + my_lo},
        )

    def small_hi_arrival(k):
        return remote(
            small_c.at[my_hi], small_c.at[hi_peer(k)], sc_send.at[k], sc_recv.at[k],
            {"emb": hi_peer(k) * lo + my_lo},
        )

    for k in range(1, hi):
        hi_copy(k).start()
        small_hi(k).start()
    for k in range(1, hi):
        hi_arrival(k).wait_recv()
        small_hi_arrival(k).wait_recv()
    total = quarter[pl.ds(pl.multiple_of(my_hi * hi_rows, hi_rows), hi_rows), :].astype(F32)
    for k in range(1, hi):
        total = total + hi_buf[k].astype(F32)
    base = core * half_rows + my_lo * lo_rows

    def piece(h):
        return pl.ds(pl.multiple_of(base + h * hi_rows, hi_rows), hi_rows)

    def quarter_at(l):
        return pl.ds(pl.multiple_of(core * half_rows + l * lo_rows, lo_rows), lo_rows)

    def other_quarter_at(l):
        return pl.ds(pl.multiple_of((1 - core) * half_rows + l * lo_rows, lo_rows), lo_rows)

    w_tot[piece(my_hi), :] = total.astype(BF16)
    total = small_c[0]
    for k in range(1, hi):
        total = total + small_c[k]
    small_tot[...] = total

    def gather_hi(k):
        return remote(
            w_tot.at[piece(my_hi)], w_tot.at[piece(my_hi)], gh_send.at[k], gh_recv.at[hi - k],
            {"emb": hi_peer(k) * lo + my_lo},
        )

    def gather_hi_arrival(k):
        return remote(
            w_tot.at[piece(my_hi)], w_tot.at[piece(hi_peer(k))], gh_send.at[k], gh_recv.at[k],
            {"emb": hi_peer(k) * lo + my_lo},
        )

    def gather_lo(k):
        return remote(
            w_tot.at[quarter_at(my_lo)], w_tot.at[quarter_at(my_lo)], gl_send.at[k],
            gl_recv.at[lo - k], {"emb": my_hi * lo + lo_peer(k)},
        )

    def gather_lo_arrival(k):
        return remote(
            w_tot.at[quarter_at(my_lo)], w_tot.at[quarter_at(lo_peer(k))], gl_send.at[k],
            gl_recv.at[k], {"emb": my_hi * lo + lo_peer(k)},
        )

    def gather_core(l):
        return to_core(
            w_tot.at[quarter_at(l)], w_tot.at[quarter_at(l)], gc_send.at[l], gc_recv.at[l]
        )

    def gather_core_arrival(l):
        return to_core(
            w_tot.at[quarter_at(l)], w_tot.at[other_quarter_at(l)], gc_send.at[l], gc_recv.at[l]
        )

    for k in range(1, hi):
        gather_hi(k).start()
    for k in range(1, hi):
        gather_hi_arrival(k).wait_recv()
    for k in range(1, lo):
        gather_lo(k).start()
    gather_core(my_lo).start()

    def pass_on(j, carry):
        row_arrival(j).wait_recv()
        forward(j).start()
        return carry

    lax.fori_loop(1, n, pass_on, 0)
    for k in range(1, lo):
        gather_lo_arrival(k).wait_recv()
        gather_core(lo_peer(k)).start()
    for l in range(lo):
        gather_core_arrival(l).wait_recv()

    def rows_in(j, carry):
        forwarded(j).wait_recv()
        forward(j).wait_send()
        return carry

    lax.fori_loop(0, n, rows_in, 0)

    def rows_out(j, carry):
        row_copy(j).wait_send()
        return carry

    lax.fori_loop(1, n, rows_out, 0)
    for k in range(1, lo):
        lo_copy(k).wait_send()
        small_lo(k).wait_send()
        gather_lo(k).wait_send()
    for k in range(1, hi):
        hi_copy(k).wait_send()
        small_hi(k).wait_send()
        gather_hi(k).wait_send()
    for l in range(lo):
        gather_core(l).wait_send()


def scatter_body(
    n, cap, asked, inc, w_tot, small,
    grad, g1, wq, wk, wv, wo, bias, g2, win, wout,
    acc, wide, zero, out_sem,
):
    used = acc.shape[0]
    rows_dev = grad.shape[0]
    zero_rows = zero.shape[0]
    zero[...] = jnp.zeros_like(zero)

    def clear_copy(k):
        return pltpu.make_async_copy(
            zero, grad.at[pl.ds(used + k * zero_rows, zero_rows)], out_sem.at[3 + k]
        )

    spare = (rows_dev - used) // zero_rows
    for k in range(spare):
        clear_copy(k).start()

    def clear(r, carry):
        acc[pl.ds(pl.multiple_of(r * 256, 256), 256), :] = jnp.zeros((256, acc.shape[1]), F32)
        return carry

    lax.fori_loop(0, used // 256, clear, 0)

    for c in range(2):
        def source(j, carry):
            part = pl.ds(pl.multiple_of(j * cap, cap), cap)
            wide[part, :] = inc[c, part, :].astype(F32)

            def eight(k, inner):
                for r in range(8):
                    at = asked[c, j, 0, k * 8 + r] & (LIVE - 1)
                    acc[pl.ds(at, 1), :] += wide[pl.ds(j * cap + k * 8 + r, 1), :]
                return inner

            lax.fori_loop(0, (asked[c, j, 1, 0] + 7) // 8, eight, 0)
            return carry

        lax.fori_loop(0, n, source, 0)

    third = used // 3

    def out_copy(k):
        part = pl.ds(k * third, third)
        return pltpu.make_async_copy(acc.at[part], grad.at[part], out_sem.at[k])

    for k in range(3):
        out_copy(k).start()

    width = wq.shape[0]
    hd = wq.shape[1]
    ff = win.shape[1]
    at = 0
    for ref in (wq, wk, wv, win):
        for k in range(ref.shape[1] // width):
            ref[:, k * width : (k + 1) * width] = w_tot[at : at + width, :].astype(F32)
            at += width
    wo[...] = w_tot[at : at + hd, :].astype(F32)
    at += hd
    wout[...] = w_tot[at : at + ff, :].astype(F32)
    g1[...] = small[0:1, :]
    g2[...] = small[1:2, :]
    heads, buckets = bias.shape
    bias[...] = small[2 : 2 + heads, 0:buckets]
    for k in range(3):
        out_copy(k).wait()
    for k in range(spare):
        clear_copy(k).wait()


def on_device(
    hashed_ids, owners, domain_tags, user_counts, lengths, buckets, table, gain_one,
    query_weight_matrix, key_weight_matrix, value_weight_matrix, attention_output_weight,
    bias_table, gain_two, feedforward_input_weight, feedforward_output_weight, cotangent,
):
    n = lax.axis_size("emb")
    seqs, length = hashed_ids.shape
    tokens = seqs * length
    rows_dev, width = table.shape
    used = 3 * (rows_dev // 4)
    cap = max(2, 2 * tokens // n)
    hd = query_weight_matrix.shape[1]
    ff = feedforward_input_weight.shape[1]
    heads = hd // DH
    pairs = heads // 2
    bucket_count = bias_table.shape[0]
    slots = n * cap
    lo = 2 ** ((n.bit_length()) // 2)
    hi = n // lo
    unit = 2 * n * 16
    w_rows = 4 * hd + 2 * ff
    w_rows = -(-w_rows // unit) * unit
    vmem = pl.BlockSpec(memory_space=pltpu.VMEM)
    smem = pl.BlockSpec(memory_space=pltpu.SMEM)
    anywhere = pl.BlockSpec(memory_space=pl.ANY)
    dma = pltpu.SemaphoreType.DMA
    shape = jax.ShapeDtypeStruct

    x_t, pos, asked = pl.pallas_call(
        functools.partial(lookup_body, n, cap, used),
        out_shape=(
            shape((width, tokens), BF16),
            shape((seqs, length), jnp.int32),
            shape((2, n, 2, LANES), jnp.int32),
        ),
        in_specs=[vmem, vmem, smem, smem, smem, anywhere],
        out_specs=(vmem, vmem, vmem),
        scratch_shapes=[
            pltpu.VMEM((n, 1, LANES), jnp.int32),
            pltpu.VMEM((n, 1, LANES), jnp.int32),
            pltpu.SMEM((n, 1, LANES), jnp.int32),
            pltpu.VMEM((used, width), BF16),
            pltpu.VMEM((used, width), F32),
            pltpu.VMEM((cap, width), F32),
            pltpu.VMEM((slots, width), BF16),
            pltpu.VMEM((slots, width), BF16),
            pltpu.VMEM((width, tokens), F32),
            dma((n,)), dma((n,)), dma((n,)), dma((n,)), dma, dma, dma((6,)), dma,
        ],
        compiler_params=pltpu.CompilerParams(
            collective_id=0, has_side_effects=True, vmem_limit_bytes=VMEM_LIMIT
        ),
        name="lookup",
    )(hashed_ids, owners.reshape(seqs, length), domain_tags, user_counts, lengths, table)

    output, input_grad, slot_grads, w_part, small_part = pl.pallas_call(
        functools.partial(block_body, 256),
        out_shape=(
            shape((seqs, length, width), BF16),
            shape((seqs, length, width), F32),
            shape((slots, width), BF16),
            shape((w_rows, width), BF16),
            shape((8, LANES), F32),
        ),
        in_specs=[smem, smem] + [vmem] * 12,
        out_specs=(vmem,) * 5,
        scratch_shapes=[
            pltpu.VMEM((3 * hd, width), BF16),
            pltpu.VMEM((width, 3 * hd), BF16),
            pltpu.VMEM((width, hd), BF16),
            pltpu.VMEM((ff, width), BF16),
            pltpu.VMEM((width, ff), BF16),
            pltpu.VMEM((length, length), F32),
            pltpu.VMEM((pairs, length, 2 * length), F32),
            pltpu.VMEM((width, tokens), BF16),
            pltpu.VMEM((3 * hd, tokens), BF16),
            pltpu.VMEM((tokens, 2 * hd), BF16),
            pltpu.VMEM((seqs, pairs, length, 2 * length), F32),
            pltpu.VMEM((hd, tokens), BF16),
            pltpu.VMEM((width, tokens), BF16),
            pltpu.VMEM((ff, tokens), BF16),
            pltpu.VMEM((ff, tokens), BF16),
            pltpu.VMEM((width, tokens), BF16),
            pltpu.VMEM((width, tokens), F32),
            pltpu.VMEM((width, tokens), BF16),
            pltpu.VMEM((hd, tokens), BF16),
            pltpu.VMEM((3 * hd, tokens), BF16),
            pltpu.VMEM((pairs, length, 2 * length), F32),
            pltpu.VMEM((width, tokens), BF16),
            pltpu.VMEM((width, length), F32),
            pltpu.VMEM((width, length), F32),
            pltpu.VMEM((heads, bucket_count, 8, length), F32),
        ],
        compiler_params=pltpu.CompilerParams(vmem_limit_bytes=VMEM_LIMIT),
        name="block",
    )(
        lengths, bias_table.T, buckets, x_t, cotangent, gain_one.reshape(1, width),
        query_weight_matrix, key_weight_matrix, value_weight_matrix, attention_output_weight,
        gain_two.reshape(1, width), feedforward_input_weight, feedforward_output_weight, pos,
    )

    incoming, w_total, small_total = pl.pallas_call(
        functools.partial(exchange_body, n, lo, cap),
        out_shape=(
            shape((2, slots, width), BF16),
            shape((w_rows, width), BF16),
            shape((8, LANES), F32),
        ),
        in_specs=[vmem] * 3,
        out_specs=(vmem,) * 3,
        scratch_shapes=[
            pltpu.VMEM((w_rows // 2, width), BF16),
            pltpu.VMEM((w_rows // 2, width), BF16),
            pltpu.VMEM((lo, w_rows // 2 // lo, width), BF16),
            pltpu.VMEM((w_rows // 2 // lo, width), BF16),
            pltpu.VMEM((hi, w_rows // 2 // n, width), BF16),
            pltpu.VMEM((2, 8, LANES), F32),
            pltpu.VMEM((lo, 8, LANES), F32),
            pltpu.VMEM((hi, 8, LANES), F32),
            dma((n,)), dma((n,)), dma((n,)), dma((n,)), dma((2,)),
            dma((lo,)), dma((lo,)), dma((hi,)), dma((hi,)), dma((2,)),
            dma((lo,)), dma((lo,)), dma((hi,)), dma((hi,)),
            dma((hi,)), dma((hi,)), dma((lo,)), dma((lo,)), dma((lo,)), dma((lo,)),
        ],
        compiler_params=pltpu.CompilerParams(
            collective_id=1, has_side_effects=True, vmem_limit_bytes=VMEM_LIMIT
        ),
        name="exchange",
    )(slot_grads, w_part, small_part)

    zero_rows = min(1024, rows_dev - used)
    table_grad, g1, gq, gk, gv, go, gb, g2, gin, gout = pl.pallas_call(
        functools.partial(scatter_body, n, cap),
        out_shape=(
            shape((rows_dev, width), F32),
            shape((1, width), F32),
            shape((width, hd), F32),
            shape((width, hd), F32),
            shape((width, hd), F32),
            shape((hd, width), F32),
            shape((heads, bucket_count), F32),
            shape((1, width), F32),
            shape((width, ff), F32),
            shape((ff, width), F32),
        ),
        in_specs=[smem, vmem, vmem, vmem],
        out_specs=(anywhere,) + (vmem,) * 9,
        scratch_shapes=[
            pltpu.VMEM((used, width), F32),
            pltpu.VMEM((slots, width), F32),
            pltpu.VMEM((zero_rows, width), F32),
            dma((3 + (rows_dev - used) // zero_rows,)),
        ],
        compiler_params=pltpu.CompilerParams(vmem_limit_bytes=VMEM_LIMIT),
        name="scatter",
    )(asked, incoming, w_total, small_total)
    return (
        output, input_grad, table_grad, g1.reshape(width), gq, gk, gv, go, gb.T, g2.reshape(width),
        gin, gout,
    )


def solution(mesh):
    split = ("emb", "dp")
    return jax.shard_map(
        on_device,
        mesh=mesh,
        in_specs=(
            P(split, None), P(split, None, None), P(split), P(), P(split, None), P(),
            P("emb", None), P(), P(), P(), P(), P(), P(), P(), P(), P(), P(split, None, None),
        ),
        out_specs=(
            P(split, None, None), P(split, None, None), P("emb", None), P(), P(), P(), P(), P(),
            P(), P(), P(), P(),
        ),
        check_vma=False,
    )
```

```python
import functools
import math

import jax
import jax.numpy as jnp
from jax import lax
from jax.experimental import pallas as pl
from jax.experimental.pallas import tpu as pltpu
from jax.sharding import PartitionSpec as P

DH = 64
LANES = 128
EPSILON = 1e-06
LIVE = 32768
MESH = pl.DeviceIdType.MESH
F32 = jnp.float32
BF16 = jnp.bfloat16
VMEM_LIMIT = 56 * 1024 * 1024


def dot_nn(a, b):
    return lax.dot_general(a, b, (((1,), (0,)), ((), ())), preferred_element_type=F32)


def dot_nt(a, b):
    return lax.dot_general(a, b, (((1,), (1,)), ((), ())), preferred_element_type=F32)


def dot_tn(a, b):
    return lax.dot_general(a, b, (((0,), (0,)), ((), ())), preferred_element_type=F32)


def hot_slots(pos, first, count):
    rows = lax.broadcasted_iota(jnp.int32, (count, LANES), 0) + first
    parts = [
        jnp.where(rows == pos[s : s + 1, :], 1.0, 0.0).astype(BF16) for s in range(pos.shape[0])
    ]
    return jnp.concatenate(parts, axis=1)


def remote(src, dst, send_sem, recv_sem, device):
    return pltpu.make_async_remote_copy(
        src_ref=src, dst_ref=dst, send_sem=send_sem, recv_sem=recv_sem,
        device_id=device, device_id_type=MESH,
    )


def gelu_parts(u):
    k0 = math.sqrt(2.0 / math.pi)
    k1 = k0 * 0.044715
    square = u * u
    half = 0.5 * jnp.tanh(u * (k1 * square + k0)) + 0.5
    value = u * half
    slope = half + (2.0 * value) * (1.0 - half) * (3.0 * k1 * square + k0)
    return value, slope


def split_pair(both):
    zero = jnp.zeros((DH, LANES), both.dtype)
    left = jnp.concatenate([both[:DH], zero], axis=0)
    right = jnp.concatenate([zero, both[DH:]], axis=0)
    return jnp.concatenate([left, right], axis=1)


class Reducer:
    def __init__(self, n, lo, me, core, part, total, bufs):
        self.n, self.lo, self.hi, self.core = n, lo, n // lo, core
        self.my_hi, self.my_lo = me // lo, lax.rem(me, lo)
        self.part, self.total = part, total
        (
            self.core_buf, self.half, self.lo_buf, self.quarter, self.hi_buf, self.core_sem,
            self.lo_sem, self.hi_sem, self.gh_sem, self.gl_sem, self.gc_sem,
        ) = bufs
        self.half_rows, self.lo_rows = self.half.shape[0], self.quarter.shape[0]
        self.hi_rows = self.hi_buf.shape[1]

    @staticmethod
    def scratch(n, lo, rows):
        hi, dma, width = n // lo, pltpu.SemaphoreType.DMA, LANES
        return [
            pltpu.VMEM((rows // 2, width), BF16),
            pltpu.VMEM((rows // 2, width), BF16),
            pltpu.VMEM((lo, rows // 2 // lo, width), BF16),
            pltpu.VMEM((rows // 2 // lo, width), BF16),
            pltpu.VMEM((hi, rows // 2 // n, width), BF16),
            dma((2,)), dma((2, lo)), dma((2, hi)), dma((2, hi)), dma((2, lo)), dma((2, lo)),
        ]

    def lo_device(self, k):
        return {"emb": self.my_hi * self.lo + self.lo_peer(k)}

    def hi_device(self, k):
        return {"emb": self.hi_peer(k) * self.lo + self.my_lo}

    def lo_peer(self, k):
        return lax.rem(self.my_lo + k, self.lo)

    def hi_peer(self, k):
        return lax.rem(self.my_hi + k, self.hi)

    def swap(self):
        at = pl.ds(pl.multiple_of((1 - self.core) * self.half_rows, self.half_rows), self.half_rows)
        return remote(
            self.part.at[at], self.core_buf, self.core_sem.at[0], self.core_sem.at[1],
            {"dp": 1 - self.core},
        )

    def lo_copy(self, k):
        at = pl.ds(pl.multiple_of(self.lo_peer(k) * self.lo_rows, self.lo_rows), self.lo_rows)
        return remote(
            self.half.at[at], self.lo_buf.at[self.lo - k],
            self.lo_sem.at[0, k], self.lo_sem.at[1, self.lo - k], self.lo_device(k),
        )

    def lo_arrival(self, k):
        return remote(
            self.quarter, self.lo_buf.at[k],
            self.lo_sem.at[0, k], self.lo_sem.at[1, k], self.lo_device(k),
        )

    def hi_copy(self, k):
        at = pl.ds(pl.multiple_of(self.hi_peer(k) * self.hi_rows, self.hi_rows), self.hi_rows)
        return remote(
            self.quarter.at[at], self.hi_buf.at[self.hi - k],
            self.hi_sem.at[0, k], self.hi_sem.at[1, self.hi - k], self.hi_device(k),
        )

    def hi_arrival(self, k):
        return remote(
            self.hi_buf.at[k], self.hi_buf.at[k],
            self.hi_sem.at[0, k], self.hi_sem.at[1, k], self.hi_device(k),
        )

    def piece(self, h):
        at = self.core * self.half_rows + self.my_lo * self.lo_rows + h * self.hi_rows
        return self.total.at[pl.ds(pl.multiple_of(at, self.hi_rows), self.hi_rows)]

    def block(self, core, low):
        at = core * self.half_rows + low * self.lo_rows
        return self.total.at[pl.ds(pl.multiple_of(at, self.lo_rows), self.lo_rows)]

    def gather_hi(self, k):
        mine = self.piece(self.my_hi)
        return remote(
            mine, mine, self.gh_sem.at[0, k], self.gh_sem.at[1, self.hi - k], self.hi_device(k)
        )

    def gather_hi_arrival(self, k):
        other = self.piece(self.hi_peer(k))
        return remote(other, other, self.gh_sem.at[0, k], self.gh_sem.at[1, k], self.hi_device(k))

    def gather_lo(self, k):
        mine = self.block(self.core, self.my_lo)
        return remote(
            mine, mine, self.gl_sem.at[0, k], self.gl_sem.at[1, self.lo - k], self.lo_device(k)
        )

    def gather_lo_arrival(self, k):
        other = self.block(self.core, self.lo_peer(k))
        return remote(other, other, self.gl_sem.at[0, k], self.gl_sem.at[1, k], self.lo_device(k))

    def gather_core(self, low):
        mine = self.block(self.core, low)
        return remote(
            mine, mine, self.gc_sem.at[0, low], self.gc_sem.at[1, low], {"dp": 1 - self.core}
        )

    def gather_core_arrival(self, low):
        other = self.block(1 - self.core, low)
        return remote(
            other, other, self.gc_sem.at[0, low], self.gc_sem.at[1, low], {"dp": 1 - self.core}
        )

    def start(self):
        self.swap().start()

    def core_to_lo(self):
        self.swap().wait()
        step = self.hi_rows

        def add(r, carry):
            at = pl.multiple_of(r * step, step)
            own = self.part[pl.ds(pl.multiple_of(self.core * self.half_rows + at, step), step), :]
            other = self.core_buf[pl.ds(at, step), :]
            self.half[pl.ds(at, step), :] = (own.astype(F32) + other.astype(F32)).astype(BF16)
            return carry

        lax.fori_loop(0, self.half_rows // step, add, 0)
        for k in range(1, self.lo):
            self.lo_copy(k).start()

    def lo_to_hi(self):
        for k in range(1, self.lo):
            self.lo_arrival(k).wait_recv()
        step = self.hi_rows

        def add(r, carry):
            at = pl.multiple_of(r * step, step)
            mine = pl.ds(pl.multiple_of(self.my_lo * self.lo_rows + at, step), step)
            total = self.half[mine, :].astype(F32)
            for k in range(1, self.lo):
                total = total + self.lo_buf[k, pl.ds(at, step), :].astype(F32)
            self.quarter[pl.ds(at, step), :] = total.astype(BF16)
            return carry

        lax.fori_loop(0, self.lo_rows // step, add, 0)
        for k in range(1, self.hi):
            self.hi_copy(k).start()

    def hi_to_gather(self):
        for k in range(1, self.hi):
            self.hi_arrival(k).wait_recv()
        mine = pl.ds(pl.multiple_of(self.my_hi * self.hi_rows, self.hi_rows), self.hi_rows)
        total = self.quarter[mine, :].astype(F32)
        for k in range(1, self.hi):
            total = total + self.hi_buf[k].astype(F32)
        self.piece(self.my_hi)[...] = total.astype(BF16)
        for k in range(1, self.hi):
            self.gather_hi(k).start()

    def gather_to_lo(self):
        for k in range(1, self.hi):
            self.gather_hi_arrival(k).wait_recv()
        for k in range(1, self.lo):
            self.gather_lo(k).start()
        self.gather_core(self.my_lo).start()

    def gather_to_core(self):
        for k in range(1, self.lo):
            self.gather_lo_arrival(k).wait_recv()
            self.gather_core(self.lo_peer(k)).start()

    def finish(self):
        for low in range(self.lo):
            self.gather_core_arrival(low).wait_recv()
        for k in range(1, self.lo):
            self.lo_copy(k).wait_send()
            self.gather_lo(k).wait_send()
        for k in range(1, self.hi):
            self.hi_copy(k).wait_send()
            self.gather_hi(k).wait_send()
        for low in range(self.lo):
            self.gather_core(low).wait_send()


class SmallReducer:
    def __init__(self, n, lo, me, core, total, bufs):
        self.lo, self.hi, self.core = lo, n // lo, core
        self.my_hi, self.my_lo = me // lo, lax.rem(me, lo)
        self.total = total
        self.a, self.b, self.c, self.a_sem, self.b_sem, self.c_sem = bufs

    @staticmethod
    def scratch(n, lo):
        hi, dma = n // lo, pltpu.SemaphoreType.DMA
        return [
            pltpu.VMEM((2, 8, LANES), F32),
            pltpu.VMEM((lo, 8, LANES), F32),
            pltpu.VMEM((hi, 8, LANES), F32),
            dma((2,)), dma((2, lo)), dma((2, hi)),
        ]

    def swap(self, slot):
        ref = self.a.at[slot]
        return remote(ref, ref, self.a_sem.at[0], self.a_sem.at[1], {"dp": 1 - self.core})

    def lo_copy(self, k, slot, come):
        device = {"emb": self.my_hi * self.lo + lax.rem(self.my_lo + k, self.lo)}
        ref = self.b.at[slot]
        return remote(ref, ref, self.b_sem.at[0, k], self.b_sem.at[1, come], device)

    def hi_copy(self, k, slot, come):
        device = {"emb": lax.rem(self.my_hi + k, self.hi) * self.lo + self.my_lo}
        ref = self.c.at[slot]
        return remote(ref, ref, self.c_sem.at[0, k], self.c_sem.at[1, come], device)

    def start(self, value):
        self.a[self.core] = value
        self.swap(self.core).start()

    def core_to_lo(self):
        self.swap(self.core).wait_send()
        self.swap(1 - self.core).wait_recv()
        self.b[self.my_lo] = self.a[0] + self.a[1]
        for k in range(1, self.lo):
            self.lo_copy(k, self.my_lo, self.lo - k).start()

    def lo_to_hi(self):
        for k in range(1, self.lo):
            self.lo_copy(k, lax.rem(self.my_lo + k, self.lo), k).wait_recv()
        total = self.b[0]
        for k in range(1, self.lo):
            total = total + self.b[k]
        self.c[self.my_hi] = total
        for k in range(1, self.hi):
            self.hi_copy(k, self.my_hi, self.hi - k).start()

    def finish(self):
        for k in range(1, self.hi):
            self.hi_copy(k, lax.rem(self.my_hi + k, self.hi), k).wait_recv()
        total = self.c[0]
        for k in range(1, self.hi):
            total = total + self.c[k]
        self.total[...] = total
        for k in range(1, self.lo):
            self.lo_copy(k, self.my_lo, self.lo - k).wait_send()
        for k in range(1, self.hi):
            self.hi_copy(k, self.my_hi, self.hi - k).wait_send()


def step_body(
    n, lo, cap, used, refs_in, refs_out, lookup_refs, block_refs, early_refs, late_refs, small_refs,
):
    (
        ids, own, tags, counts, lens, btab, table, buckets, cot, g1, wq, wk, wv, wo, g2, win, wout,
    ) = refs_in
    y_out, ig_out, inc, asked_out, early_tot, late_tot, small_tot = refs_out
    (
        req, asked_v, asked_s, tab_low, tab, gbuf, send, recv, x_acc, pos_ref, slots, early, late,
        req_send, req_recv, row_send, row_recv, pair_sem, tab_sem, smem_sem,
        grad_send, grad_recv, fwd_send, fwd_recv,
    ) = lookup_refs
    (
        wqkv_t, wqkv, wo_t, win_t, wout_t, buck_t, bias, x_t, a_t, qkv_t, kv, p_s, o_t, c_t, act_t,
        du_t, dy_t, dm_t, dmb_t, do_t, dqkv_t, dsum, igb_t, b_acc,
    ) = block_refs
    me = lax.axis_index("emb")
    core = lax.axis_index("dp")
    seqs, length = ids.shape
    width = cot.shape[2]
    tokens = seqs * length
    hd, ff = wq.shape[1], win.shape[1]
    heads = hd // DH
    pairs = heads // 2
    bucket_count = btab.shape[1]
    domain_rows = used // 3
    pieces = tab_sem.shape[0]
    piece = used // pieces
    group = 4
    wide_slots = 256
    early_sum = Reducer(n, lo, me, core, early, early_tot, early_refs)
    late_sum = Reducer(n, lo, me, core, late, late_tot, late_refs)
    small_sum = SmallReducer(n, lo, me, core, small_tot, small_refs)

    barrier = pltpu.get_barrier_semaphore()

    def peer(j):
        return {"emb": lax.rem(me + j, n)}

    def greet(k, carry):
        pl.semaphore_signal(barrier, inc=1, device_id=peer(k), device_id_type=MESH)
        return carry

    lax.fori_loop(1, n, greet, 0)
    pl.semaphore_signal(barrier, inc=1, device_id={"dp": 1 - core}, device_id_type=MESH)

    def table_copy(c):
        part = pl.ds(c * piece, piece)
        return pltpu.make_async_copy(table.at[part], tab_low.at[part], tab_sem.at[c])

    for c in range(pieces):
        table_copy(c).start()

    row_id = lax.broadcasted_iota(jnp.int32, (seqs, length), 0)
    lane_id = lax.broadcasted_iota(jnp.int32, (seqs, length), 1)
    count_of = jnp.ones((seqs, length), F32)
    tag_of = jnp.zeros((seqs, length), jnp.int32)
    len_of = jnp.zeros((seqs, length), jnp.int32)
    for s in range(seqs):
        tag = tags[s]
        count_of = jnp.where(row_id == s, counts[tag].astype(F32), count_of)
        tag_of = jnp.where(row_id == s, tag, tag_of)
        len_of = jnp.where(row_id == s, lens[0, s], len_of)
    code = ids[...].astype(F32)
    turns = jnp.floor((code + 0.5) / jnp.maximum(count_of, 1.0))
    local = tag_of * domain_rows + (code - turns * count_of).astype(jnp.int32)
    live = lane_id < len_of
    rel = own[...] - me
    rel = jnp.where(rel < 0, rel + n, rel)

    owner_id = lax.broadcasted_iota(jnp.int32, (n, length), 0)
    hot_live, hot_dead = [], []
    for s in range(seqs):
        hot = owner_id == rel[s : s + 1, :]
        alive = jnp.broadcast_to(live[s : s + 1, :].astype(F32), (n, length))
        hot_live.append(jnp.where(hot, alive, 0.0))
        hot_dead.append(jnp.where(hot, 1.0 - alive, 0.0))
    both = jnp.concatenate(hot_live + hot_dead, axis=0).astype(BF16)
    before = (
        lax.broadcasted_iota(jnp.int32, (length, length), 0)
        < lax.broadcasted_iota(jnp.int32, (length, length), 1)
    )
    prefix = dot_nn(both, jnp.where(before, 1.0, 0.0).astype(BF16))
    running = jnp.zeros((n, 1), F32)
    ranks = []
    for part, hots in enumerate((hot_live, hot_dead)):
        for s in range(seqs):
            at = (part * seqs + s) * n
            ranks.append(
                jnp.sum(hots[s] * (prefix[at : at + n] + running), axis=0, keepdims=True)
            )
            running = running + jnp.sum(hots[s], axis=1, keepdims=True)
    rank = jnp.concatenate([ranks[s] + ranks[seqs + s] for s in range(seqs)], axis=0)
    rank = rank.astype(jnp.int32)
    pos_ref[...] = rel * cap + rank

    low = (local & 255).astype(F32)
    high = (lax.shift_right_logical(local, 8) + jnp.where(live, LIVE // 256, 0)).astype(F32)
    slot_id = lax.broadcasted_iota(jnp.int32, (LANES, length), 0)
    asking = jnp.zeros((2 * n, LANES), F32)
    for s in range(seqs):
        hot = hot_live[s] + hot_dead[s]
        values = jnp.concatenate([hot * high[s : s + 1, :], hot * low[s : s + 1, :]], axis=0)
        slot_hot = jnp.where(slot_id == rank[s : s + 1, :], 1.0, 0.0).astype(BF16)
        asking = asking + dot_nt(values.astype(BF16), slot_hot)
    wanted = (asking[:n] * 256.0 + asking[n:]).astype(jnp.int32)
    for j in range(n):
        req[j] = wanted[j : j + 1, :]

    pl.semaphore_wait(barrier, n)

    def request(j):
        back = lax.rem(n - j, n)
        return remote(req.at[j], asked_v.at[back], req_send.at[j], req_recv.at[back], peer(j))

    def request_arrival(j):
        return remote(req.at[j], asked_v.at[j], req_send.at[j], req_recv.at[j], peer(j))

    def ask(j, carry):
        request(j).start()
        return carry

    lax.fori_loop(1, n, ask, 0)
    asked_v[0] = req[0]

    for c in range(pieces):
        table_copy(c).wait()

        def widen(r, carry):
            part = pl.ds(pl.multiple_of(c * piece + r * 256, 256), 256)
            tab[part, :] = tab_low[part, :].astype(F32)
            return carry

        lax.fori_loop(0, piece // 256, widen, 0)

    def all_asked(j, carry):
        request_arrival(j).wait_recv()
        return carry

    lax.fori_loop(1, n, all_asked, 0)
    to_scalar = pltpu.make_async_copy(asked_v, asked_s, smem_sem)
    to_scalar.start()
    to_scalar.wait()

    def slot_block(j):
        return pl.ds(pl.multiple_of(j * cap, cap), cap)

    def row_copy(j):
        back = lax.rem(n - j, n)
        return remote(
            send.at[slot_block(j)], recv.at[slot_block(back)],
            row_send.at[j], row_recv.at[back], peer(j),
        )

    def row_arrival(j):
        at = slot_block(j)
        return remote(send.at[at], recv.at[at], row_send.at[j], row_recv.at[j], peer(j))

    def gather(j):
        def eight(c, carry):
            for r in range(8):
                at = jnp.minimum(asked_s[j, 0, c * 8 + r] & (LIVE - 1), used - 1)
                gbuf[pl.ds(c * 8 + r, 1), :] = tab[pl.ds(at, 1), :]
            return carry

        lax.fori_loop(0, cap // 8, eight, 0)
        return gbuf[...].astype(BF16)

    def serve(j, carry):
        send[slot_block(j), :] = gather(j)
        row_copy(j).start()
        return carry

    lax.fori_loop(1, n, serve, 0)
    recv[0:cap, :] = gather(0)

    def tally(j, carry):
        values = asked_v[j]
        asked_out[core, j, 0:1] = values
        number = jnp.sum(jnp.where(values >= LIVE, 1.0, 0.0), axis=1, keepdims=True)
        asked_out[core, j, 1:2] = jnp.broadcast_to(number.astype(jnp.int32), (1, LANES))
        return carry

    lax.fori_loop(0, n, tally, 0)

    def share(which):
        ref = asked_out.at[which]
        return remote(ref, ref, pair_sem.at[0], pair_sem.at[1], {"dp": 1 - core})

    share(core).start()
    for part, w in enumerate((wq, wk, wv)):
        wqkv[:, part * hd : (part + 1) * hd] = w[...]
        wqkv_t[part * hd : (part + 1) * hd, :] = w[...].T
    wo_t[...] = wo[...].T
    win_t[...] = win[...].T
    wout_t[...] = wout[...].T
    buck_t[...] = buckets[...].astype(F32).T
    g1_col = jnp.broadcast_to(g1[...], (8, width)).T[:, 0:1]
    g2_col = jnp.broadcast_to(g2[...], (8, width)).T[:, 0:1]
    dsum[...] = jnp.zeros_like(dsum)
    b_acc[...] = jnp.zeros_like(b_acc)

    def bias_rows(r, carry):
        part = pl.ds(pl.multiple_of(r * 8, 8), 8)
        bt = buck_t[part, :]
        rows = [jnp.zeros((8, length), F32) for _ in range(heads)]
        for b in range(bucket_count):
            here = bt == float(b)
            rows = [jnp.where(here, btab[h, b], rows[h]) for h in range(heads)]
        for p in range(pairs):
            bias[p, part, :] = jnp.concatenate(rows[2 * p : 2 * p + 2], axis=1)
        return carry

    lax.fori_loop(0, length // 8, bias_rows, 0)

    def load_dy(s, carry):
        part = pl.ds(pl.multiple_of(s * length, length), length)
        alive = lax.broadcasted_iota(jnp.int32, (width, length), 1) < lens[0, s]
        dy_t[:, part] = jnp.where(alive, cot[s].astype(F32).T, 0.0).astype(BF16)
        return carry

    lax.fori_loop(0, seqs, load_dy, 0)

    def place(pair, carry):
        def ready(j, inner):
            row_arrival(j).wait_recv()
            return inner

        lax.fori_loop(jnp.maximum(2 * pair, 1), 2 * pair + 2, ready, 0)
        first = pl.multiple_of(pair * 2 * cap, 2 * cap)
        hot = hot_slots(pos_ref[...], first, 2 * cap)
        got = dot_tn(recv[pl.ds(first, 2 * cap), :], hot)

        @pl.when(pair == 0)
        def _():
            x_acc[...] = got

        @pl.when(pair > 0)
        def _():
            x_acc[...] += got

        return carry

    lax.fori_loop(0, n // 2, place, 0)
    x_t[...] = x_acc[...].astype(BF16)

    xf = x_acc[...]
    scale = lax.rsqrt(jnp.mean(xf * xf, axis=0, keepdims=True) + EPSILON)
    a = (xf * scale * g1_col).astype(BF16)
    a_t[...] = a
    out = dot_nn(wqkv_t[...], a)
    qkv_t[0:hd, :] = out[:hd].astype(BF16) * jnp.array(1.0 / math.sqrt(DH), BF16)
    qkv_t[hd:, :] = out[hd:].astype(BF16)
    kv[...] = dot_nn(a.T, wqkv[:, hd:]).astype(BF16)

    rows = [slice(p * 2 * DH, (p + 1) * 2 * DH) for p in range(pairs)]
    krows = [slice(hd + p * 2 * DH, hd + (p + 1) * 2 * DH) for p in range(pairs)]
    vrows = [slice(2 * hd + p * 2 * DH, 2 * hd + (p + 1) * 2 * DH) for p in range(pairs)]
    jobs = [(i, p) for i in range(group) for p in range(pairs)]

    def members(g):
        return [pl.ds(pl.multiple_of((g * group + i) * length, length), length) for i in range(group)]

    def attend(g, carry):
        parts = members(g)
        key_id = lax.broadcasted_iota(jnp.int32, (length, 2 * length), 0)
        visible = [key_id < lens[0, g * group + i] for i in range(group)]
        scores = [
            dot_nn(kv[parts[i], rows[p]], split_pair(qkv_t[rows[p], parts[i]])) for i, p in jobs
        ]
        probs = []
        for (i, p), score in zip(jobs, scores):
            score = jnp.where(visible[i], score + bias[p], -1000000000.0)
            expo = jnp.exp(score - jnp.max(score, axis=0, keepdims=True))
            prob = expo * (1.0 / jnp.sum(expo, axis=0, keepdims=True))
            p_s[g * group + i, p] = prob
            probs.append(prob.astype(BF16))
        for (i, p), prob in zip(jobs, probs):
            mixed = dot_nn(qkv_t[vrows[p], parts[i]], prob)
            o_t[rows[p], parts[i]] = jnp.concatenate(
                [mixed[:DH, :length], mixed[DH:, length:]], axis=0
            ).astype(BF16)
        return carry

    lax.fori_loop(0, seqs // group, attend, 0)

    m = x_t[...].astype(F32) + dot_nn(wo_t[...], o_t[...])
    scale = lax.rsqrt(jnp.mean(m * m, axis=0, keepdims=True) + EPSILON)
    z = m * scale
    normed = (z * g2_col).astype(BF16)
    c_t[...] = normed
    value, slope = gelu_parts(dot_nn(win_t[...], normed))
    act = value.astype(BF16)
    act_t[...] = act
    du = (dot_nn(wout[...], dy_t[...]) * slope).astype(BF16)
    du_t[...] = du
    y = m + dot_nn(wout_t[...], act)
    for s in range(seqs):
        y_out[s] = y[:, s * length : (s + 1) * length].T.astype(BF16)
    dc = dot_nn(win[...], du)
    gain_two = dc * z
    gain_two = sum(gain_two[:, s * length : (s + 1) * length] for s in range(seqs))
    small_tot[1:2, :] = jnp.sum(gain_two.T, axis=0, keepdims=True)
    e = dc * g2_col
    dm = dy_t[...].astype(F32) + scale * (e - z * jnp.mean(e * z, axis=0, keepdims=True))
    dm_t[...] = dm
    dmb = dm.astype(BF16)
    dmb_t[...] = dmb
    do_t[...] = dot_nn(wo[...], dmb).astype(BF16)

    for k in range(ff // width):
        at = slice(k * width, (k + 1) * width)
        early[at, :] = dot_nt(c_t[...], du_t[at, :]).astype(BF16)
    early[ff : 2 * ff, :] = dot_nt(act_t[...], dy_t[...]).astype(BF16)
    if early.shape[0] > 2 * ff:
        early[2 * ff :, :] = jnp.zeros((early.shape[0] - 2 * ff, width), BF16)
    early_sum.start()

    def attend_back(g):
        parts = members(g)
        do2s = [split_pair(do_t[rows[p], parts[i]]) for i, p in jobs]
        dprobs = [dot_nn(kv[parts[i], krows[p]], do2) for (i, p), do2 in zip(jobs, do2s)]
        lows = []
        for (i, p), dprob in zip(jobs, dprobs):
            prob = p_s[g * group + i, p]
            ds = prob * (dprob - jnp.sum(dprob * prob, axis=0, keepdims=True))
            dsum[p] += ds
            lows.append(ds.astype(BF16))
        for (i, p), do2 in zip(jobs, do2s):
            prob = p_s[g * group + i, p].astype(BF16)
            dqkv_t[vrows[p], parts[i]] = dot_nt(do2, prob).astype(BF16)
        for (i, p), low in zip(jobs, lows):
            q2 = split_pair(qkv_t[rows[p], parts[i]])
            dqkv_t[krows[p], parts[i]] = dot_nt(q2, low).astype(BF16)
        for (i, p), low in zip(jobs, lows):
            dq = dot_nn(qkv_t[krows[p], parts[i]], low) * (1.0 / math.sqrt(DH))
            dqkv_t[rows[p], parts[i]] = jnp.concatenate(
                [dq[:DH, :length], dq[DH:, length:]], axis=0
            ).astype(BF16)

    groups = seqs // group

    def back_loop(g, carry):
        attend_back(g)

        @pl.when(g == 0)
        def _():
            early_sum.core_to_lo()

        return carry

    lax.fori_loop(0, groups, back_loop, 0)

    xf = x_t[...].astype(F32)
    scale = lax.rsqrt(jnp.mean(xf * xf, axis=0, keepdims=True) + EPSILON)
    z = xf * scale
    da = dot_nn(wqkv[...], dqkv_t[...])
    gain_one = da * z
    gain_one = sum(gain_one[:, s * length : (s + 1) * length] for s in range(seqs))
    e = da * g1_col
    ig = dm_t[...] + scale * (e - z * jnp.mean(e * z, axis=0, keepdims=True))
    igb_t[...] = ig.astype(BF16)

    def grad_copy(j):
        back = lax.rem(n - j, n)
        return remote(
            slots.at[slot_block(j)], inc.at[core, slot_block(back)],
            grad_send.at[j], grad_recv.at[back], peer(j),
        )

    def grad_arrival(j):
        return remote(
            slots.at[slot_block(j)], inc.at[core, slot_block(j)],
            grad_send.at[j], grad_recv.at[j], peer(j),
        )

    def forward(j, which):
        ref = inc.at[which, slot_block(j)]
        return remote(ref, ref, fwd_send.at[j], fwd_recv.at[j], {"dp": 1 - core})

    def to_slots(k, carry):
        first = pl.multiple_of(k * wide_slots, wide_slots)
        slots[pl.ds(first, wide_slots), :] = dot_nt(
            hot_slots(pos_ref[...], first, wide_slots), igb_t[...]
        ).astype(BF16)

        def go(j, inner):
            grad_copy(j).start()
            return inner

        owners = wide_slots // cap
        lax.fori_loop(jnp.maximum(k * owners, 1), (k + 1) * owners, go, 0)
        return carry

    lax.fori_loop(0, slots.shape[0] // wide_slots, to_slots, 0)
    inc[core, 0:cap, :] = slots[0:cap, :]
    forward(0, core).start()
    early_sum.lo_to_hi()

    for k in range(3 * hd // width):
        at = slice(k * width, (k + 1) * width)
        late[at, :] = dot_nt(a_t[...], dqkv_t[at, :]).astype(BF16)
    late[3 * hd : 4 * hd, :] = dot_nt(o_t[...], dmb_t[...]).astype(BF16)
    if late.shape[0] > 4 * hd:
        late[4 * hd :, :] = jnp.zeros((late.shape[0] - 4 * hd, width), BF16)
    late_sum.start()

    for s in range(seqs):
        ig_out[s] = ig[:, s * length : (s + 1) * length].T

    def bias_back(r, carry):
        part = pl.ds(pl.multiple_of(r * 8, 8), 8)
        bt = buck_t[part, :]
        grads = [dsum[h // 2, part, (h % 2) * length : (h % 2 + 1) * length] for h in range(heads)]
        for b in range(bucket_count):
            here = bt == float(b)
            for h in range(heads):
                b_acc[h, b] += jnp.where(here, grads[h], 0.0)
        return carry

    lax.fori_loop(0, length // 8, bias_back, 0)
    late_sum.core_to_lo()
    early_sum.hi_to_gather()
    small_parts = [jnp.sum(gain_one.T, axis=0, keepdims=True), small_tot[1:2, :]]
    for h in range(heads):
        by_bucket = jnp.sum(b_acc[h], axis=1)
        row = jnp.sum(by_bucket.T, axis=0, keepdims=True)
        small_parts.append(
            jnp.concatenate([row, jnp.zeros((1, LANES - bucket_count), F32)], axis=1)
        )
    small_sum.start(jnp.concatenate(small_parts, axis=0))
    early_sum.gather_to_lo()

    def pass_on(j, carry):
        grad_arrival(j).wait_recv()
        forward(j, core).start()
        return carry

    small_sum.core_to_lo()
    late_sum.lo_to_hi()
    lax.fori_loop(1, n // 2, pass_on, 0)
    small_sum.lo_to_hi()
    late_sum.hi_to_gather()
    early_sum.gather_to_core()
    late_sum.gather_to_lo()
    lax.fori_loop(n // 2, n, pass_on, 0)
    late_sum.gather_to_core()
    small_sum.finish()
    early_sum.finish()
    late_sum.finish()

    def rows_in(j, carry):
        forward(j, 1 - core).wait_recv()
        forward(j, core).wait_send()
        return carry

    lax.fori_loop(0, n, rows_in, 0)

    def sent(j, carry):
        request(j).wait_send()
        row_copy(j).wait_send()
        grad_copy(j).wait_send()
        return carry

    lax.fori_loop(1, n, sent, 0)
    share(core).wait_send()
    share(1 - core).wait_recv()


def step_kernel(n, lo, cap, used, sizes, *refs):
    parts, at = [], 0
    for size in sizes:
        parts.append(refs[at : at + size])
        at += size
    step_body(n, lo, cap, used, *parts)


def scatter_body(
    n, cap, asked, inc, early, late, small, y_in, ig_in,
    y_out, ig_out, grad, g1, wq, wk, wv, wo, bias, g2, win, wout,
    acc, wide, zero, out_sem, pass_sem,
):
    through = [
        pltpu.make_async_copy(y_in, y_out, pass_sem.at[0]),
        pltpu.make_async_copy(ig_in, ig_out, pass_sem.at[1]),
    ]
    for copy in through:
        copy.start()
    used = acc.shape[0]
    rows_dev = grad.shape[0]
    zero_rows = zero.shape[0]
    zero[...] = jnp.zeros_like(zero)

    def clear_copy(k):
        return pltpu.make_async_copy(
            zero, grad.at[pl.ds(used + k * zero_rows, zero_rows)], out_sem.at[3 + k]
        )

    spare = (rows_dev - used) // zero_rows
    for k in range(spare):
        clear_copy(k).start()

    def clear(r, carry):
        acc[pl.ds(pl.multiple_of(r * 256, 256), 256), :] = jnp.zeros((256, acc.shape[1]), F32)
        return carry

    lax.fori_loop(0, used // 256, clear, 0)

    for c in range(2):
        def source(j, carry):
            part = pl.ds(pl.multiple_of(j * cap, cap), cap)
            wide[part, :] = inc[c, part, :].astype(F32)

            def eight(k, inner):
                for r in range(8):
                    at = asked[c, j, 0, k * 8 + r] & (LIVE - 1)
                    acc[pl.ds(at, 1), :] += wide[pl.ds(j * cap + k * 8 + r, 1), :]
                return inner

            lax.fori_loop(0, (asked[c, j, 1, 0] + 7) // 8, eight, 0)
            return carry

        lax.fori_loop(0, n, source, 0)

    third = used // 3

    def out_copy(k):
        part = pl.ds(k * third, third)
        return pltpu.make_async_copy(acc.at[part], grad.at[part], out_sem.at[k])

    for k in range(3):
        out_copy(k).start()

    width = wq.shape[0]
    hd = wq.shape[1]
    ff = win.shape[1]
    for i, ref in enumerate((wq, wk, wv)):
        for k in range(hd // width):
            at = i * hd + k * width
            ref[:, k * width : (k + 1) * width] = late[at : at + width, :].astype(F32)
    wo[...] = late[3 * hd : 4 * hd, :].astype(F32)
    for k in range(ff // width):
        at = slice(k * width, (k + 1) * width)
        win[:, at] = early[at, :].astype(F32)
    wout[...] = early[ff : 2 * ff, :].astype(F32)
    g1[...] = small[0:1, :]
    g2[...] = small[1:2, :]
    heads, buckets = bias.shape
    bias[...] = small[2 : 2 + heads, 0:buckets]
    for k in range(3):
        out_copy(k).wait()
    for k in range(spare):
        clear_copy(k).wait()
    for copy in through:
        copy.wait()


def on_device(
    hashed_ids, owners, domain_tags, user_counts, lengths, buckets, table, gain_one,
    query_weight_matrix, key_weight_matrix, value_weight_matrix, attention_output_weight,
    bias_table, gain_two, feedforward_input_weight, feedforward_output_weight, cotangent,
):
    n = lax.axis_size("emb")
    seqs, length = hashed_ids.shape
    tokens = seqs * length
    rows_dev, width = table.shape
    used = 3 * (rows_dev // 4)
    cap = max(2, 2 * tokens // n)
    hd = query_weight_matrix.shape[1]
    ff = feedforward_input_weight.shape[1]
    heads = hd // DH
    pairs = heads // 2
    bucket_count = bias_table.shape[0]
    slots = n * cap
    lo = 2 ** ((n.bit_length()) // 2)
    unit = 2 * n * 16
    early_rows = -(-2 * ff // unit) * unit
    late_rows = -(-4 * hd // unit) * unit
    vmem = pl.BlockSpec(memory_space=pltpu.VMEM)
    smem = pl.BlockSpec(memory_space=pltpu.SMEM)
    anywhere = pl.BlockSpec(memory_space=pl.ANY)
    dma = pltpu.SemaphoreType.DMA
    shape = jax.ShapeDtypeStruct

    operands = (
        hashed_ids, owners.reshape(seqs, length), domain_tags, user_counts, lengths, bias_table.T,
        table, buckets, cotangent, gain_one.reshape(1, width), query_weight_matrix,
        key_weight_matrix, value_weight_matrix, attention_output_weight,
        gain_two.reshape(1, width), feedforward_input_weight, feedforward_output_weight,
    )
    results = (
        shape((seqs, length, width), BF16),
        shape((seqs, length, width), F32),
        shape((2, slots, width), BF16),
        shape((2, n, 2, LANES), jnp.int32),
        shape((early_rows, width), BF16),
        shape((late_rows, width), BF16),
        shape((8, LANES), F32),
    )
    lookup_scratch = [
        pltpu.VMEM((n, 1, LANES), jnp.int32),
        pltpu.VMEM((n, 1, LANES), jnp.int32),
        pltpu.SMEM((n, 1, LANES), jnp.int32),
        pltpu.VMEM((used, width), BF16),
        pltpu.VMEM((used, width), F32),
        pltpu.VMEM((cap, width), F32),
        pltpu.VMEM((slots, width), BF16),
        pltpu.VMEM((slots, width), BF16),
        pltpu.VMEM((width, tokens), F32),
        pltpu.VMEM((seqs, length), jnp.int32),
        pltpu.VMEM((slots, width), BF16),
        pltpu.VMEM((early_rows, width), BF16),
        pltpu.VMEM((late_rows, width), BF16),
        dma((n,)), dma((n,)), dma((n,)), dma((n,)), dma((2,)), dma((6,)), dma,
        dma((n,)), dma((n,)), dma((n,)), dma((n,)),
    ]
    block_scratch = [
        pltpu.VMEM((3 * hd, width), BF16),
        pltpu.VMEM((width, 3 * hd), BF16),
        pltpu.VMEM((width, hd), BF16),
        pltpu.VMEM((ff, width), BF16),
        pltpu.VMEM((width, ff), BF16),
        pltpu.VMEM((length, length), F32),
        pltpu.VMEM((pairs, length, 2 * length), F32),
        pltpu.VMEM((width, tokens), BF16),
        pltpu.VMEM((width, tokens), BF16),
        pltpu.VMEM((3 * hd, tokens), BF16),
        pltpu.VMEM((tokens, 2 * hd), BF16),
        pltpu.VMEM((seqs, pairs, length, 2 * length), F32),
        pltpu.VMEM((hd, tokens), BF16),
        pltpu.VMEM((width, tokens), BF16),
        pltpu.VMEM((ff, tokens), BF16),
        pltpu.VMEM((ff, tokens), BF16),
        pltpu.VMEM((width, tokens), BF16),
        pltpu.VMEM((width, tokens), F32),
        pltpu.VMEM((width, tokens), BF16),
        pltpu.VMEM((hd, tokens), BF16),
        pltpu.VMEM((3 * hd, tokens), BF16),
        pltpu.VMEM((pairs, length, 2 * length), F32),
        pltpu.VMEM((width, tokens), BF16),
        pltpu.VMEM((heads, bucket_count, 8, length), F32),
    ]
    early_scratch = Reducer.scratch(n, lo, early_rows)
    late_scratch = Reducer.scratch(n, lo, late_rows)
    small_scratch = SmallReducer.scratch(n, lo)
    scratch = [lookup_scratch, block_scratch, early_scratch, late_scratch, small_scratch]
    sizes = [len(operands), len(results)] + [len(part) for part in scratch]
    y, ig, incoming, asked, early_total, late_total, small_total = pl.pallas_call(
        functools.partial(step_kernel, n, lo, cap, used, sizes),
        out_shape=results,
        in_specs=[vmem, vmem, smem, smem, smem, smem, anywhere] + [vmem] * 10,
        out_specs=(vmem,) * len(results),
        scratch_shapes=sum(scratch, []),
        compiler_params=pltpu.CompilerParams(
            collective_id=0, has_side_effects=True, vmem_limit_bytes=VMEM_LIMIT
        ),
        name="step",
    )(*operands)

    zero_rows = min(1024, rows_dev - used)
    output, input_grad, table_grad, g1, gq, gk, gv, go, gb, g2, gin, gout = pl.pallas_call(
        functools.partial(scatter_body, n, cap),
        out_shape=(
            shape((seqs, length, width), BF16),
            shape((seqs, length, width), F32),
            shape((rows_dev, width), F32),
            shape((1, width), F32),
            shape((width, hd), F32),
            shape((width, hd), F32),
            shape((width, hd), F32),
            shape((hd, width), F32),
            shape((heads, bucket_count), F32),
            shape((1, width), F32),
            shape((width, ff), F32),
            shape((ff, width), F32),
        ),
        in_specs=[smem] + [vmem] * 6,
        out_specs=(anywhere,) * 3 + (vmem,) * 9,
        scratch_shapes=[
            pltpu.VMEM((used, width), F32),
            pltpu.VMEM((slots, width), F32),
            pltpu.VMEM((zero_rows, width), F32),
            dma((3 + (rows_dev - used) // zero_rows,)),
            dma((2,)),
        ],
        compiler_params=pltpu.CompilerParams(vmem_limit_bytes=VMEM_LIMIT),
        name="scatter",
    )(asked, incoming, early_total, late_total, small_total, y, ig)
    return (
        output, input_grad, table_grad, g1.reshape(width), gq, gk, gv, go, gb.T, g2.reshape(width),
        gin, gout,
    )


def solution(mesh):
    split = ("emb", "dp")
    return jax.shard_map(
        on_device,
        mesh=mesh,
        in_specs=(
            P(split, None), P(split, None, None), P(split), P(), P(split, None), P(),
            P("emb", None), P(), P(), P(), P(), P(), P(), P(), P(), P(), P(split, None, None),
        ),
        out_specs=(
            P(split, None, None), P(split, None, None), P("emb", None), P(), P(), P(), P(), P(),
            P(), P(), P(), P(),
        ),
        check_vma=False,
    )
```

```python
import functools
import math

import jax
import jax.numpy as jnp
from jax import lax
from jax.experimental import pallas as pl
from jax.experimental.pallas import tpu as pltpu
from jax.sharding import PartitionSpec as P

DH = 64
LANES = 128
EPSILON = 1e-06
MESH = pl.DeviceIdType.MESH
F32 = jnp.float32
BF16 = jnp.bfloat16
VMEM_LIMIT = 56 * 1024 * 1024


def dot_nn(a, b):
    return lax.dot_general(a, b, (((1,), (0,)), ((), ())), preferred_element_type=F32)


def dot_nt(a, b):
    return lax.dot_general(a, b, (((1,), (1,)), ((), ())), preferred_element_type=F32)


def dot_tn(a, b):
    return lax.dot_general(a, b, (((0,), (0,)), ((), ())), preferred_element_type=F32)


def hot_slots(pos, first, count):
    rows = lax.broadcasted_iota(jnp.int32, (count, LANES), 0) + first
    parts = [
        jnp.where(rows == pos[s : s + 1, :], 1.0, 0.0).astype(BF16) for s in range(pos.shape[0])
    ]
    return jnp.concatenate(parts, axis=1)


def remote(src, dst, send_sem, recv_sem, device):
    return pltpu.make_async_remote_copy(
        src_ref=src, dst_ref=dst, send_sem=send_sem, recv_sem=recv_sem,
        device_id=device, device_id_type=MESH,
    )


def gelu_parts(u):
    k0 = math.sqrt(2.0 / math.pi)
    k1 = k0 * 0.044715
    square = u * u
    half = 0.5 * jnp.tanh(u * (k1 * square + k0)) + 0.5
    value = u * half
    slope = half + (2.0 * value) * (1.0 - half) * (3.0 * k1 * square + k0)
    return value, slope


def split_pair(both):
    zero = jnp.zeros((DH, LANES), both.dtype)
    left = jnp.concatenate([both[:DH], zero], axis=0)
    right = jnp.concatenate([zero, both[DH:]], axis=0)
    return jnp.concatenate([left, right], axis=1)


class Reducer:
    def __init__(self, n, lo, me, core, part, total, bufs):
        self.n, self.lo, self.hi, self.core = n, lo, n // lo, core
        self.my_hi, self.my_lo = me // lo, lax.rem(me, lo)
        self.part, self.total = part, total
        (
            self.core_buf, self.half, self.lo_buf, self.quarter, self.hi_buf, self.core_sem,
            self.lo_sem, self.hi_sem, self.gh_sem, self.gl_sem, self.gc_sem,
        ) = bufs
        self.half_rows, self.lo_rows = self.half.shape[0], self.quarter.shape[0]
        self.hi_rows = self.hi_buf.shape[1]

    @staticmethod
    def scratch(n, lo, rows):
        hi, dma, width = n // lo, pltpu.SemaphoreType.DMA, LANES
        return [
            pltpu.VMEM((rows // 2, width), BF16),
            pltpu.VMEM((rows // 2, width), BF16),
            pltpu.VMEM((lo, rows // 2 // lo, width), BF16),
            pltpu.VMEM((rows // 2 // lo, width), BF16),
            pltpu.VMEM((hi, rows // 2 // n, width), BF16),
            dma((2,)), dma((2, lo)), dma((2, hi)), dma((2, hi)), dma((2, lo)), dma((2, lo)),
        ]

    def lo_device(self, k):
        return {"emb": self.my_hi * self.lo + self.lo_peer(k)}

    def hi_device(self, k):
        return {"emb": self.hi_peer(k) * self.lo + self.my_lo}

    def lo_peer(self, k):
        return lax.rem(self.my_lo + k, self.lo)

    def hi_peer(self, k):
        return lax.rem(self.my_hi + k, self.hi)

    def swap(self):
        at = pl.ds(pl.multiple_of((1 - self.core) * self.half_rows, self.half_rows), self.half_rows)
        return remote(
            self.part.at[at], self.core_buf, self.core_sem.at[0], self.core_sem.at[1],
            {"dp": 1 - self.core},
        )

    def lo_copy(self, k):
        at = pl.ds(pl.multiple_of(self.lo_peer(k) * self.lo_rows, self.lo_rows), self.lo_rows)
        return remote(
            self.half.at[at], self.lo_buf.at[self.lo - k],
            self.lo_sem.at[0, k], self.lo_sem.at[1, self.lo - k], self.lo_device(k),
        )

    def lo_arrival(self, k):
        return remote(
            self.quarter, self.lo_buf.at[k],
            self.lo_sem.at[0, k], self.lo_sem.at[1, k], self.lo_device(k),
        )

    def hi_copy(self, k):
        at = pl.ds(pl.multiple_of(self.hi_peer(k) * self.hi_rows, self.hi_rows), self.hi_rows)
        return remote(
            self.quarter.at[at], self.hi_buf.at[self.hi - k],
            self.hi_sem.at[0, k], self.hi_sem.at[1, self.hi - k], self.hi_device(k),
        )

    def hi_arrival(self, k):
        return remote(
            self.hi_buf.at[k], self.hi_buf.at[k],
            self.hi_sem.at[0, k], self.hi_sem.at[1, k], self.hi_device(k),
        )

    def piece(self, h):
        at = self.core * self.half_rows + self.my_lo * self.lo_rows + h * self.hi_rows
        return self.total.at[pl.ds(pl.multiple_of(at, self.hi_rows), self.hi_rows)]

    def block(self, core, low):
        at = core * self.half_rows + low * self.lo_rows
        return self.total.at[pl.ds(pl.multiple_of(at, self.lo_rows), self.lo_rows)]

    def gather_hi(self, k):
        mine = self.piece(self.my_hi)
        return remote(
            mine, mine, self.gh_sem.at[0, k], self.gh_sem.at[1, self.hi - k], self.hi_device(k)
        )

    def gather_hi_arrival(self, k):
        other = self.piece(self.hi_peer(k))
        return remote(other, other, self.gh_sem.at[0, k], self.gh_sem.at[1, k], self.hi_device(k))

    def gather_lo(self, k):
        mine = self.block(self.core, self.my_lo)
        return remote(
            mine, mine, self.gl_sem.at[0, k], self.gl_sem.at[1, self.lo - k], self.lo_device(k)
        )

    def gather_lo_arrival(self, k):
        other = self.block(self.core, self.lo_peer(k))
        return remote(other, other, self.gl_sem.at[0, k], self.gl_sem.at[1, k], self.lo_device(k))

    def gather_core(self, low):
        mine = self.block(self.core, low)
        return remote(
            mine, mine, self.gc_sem.at[0, low], self.gc_sem.at[1, low], {"dp": 1 - self.core}
        )

    def gather_core_arrival(self, low):
        other = self.block(1 - self.core, low)
        return remote(
            other, other, self.gc_sem.at[0, low], self.gc_sem.at[1, low], {"dp": 1 - self.core}
        )

    def start(self):
        self.swap().start()

    def core_to_lo(self):
        self.swap().wait()
        step = self.hi_rows

        def add(r, carry):
            at = pl.multiple_of(r * step, step)
            own = self.part[pl.ds(pl.multiple_of(self.core * self.half_rows + at, step), step), :]
            other = self.core_buf[pl.ds(at, step), :]
            self.half[pl.ds(at, step), :] = (own.astype(F32) + other.astype(F32)).astype(BF16)
            return carry

        lax.fori_loop(0, self.half_rows // step, add, 0)
        for k in range(1, self.lo):
            self.lo_copy(k).start()

    def lo_to_hi(self):
        for k in range(1, self.lo):
            self.lo_arrival(k).wait_recv()
        step = self.hi_rows

        def add(r, carry):
            at = pl.multiple_of(r * step, step)
            mine = pl.ds(pl.multiple_of(self.my_lo * self.lo_rows + at, step), step)
            total = self.half[mine, :].astype(F32)
            for k in range(1, self.lo):
                total = total + self.lo_buf[k, pl.ds(at, step), :].astype(F32)
            self.quarter[pl.ds(at, step), :] = total.astype(BF16)
            return carry

        lax.fori_loop(0, self.lo_rows // step, add, 0)
        for k in range(1, self.hi):
            self.hi_copy(k).start()

    def hi_to_gather(self):
        for k in range(1, self.hi):
            self.hi_arrival(k).wait_recv()
        mine = pl.ds(pl.multiple_of(self.my_hi * self.hi_rows, self.hi_rows), self.hi_rows)
        total = self.quarter[mine, :].astype(F32)
        for k in range(1, self.hi):
            total = total + self.hi_buf[k].astype(F32)
        self.piece(self.my_hi)[...] = total.astype(BF16)
        for k in range(1, self.hi):
            self.gather_hi(k).start()

    def gather_to_lo(self):
        for k in range(1, self.hi):
            self.gather_hi_arrival(k).wait_recv()
        for k in range(1, self.lo):
            self.gather_lo(k).start()
        self.gather_core(self.my_lo).start()

    def gather_to_core(self):
        for k in range(1, self.lo):
            self.gather_lo_arrival(k).wait_recv()
            self.gather_core(self.lo_peer(k)).start()

    def finish(self):
        for low in range(self.lo):
            self.gather_core_arrival(low).wait_recv()
        for k in range(1, self.lo):
            self.lo_copy(k).wait_send()
            self.gather_lo(k).wait_send()
        for k in range(1, self.hi):
            self.hi_copy(k).wait_send()
            self.gather_hi(k).wait_send()
        for low in range(self.lo):
            self.gather_core(low).wait_send()


class SmallReducer:
    def __init__(self, n, lo, me, core, total, bufs):
        self.lo, self.hi, self.core = lo, n // lo, core
        self.my_hi, self.my_lo = me // lo, lax.rem(me, lo)
        self.total = total
        self.a, self.b, self.c, self.a_sem, self.b_sem, self.c_sem = bufs

    @staticmethod
    def scratch(n, lo):
        hi, dma = n // lo, pltpu.SemaphoreType.DMA
        return [
            pltpu.VMEM((2, 8, LANES), F32),
            pltpu.VMEM((lo, 8, LANES), F32),
            pltpu.VMEM((hi, 8, LANES), F32),
            dma((2,)), dma((2, lo)), dma((2, hi)),
        ]

    def swap(self, slot):
        ref = self.a.at[slot]
        return remote(ref, ref, self.a_sem.at[0], self.a_sem.at[1], {"dp": 1 - self.core})

    def lo_copy(self, k, slot, come):
        device = {"emb": self.my_hi * self.lo + lax.rem(self.my_lo + k, self.lo)}
        ref = self.b.at[slot]
        return remote(ref, ref, self.b_sem.at[0, k], self.b_sem.at[1, come], device)

    def hi_copy(self, k, slot, come):
        device = {"emb": lax.rem(self.my_hi + k, self.hi) * self.lo + self.my_lo}
        ref = self.c.at[slot]
        return remote(ref, ref, self.c_sem.at[0, k], self.c_sem.at[1, come], device)

    def start(self, value):
        self.a[self.core] = value
        self.swap(self.core).start()

    def core_to_lo(self):
        self.swap(self.core).wait_send()
        self.swap(1 - self.core).wait_recv()
        self.b[self.my_lo] = self.a[0] + self.a[1]
        for k in range(1, self.lo):
            self.lo_copy(k, self.my_lo, self.lo - k).start()

    def lo_to_hi(self):
        for k in range(1, self.lo):
            self.lo_copy(k, lax.rem(self.my_lo + k, self.lo), k).wait_recv()
        total = self.b[0]
        for k in range(1, self.lo):
            total = total + self.b[k]
        self.c[self.my_hi] = total
        for k in range(1, self.hi):
            self.hi_copy(k, self.my_hi, self.hi - k).start()

    def finish(self):
        for k in range(1, self.hi):
            self.hi_copy(k, lax.rem(self.my_hi + k, self.hi), k).wait_recv()
        total = self.c[0]
        for k in range(1, self.hi):
            total = total + self.c[k]
        self.total[...] = total
        for k in range(1, self.lo):
            self.lo_copy(k, self.my_lo, self.lo - k).wait_send()
        for k in range(1, self.hi):
            self.hi_copy(k, self.my_hi, self.hi - k).wait_send()


def step_body(
    n, lo, cap, used, refs_in, refs_out, lookup_refs, block_refs, early_refs, late_refs, small_refs,
):
    (
        ids, own, tags, counts, lens, btab, buckets, g1, g2, table, *far,
    ) = refs_in
    y_out, ig_out, inc, asked_out, early_tot, late_tot, small_tot = refs_out
    (
        req, asked_v, asked_s, tab_low, tab, gbuf, send, recv, x_acc, pos_ref, slots, early, late,
        back_pos, back_req, back_send, back_recv,
        req_send, req_recv, row_send, row_recv, pair_sem, tab_sem, smem_sem,
        grad_send, grad_recv, fwd_send, fwd_recv,
    ) = lookup_refs
    (
        wqkv_t, wqkv, wo_t, win_t, wout_t, buck_t, bias, x_t, a_t, qkv_t, kv, p_s, o_t, c_t, act_t,
        du_t, dy_t, dm_t, dmb_t, do_t, dqkv_t, dsum, igb_t, b_acc,
        cot, wq, wk, wv, wo, win, wout, near_sem,
    ) = block_refs
    near = (cot, wq, wk, wv, wo, win, wout)
    me = lax.axis_index("emb")
    core = lax.axis_index("dp")
    seqs, length = ids.shape
    width = cot.shape[2]
    tokens = seqs * length
    hd, ff = wq.shape[1], win.shape[1]
    heads = hd // DH
    pairs = heads // 2
    bucket_count = btab.shape[1]
    domain_rows = used // 3
    row_limit = 4 * domain_rows
    pieces = tab_sem.shape[0]
    piece = used // pieces
    group = 4
    wide_slots = 256
    early_sum = Reducer(n, lo, me, core, early, early_tot, early_refs)
    late_sum = Reducer(n, lo, me, core, late, late_tot, late_refs)
    small_sum = SmallReducer(n, lo, me, core, small_tot, small_refs)

    barrier = pltpu.get_barrier_semaphore()

    def peer(j):
        return {"emb": lax.rem(me + j, n)}

    def greet(k, carry):
        pl.semaphore_signal(barrier, inc=1, device_id=peer(k), device_id_type=MESH)
        return carry

    lax.fori_loop(1, n, greet, 0)
    pl.semaphore_signal(barrier, inc=1, device_id={"dp": 1 - core}, device_id_type=MESH)

    def table_copy(c):
        part = pl.ds(c * piece, piece)
        return pltpu.make_async_copy(table.at[part], tab_low.at[part], tab_sem.at[c])

    for c in range(pieces):
        table_copy(c).start()
    fetches = [
        pltpu.make_async_copy(src, dst, near_sem.at[k])
        for k, (src, dst) in enumerate(zip(far, near))
    ]
    for fetch in fetches:
        fetch.start()

    row_id = lax.broadcasted_iota(jnp.int32, (seqs, length), 0)
    lane_id = lax.broadcasted_iota(jnp.int32, (seqs, length), 1)
    count_of = jnp.ones((seqs, length), F32)
    tag_of = jnp.zeros((seqs, length), jnp.int32)
    len_of = jnp.zeros((seqs, length), jnp.int32)
    for s in range(seqs):
        tag = tags[s]
        count_of = jnp.where(row_id == s, counts[tag].astype(F32), count_of)
        tag_of = jnp.where(row_id == s, tag, tag_of)
        len_of = jnp.where(row_id == s, lens[0, s], len_of)
    code = ids[...].astype(F32)
    turns = jnp.floor((code + 0.5) / jnp.maximum(count_of, 1.0))
    local = tag_of * domain_rows + (code - turns * count_of).astype(jnp.int32)
    live = lane_id < len_of
    rel = own[...] - me
    rel = jnp.where(rel < 0, rel + n, rel)

    owner_id = lax.broadcasted_iota(jnp.int32, (n, length), 0)
    hots = [jnp.where(owner_id == rel[s : s + 1, :], 1.0, 0.0) for s in range(seqs)]
    before = (
        lax.broadcasted_iota(jnp.int32, (length, length), 0)
        < lax.broadcasted_iota(jnp.int32, (length, length), 1)
    )
    earlier = jnp.where(before, 1.0, 0.0).astype(BF16)
    prefix = dot_nn(jnp.concatenate(hots, axis=0).astype(BF16), earlier)
    running = jnp.zeros((n, 1), F32)
    ranks = []
    for s in range(seqs):
        ranks.append(
            jnp.sum(hots[s] * (prefix[s * n : s * n + n] + running), axis=0, keepdims=True)
        )
        running = running + jnp.sum(hots[s], axis=1, keepdims=True)
    rank = jnp.concatenate(ranks, axis=0).astype(jnp.int32)
    pos_ref[...] = rel * cap + rank

    low = (local & 255).astype(F32)
    high = lax.shift_right_logical(local, 8).astype(F32)
    slot_id = lax.broadcasted_iota(jnp.int32, (LANES, length), 0)
    asking = jnp.zeros((2 * n, LANES), F32)
    for s in range(seqs):
        hot = hots[s]
        values = jnp.concatenate([hot * high[s : s + 1, :], hot * low[s : s + 1, :]], axis=0)
        slot_hot = jnp.where(slot_id == rank[s : s + 1, :], 1.0, 0.0).astype(BF16)
        asking = asking + dot_nt(values.astype(BF16), slot_hot)
    wanted = (asking[:n] * 256.0 + asking[n:]).astype(jnp.int32)
    for j in range(n):
        req[j] = wanted[j : j + 1, :]

    pl.semaphore_wait(barrier, n)

    def request(j):
        back = lax.rem(n - j, n)
        return remote(req.at[j], asked_v.at[back], req_send.at[j], req_recv.at[back], peer(j))

    def request_arrival(j):
        return remote(req.at[j], asked_v.at[j], req_send.at[j], req_recv.at[j], peer(j))

    def ask(j, carry):
        request(j).start()
        return carry

    lax.fori_loop(1, n, ask, 0)
    asked_v[0] = req[0]

    for c in range(pieces):
        table_copy(c).wait()

        def widen(r, carry):
            part = pl.ds(pl.multiple_of(c * piece + r * 256, 256), 256)
            tab[part, :] = tab_low[part, :].astype(F32)
            return carry

        lax.fori_loop(0, piece // 256, widen, 0)

    def all_asked(j, carry):
        request_arrival(j).wait_recv()
        return carry

    lax.fori_loop(1, n, all_asked, 0)
    to_scalar = pltpu.make_async_copy(asked_v, asked_s, smem_sem)
    to_scalar.start()
    to_scalar.wait()

    def slot_block(j):
        return pl.ds(pl.multiple_of(j * cap, cap), cap)

    def row_copy(j):
        back = lax.rem(n - j, n)
        return remote(
            send.at[slot_block(j)], recv.at[slot_block(back)],
            row_send.at[j], row_recv.at[back], peer(j),
        )

    def row_arrival(j):
        at = slot_block(j)
        return remote(send.at[at], recv.at[at], row_send.at[j], row_recv.at[j], peer(j))

    def gather(j):
        def eight(c, carry):
            for r in range(8):
                at = jnp.minimum(asked_s[j, 0, c * 8 + r] & (row_limit - 1), used - 1)
                gbuf[pl.ds(c * 8 + r, 1), :] = tab[pl.ds(at, 1), :]
            return carry

        lax.fori_loop(0, cap // 8, eight, 0)
        return gbuf[...].astype(BF16)

    def serve(j, carry):
        send[slot_block(j), :] = gather(j)
        row_copy(j).start()
        return carry

    lax.fori_loop(1, n, serve, 0)
    recv[0:cap, :] = gather(0)

    key = jnp.where(live, (rel * row_limit + local).astype(F32), -1.0)
    key_cols = [
        jnp.broadcast_to(key[s : s + 1, :], (length, length)).T for s in range(seqs)
    ]
    fresh = []
    for s in range(seqs):
        seen = jnp.where(before & (key_cols[s] == key[s : s + 1, :]), 1.0, 0.0)
        for e in range(s):
            seen = jnp.maximum(seen, jnp.where(key_cols[e] == key[s : s + 1, :], 1.0, 0.0))
        fresh.append(1.0 - jnp.max(seen, axis=0, keepdims=True))
    fresh = [jnp.where(live[s : s + 1, :], fresh[s], 0.0) for s in range(seqs)]
    news = [hots[s] * fresh[s] for s in range(seqs)]
    prefix = dot_nn(jnp.concatenate(news, axis=0).astype(BF16), earlier)
    running = jnp.zeros((n, 1), F32)
    firsts = []
    for s in range(seqs):
        firsts.append(
            jnp.sum(news[s] * (prefix[s * n : s * n + n] + running), axis=0, keepdims=True)
        )
        running = running + jnp.sum(news[s], axis=1, keepdims=True)
    first_cols = [
        jnp.broadcast_to(firsts[s] * fresh[s] + fresh[s], (length, length)).T for s in range(seqs)
    ]
    found = []
    for s in range(seqs):
        at = jnp.zeros((length, length), F32)
        for e in range(s + 1):
            at = jnp.maximum(at, jnp.where(key_cols[e] == key[s : s + 1, :], first_cols[e], 0.0))
        found.append(jnp.max(at, axis=0, keepdims=True))
    found = jnp.concatenate(found, axis=0).astype(jnp.int32) - 1
    back_pos[...] = jnp.where(live, rel * cap + found, -1)
    below = used - local
    low = (below & 255).astype(F32)
    high = lax.shift_right_logical(below, 8).astype(F32)
    asking = jnp.zeros((2 * n, LANES), F32)
    for s in range(seqs):
        values = jnp.concatenate(
            [news[s] * high[s : s + 1, :], news[s] * low[s : s + 1, :]], axis=0
        )
        slot_hot = jnp.where(slot_id == firsts[s].astype(jnp.int32), 1.0, 0.0).astype(BF16)
        asking = asking + dot_nt(values.astype(BF16), slot_hot)
    wanted = used - (asking[:n] * 256.0 + asking[n:]).astype(jnp.int32)
    limits = jnp.broadcast_to(running, (n, LANES)).astype(jnp.int32)
    for j in range(n):
        back_req[j, 0:1] = wanted[j : j + 1, :]
        back_req[j, 1:2] = limits[j : j + 1, :]
    asked_out[core, 0] = back_req[0]

    def back_request(j):
        back = lax.rem(n - j, n)
        return remote(
            back_req.at[j], asked_out.at[core, back], back_send.at[j], back_recv.at[back], peer(j)
        )

    def back_request_arrival(j):
        return remote(
            back_req.at[j], asked_out.at[core, j], back_send.at[j], back_recv.at[j], peer(j)
        )

    def tell(j, carry):
        back_request(j).start()
        return carry

    lax.fori_loop(1, n, tell, 0)

    def share(which):
        ref = asked_out.at[which]
        return remote(ref, ref, pair_sem.at[0], pair_sem.at[1], {"dp": 1 - core})

    for fetch in fetches:
        fetch.wait()
    for part, w in enumerate((wq, wk, wv)):
        wqkv[:, part * hd : (part + 1) * hd] = w[...]
        wqkv_t[part * hd : (part + 1) * hd, :] = w[...].T
    wo_t[...] = wo[...].T
    win_t[...] = win[...].T
    wout_t[...] = wout[...].T
    buck_t[...] = buckets[...].astype(F32).T
    g1_col = jnp.broadcast_to(g1[...], (8, width)).T[:, 0:1]
    g2_col = jnp.broadcast_to(g2[...], (8, width)).T[:, 0:1]
    dsum[...] = jnp.zeros_like(dsum)
    b_acc[...] = jnp.zeros_like(b_acc)

    def bias_rows(r, carry):
        part = pl.ds(pl.multiple_of(r * 8, 8), 8)
        bt = buck_t[part, :]
        rows = [jnp.zeros((8, length), F32) for _ in range(heads)]
        for b in range(bucket_count):
            here = bt == float(b)
            rows = [jnp.where(here, btab[h, b], rows[h]) for h in range(heads)]
        for p in range(pairs):
            bias[p, part, :] = jnp.concatenate(rows[2 * p : 2 * p + 2], axis=1)
        return carry

    lax.fori_loop(0, length // 8, bias_rows, 0)

    def load_dy(s, carry):
        part = pl.ds(pl.multiple_of(s * length, length), length)
        alive = lax.broadcasted_iota(jnp.int32, (width, length), 1) < lens[0, s]
        dy_t[:, part] = jnp.where(alive, cot[s].astype(F32).T, 0.0).astype(BF16)
        return carry

    lax.fori_loop(0, seqs, load_dy, 0)

    def place(step, carry):
        pair = n // 2 - 1 - step

        def ready(j, inner):
            row_arrival(j).wait_recv()
            return inner

        lax.fori_loop(jnp.maximum(2 * pair, 1), 2 * pair + 2, ready, 0)
        first = pl.multiple_of(pair * 2 * cap, 2 * cap)
        hot = hot_slots(pos_ref[...], first, 2 * cap)
        got = dot_tn(recv[pl.ds(first, 2 * cap), :], hot)

        @pl.when(step == 0)
        def _():
            x_acc[...] = got

        @pl.when(step > 0)
        def _():
            x_acc[...] += got

        return carry

    lax.fori_loop(0, n // 2, place, 0)

    def told(j, carry):
        back_request_arrival(j).wait_recv()
        return carry

    lax.fori_loop(1, n, told, 0)
    share(core).start()
    x_t[...] = x_acc[...].astype(BF16)

    xf = x_acc[...]
    scale = lax.rsqrt(jnp.mean(xf * xf, axis=0, keepdims=True) + EPSILON)
    a = (xf * scale * g1_col).astype(BF16)
    a_t[...] = a
    out = dot_nn(wqkv_t[...], a)
    qkv_t[0:hd, :] = out[:hd].astype(BF16) * jnp.array(1.0 / math.sqrt(DH), BF16)
    qkv_t[hd:, :] = out[hd:].astype(BF16)
    kv[...] = dot_nn(a.T, wqkv[:, hd:]).astype(BF16)

    rows = [slice(p * 2 * DH, (p + 1) * 2 * DH) for p in range(pairs)]
    krows = [slice(hd + p * 2 * DH, hd + (p + 1) * 2 * DH) for p in range(pairs)]
    vrows = [slice(2 * hd + p * 2 * DH, 2 * hd + (p + 1) * 2 * DH) for p in range(pairs)]
    jobs = [(i, p) for i in range(group) for p in range(pairs)]

    def members(g):
        return [pl.ds(pl.multiple_of((g * group + i) * length, length), length) for i in range(group)]

    def attend(g, carry):
        parts = members(g)
        key_id = lax.broadcasted_iota(jnp.int32, (length, 2 * length), 0)
        visible = [key_id < lens[0, g * group + i] for i in range(group)]
        scores = [
            dot_nn(kv[parts[i], rows[p]], split_pair(qkv_t[rows[p], parts[i]])) for i, p in jobs
        ]
        probs = []
        for (i, p), score in zip(jobs, scores):
            score = jnp.where(visible[i], score + bias[p], -1000000000.0)
            expo = jnp.exp(score - jnp.max(score, axis=0, keepdims=True))
            prob = expo * (1.0 / jnp.sum(expo, axis=0, keepdims=True))
            p_s[g * group + i, p] = prob
            probs.append(prob.astype(BF16))
        for (i, p), prob in zip(jobs, probs):
            mixed = dot_nn(qkv_t[vrows[p], parts[i]], prob)
            o_t[rows[p], parts[i]] = jnp.concatenate(
                [mixed[:DH, :length], mixed[DH:, length:]], axis=0
            ).astype(BF16)
        return carry

    lax.fori_loop(0, seqs // group, attend, 0)

    m = x_t[...].astype(F32) + dot_nn(wo_t[...], o_t[...])
    scale = lax.rsqrt(jnp.mean(m * m, axis=0, keepdims=True) + EPSILON)
    z = m * scale
    normed = (z * g2_col).astype(BF16)
    c_t[...] = normed
    value, slope = gelu_parts(dot_nn(win_t[...], normed))
    act = value.astype(BF16)
    act_t[...] = act
    du = (dot_nn(wout[...], dy_t[...]) * slope).astype(BF16)
    du_t[...] = du
    y = m + dot_nn(wout_t[...], act)
    for s in range(seqs):
        y_out[s] = y[:, s * length : (s + 1) * length].T.astype(BF16)
    dc = dot_nn(win[...], du)
    gain_two = dc * z
    gain_two = sum(gain_two[:, s * length : (s + 1) * length] for s in range(seqs))
    small_tot[1:2, :] = jnp.sum(gain_two.T, axis=0, keepdims=True)
    e = dc * g2_col
    dm = dy_t[...].astype(F32) + scale * (e - z * jnp.mean(e * z, axis=0, keepdims=True))
    dm_t[...] = dm
    dmb = dm.astype(BF16)
    dmb_t[...] = dmb
    do_t[...] = dot_nn(wo[...], dmb).astype(BF16)

    for k in range(ff // width):
        at = slice(k * width, (k + 1) * width)
        early[at, :] = dot_nt(c_t[...], du_t[at, :]).astype(BF16)
    early[ff : 2 * ff, :] = dot_nt(act_t[...], dy_t[...]).astype(BF16)
    if early.shape[0] > 2 * ff:
        early[2 * ff :, :] = jnp.zeros((early.shape[0] - 2 * ff, width), BF16)
    early_sum.start()

    def attend_back(g):
        parts = members(g)
        do2s = [split_pair(do_t[rows[p], parts[i]]) for i, p in jobs]
        dprobs = [dot_nn(kv[parts[i], krows[p]], do2) for (i, p), do2 in zip(jobs, do2s)]
        lows = []
        for (i, p), dprob in zip(jobs, dprobs):
            prob = p_s[g * group + i, p]
            ds = prob * (dprob - jnp.sum(dprob * prob, axis=0, keepdims=True))
            dsum[p] += ds
            lows.append(ds.astype(BF16))
        for (i, p), do2 in zip(jobs, do2s):
            prob = p_s[g * group + i, p].astype(BF16)
            dqkv_t[vrows[p], parts[i]] = dot_nt(do2, prob).astype(BF16)
        for (i, p), low in zip(jobs, lows):
            q2 = split_pair(qkv_t[rows[p], parts[i]])
            dqkv_t[krows[p], parts[i]] = dot_nt(q2, low).astype(BF16)
        for (i, p), low in zip(jobs, lows):
            dq = dot_nn(qkv_t[krows[p], parts[i]], low) * (1.0 / math.sqrt(DH))
            dqkv_t[rows[p], parts[i]] = jnp.concatenate(
                [dq[:DH, :length], dq[DH:, length:]], axis=0
            ).astype(BF16)

    groups = seqs // group

    def back_loop(g, carry):
        attend_back(g)

        @pl.when(g == 0)
        def _():
            early_sum.core_to_lo()

        return carry

    lax.fori_loop(0, groups, back_loop, 0)

    xf = x_t[...].astype(F32)
    scale = lax.rsqrt(jnp.mean(xf * xf, axis=0, keepdims=True) + EPSILON)
    z = xf * scale
    da = dot_nn(wqkv[...], dqkv_t[...])
    gain_one = da * z
    gain_one = sum(gain_one[:, s * length : (s + 1) * length] for s in range(seqs))
    e = da * g1_col
    ig = dm_t[...] + scale * (e - z * jnp.mean(e * z, axis=0, keepdims=True))
    igb_t[...] = ig.astype(BF16)

    def grad_copy(j):
        back = lax.rem(n - j, n)
        return remote(
            slots.at[slot_block(j)], inc.at[core, slot_block(back)],
            grad_send.at[j], grad_recv.at[back], peer(j),
        )

    def grad_arrival(j):
        return remote(
            slots.at[slot_block(j)], inc.at[core, slot_block(j)],
            grad_send.at[j], grad_recv.at[j], peer(j),
        )

    def forward(j, which):
        ref = inc.at[which, slot_block(j)]
        return remote(ref, ref, fwd_send.at[j], fwd_recv.at[j], {"dp": 1 - core})

    def to_slots(k, carry):
        first = pl.multiple_of(k * wide_slots, wide_slots)
        slots[pl.ds(first, wide_slots), :] = dot_nt(
            hot_slots(back_pos[...], first, wide_slots), igb_t[...]
        ).astype(BF16)

        def go(j, inner):
            grad_copy(j).start()
            return inner

        owners = wide_slots // cap
        lax.fori_loop(jnp.maximum(k * owners, 1), (k + 1) * owners, go, 0)
        return carry

    steps = slots.shape[0] // wide_slots

    def send_rows(first, last):
        lax.fori_loop(first * steps // 8, last * steps // 8, to_slots, 0)

    for k in range(3 * hd // width):
        at = slice(k * width, (k + 1) * width)
        late[at, :] = dot_nt(a_t[...], dqkv_t[at, :]).astype(BF16)
    late[3 * hd : 4 * hd, :] = dot_nt(o_t[...], dmb_t[...]).astype(BF16)
    if late.shape[0] > 4 * hd:
        late[4 * hd :, :] = jnp.zeros((late.shape[0] - 4 * hd, width), BF16)
    late_sum.start()

    send_rows(0, 2)
    inc[core, 0:cap, :] = slots[0:cap, :]
    forward(0, core).start()
    late_sum.core_to_lo()
    send_rows(2, 4)
    early_sum.lo_to_hi()
    send_rows(4, 6)

    def bias_back(r, carry):
        part = pl.ds(pl.multiple_of(r * 8, 8), 8)
        bt = buck_t[part, :]
        grads = [dsum[h // 2, part, (h % 2) * length : (h % 2 + 1) * length] for h in range(heads)]
        for b in range(bucket_count):
            here = bt == float(b)
            for h in range(heads):
                b_acc[h, b] += jnp.where(here, grads[h], 0.0)
        return carry

    lax.fori_loop(0, length // 8, bias_back, 0)
    small_parts = [jnp.sum(gain_one.T, axis=0, keepdims=True), small_tot[1:2, :]]
    for h in range(heads):
        by_bucket = jnp.sum(b_acc[h], axis=1)
        row = jnp.sum(by_bucket.T, axis=0, keepdims=True)
        small_parts.append(
            jnp.concatenate([row, jnp.zeros((1, LANES - bucket_count), F32)], axis=1)
        )
    small_sum.start(jnp.concatenate(small_parts, axis=0))
    early_sum.hi_to_gather()
    late_sum.lo_to_hi()
    small_sum.core_to_lo()
    send_rows(6, 8)
    for s in range(seqs):
        ig_out[s] = ig[:, s * length : (s + 1) * length].T
    early_sum.gather_to_lo()
    small_sum.lo_to_hi()
    late_sum.hi_to_gather()

    def pass_on(step, carry):
        j = n - 1 - step
        grad_arrival(j).wait_recv()
        forward(j, core).start()
        return carry

    lax.fori_loop(0, n // 2, pass_on, 0)
    early_sum.gather_to_core()
    late_sum.gather_to_lo()
    lax.fori_loop(n // 2, n - 1, pass_on, 0)
    late_sum.gather_to_core()
    small_sum.finish()
    early_sum.finish()
    late_sum.finish()

    def rows_in(j, carry):
        forward(j, 1 - core).wait_recv()
        forward(j, core).wait_send()
        return carry

    lax.fori_loop(0, n, rows_in, 0)

    def sent(j, carry):
        request(j).wait_send()
        back_request(j).wait_send()
        row_copy(j).wait_send()
        grad_copy(j).wait_send()
        return carry

    lax.fori_loop(1, n, sent, 0)
    share(core).wait_send()
    share(1 - core).wait_recv()


def step_kernel(n, lo, cap, used, sizes, *refs):
    parts, at = [], 0
    for size in sizes:
        parts.append(refs[at : at + size])
        at += size
    step_body(n, lo, cap, used, *parts)


def scatter_body(
    n, cap, used, asked, counts, inc, early, late, small, y_in, ig_in,
    y_out, ig_out, grad, g1, wq, wk, wv, wo, bias, g2, win, wout,
    acc, wide, zero, inc_v, y_v, ig_v, early_v, late_v, wq_v, wk_v, wv_v, wo_v, win_v, wout_v,
    out_sem, in_sem, pass_sem,
):
    rows_dev, width = grad.shape
    chunk = zero.shape[0]
    domain_rows = used // 3
    per_domain = domain_rows // chunk
    slots = n * cap
    hd = wq.shape[1]
    ff = win.shape[1]
    loads = [
        pltpu.make_async_copy(src, dst, in_sem.at[k])
        for k, (src, dst) in enumerate(
            ((inc, inc_v), (early, early_v), (late, late_v), (y_in, y_v), (ig_in, ig_v))
        )
    ]
    for load in loads:
        load.start()
    zero[...] = jnp.zeros_like(zero)

    def chunk_at(k):
        return pl.ds(pl.multiple_of(k * chunk, chunk), chunk)

    def clear_copy(k):
        return pltpu.make_async_copy(zero, grad.at[chunk_at(k)], out_sem.at[k])

    def out_copy(k):
        return pltpu.make_async_copy(acc.at[chunk_at(k)], grad.at[chunk_at(k)], out_sem.at[k])

    def in_use(k):
        return (k % per_domain) * chunk < counts[k // per_domain]

    def spare(k, carry):
        clear_copy(k).start()
        return carry

    lax.fori_loop(used // chunk, rows_dev // chunk, spare, 0)

    def prepare(k, carry):
        @pl.when(in_use(k))
        def _():
            def clear(r, inner):
                at = pl.multiple_of(k * chunk + r * 256, 256)
                acc[pl.ds(at, 256), :] = jnp.zeros((256, width), F32)
                return inner

            lax.fori_loop(0, chunk // 256, clear, 0)

        @pl.when(jnp.logical_not(in_use(k)))
        def _():
            clear_copy(k).start()

        return carry

    lax.fori_loop(0, used // chunk, prepare, 0)
    loads[0].wait()

    def widen(r, carry):
        at = pl.ds(pl.multiple_of(r * 256, 256), 256)
        wide[at, :] = inc_v[at, :].astype(F32)
        return carry

    lax.fori_loop(0, 2 * slots // 256, widen, 0)

    def source(k, carry):
        base = k * 2 * LANES

        def eight(g, inner):
            first = g * 8
            ats = [asked[base + first + r] for r in range(8)]
            sums = [
                acc[pl.ds(ats[r], 1), :] + wide[pl.ds(k * cap + first + r, 1), :] for r in range(8)
            ]
            for r in range(8):
                acc[pl.ds(ats[r], 1), :] = sums[r]
            return inner

        lax.fori_loop(0, (asked[base + LANES] + 7) // 8, eight, 0)
        return carry

    lax.fori_loop(0, 2 * n, source, 0)

    def write(k, carry):
        @pl.when(in_use(k))
        def _():
            out_copy(k).start()

        return carry

    lax.fori_loop(0, used // chunk, write, 0)

    passes = []

    def hand_on(src, dst):
        passes.append(pltpu.make_async_copy(src, dst, pass_sem.at[len(passes)]))
        passes[-1].start()

    for load in loads[1:]:
        load.wait()
    hand_on(y_v, y_out)
    hand_on(ig_v, ig_out)
    for i, (value, out) in enumerate(((wq_v, wq), (wk_v, wk), (wv_v, wv))):
        for k in range(hd // width):
            at = i * hd + k * width
            value[:, k * width : (k + 1) * width] = late_v[at : at + width, :].astype(F32)
        hand_on(value, out)
    wo_v[...] = late_v[3 * hd : 4 * hd, :].astype(F32)
    hand_on(wo_v, wo)
    for k in range(ff // width):
        at = slice(k * width, (k + 1) * width)
        win_v[:, at] = early_v[at, :].astype(F32)
    hand_on(win_v, win)
    wout_v[...] = early_v[ff : 2 * ff, :].astype(F32)
    hand_on(wout_v, wout)
    g1[...] = small[0:1, :]
    g2[...] = small[1:2, :]
    heads, buckets = bias.shape
    bias[...] = small[2 : 2 + heads, 0:buckets]

    def finish(k, carry):
        clear_copy(k).wait()
        return carry

    lax.fori_loop(0, rows_dev // chunk, finish, 0)
    for copy in passes:
        copy.wait()


def on_device(
    hashed_ids, owners, domain_tags, user_counts, lengths, buckets, table, gain_one,
    query_weight_matrix, key_weight_matrix, value_weight_matrix, attention_output_weight,
    bias_table, gain_two, feedforward_input_weight, feedforward_output_weight, cotangent,
):
    n = lax.axis_size("emb")
    seqs, length = hashed_ids.shape
    tokens = seqs * length
    rows_dev, width = table.shape
    used = 3 * (rows_dev // 4)
    cap = max(2, 2 * tokens // n)
    hd = query_weight_matrix.shape[1]
    ff = feedforward_input_weight.shape[1]
    heads = hd // DH
    pairs = heads // 2
    bucket_count = bias_table.shape[0]
    slots = n * cap
    lo = 2 ** ((n.bit_length()) // 2)
    unit = 2 * n * 16
    early_rows = -(-2 * ff // unit) * unit
    late_rows = -(-4 * hd // unit) * unit
    vmem = pl.BlockSpec(memory_space=pltpu.VMEM)
    smem = pl.BlockSpec(memory_space=pltpu.SMEM)
    anywhere = pl.BlockSpec(memory_space=pl.ANY)
    dma = pltpu.SemaphoreType.DMA
    shape = jax.ShapeDtypeStruct

    operands = (
        hashed_ids, owners.reshape(seqs, length), domain_tags, user_counts, lengths, bias_table.T,
        buckets, gain_one.reshape(1, width), gain_two.reshape(1, width), table, cotangent,
        query_weight_matrix, key_weight_matrix, value_weight_matrix, attention_output_weight,
        feedforward_input_weight, feedforward_output_weight,
    )
    results = (
        shape((seqs, length, width), BF16),
        shape((seqs, length, width), F32),
        shape((2, slots, width), BF16),
        shape((2, n, 2, LANES), jnp.int32),
        shape((early_rows, width), BF16),
        shape((late_rows, width), BF16),
        shape((8, LANES), F32),
    )
    lookup_scratch = [
        pltpu.VMEM((n, 1, LANES), jnp.int32),
        pltpu.VMEM((n, 1, LANES), jnp.int32),
        pltpu.SMEM((n, 1, LANES), jnp.int32),
        pltpu.VMEM((used, width), BF16),
        pltpu.VMEM((used, width), F32),
        pltpu.VMEM((cap, width), F32),
        pltpu.VMEM((slots, width), BF16),
        pltpu.VMEM((slots, width), BF16),
        pltpu.VMEM((width, tokens), F32),
        pltpu.VMEM((seqs, length), jnp.int32),
        pltpu.VMEM((slots, width), BF16),
        pltpu.VMEM((early_rows, width), BF16),
        pltpu.VMEM((late_rows, width), BF16),
        pltpu.VMEM((seqs, length), jnp.int32),
        pltpu.VMEM((n, 2, LANES), jnp.int32),
        dma((n,)), dma((n,)),
        dma((n,)), dma((n,)), dma((n,)), dma((n,)), dma((2,)), dma((6,)), dma,
        dma((n,)), dma((n,)), dma((n,)), dma((n,)),
    ]
    block_scratch = [
        pltpu.VMEM((3 * hd, width), BF16),
        pltpu.VMEM((width, 3 * hd), BF16),
        pltpu.VMEM((width, hd), BF16),
        pltpu.VMEM((ff, width), BF16),
        pltpu.VMEM((width, ff), BF16),
        pltpu.VMEM((length, length), F32),
        pltpu.VMEM((pairs, length, 2 * length), F32),
        pltpu.VMEM((width, tokens), BF16),
        pltpu.VMEM((width, tokens), BF16),
        pltpu.VMEM((3 * hd, tokens), BF16),
        pltpu.VMEM((tokens, 2 * hd), BF16),
        pltpu.VMEM((seqs, pairs, length, 2 * length), F32),
        pltpu.VMEM((hd, tokens), BF16),
        pltpu.VMEM((width, tokens), BF16),
        pltpu.VMEM((ff, tokens), BF16),
        pltpu.VMEM((ff, tokens), BF16),
        pltpu.VMEM((width, tokens), BF16),
        pltpu.VMEM((width, tokens), F32),
        pltpu.VMEM((width, tokens), BF16),
        pltpu.VMEM((hd, tokens), BF16),
        pltpu.VMEM((3 * hd, tokens), BF16),
        pltpu.VMEM((pairs, length, 2 * length), F32),
        pltpu.VMEM((width, tokens), BF16),
        pltpu.VMEM((heads, bucket_count, 8, length), F32),
        pltpu.VMEM((seqs, length, width), BF16),
        pltpu.VMEM((width, hd), BF16),
        pltpu.VMEM((width, hd), BF16),
        pltpu.VMEM((width, hd), BF16),
        pltpu.VMEM((hd, width), BF16),
        pltpu.VMEM((width, ff), BF16),
        pltpu.VMEM((ff, width), BF16),
        dma((7,)),
    ]
    early_scratch = Reducer.scratch(n, lo, early_rows)
    late_scratch = Reducer.scratch(n, lo, late_rows)
    small_scratch = SmallReducer.scratch(n, lo)
    scratch = [lookup_scratch, block_scratch, early_scratch, late_scratch, small_scratch]
    sizes = [len(operands), len(results)] + [len(part) for part in scratch]
    y, ig, incoming, asked, early_total, late_total, small_total = pl.pallas_call(
        functools.partial(step_kernel, n, lo, cap, used, sizes),
        out_shape=results,
        in_specs=[vmem, vmem, smem, smem, smem, smem, vmem, vmem, vmem] + [anywhere] * 8,
        out_specs=(vmem,) * len(results),
        scratch_shapes=sum(scratch, []),
        compiler_params=pltpu.CompilerParams(
            collective_id=0, has_side_effects=True, vmem_limit_bytes=VMEM_LIMIT
        ),
        name="step",
    )(*operands)

    chunk = math.gcd(1024, used // 3)
    output, input_grad, table_grad, g1, gq, gk, gv, go, gb, g2, gin, gout = pl.pallas_call(
        functools.partial(scatter_body, n, cap, used),
        out_shape=(
            shape((seqs, length, width), BF16),
            shape((seqs, length, width), F32),
            shape((rows_dev, width), F32),
            shape((1, width), F32),
            shape((width, hd), F32),
            shape((width, hd), F32),
            shape((width, hd), F32),
            shape((hd, width), F32),
            shape((heads, bucket_count), F32),
            shape((1, width), F32),
            shape((width, ff), F32),
            shape((ff, width), F32),
        ),
        in_specs=[smem, smem, anywhere, anywhere, anywhere, vmem, anywhere, anywhere],
        out_specs=(anywhere,) * 3 + (vmem,) + (anywhere,) * 4 + (vmem,) * 2 + (anywhere,) * 2,
        scratch_shapes=[
            pltpu.VMEM((used + 8, width), F32),
            pltpu.VMEM((2 * slots, width), F32),
            pltpu.VMEM((chunk, width), F32),
            pltpu.VMEM((2 * slots, width), BF16),
            pltpu.VMEM((seqs, length, width), BF16),
            pltpu.VMEM((seqs, length, width), F32),
            pltpu.VMEM((early_rows, width), BF16),
            pltpu.VMEM((late_rows, width), BF16),
            pltpu.VMEM((width, hd), F32),
            pltpu.VMEM((width, hd), F32),
            pltpu.VMEM((width, hd), F32),
            pltpu.VMEM((hd, width), F32),
            pltpu.VMEM((width, ff), F32),
            pltpu.VMEM((ff, width), F32),
            dma((rows_dev // chunk,)), dma((5,)), dma((8,)),
        ],
        compiler_params=pltpu.CompilerParams(vmem_limit_bytes=VMEM_LIMIT),
        name="scatter",
    )(
        asked.reshape(-1), user_counts, incoming.reshape(2 * slots, width), early_total, late_total,
        small_total, y, ig,
    )
    return (
        output, input_grad, table_grad, g1.reshape(width), gq, gk, gv, go, gb.T, g2.reshape(width),
        gin, gout,
    )


def solution(mesh):
    split = ("emb", "dp")
    return jax.shard_map(
        on_device,
        mesh=mesh,
        in_specs=(
            P(split, None), P(split, None, None), P(split), P(), P(split, None), P(),
            P("emb", None), P(), P(), P(), P(), P(), P(), P(), P(), P(), P(split, None, None),
        ),
        out_specs=(
            P(split, None, None), P(split, None, None), P("emb", None), P(), P(), P(), P(), P(),
            P(), P(), P(), P(),
        ),
        check_vma=False,
    )
```

```python
import functools
import math

import jax
import jax.numpy as jnp
from jax import lax
from jax.experimental import pallas as pl
from jax.experimental.pallas import tpu as pltpu
from jax.sharding import PartitionSpec as P

DH = 64
LANES = 128
EPSILON = 1e-06
MESH = pl.DeviceIdType.MESH
F32 = jnp.float32
BF16 = jnp.bfloat16
VMEM_LIMIT = 56 * 1024 * 1024


def dot_nn(a, b):
    return lax.dot_general(a, b, (((1,), (0,)), ((), ())), preferred_element_type=F32)


def dot_nt(a, b):
    return lax.dot_general(a, b, (((1,), (1,)), ((), ())), preferred_element_type=F32)


def dot_tn(a, b):
    return lax.dot_general(a, b, (((0,), (0,)), ((), ())), preferred_element_type=F32)


def hot_slots(pos, first, count):
    rows = lax.broadcasted_iota(jnp.int32, (count, LANES), 0) + first
    parts = [
        jnp.where(rows == pos[s : s + 1, :], 1.0, 0.0).astype(BF16) for s in range(pos.shape[0])
    ]
    return jnp.concatenate(parts, axis=1)


def remote(src, dst, send_sem, recv_sem, device):
    return pltpu.make_async_remote_copy(
        src_ref=src, dst_ref=dst, send_sem=send_sem, recv_sem=recv_sem,
        device_id=device, device_id_type=MESH,
    )


def gelu_parts(u):
    k0 = math.sqrt(2.0 / math.pi)
    k1 = k0 * 0.044715
    square = u * u
    half = 0.5 * jnp.tanh(u * (k1 * square + k0)) + 0.5
    value = u * half
    slope = half + (2.0 * value) * (1.0 - half) * (3.0 * k1 * square + k0)
    return value, slope


def split_pair(both):
    zero = jnp.zeros((DH, LANES), both.dtype)
    left = jnp.concatenate([both[:DH], zero], axis=0)
    right = jnp.concatenate([zero, both[DH:]], axis=0)
    return jnp.concatenate([left, right], axis=1)


class Reducer:
    def __init__(self, n, lo, me, core, part, total, bufs):
        self.n, self.lo, self.hi, self.core = n, lo, n // lo, core
        self.my_hi, self.my_lo = me // lo, lax.rem(me, lo)
        self.part, self.total = part, total
        (
            self.core_buf, self.half, self.lo_buf, self.quarter, self.hi_buf, self.core_sem,
            self.lo_sem, self.hi_sem, self.gh_sem, self.gl_sem, self.gc_sem,
        ) = bufs
        self.half_rows, self.lo_rows = self.half.shape[0], self.quarter.shape[0]
        self.hi_rows = self.hi_buf.shape[1]

    @staticmethod
    def scratch(n, lo, rows):
        hi, dma, width = n // lo, pltpu.SemaphoreType.DMA, LANES
        return [
            pltpu.VMEM((rows // 2, width), BF16),
            pltpu.VMEM((rows // 2, width), BF16),
            pltpu.VMEM((lo, rows // 2 // lo, width), BF16),
            pltpu.VMEM((rows // 2 // lo, width), BF16),
            pltpu.VMEM((hi, rows // 2 // n, width), BF16),
            dma((2,)), dma((2, lo)), dma((2, hi)), dma((2, hi)), dma((2, lo)), dma((2, lo)),
        ]

    def lo_device(self, k):
        return {"emb": self.my_hi * self.lo + self.lo_peer(k)}

    def hi_device(self, k):
        return {"emb": self.hi_peer(k) * self.lo + self.my_lo}

    def lo_peer(self, k):
        return lax.rem(self.my_lo + k, self.lo)

    def hi_peer(self, k):
        return lax.rem(self.my_hi + k, self.hi)

    def swap(self):
        at = pl.ds(pl.multiple_of((1 - self.core) * self.half_rows, self.half_rows), self.half_rows)
        return remote(
            self.part.at[at], self.core_buf, self.core_sem.at[0], self.core_sem.at[1],
            {"dp": 1 - self.core},
        )

    def lo_copy(self, k):
        at = pl.ds(pl.multiple_of(self.lo_peer(k) * self.lo_rows, self.lo_rows), self.lo_rows)
        return remote(
            self.half.at[at], self.lo_buf.at[self.lo - k],
            self.lo_sem.at[0, k], self.lo_sem.at[1, self.lo - k], self.lo_device(k),
        )

    def lo_arrival(self, k):
        return remote(
            self.quarter, self.lo_buf.at[k],
            self.lo_sem.at[0, k], self.lo_sem.at[1, k], self.lo_device(k),
        )

    def hi_copy(self, k):
        at = pl.ds(pl.multiple_of(self.hi_peer(k) * self.hi_rows, self.hi_rows), self.hi_rows)
        return remote(
            self.quarter.at[at], self.hi_buf.at[self.hi - k],
            self.hi_sem.at[0, k], self.hi_sem.at[1, self.hi - k], self.hi_device(k),
        )

    def hi_arrival(self, k):
        return remote(
            self.hi_buf.at[k], self.hi_buf.at[k],
            self.hi_sem.at[0, k], self.hi_sem.at[1, k], self.hi_device(k),
        )

    def piece(self, h):
        at = self.core * self.half_rows + self.my_lo * self.lo_rows + h * self.hi_rows
        return self.total.at[pl.ds(pl.multiple_of(at, self.hi_rows), self.hi_rows)]

    def block(self, core, low):
        at = core * self.half_rows + low * self.lo_rows
        return self.total.at[pl.ds(pl.multiple_of(at, self.lo_rows), self.lo_rows)]

    def gather_hi(self, k):
        mine = self.piece(self.my_hi)
        return remote(
            mine, mine, self.gh_sem.at[0, k], self.gh_sem.at[1, self.hi - k], self.hi_device(k)
        )

    def gather_hi_arrival(self, k):
        other = self.piece(self.hi_peer(k))
        return remote(other, other, self.gh_sem.at[0, k], self.gh_sem.at[1, k], self.hi_device(k))

    def gather_lo(self, k):
        mine = self.block(self.core, self.my_lo)
        return remote(
            mine, mine, self.gl_sem.at[0, k], self.gl_sem.at[1, self.lo - k], self.lo_device(k)
        )

    def gather_lo_arrival(self, k):
        other = self.block(self.core, self.lo_peer(k))
        return remote(other, other, self.gl_sem.at[0, k], self.gl_sem.at[1, k], self.lo_device(k))

    def gather_core(self, low):
        mine = self.block(self.core, low)
        return remote(
            mine, mine, self.gc_sem.at[0, low], self.gc_sem.at[1, low], {"dp": 1 - self.core}
        )

    def gather_core_arrival(self, low):
        other = self.block(1 - self.core, low)
        return remote(
            other, other, self.gc_sem.at[0, low], self.gc_sem.at[1, low], {"dp": 1 - self.core}
        )

    def start(self):
        self.swap().start()

    def core_to_lo(self):
        self.swap().wait()
        step = self.hi_rows

        def add(r, carry):
            at = pl.multiple_of(r * step, step)
            own = self.part[pl.ds(pl.multiple_of(self.core * self.half_rows + at, step), step), :]
            other = self.core_buf[pl.ds(at, step), :]
            self.half[pl.ds(at, step), :] = (own.astype(F32) + other.astype(F32)).astype(BF16)
            return carry

        lax.fori_loop(0, self.half_rows // step, add, 0)
        for k in range(1, self.lo):
            self.lo_copy(k).start()

    def lo_to_hi(self):
        for k in range(1, self.lo):
            self.lo_arrival(k).wait_recv()
        step = self.hi_rows

        def add(r, carry):
            at = pl.multiple_of(r * step, step)
            mine = pl.ds(pl.multiple_of(self.my_lo * self.lo_rows + at, step), step)
            total = self.half[mine, :].astype(F32)
            for k in range(1, self.lo):
                total = total + self.lo_buf[k, pl.ds(at, step), :].astype(F32)
            self.quarter[pl.ds(at, step), :] = total.astype(BF16)
            return carry

        lax.fori_loop(0, self.lo_rows // step, add, 0)
        for k in range(1, self.hi):
            self.hi_copy(k).start()

    def hi_to_gather(self):
        for k in range(1, self.hi):
            self.hi_arrival(k).wait_recv()
        mine = pl.ds(pl.multiple_of(self.my_hi * self.hi_rows, self.hi_rows), self.hi_rows)
        total = self.quarter[mine, :].astype(F32)
        for k in range(1, self.hi):
            total = total + self.hi_buf[k].astype(F32)
        self.piece(self.my_hi)[...] = total.astype(BF16)
        for k in range(1, self.hi):
            self.gather_hi(k).start()

    def gather_to_lo(self):
        for k in range(1, self.hi):
            self.gather_hi_arrival(k).wait_recv()
        for k in range(1, self.lo):
            self.gather_lo(k).start()
        self.gather_core(self.my_lo).start()

    def gather_to_core(self):
        for k in range(1, self.lo):
            self.gather_lo_arrival(k).wait_recv()
            self.gather_core(self.lo_peer(k)).start()

    def finish(self):
        for low in range(self.lo):
            self.gather_core_arrival(low).wait_recv()
        for k in range(1, self.lo):
            self.lo_copy(k).wait_send()
            self.gather_lo(k).wait_send()
        for k in range(1, self.hi):
            self.hi_copy(k).wait_send()
            self.gather_hi(k).wait_send()
        for low in range(self.lo):
            self.gather_core(low).wait_send()


class SmallReducer:
    def __init__(self, n, lo, me, core, total, bufs):
        self.lo, self.hi, self.core = lo, n // lo, core
        self.my_hi, self.my_lo = me // lo, lax.rem(me, lo)
        self.total = total
        self.a, self.b, self.c, self.a_sem, self.b_sem, self.c_sem = bufs

    @staticmethod
    def scratch(n, lo):
        hi, dma = n // lo, pltpu.SemaphoreType.DMA
        return [
            pltpu.VMEM((2, 8, LANES), F32),
            pltpu.VMEM((lo, 8, LANES), F32),
            pltpu.VMEM((hi, 8, LANES), F32),
            dma((2,)), dma((2, lo)), dma((2, hi)),
        ]

    def swap(self, slot):
        ref = self.a.at[slot]
        return remote(ref, ref, self.a_sem.at[0], self.a_sem.at[1], {"dp": 1 - self.core})

    def lo_copy(self, k, slot, come):
        device = {"emb": self.my_hi * self.lo + lax.rem(self.my_lo + k, self.lo)}
        ref = self.b.at[slot]
        return remote(ref, ref, self.b_sem.at[0, k], self.b_sem.at[1, come], device)

    def hi_copy(self, k, slot, come):
        device = {"emb": lax.rem(self.my_hi + k, self.hi) * self.lo + self.my_lo}
        ref = self.c.at[slot]
        return remote(ref, ref, self.c_sem.at[0, k], self.c_sem.at[1, come], device)

    def start(self, value):
        self.a[self.core] = value
        self.swap(self.core).start()

    def core_to_lo(self):
        self.swap(self.core).wait_send()
        self.swap(1 - self.core).wait_recv()
        self.b[self.my_lo] = self.a[0] + self.a[1]
        for k in range(1, self.lo):
            self.lo_copy(k, self.my_lo, self.lo - k).start()

    def lo_to_hi(self):
        for k in range(1, self.lo):
            self.lo_copy(k, lax.rem(self.my_lo + k, self.lo), k).wait_recv()
        total = self.b[0]
        for k in range(1, self.lo):
            total = total + self.b[k]
        self.c[self.my_hi] = total
        for k in range(1, self.hi):
            self.hi_copy(k, self.my_hi, self.hi - k).start()

    def finish(self):
        for k in range(1, self.hi):
            self.hi_copy(k, lax.rem(self.my_hi + k, self.hi), k).wait_recv()
        total = self.c[0]
        for k in range(1, self.hi):
            total = total + self.c[k]
        self.total[...] = total
        for k in range(1, self.lo):
            self.lo_copy(k, self.my_lo, self.lo - k).wait_send()
        for k in range(1, self.hi):
            self.hi_copy(k, self.my_hi, self.hi - k).wait_send()


def step_body(
    n, lo, cap, used, refs_in, refs_out, lookup_refs, block_refs, early_refs, late_refs, small_refs,
):
    (
        ids_far, own_far, tags_far, counts_far, lens_far, btab_far, buckets_far, g1_far, g2_far,
        table, *far,
    ) = refs_in
    y_far, ig_far, inc, asked_far, early_far, late_far, small_far = refs_out
    (
        req, asked_v, asked_s, tab_low, tab, gbuf, send, recv, x_acc, pos_ref, slots, early, late,
        back_pos, back_req, back_send, back_recv,
        req_send, req_recv, row_send, row_recv, pair_sem, tab_sem, smem_sem,
        grad_send, grad_recv, fwd_send, fwd_recv,
    ) = lookup_refs
    (
        wqkv_t, wqkv, wo_t, win_t, wout_t, buck_t, bias, x_t, a_t, qkv_t, kv, p_s, o_t, c_t, act_t,
        du_t, dy_t, dm_t, dmb_t, do_t, dqkv_t, dsum, igb_t, b_acc,
        cot, wq, wk, wv, wo, win, wout, near_sem,
        ids, own, tags, counts, lens, btab, buckets, g1, g2, first_sem,
        y_out, ig_out, asked_out, early_tot, late_tot, small_tot, out_sem,
    ) = block_refs
    near = (cot, wq, wk, wv, wo, win, wout, btab, buckets, g1, g2)
    far = tuple(far) + (btab_far, buckets_far, g1_far, g2_far)
    me = lax.axis_index("emb")
    core = lax.axis_index("dp")
    seqs, length = ids.shape
    width = cot.shape[2]
    tokens = seqs * length
    hd, ff = wq.shape[1], win.shape[1]
    heads = hd // DH
    pairs = heads // 2
    bucket_count = btab.shape[1]
    domain_rows = used // 3
    row_limit = 4 * domain_rows
    pieces = tab_sem.shape[0]
    piece = used // pieces
    group = 4
    wide_slots = 256
    early_sum = Reducer(n, lo, me, core, early, early_tot, early_refs)
    late_sum = Reducer(n, lo, me, core, late, late_tot, late_refs)
    small_sum = SmallReducer(n, lo, me, core, small_tot, small_refs)

    barrier = pltpu.get_barrier_semaphore()

    def peer(j):
        return {"emb": lax.rem(me + j, n)}

    def greet(k, carry):
        pl.semaphore_signal(barrier, inc=1, device_id=peer(k), device_id_type=MESH)
        return carry

    lax.fori_loop(1, n, greet, 0)
    pl.semaphore_signal(barrier, inc=1, device_id={"dp": 1 - core}, device_id_type=MESH)
    first = [
        pltpu.make_async_copy(src, dst, first_sem.at[k])
        for k, (src, dst) in enumerate(
            (
                (ids_far, ids), (own_far, own), (tags_far, tags), (counts_far, counts),
                (lens_far, lens),
            )
        )
    ]
    for fetch in first:
        fetch.start()

    def table_copy(c):
        part = pl.ds(c * piece, piece)
        return pltpu.make_async_copy(table.at[part], tab_low.at[part], tab_sem.at[c])

    for c in range(pieces):
        table_copy(c).start()
    fetches = [
        pltpu.make_async_copy(src, dst, near_sem.at[k])
        for k, (src, dst) in enumerate(zip(far, near))
    ]
    for fetch in fetches:
        fetch.start()

    for fetch in first:
        fetch.wait()

    row_id = lax.broadcasted_iota(jnp.int32, (seqs, length), 0)
    lane_id = lax.broadcasted_iota(jnp.int32, (seqs, length), 1)
    count_of = jnp.ones((seqs, length), F32)
    tag_of = jnp.zeros((seqs, length), jnp.int32)
    len_of = jnp.zeros((seqs, length), jnp.int32)
    for s in range(seqs):
        tag = tags[s]
        count_of = jnp.where(row_id == s, counts[tag].astype(F32), count_of)
        tag_of = jnp.where(row_id == s, tag, tag_of)
        len_of = jnp.where(row_id == s, lens[0, s], len_of)
    code = ids[...].astype(F32)
    turns = jnp.floor((code + 0.5) / jnp.maximum(count_of, 1.0))
    local = tag_of * domain_rows + (code - turns * count_of).astype(jnp.int32)
    live = lane_id < len_of
    rel = own[...] - me
    rel = jnp.where(rel < 0, rel + n, rel)

    owner_id = lax.broadcasted_iota(jnp.int32, (n, length), 0)
    hots = [jnp.where(owner_id == rel[s : s + 1, :], 1.0, 0.0) for s in range(seqs)]
    before = (
        lax.broadcasted_iota(jnp.int32, (length, length), 0)
        < lax.broadcasted_iota(jnp.int32, (length, length), 1)
    )
    earlier = jnp.where(before, 1.0, 0.0).astype(BF16)
    prefix = dot_nn(jnp.concatenate(hots, axis=0).astype(BF16), earlier)
    running = jnp.zeros((n, 1), F32)
    ranks = []
    for s in range(seqs):
        ranks.append(
            jnp.sum(hots[s] * (prefix[s * n : s * n + n] + running), axis=0, keepdims=True)
        )
        running = running + jnp.sum(hots[s], axis=1, keepdims=True)
    rank = jnp.concatenate(ranks, axis=0).astype(jnp.int32)
    pos_ref[...] = rel * cap + rank

    low = (local & 255).astype(F32)
    high = lax.shift_right_logical(local, 8).astype(F32)
    slot_id = lax.broadcasted_iota(jnp.int32, (LANES, length), 0)
    asking = jnp.zeros((2 * n, LANES), F32)
    for s in range(seqs):
        hot = hots[s]
        values = jnp.concatenate([hot * high[s : s + 1, :], hot * low[s : s + 1, :]], axis=0)
        slot_hot = jnp.where(slot_id == rank[s : s + 1, :], 1.0, 0.0).astype(BF16)
        asking = asking + dot_nt(values.astype(BF16), slot_hot)
    wanted = (asking[:n] * 256.0 + asking[n:]).astype(jnp.int32)
    for j in range(n):
        req[j] = wanted[j : j + 1, :]

    pl.semaphore_wait(barrier, n)

    def request(j):
        back = lax.rem(n - j, n)
        return remote(req.at[j], asked_v.at[back], req_send.at[j], req_recv.at[back], peer(j))

    def request_arrival(j):
        return remote(req.at[j], asked_v.at[j], req_send.at[j], req_recv.at[j], peer(j))

    def ask(j, carry):
        request(j).start()
        return carry

    lax.fori_loop(1, n, ask, 0)
    asked_v[0] = req[0]

    for c in range(pieces):
        table_copy(c).wait()

        def widen(r, carry):
            part = pl.ds(pl.multiple_of(c * piece + r * 256, 256), 256)
            tab[part, :] = tab_low[part, :].astype(F32)
            return carry

        lax.fori_loop(0, piece // 256, widen, 0)

    def all_asked(j, carry):
        request_arrival(j).wait_recv()
        return carry

    lax.fori_loop(1, n, all_asked, 0)
    to_scalar = pltpu.make_async_copy(asked_v, asked_s, smem_sem)
    to_scalar.start()
    to_scalar.wait()

    def slot_block(j):
        return pl.ds(pl.multiple_of(j * cap, cap), cap)

    def row_copy(j):
        back = lax.rem(n - j, n)
        return remote(
            send.at[slot_block(j)], recv.at[slot_block(back)],
            row_send.at[j], row_recv.at[back], peer(j),
        )

    def row_arrival(j):
        at = slot_block(j)
        return remote(send.at[at], recv.at[at], row_send.at[j], row_recv.at[j], peer(j))

    def gather(j):
        def eight(c, carry):
            for r in range(8):
                at = jnp.minimum(asked_s[j, 0, c * 8 + r] & (row_limit - 1), used - 1)
                gbuf[pl.ds(c * 8 + r, 1), :] = tab[pl.ds(at, 1), :]
            return carry

        lax.fori_loop(0, cap // 8, eight, 0)
        return gbuf[...].astype(BF16)

    def serve(j, carry):
        send[slot_block(j), :] = gather(j)
        row_copy(j).start()
        return carry

    lax.fori_loop(1, n, serve, 0)
    recv[0:cap, :] = gather(0)

    key = jnp.where(live, (rel * row_limit + local).astype(F32), -1.0)
    key_cols = [
        jnp.broadcast_to(key[s : s + 1, :], (length, length)).T for s in range(seqs)
    ]
    fresh = []
    for s in range(seqs):
        seen = jnp.where(before & (key_cols[s] == key[s : s + 1, :]), 1.0, 0.0)
        for e in range(s):
            seen = jnp.maximum(seen, jnp.where(key_cols[e] == key[s : s + 1, :], 1.0, 0.0))
        fresh.append(1.0 - jnp.max(seen, axis=0, keepdims=True))
    fresh = [jnp.where(live[s : s + 1, :], fresh[s], 0.0) for s in range(seqs)]
    news = [hots[s] * fresh[s] for s in range(seqs)]
    prefix = dot_nn(jnp.concatenate(news, axis=0).astype(BF16), earlier)
    running = jnp.zeros((n, 1), F32)
    firsts = []
    for s in range(seqs):
        firsts.append(
            jnp.sum(news[s] * (prefix[s * n : s * n + n] + running), axis=0, keepdims=True)
        )
        running = running + jnp.sum(news[s], axis=1, keepdims=True)
    first_cols = [
        jnp.broadcast_to(firsts[s] * fresh[s] + fresh[s], (length, length)).T for s in range(seqs)
    ]
    found = []
    for s in range(seqs):
        at = jnp.zeros((length, length), F32)
        for e in range(s + 1):
            at = jnp.maximum(at, jnp.where(key_cols[e] == key[s : s + 1, :], first_cols[e], 0.0))
        found.append(jnp.max(at, axis=0, keepdims=True))
    found = jnp.concatenate(found, axis=0).astype(jnp.int32) - 1
    back_pos[...] = jnp.where(live, rel * cap + found, -1)
    below = used - local
    low = (below & 255).astype(F32)
    high = lax.shift_right_logical(below, 8).astype(F32)
    asking = jnp.zeros((2 * n, LANES), F32)
    for s in range(seqs):
        values = jnp.concatenate(
            [news[s] * high[s : s + 1, :], news[s] * low[s : s + 1, :]], axis=0
        )
        slot_hot = jnp.where(slot_id == firsts[s].astype(jnp.int32), 1.0, 0.0).astype(BF16)
        asking = asking + dot_nt(values.astype(BF16), slot_hot)
    wanted = used - (asking[:n] * 256.0 + asking[n:]).astype(jnp.int32)
    limits = jnp.broadcast_to(running, (n, LANES)).astype(jnp.int32)
    for j in range(n):
        back_req[j, 0:1] = wanted[j : j + 1, :]
        back_req[j, 1:2] = limits[j : j + 1, :]
    asked_out[core, 0] = back_req[0]

    def back_request(j):
        back = lax.rem(n - j, n)
        return remote(
            back_req.at[j], asked_out.at[core, back], back_send.at[j], back_recv.at[back], peer(j)
        )

    def back_request_arrival(j):
        return remote(
            back_req.at[j], asked_out.at[core, j], back_send.at[j], back_recv.at[j], peer(j)
        )

    def tell(j, carry):
        back_request(j).start()
        return carry

    lax.fori_loop(1, n, tell, 0)

    def share(which):
        ref = asked_out.at[which]
        return remote(ref, ref, pair_sem.at[0], pair_sem.at[1], {"dp": 1 - core})

    for fetch in fetches:
        fetch.wait()
    for part, w in enumerate((wq, wk, wv)):
        wqkv[:, part * hd : (part + 1) * hd] = w[...]
        wqkv_t[part * hd : (part + 1) * hd, :] = w[...].T
    wo_t[...] = wo[...].T
    win_t[...] = win[...].T
    wout_t[...] = wout[...].T
    buck_t[...] = buckets[...].astype(F32).T
    g1_col = jnp.broadcast_to(g1[...], (8, width)).T[:, 0:1]
    g2_col = jnp.broadcast_to(g2[...], (8, width)).T[:, 0:1]
    dsum[...] = jnp.zeros_like(dsum)
    b_acc[...] = jnp.zeros_like(b_acc)

    def bias_rows(r, carry):
        part = pl.ds(pl.multiple_of(r * 8, 8), 8)
        bt = buck_t[part, :]
        rows = [jnp.zeros((8, length), F32) for _ in range(heads)]
        for b in range(bucket_count):
            here = bt == float(b)
            rows = [jnp.where(here, btab[h, b], rows[h]) for h in range(heads)]
        for p in range(pairs):
            bias[p, part, :] = jnp.concatenate(rows[2 * p : 2 * p + 2], axis=1)
        return carry

    lax.fori_loop(0, length // 8, bias_rows, 0)

    def load_dy(s, carry):
        part = pl.ds(pl.multiple_of(s * length, length), length)
        alive = lax.broadcasted_iota(jnp.int32, (width, length), 1) < lens[0, s]
        dy_t[:, part] = jnp.where(alive, cot[s].astype(F32).T, 0.0).astype(BF16)
        return carry

    lax.fori_loop(0, seqs, load_dy, 0)

    def place(step, carry):
        pair = n // 2 - 1 - step

        def ready(j, inner):
            row_arrival(j).wait_recv()
            return inner

        lax.fori_loop(jnp.maximum(2 * pair, 1), 2 * pair + 2, ready, 0)
        first = pl.multiple_of(pair * 2 * cap, 2 * cap)
        hot = hot_slots(pos_ref[...], first, 2 * cap)
        got = dot_tn(recv[pl.ds(first, 2 * cap), :], hot)

        @pl.when(step == 0)
        def _():
            x_acc[...] = got

        @pl.when(step > 0)
        def _():
            x_acc[...] += got

        return carry

    lax.fori_loop(0, n // 2, place, 0)

    def told(j, carry):
        back_request_arrival(j).wait_recv()
        return carry

    lax.fori_loop(1, n, told, 0)
    share(core).start()
    x_t[...] = x_acc[...].astype(BF16)

    xf = x_acc[...]
    scale = lax.rsqrt(jnp.mean(xf * xf, axis=0, keepdims=True) + EPSILON)
    a = (xf * scale * g1_col).astype(BF16)
    a_t[...] = a
    out = dot_nn(wqkv_t[...], a)
    qkv_t[0:hd, :] = out[:hd].astype(BF16) * jnp.array(1.0 / math.sqrt(DH), BF16)
    qkv_t[hd:, :] = out[hd:].astype(BF16)
    kv[...] = dot_nn(a.T, wqkv[:, hd:]).astype(BF16)

    rows = [slice(p * 2 * DH, (p + 1) * 2 * DH) for p in range(pairs)]
    krows = [slice(hd + p * 2 * DH, hd + (p + 1) * 2 * DH) for p in range(pairs)]
    vrows = [slice(2 * hd + p * 2 * DH, 2 * hd + (p + 1) * 2 * DH) for p in range(pairs)]
    jobs = [(i, p) for i in range(group) for p in range(pairs)]

    def members(g):
        return [pl.ds(pl.multiple_of((g * group + i) * length, length), length) for i in range(group)]

    def attend(g, carry):
        parts = members(g)
        key_id = lax.broadcasted_iota(jnp.int32, (length, 2 * length), 0)
        visible = [key_id < lens[0, g * group + i] for i in range(group)]
        scores = [
            dot_nn(kv[parts[i], rows[p]], split_pair(qkv_t[rows[p], parts[i]])) for i, p in jobs
        ]
        probs = []
        for (i, p), score in zip(jobs, scores):
            score = jnp.where(visible[i], score + bias[p], -1000000000.0)
            expo = jnp.exp(score - jnp.max(score, axis=0, keepdims=True))
            prob = expo * (1.0 / jnp.sum(expo, axis=0, keepdims=True))
            p_s[g * group + i, p] = prob
            probs.append(prob.astype(BF16))
        for (i, p), prob in zip(jobs, probs):
            mixed = dot_nn(qkv_t[vrows[p], parts[i]], prob)
            o_t[rows[p], parts[i]] = jnp.concatenate(
                [mixed[:DH, :length], mixed[DH:, length:]], axis=0
            ).astype(BF16)
        return carry

    lax.fori_loop(0, seqs // group, attend, 0)

    m = x_t[...].astype(F32) + dot_nn(wo_t[...], o_t[...])
    scale = lax.rsqrt(jnp.mean(m * m, axis=0, keepdims=True) + EPSILON)
    z = m * scale
    normed = (z * g2_col).astype(BF16)
    c_t[...] = normed
    value, slope = gelu_parts(dot_nn(win_t[...], normed))
    act = value.astype(BF16)
    act_t[...] = act
    du = (dot_nn(wout[...], dy_t[...]) * slope).astype(BF16)
    du_t[...] = du
    y = m + dot_nn(wout_t[...], act)
    for s in range(seqs):
        y_out[s] = y[:, s * length : (s + 1) * length].T.astype(BF16)
    flushes = [
        pltpu.make_async_copy(src, dst, out_sem.at[k])
        for k, (src, dst) in enumerate(
            (
                (y_out, y_far), (ig_out, ig_far), (asked_out, asked_far), (early_tot, early_far),
                (late_tot, late_far), (small_tot, small_far),
            )
        )
    ]
    flushes[0].start()
    dc = dot_nn(win[...], du)
    gain_two = dc * z
    gain_two = sum(gain_two[:, s * length : (s + 1) * length] for s in range(seqs))
    small_tot[1:2, :] = jnp.sum(gain_two.T, axis=0, keepdims=True)
    e = dc * g2_col
    dm = dy_t[...].astype(F32) + scale * (e - z * jnp.mean(e * z, axis=0, keepdims=True))
    dm_t[...] = dm
    dmb = dm.astype(BF16)
    dmb_t[...] = dmb
    do_t[...] = dot_nn(wo[...], dmb).astype(BF16)

    for k in range(ff // width):
        at = slice(k * width, (k + 1) * width)
        early[at, :] = dot_nt(c_t[...], du_t[at, :]).astype(BF16)
    early[ff : 2 * ff, :] = dot_nt(act_t[...], dy_t[...]).astype(BF16)
    if early.shape[0] > 2 * ff:
        early[2 * ff :, :] = jnp.zeros((early.shape[0] - 2 * ff, width), BF16)
    early_sum.start()

    def attend_back(g):
        parts = members(g)
        do2s = [split_pair(do_t[rows[p], parts[i]]) for i, p in jobs]
        dprobs = [dot_nn(kv[parts[i], krows[p]], do2) for (i, p), do2 in zip(jobs, do2s)]
        lows = []
        for (i, p), dprob in zip(jobs, dprobs):
            prob = p_s[g * group + i, p]
            ds = prob * (dprob - jnp.sum(dprob * prob, axis=0, keepdims=True))
            dsum[p] += ds
            lows.append(ds.astype(BF16))
        for (i, p), do2 in zip(jobs, do2s):
            prob = p_s[g * group + i, p].astype(BF16)
            dqkv_t[vrows[p], parts[i]] = dot_nt(do2, prob).astype(BF16)
        for (i, p), low in zip(jobs, lows):
            q2 = split_pair(qkv_t[rows[p], parts[i]])
            dqkv_t[krows[p], parts[i]] = dot_nt(q2, low).astype(BF16)
        for (i, p), low in zip(jobs, lows):
            dq = dot_nn(qkv_t[krows[p], parts[i]], low) * (1.0 / math.sqrt(DH))
            dqkv_t[rows[p], parts[i]] = jnp.concatenate(
                [dq[:DH, :length], dq[DH:, length:]], axis=0
            ).astype(BF16)

    groups = seqs // group

    def back_loop(g, carry):
        attend_back(g)

        @pl.when(g == 0)
        def _():
            early_sum.core_to_lo()

        return carry

    lax.fori_loop(0, groups, back_loop, 0)

    xf = x_t[...].astype(F32)
    scale = lax.rsqrt(jnp.mean(xf * xf, axis=0, keepdims=True) + EPSILON)
    z = xf * scale
    da = dot_nn(wqkv[...], dqkv_t[...])
    gain_one = da * z
    gain_one = sum(gain_one[:, s * length : (s + 1) * length] for s in range(seqs))
    e = da * g1_col
    ig = dm_t[...] + scale * (e - z * jnp.mean(e * z, axis=0, keepdims=True))
    igb_t[...] = ig.astype(BF16)

    def grad_copy(j):
        back = lax.rem(n - j, n)
        return remote(
            slots.at[slot_block(j)], inc.at[core, slot_block(back)],
            grad_send.at[j], grad_recv.at[back], peer(j),
        )

    def grad_arrival(j):
        return remote(
            slots.at[slot_block(j)], inc.at[core, slot_block(j)],
            grad_send.at[j], grad_recv.at[j], peer(j),
        )

    def forward(j, which):
        ref = inc.at[which, slot_block(j)]
        return remote(ref, ref, fwd_send.at[j], fwd_recv.at[j], {"dp": 1 - core})

    def to_slots(k, carry):
        first = pl.multiple_of(k * wide_slots, wide_slots)
        slots[pl.ds(first, wide_slots), :] = dot_nt(
            hot_slots(back_pos[...], first, wide_slots), igb_t[...]
        ).astype(BF16)

        def go(j, inner):
            grad_copy(j).start()
            return inner

        owners = wide_slots // cap
        lax.fori_loop(jnp.maximum(k * owners, 1), (k + 1) * owners, go, 0)
        return carry

    steps = slots.shape[0] // wide_slots

    def send_rows(first, last):
        lax.fori_loop(first * steps // 8, last * steps // 8, to_slots, 0)

    for k in range(3 * hd // width):
        at = slice(k * width, (k + 1) * width)
        late[at, :] = dot_nt(a_t[...], dqkv_t[at, :]).astype(BF16)
    late[3 * hd : 4 * hd, :] = dot_nt(o_t[...], dmb_t[...]).astype(BF16)
    if late.shape[0] > 4 * hd:
        late[4 * hd :, :] = jnp.zeros((late.shape[0] - 4 * hd, width), BF16)
    late_sum.start()

    def pass_on(step, carry):
        j = n - 1 - step
        grad_arrival(j).wait_recv()
        forward(j, core).start()
        return carry

    late_sum.core_to_lo()
    early_sum.lo_to_hi()
    send_rows(0, 3)
    keep = pltpu.make_async_copy(slots.at[slot_block(0)], inc.at[core, slot_block(0)], smem_sem)
    keep.start()
    remote(
        slots.at[slot_block(0)], inc.at[core, slot_block(0)], fwd_send.at[0], fwd_recv.at[0],
        {"dp": 1 - core},
    ).start()
    def bias_back(r, carry):
        part = pl.ds(pl.multiple_of(r * 8, 8), 8)
        bt = buck_t[part, :]
        grads = [dsum[h // 2, part, (h % 2) * length : (h % 2 + 1) * length] for h in range(heads)]
        for b in range(bucket_count):
            here = bt == float(b)
            for h in range(heads):
                b_acc[h, b] += jnp.where(here, grads[h], 0.0)
        return carry

    lax.fori_loop(0, length // 8, bias_back, 0)
    small_parts = [jnp.sum(gain_one.T, axis=0, keepdims=True), small_tot[1:2, :]]
    for h in range(heads):
        by_bucket = jnp.sum(b_acc[h], axis=1)
        row = jnp.sum(by_bucket.T, axis=0, keepdims=True)
        small_parts.append(
            jnp.concatenate([row, jnp.zeros((1, LANES - bucket_count), F32)], axis=1)
        )
    small_sum.start(jnp.concatenate(small_parts, axis=0))
    late_sum.lo_to_hi()
    small_sum.core_to_lo()
    early_sum.hi_to_gather()
    late_sum.hi_to_gather()
    small_sum.lo_to_hi()
    send_rows(3, 6)
    early_sum.gather_to_lo()
    late_sum.gather_to_lo()
    send_rows(6, 8)
    for s in range(seqs):
        ig_out[s] = ig[:, s * length : (s + 1) * length].T
    flushes[1].start()
    early_sum.gather_to_core()
    late_sum.gather_to_core()
    lax.fori_loop(0, 15, pass_on, 0)
    small_sum.finish()
    flushes[5].start()
    early_sum.finish()
    flushes[3].start()
    late_sum.finish()
    flushes[4].start()
    share(core).wait_send()
    share(1 - core).wait_recv()
    flushes[2].start()
    keep.wait()

    def rows_in(j, carry):
        forward(j, 1 - core).wait_recv()
        forward(j, core).wait_send()
        return carry

    lax.fori_loop(0, n, rows_in, 0)

    def sent(j, carry):
        request(j).wait_send()
        back_request(j).wait_send()
        row_copy(j).wait_send()
        grad_copy(j).wait_send()
        return carry

    lax.fori_loop(1, n, sent, 0)
    for flush in flushes:
        flush.wait()


def step_kernel(n, lo, cap, used, sizes, *refs):
    parts, at = [], 0
    for size in sizes:
        parts.append(refs[at : at + size])
        at += size
    step_body(n, lo, cap, used, *parts)


def scatter_body(
    n, cap, used, asked, counts, inc, early, late, small, y_in, ig_in,
    y_out, ig_out, grad, g1, wq, wk, wv, wo, bias, g2, win, wout,
    acc, wide, zero, inc_v, y_v, ig_v, early_v, late_v, wq_v, wk_v, wv_v, wo_v, win_v, wout_v,
    out_sem, in_sem, pass_sem,
):
    rows_dev, width = grad.shape
    chunk = zero.shape[0]
    domain_rows = used // 3
    per_domain = domain_rows // chunk
    slots = n * cap
    hd = wq.shape[1]
    ff = win.shape[1]
    loads = [
        pltpu.make_async_copy(src, dst, in_sem.at[k])
        for k, (src, dst) in enumerate(
            ((inc, inc_v), (early, early_v), (late, late_v), (y_in, y_v), (ig_in, ig_v))
        )
    ]
    for load in loads:
        load.start()
    zero[...] = jnp.zeros_like(zero)

    def chunk_at(k):
        return pl.ds(pl.multiple_of(k * chunk, chunk), chunk)

    def clear_copy(k):
        return pltpu.make_async_copy(zero, grad.at[chunk_at(k)], out_sem.at[k])

    def out_copy(k):
        return pltpu.make_async_copy(acc.at[chunk_at(k)], grad.at[chunk_at(k)], out_sem.at[k])

    def in_use(k):
        return (k % per_domain) * chunk < counts[k // per_domain]

    def spare(k, carry):
        clear_copy(k).start()
        return carry

    lax.fori_loop(used // chunk, rows_dev // chunk, spare, 0)

    def prepare(k, carry):
        @pl.when(in_use(k))
        def _():
            def clear(r, inner):
                at = pl.multiple_of(k * chunk + r * 256, 256)
                acc[pl.ds(at, 256), :] = jnp.zeros((256, width), F32)
                return inner

            lax.fori_loop(0, chunk // 256, clear, 0)

        @pl.when(jnp.logical_not(in_use(k)))
        def _():
            clear_copy(k).start()

        return carry

    lax.fori_loop(0, used // chunk, prepare, 0)
    loads[0].wait()

    def widen(r, carry):
        at = pl.ds(pl.multiple_of(r * 256, 256), 256)
        wide[at, :] = inc_v[at, :].astype(F32)
        return carry

    lax.fori_loop(0, 2 * slots // 256, widen, 0)

    def source(k, carry):
        base = k * 2 * LANES

        def eight(g, inner):
            first = g * 8
            ats = [asked[base + first + r] for r in range(8)]
            sums = [
                acc[pl.ds(ats[r], 1), :] + wide[pl.ds(k * cap + first + r, 1), :] for r in range(8)
            ]
            for r in range(8):
                acc[pl.ds(ats[r], 1), :] = sums[r]
            return inner

        lax.fori_loop(0, (asked[base + LANES] + 7) // 8, eight, 0)
        return carry

    lax.fori_loop(0, 2 * n, source, 0)

    def write(k, carry):
        @pl.when(in_use(k))
        def _():
            out_copy(k).start()

        return carry

    lax.fori_loop(0, used // chunk, write, 0)

    passes = []

    def hand_on(src, dst):
        passes.append(pltpu.make_async_copy(src, dst, pass_sem.at[len(passes)]))
        passes[-1].start()

    for load in loads[1:]:
        load.wait()
    hand_on(y_v, y_out)
    hand_on(ig_v, ig_out)
    for i, (value, out) in enumerate(((wq_v, wq), (wk_v, wk), (wv_v, wv))):
        for k in range(hd // width):
            at = i * hd + k * width
            value[:, k * width : (k + 1) * width] = late_v[at : at + width, :].astype(F32)
        hand_on(value, out)
    wo_v[...] = late_v[3 * hd : 4 * hd, :].astype(F32)
    hand_on(wo_v, wo)
    for k in range(ff // width):
        at = slice(k * width, (k + 1) * width)
        win_v[:, at] = early_v[at, :].astype(F32)
    hand_on(win_v, win)
    wout_v[...] = early_v[ff : 2 * ff, :].astype(F32)
    hand_on(wout_v, wout)
    g1[...] = small[0:1, :]
    g2[...] = small[1:2, :]
    heads, buckets = bias.shape
    bias[...] = small[2 : 2 + heads, 0:buckets]

    def finish(k, carry):
        clear_copy(k).wait()
        return carry

    lax.fori_loop(0, rows_dev // chunk, finish, 0)
    for copy in passes:
        copy.wait()


def on_device(
    hashed_ids, owners, domain_tags, user_counts, lengths, buckets, table, gain_one,
    query_weight_matrix, key_weight_matrix, value_weight_matrix, attention_output_weight,
    bias_table, gain_two, feedforward_input_weight, feedforward_output_weight, cotangent,
):
    n = lax.axis_size("emb")
    seqs, length = hashed_ids.shape
    tokens = seqs * length
    rows_dev, width = table.shape
    used = 3 * (rows_dev // 4)
    cap = max(2, 2 * tokens // n)
    hd = query_weight_matrix.shape[1]
    ff = feedforward_input_weight.shape[1]
    heads = hd // DH
    pairs = heads // 2
    bucket_count = bias_table.shape[0]
    slots = n * cap
    lo = 2 ** ((n.bit_length()) // 2)
    unit = 2 * n * 16
    early_rows = -(-2 * ff // unit) * unit
    late_rows = -(-4 * hd // unit) * unit
    vmem = pl.BlockSpec(memory_space=pltpu.VMEM)
    smem = pl.BlockSpec(memory_space=pltpu.SMEM)
    anywhere = pl.BlockSpec(memory_space=pl.ANY)
    dma = pltpu.SemaphoreType.DMA
    shape = jax.ShapeDtypeStruct

    operands = (
        hashed_ids, owners.reshape(seqs, length), domain_tags, user_counts, lengths, bias_table.T,
        buckets, gain_one.reshape(1, width), gain_two.reshape(1, width), table, cotangent,
        query_weight_matrix, key_weight_matrix, value_weight_matrix, attention_output_weight,
        feedforward_input_weight, feedforward_output_weight,
    )
    results = (
        shape((seqs, length, width), BF16),
        shape((seqs, length, width), F32),
        shape((2, slots, width), BF16),
        shape((2, n, 2, LANES), jnp.int32),
        shape((early_rows, width), BF16),
        shape((late_rows, width), BF16),
        shape((8, LANES), F32),
    )
    lookup_scratch = [
        pltpu.VMEM((n, 1, LANES), jnp.int32),
        pltpu.VMEM((n, 1, LANES), jnp.int32),
        pltpu.SMEM((n, 1, LANES), jnp.int32),
        pltpu.VMEM((used, width), BF16),
        pltpu.VMEM((used, width), F32),
        pltpu.VMEM((cap, width), F32),
        pltpu.VMEM((slots, width), BF16),
        pltpu.VMEM((slots, width), BF16),
        pltpu.VMEM((width, tokens), F32),
        pltpu.VMEM((seqs, length), jnp.int32),
        pltpu.VMEM((slots, width), BF16),
        pltpu.VMEM((early_rows, width), BF16),
        pltpu.VMEM((late_rows, width), BF16),
        pltpu.VMEM((seqs, length), jnp.int32),
        pltpu.VMEM((n, 2, LANES), jnp.int32),
        dma((n,)), dma((n,)),
        dma((n,)), dma((n,)), dma((n,)), dma((n,)), dma((2,)), dma((6,)), dma,
        dma((n,)), dma((n,)), dma((n,)), dma((n,)),
    ]
    block_scratch = [
        pltpu.VMEM((3 * hd, width), BF16),
        pltpu.VMEM((width, 3 * hd), BF16),
        pltpu.VMEM((width, hd), BF16),
        pltpu.VMEM((ff, width), BF16),
        pltpu.VMEM((width, ff), BF16),
        pltpu.VMEM((length, length), F32),
        pltpu.VMEM((pairs, length, 2 * length), F32),
        pltpu.VMEM((width, tokens), BF16),
        pltpu.VMEM((width, tokens), BF16),
        pltpu.VMEM((3 * hd, tokens), BF16),
        pltpu.VMEM((tokens, 2 * hd), BF16),
        pltpu.VMEM((seqs, pairs, length, 2 * length), F32),
        pltpu.VMEM((hd, tokens), BF16),
        pltpu.VMEM((width, tokens), BF16),
        pltpu.VMEM((ff, tokens), BF16),
        pltpu.VMEM((ff, tokens), BF16),
        pltpu.VMEM((width, tokens), BF16),
        pltpu.VMEM((width, tokens), F32),
        pltpu.VMEM((width, tokens), BF16),
        pltpu.VMEM((hd, tokens), BF16),
        pltpu.VMEM((3 * hd, tokens), BF16),
        pltpu.VMEM((pairs, length, 2 * length), F32),
        pltpu.VMEM((width, tokens), BF16),
        pltpu.VMEM((heads, bucket_count, 8, length), F32),
        pltpu.VMEM((seqs, length, width), BF16),
        pltpu.VMEM((width, hd), BF16),
        pltpu.VMEM((width, hd), BF16),
        pltpu.VMEM((width, hd), BF16),
        pltpu.VMEM((hd, width), BF16),
        pltpu.VMEM((width, ff), BF16),
        pltpu.VMEM((ff, width), BF16),
        dma((11,)),
        pltpu.VMEM((seqs, length), jnp.int32),
        pltpu.VMEM((seqs, length), jnp.int32),
        pltpu.SMEM((seqs,), jnp.int32),
        pltpu.SMEM((user_counts.shape[0],), jnp.int32),
        pltpu.SMEM(lengths.shape, jnp.int32),
        pltpu.SMEM((heads, bucket_count), F32),
        pltpu.VMEM((length, length), jnp.int32),
        pltpu.VMEM((1, width), F32),
        pltpu.VMEM((1, width), F32),
        dma((5,)),
    ]
    block_scratch += [pltpu.VMEM(results[k].shape, results[k].dtype) for k in (0, 1, 3, 4, 5, 6)]
    block_scratch += [dma((6,))]
    early_scratch = Reducer.scratch(n, lo, early_rows)
    late_scratch = Reducer.scratch(n, lo, late_rows)
    small_scratch = SmallReducer.scratch(n, lo)
    scratch = [lookup_scratch, block_scratch, early_scratch, late_scratch, small_scratch]
    sizes = [len(operands), len(results)] + [len(part) for part in scratch]
    y, ig, incoming, asked, early_total, late_total, small_total = pl.pallas_call(
        functools.partial(step_kernel, n, lo, cap, used, sizes),
        out_shape=results,
        in_specs=[anywhere] * len(operands),
        out_specs=(anywhere,) * len(results),
        scratch_shapes=sum(scratch, []),
        compiler_params=pltpu.CompilerParams(
            collective_id=0, has_side_effects=True, vmem_limit_bytes=VMEM_LIMIT
        ),
        name="step",
    )(*operands)

    chunk = math.gcd(1024, used // 3)
    output, input_grad, table_grad, g1, gq, gk, gv, go, gb, g2, gin, gout = pl.pallas_call(
        functools.partial(scatter_body, n, cap, used),
        out_shape=(
            shape((seqs, length, width), BF16),
            shape((seqs, length, width), F32),
            shape((rows_dev, width), F32),
            shape((1, width), F32),
            shape((width, hd), F32),
            shape((width, hd), F32),
            shape((width, hd), F32),
            shape((hd, width), F32),
            shape((heads, bucket_count), F32),
            shape((1, width), F32),
            shape((width, ff), F32),
            shape((ff, width), F32),
        ),
        in_specs=[smem, smem, anywhere, anywhere, anywhere, vmem, anywhere, anywhere],
        out_specs=(anywhere,) * 3 + (vmem,) + (anywhere,) * 4 + (vmem,) * 2 + (anywhere,) * 2,
        scratch_shapes=[
            pltpu.VMEM((used + 8, width), F32),
            pltpu.VMEM((2 * slots, width), F32),
            pltpu.VMEM((chunk, width), F32),
            pltpu.VMEM((2 * slots, width), BF16),
            pltpu.VMEM((seqs, length, width), BF16),
            pltpu.VMEM((seqs, length, width), F32),
            pltpu.VMEM((early_rows, width), BF16),
            pltpu.VMEM((late_rows, width), BF16),
            pltpu.VMEM((width, hd), F32),
            pltpu.VMEM((width, hd), F32),
            pltpu.VMEM((width, hd), F32),
            pltpu.VMEM((hd, width), F32),
            pltpu.VMEM((width, ff), F32),
            pltpu.VMEM((ff, width), F32),
            dma((rows_dev // chunk,)), dma((5,)), dma((8,)),
        ],
        compiler_params=pltpu.CompilerParams(vmem_limit_bytes=VMEM_LIMIT),
        name="scatter",
    )(
        asked.reshape(-1), user_counts, incoming.reshape(2 * slots, width), early_total, late_total,
        small_total, y, ig,
    )
    return (
        output, input_grad, table_grad, g1.reshape(width), gq, gk, gv, go, gb.T, g2.reshape(width),
        gin, gout,
    )


def solution(mesh):
    split = ("emb", "dp")
    return jax.shard_map(
        on_device,
        mesh=mesh,
        in_specs=(
            P(split, None), P(split, None, None), P(split), P(), P(split, None), P(),
            P("emb", None), P(), P(), P(), P(), P(), P(), P(), P(), P(), P(split, None, None),
        ),
        out_specs=(
            P(split, None, None), P(split, None, None), P("emb", None), P(), P(), P(), P(), P(),
            P(), P(), P(), P(),
        ),
        check_vma=False,
    )
```

```python
import functools
import math

import jax
import jax.numpy as jnp
from jax import lax
from jax.experimental import pallas as pl
from jax.experimental.pallas import tpu as pltpu
from jax.sharding import PartitionSpec as P

DH = 64
LANES = 128
EPSILON = 1e-06
MESH = pl.DeviceIdType.MESH
F32 = jnp.float32
BF16 = jnp.bfloat16
VMEM_LIMIT = 60 * 1024 * 1024


def dot_nn(a, b):
    return lax.dot_general(a, b, (((1,), (0,)), ((), ())), preferred_element_type=F32)


def dot_nt(a, b):
    return lax.dot_general(a, b, (((1,), (1,)), ((), ())), preferred_element_type=F32)


def dot_tn(a, b):
    return lax.dot_general(a, b, (((0,), (0,)), ((), ())), preferred_element_type=F32)


def hot_slots(pos, first, count):
    rows = lax.broadcasted_iota(jnp.int32, (count, LANES), 0) + first
    parts = [
        jnp.where(rows == pos[s : s + 1, :], 1.0, 0.0).astype(BF16) for s in range(pos.shape[0])
    ]
    return jnp.concatenate(parts, axis=1)


def remote(src, dst, send_sem, recv_sem, device):
    return pltpu.make_async_remote_copy(
        src_ref=src, dst_ref=dst, send_sem=send_sem, recv_sem=recv_sem,
        device_id=device, device_id_type=MESH,
    )


def gelu_parts(u):
    k0 = math.sqrt(2.0 / math.pi)
    k1 = k0 * 0.044715
    square = u * u
    half = 0.5 * jnp.tanh(u * (k1 * square + k0)) + 0.5
    value = u * half
    slope = half + (2.0 * value) * (1.0 - half) * (3.0 * k1 * square + k0)
    return value, slope


def split_pair(both):
    zero = jnp.zeros((DH, LANES), both.dtype)
    left = jnp.concatenate([both[:DH], zero], axis=0)
    right = jnp.concatenate([zero, both[DH:]], axis=0)
    return jnp.concatenate([left, right], axis=1)


class Reducer:
    def __init__(self, n, lo, me, core, part, total, bufs):
        self.n, self.lo, self.hi, self.core = n, lo, n // lo, core
        self.my_hi, self.my_lo = me // lo, lax.rem(me, lo)
        self.part, self.total = part, total
        (
            self.core_buf, self.half, self.lo_buf, self.quarter, self.hi_buf, self.core_sem,
            self.lo_sem, self.hi_sem, self.gh_sem, self.gl_sem, self.gc_sem,
        ) = bufs
        self.half_rows, self.lo_rows = self.half.shape[0], self.quarter.shape[0]
        self.hi_rows = self.hi_buf.shape[1]

    @staticmethod
    def scratch(n, lo, rows):
        hi, dma, width = n // lo, pltpu.SemaphoreType.DMA, LANES
        return [
            pltpu.VMEM((rows // 2, width), BF16),
            pltpu.VMEM((rows // 2, width), BF16),
            pltpu.VMEM((lo, rows // 2 // lo, width), BF16),
            pltpu.VMEM((rows // 2 // lo, width), BF16),
            pltpu.VMEM((hi, rows // 2 // n, width), BF16),
            dma((2,)), dma((2, lo)), dma((2, hi)), dma((2, hi)), dma((2, lo)), dma((2, lo)),
        ]

    def lo_device(self, k):
        return {"emb": self.my_hi * self.lo + self.lo_peer(k)}

    def hi_device(self, k):
        return {"emb": self.hi_peer(k) * self.lo + self.my_lo}

    def lo_peer(self, k):
        return lax.rem(self.my_lo + k, self.lo)

    def hi_peer(self, k):
        return lax.rem(self.my_hi + k, self.hi)

    def swap(self):
        at = pl.ds(pl.multiple_of((1 - self.core) * self.half_rows, self.half_rows), self.half_rows)
        return remote(
            self.part.at[at], self.core_buf, self.core_sem.at[0], self.core_sem.at[1],
            {"dp": 1 - self.core},
        )

    def lo_copy(self, k):
        at = pl.ds(pl.multiple_of(self.lo_peer(k) * self.lo_rows, self.lo_rows), self.lo_rows)
        return remote(
            self.half.at[at], self.lo_buf.at[self.lo - k],
            self.lo_sem.at[0, k], self.lo_sem.at[1, self.lo - k], self.lo_device(k),
        )

    def lo_arrival(self, k):
        return remote(
            self.quarter, self.lo_buf.at[k],
            self.lo_sem.at[0, k], self.lo_sem.at[1, k], self.lo_device(k),
        )

    def hi_copy(self, k):
        at = pl.ds(pl.multiple_of(self.hi_peer(k) * self.hi_rows, self.hi_rows), self.hi_rows)
        return remote(
            self.quarter.at[at], self.hi_buf.at[self.hi - k],
            self.hi_sem.at[0, k], self.hi_sem.at[1, self.hi - k], self.hi_device(k),
        )

    def hi_arrival(self, k):
        return remote(
            self.hi_buf.at[k], self.hi_buf.at[k],
            self.hi_sem.at[0, k], self.hi_sem.at[1, k], self.hi_device(k),
        )

    def piece(self, h):
        at = self.core * self.half_rows + self.my_lo * self.lo_rows + h * self.hi_rows
        return self.total.at[pl.ds(pl.multiple_of(at, self.hi_rows), self.hi_rows)]

    def block(self, core, low):
        at = core * self.half_rows + low * self.lo_rows
        return self.total.at[pl.ds(pl.multiple_of(at, self.lo_rows), self.lo_rows)]

    def gather_hi(self, k):
        mine = self.piece(self.my_hi)
        return remote(
            mine, mine, self.gh_sem.at[0, k], self.gh_sem.at[1, self.hi - k], self.hi_device(k)
        )

    def gather_hi_arrival(self, k):
        other = self.piece(self.hi_peer(k))
        return remote(other, other, self.gh_sem.at[0, k], self.gh_sem.at[1, k], self.hi_device(k))

    def gather_lo(self, k):
        mine = self.block(self.core, self.my_lo)
        return remote(
            mine, mine, self.gl_sem.at[0, k], self.gl_sem.at[1, self.lo - k], self.lo_device(k)
        )

    def gather_lo_arrival(self, k):
        other = self.block(self.core, self.lo_peer(k))
        return remote(other, other, self.gl_sem.at[0, k], self.gl_sem.at[1, k], self.lo_device(k))

    def gather_core(self, low):
        mine = self.block(self.core, low)
        return remote(
            mine, mine, self.gc_sem.at[0, low], self.gc_sem.at[1, low], {"dp": 1 - self.core}
        )

    def gather_core_arrival(self, low):
        other = self.block(1 - self.core, low)
        return remote(
            other, other, self.gc_sem.at[0, low], self.gc_sem.at[1, low], {"dp": 1 - self.core}
        )

    def start(self):
        self.swap().start()

    def core_to_lo(self):
        self.swap().wait()
        step = self.hi_rows

        def add(r, carry):
            at = pl.multiple_of(r * step, step)
            own = self.part[pl.ds(pl.multiple_of(self.core * self.half_rows + at, step), step), :]
            other = self.core_buf[pl.ds(at, step), :]
            self.half[pl.ds(at, step), :] = (own.astype(F32) + other.astype(F32)).astype(BF16)
            return carry

        lax.fori_loop(0, self.half_rows // step, add, 0)
        for k in range(1, self.lo):
            self.lo_copy(k).start()

    def lo_to_hi(self):
        for k in range(1, self.lo):
            self.lo_arrival(k).wait_recv()
        step = self.hi_rows

        def add(r, carry):
            at = pl.multiple_of(r * step, step)
            mine = pl.ds(pl.multiple_of(self.my_lo * self.lo_rows + at, step), step)
            total = self.half[mine, :].astype(F32)
            for k in range(1, self.lo):
                total = total + self.lo_buf[k, pl.ds(at, step), :].astype(F32)
            self.quarter[pl.ds(at, step), :] = total.astype(BF16)
            return carry

        lax.fori_loop(0, self.lo_rows // step, add, 0)
        for k in range(1, self.hi):
            self.hi_copy(k).start()

    def hi_to_gather(self):
        for k in range(1, self.hi):
            self.hi_arrival(k).wait_recv()
        mine = pl.ds(pl.multiple_of(self.my_hi * self.hi_rows, self.hi_rows), self.hi_rows)
        total = self.quarter[mine, :].astype(F32)
        for k in range(1, self.hi):
            total = total + self.hi_buf[k].astype(F32)
        self.piece(self.my_hi)[...] = total.astype(BF16)
        for k in range(1, self.hi):
            self.gather_hi(k).start()

    def gather_to_lo(self):
        for k in range(1, self.hi):
            self.gather_hi_arrival(k).wait_recv()
        for k in range(1, self.lo):
            self.gather_lo(k).start()
        self.gather_core(self.my_lo).start()

    def gather_to_core(self):
        for k in range(1, self.lo):
            self.gather_lo_arrival(k).wait_recv()
            self.gather_core(self.lo_peer(k)).start()

    def finish(self):
        for low in range(self.lo):
            self.gather_core_arrival(low).wait_recv()
        for k in range(1, self.lo):
            self.lo_copy(k).wait_send()
            self.gather_lo(k).wait_send()
        for k in range(1, self.hi):
            self.hi_copy(k).wait_send()
            self.gather_hi(k).wait_send()
        for low in range(self.lo):
            self.gather_core(low).wait_send()


class SmallReducer:
    def __init__(self, n, lo, me, core, total, bufs):
        self.lo, self.hi, self.core = lo, n // lo, core
        self.my_hi, self.my_lo = me // lo, lax.rem(me, lo)
        self.total = total
        self.a, self.b, self.c, self.a_sem, self.b_sem, self.c_sem = bufs

    @staticmethod
    def scratch(n, lo):
        hi, dma = n // lo, pltpu.SemaphoreType.DMA
        return [
            pltpu.VMEM((2, 8, LANES), F32),
            pltpu.VMEM((lo, 8, LANES), F32),
            pltpu.VMEM((hi, 8, LANES), F32),
            dma((2,)), dma((2, lo)), dma((2, hi)),
        ]

    def swap(self, slot):
        ref = self.a.at[slot]
        return remote(ref, ref, self.a_sem.at[0], self.a_sem.at[1], {"dp": 1 - self.core})

    def lo_copy(self, k, slot, come):
        device = {"emb": self.my_hi * self.lo + lax.rem(self.my_lo + k, self.lo)}
        ref = self.b.at[slot]
        return remote(ref, ref, self.b_sem.at[0, k], self.b_sem.at[1, come], device)

    def hi_copy(self, k, slot, come):
        device = {"emb": lax.rem(self.my_hi + k, self.hi) * self.lo + self.my_lo}
        ref = self.c.at[slot]
        return remote(ref, ref, self.c_sem.at[0, k], self.c_sem.at[1, come], device)

    def start(self, value):
        self.a[self.core] = value
        self.swap(self.core).start()

    def core_to_lo(self):
        self.swap(self.core).wait_send()
        self.swap(1 - self.core).wait_recv()
        self.b[self.my_lo] = self.a[0] + self.a[1]
        for k in range(1, self.lo):
            self.lo_copy(k, self.my_lo, self.lo - k).start()

    def lo_to_hi(self):
        for k in range(1, self.lo):
            self.lo_copy(k, lax.rem(self.my_lo + k, self.lo), k).wait_recv()
        total = self.b[0]
        for k in range(1, self.lo):
            total = total + self.b[k]
        self.c[self.my_hi] = total
        for k in range(1, self.hi):
            self.hi_copy(k, self.my_hi, self.hi - k).start()

    def finish(self):
        for k in range(1, self.hi):
            self.hi_copy(k, lax.rem(self.my_hi + k, self.hi), k).wait_recv()
        total = self.c[0]
        for k in range(1, self.hi):
            total = total + self.c[k]
        self.total[...] = total
        for k in range(1, self.lo):
            self.lo_copy(k, self.my_lo, self.lo - k).wait_send()
        for k in range(1, self.hi):
            self.hi_copy(k, self.my_hi, self.hi - k).wait_send()


def step_body(
    n, lo, cap, used, refs_in, refs_out, lookup_refs, block_refs, early_refs, late_refs, small_refs,
):
    (
        ids_far, own_far, tags_far, counts_far, lens_far, btab_far, buckets_far, g1_far, g2_far,
        table, *far,
    ) = refs_in
    y_far, ig_far, inc, asked_far, early_far, late_far, small_far = refs_out
    (
        req, asked_v, asked_s, tab_low, tab, gbuf, send, recv, x_acc, pos_ref, slots, early, late,
        back_pos, back_req, back_send, back_recv,
        req_send, req_recv, row_send, row_recv, pair_sem, tab_sem, smem_sem,
        grad_send, grad_recv, fwd_send, fwd_recv,
    ) = lookup_refs
    (
        wqkv_t, wqkv, wo_t, win_t, wout_t, buck_t, bias, x_t, a_t, qkv_t, kv, p_s, o_t, c_t, act_t,
        du_t, dy_t, dm_t, dmb_t, do_t, dqkv_t, dsum, igb_t, b_acc,
        cot, wq, wk, wv, wo, win, wout, near_sem,
        ids, own, tags, counts, lens, btab, buckets, g1, g2, first_sem,
        y_out, ig_out, asked_out, early_tot, late_tot, small_tot, out_sem,
    ) = block_refs
    near = (cot, wq, wk, wv, wo, win, wout, btab, buckets, g1, g2)
    far = tuple(far) + (btab_far, buckets_far, g1_far, g2_far)
    me = lax.axis_index("emb")
    core = lax.axis_index("dp")
    seqs, length = ids.shape
    width = cot.shape[2]
    tokens = seqs * length
    hd, ff = wq.shape[1], win.shape[1]
    heads = hd // DH
    pairs = heads // 2
    bucket_count = btab.shape[1]
    domain_rows = used // 3
    row_limit = 4 * domain_rows
    pieces = tab_sem.shape[0]
    piece = used // pieces
    group = 4
    wide_slots = 256
    early_sum = Reducer(n, lo, me, core, early, early_tot, early_refs)
    late_sum = Reducer(n, lo, me, core, late, late_tot, late_refs)
    small_sum = SmallReducer(n, lo, me, core, small_tot, small_refs)

    barrier = pltpu.get_barrier_semaphore()

    def peer(j):
        return {"emb": lax.rem(me + j, n)}

    def greet(k, carry):
        pl.semaphore_signal(barrier, inc=1, device_id=peer(k), device_id_type=MESH)
        return carry

    lax.fori_loop(1, n, greet, 0)
    pl.semaphore_signal(barrier, inc=1, device_id={"dp": 1 - core}, device_id_type=MESH)
    first = [
        pltpu.make_async_copy(src, dst, first_sem.at[k])
        for k, (src, dst) in enumerate(
            (
                (ids_far, ids), (own_far, own), (tags_far, tags), (counts_far, counts),
                (lens_far, lens),
            )
        )
    ]
    for fetch in first:
        fetch.start()

    def table_copy(c):
        part = pl.ds(c * piece, piece)
        return pltpu.make_async_copy(table.at[part], tab_low.at[part], tab_sem.at[c])

    for c in range(pieces):
        table_copy(c).start()
    fetches = [
        pltpu.make_async_copy(src, dst, near_sem.at[k])
        for k, (src, dst) in enumerate(zip(far, near))
    ]
    for fetch in fetches:
        fetch.start()

    for fetch in first:
        fetch.wait()

    row_id = lax.broadcasted_iota(jnp.int32, (seqs, length), 0)
    lane_id = lax.broadcasted_iota(jnp.int32, (seqs, length), 1)
    count_of = jnp.ones((seqs, length), F32)
    tag_of = jnp.zeros((seqs, length), jnp.int32)
    len_of = jnp.zeros((seqs, length), jnp.int32)
    for s in range(seqs):
        tag = tags[s]
        count_of = jnp.where(row_id == s, counts[tag].astype(F32), count_of)
        tag_of = jnp.where(row_id == s, tag, tag_of)
        len_of = jnp.where(row_id == s, lens[0, s], len_of)
    code = ids[...].astype(F32)
    turns = jnp.floor((code + 0.5) / jnp.maximum(count_of, 1.0))
    local = tag_of * domain_rows + (code - turns * count_of).astype(jnp.int32)
    live = lane_id < len_of
    rel = own[...] - me
    rel = jnp.where(rel < 0, rel + n, rel)

    owner_id = lax.broadcasted_iota(jnp.int32, (n, length), 0)
    hots = [jnp.where(owner_id == rel[s : s + 1, :], 1.0, 0.0) for s in range(seqs)]
    before = (
        lax.broadcasted_iota(jnp.int32, (length, length), 0)
        < lax.broadcasted_iota(jnp.int32, (length, length), 1)
    )
    earlier = jnp.where(before, 1.0, 0.0).astype(BF16)
    prefix = dot_nn(jnp.concatenate(hots, axis=0).astype(BF16), earlier)
    running = jnp.zeros((n, 1), F32)
    ranks = []
    for s in range(seqs):
        ranks.append(
            jnp.sum(hots[s] * (prefix[s * n : s * n + n] + running), axis=0, keepdims=True)
        )
        running = running + jnp.sum(hots[s], axis=1, keepdims=True)
    rank = jnp.concatenate(ranks, axis=0).astype(jnp.int32)
    pos_ref[...] = rel * cap + rank

    low = (local & 255).astype(F32)
    high = lax.shift_right_logical(local, 8).astype(F32)
    slot_id = lax.broadcasted_iota(jnp.int32, (LANES, length), 0)
    asking = jnp.zeros((2 * n, LANES), F32)
    for s in range(seqs):
        hot = hots[s]
        values = jnp.concatenate([hot * high[s : s + 1, :], hot * low[s : s + 1, :]], axis=0)
        slot_hot = jnp.where(slot_id == rank[s : s + 1, :], 1.0, 0.0).astype(BF16)
        asking = asking + dot_nt(values.astype(BF16), slot_hot)
    wanted = (asking[:n] * 256.0 + asking[n:]).astype(jnp.int32)
    for j in range(n):
        req[j] = wanted[j : j + 1, :]

    pl.semaphore_wait(barrier, n)

    def request(j):
        back = lax.rem(n - j, n)
        return remote(req.at[j], asked_v.at[back], req_send.at[j], req_recv.at[back], peer(j))

    def request_arrival(j):
        return remote(req.at[j], asked_v.at[j], req_send.at[j], req_recv.at[j], peer(j))

    def ask(j, carry):
        request(j).start()
        return carry

    lax.fori_loop(1, n, ask, 0)
    asked_v[0] = req[0]

    for c in range(pieces):
        table_copy(c).wait()

        def widen(r, carry):
            part = pl.ds(pl.multiple_of(c * piece + r * 256, 256), 256)
            tab[part, :] = tab_low[part, :].astype(F32)
            return carry

        lax.fori_loop(0, piece // 256, widen, 0)

    def all_asked(j, carry):
        request_arrival(j).wait_recv()
        return carry

    lax.fori_loop(1, n, all_asked, 0)
    to_scalar = pltpu.make_async_copy(asked_v, asked_s, smem_sem)
    to_scalar.start()
    to_scalar.wait()

    def slot_block(j):
        return pl.ds(pl.multiple_of(j * cap, cap), cap)

    def row_copy(j):
        back = lax.rem(n - j, n)
        return remote(
            send.at[slot_block(j)], recv.at[slot_block(back)],
            row_send.at[j], row_recv.at[back], peer(j),
        )

    def row_arrival(j):
        at = slot_block(j)
        return remote(send.at[at], recv.at[at], row_send.at[j], row_recv.at[j], peer(j))

    def gather(j):
        def some(c, carry):
            for r in range(16):
                at = asked_s[j, 0, c * 16 + r] & (row_limit - 1)
                gbuf[pl.ds(c * 16 + r, 1), :] = tab[pl.ds(at, 1), :]
            return carry

        lax.fori_loop(0, cap // 16, some, 0)
        return gbuf[...].astype(BF16)

    def pair_at(step):
        half = (step + 1) // 2
        return jnp.where(lax.rem(step, 2) == 1, n // 4 - half, n // 4 + half)

    def serve(step, carry):
        def one(j, inner):
            send[slot_block(j), :] = gather(j)
            row_copy(j).start()
            return inner

        last = n - 2 * pair_at(step)
        return lax.fori_loop(last - 1, jnp.minimum(last + 1, n), one, carry)

    lax.fori_loop(0, n // 2, serve, 0)
    recv[0:cap, :] = gather(0)

    key = jnp.where(live, (rel * row_limit + local).astype(F32), -1.0)
    key_cols = [
        jnp.broadcast_to(key[s : s + 1, :], (length, length)).T for s in range(seqs)
    ]
    fresh = []
    for s in range(seqs):
        seen = jnp.where(before & (key_cols[s] == key[s : s + 1, :]), 1.0, 0.0)
        for e in range(s):
            seen = jnp.maximum(seen, jnp.where(key_cols[e] == key[s : s + 1, :], 1.0, 0.0))
        fresh.append(1.0 - jnp.max(seen, axis=0, keepdims=True))
    fresh = [jnp.where(live[s : s + 1, :], fresh[s], 0.0) for s in range(seqs)]
    news = [hots[s] * fresh[s] for s in range(seqs)]
    prefix = dot_nn(jnp.concatenate(news, axis=0).astype(BF16), earlier)
    running = jnp.zeros((n, 1), F32)
    firsts = []
    for s in range(seqs):
        firsts.append(
            jnp.sum(news[s] * (prefix[s * n : s * n + n] + running), axis=0, keepdims=True)
        )
        running = running + jnp.sum(news[s], axis=1, keepdims=True)
    first_cols = [
        jnp.broadcast_to(firsts[s] * fresh[s] + fresh[s], (length, length)).T for s in range(seqs)
    ]
    found = []
    for s in range(seqs):
        at = jnp.zeros((length, length), F32)
        for e in range(s + 1):
            at = jnp.maximum(at, jnp.where(key_cols[e] == key[s : s + 1, :], first_cols[e], 0.0))
        found.append(jnp.max(at, axis=0, keepdims=True))
    found = jnp.concatenate(found, axis=0).astype(jnp.int32) - 1
    back_pos[...] = jnp.where(live, rel * cap + found, -1)
    below = used - local
    low = (below & 255).astype(F32)
    high = lax.shift_right_logical(below, 8).astype(F32)
    asking = jnp.zeros((2 * n, LANES), F32)
    for s in range(seqs):
        values = jnp.concatenate(
            [news[s] * high[s : s + 1, :], news[s] * low[s : s + 1, :]], axis=0
        )
        slot_hot = jnp.where(slot_id == firsts[s].astype(jnp.int32), 1.0, 0.0).astype(BF16)
        asking = asking + dot_nt(values.astype(BF16), slot_hot)
    wanted = used - (asking[:n] * 256.0 + asking[n:]).astype(jnp.int32)
    limits = jnp.broadcast_to(running, (n, LANES)).astype(jnp.int32)
    for j in range(n):
        back_req[j, 0:1] = wanted[j : j + 1, :]
        back_req[j, 1:2] = limits[j : j + 1, :]
    asked_out[core, 0] = back_req[0]

    def back_request(j):
        back = lax.rem(n - j, n)
        return remote(
            back_req.at[j], asked_out.at[core, back], back_send.at[j], back_recv.at[back], peer(j)
        )

    def back_request_arrival(j):
        return remote(
            back_req.at[j], asked_out.at[core, j], back_send.at[j], back_recv.at[j], peer(j)
        )

    def tell(j, carry):
        back_request(j).start()
        return carry

    lax.fori_loop(1, n, tell, 0)

    def share(which):
        ref = asked_out.at[which]
        return remote(ref, ref, pair_sem.at[0], pair_sem.at[1], {"dp": 1 - core})

    for fetch in fetches:
        fetch.wait()
    for part, w in enumerate((wq, wk, wv)):
        wqkv[:, part * hd : (part + 1) * hd] = w[...]
        wqkv_t[part * hd : (part + 1) * hd, :] = w[...].T
    wo_t[...] = wo[...].T
    win_t[...] = win[...].T
    wout_t[...] = wout[...].T
    buck_t[...] = buckets[...].astype(F32).T
    g1_col = jnp.broadcast_to(g1[...], (8, width)).T[:, 0:1]
    g2_col = jnp.broadcast_to(g2[...], (8, width)).T[:, 0:1]
    dsum[...] = jnp.zeros_like(dsum)
    b_acc[...] = jnp.zeros_like(b_acc)

    def bias_rows(r, carry):
        part = pl.ds(pl.multiple_of(r * 8, 8), 8)
        bt = buck_t[part, :]
        rows = [jnp.zeros((8, length), F32) for _ in range(heads)]
        for b in range(bucket_count):
            here = bt == float(b)
            rows = [jnp.where(here, btab[h, b], rows[h]) for h in range(heads)]
        for p in range(pairs):
            bias[p, part, :] = jnp.concatenate(rows[2 * p : 2 * p + 2], axis=1)
        return carry

    lax.fori_loop(0, length // 8, bias_rows, 0)

    def load_dy(s, carry):
        part = pl.ds(pl.multiple_of(s * length, length), length)
        alive = lax.broadcasted_iota(jnp.int32, (width, length), 1) < lens[0, s]
        dy_t[:, part] = jnp.where(alive, cot[s].astype(F32).T, 0.0).astype(BF16)
        return carry

    lax.fori_loop(0, seqs, load_dy, 0)

    def place(step, carry):
        pair = pair_at(step)

        def ready(j, inner):
            row_arrival(j).wait_recv()
            return inner

        lax.fori_loop(jnp.maximum(2 * pair, 1), 2 * pair + 2, ready, 0)
        first = pl.multiple_of(pair * 2 * cap, 2 * cap)
        hot = hot_slots(pos_ref[...], first, 2 * cap)
        got = dot_tn(recv[pl.ds(first, 2 * cap), :], hot)

        @pl.when(step == 0)
        def _():
            x_acc[...] = got

        @pl.when(step > 0)
        def _():
            x_acc[...] += got

        return carry

    lax.fori_loop(0, n // 2, place, 0)

    def told(j, carry):
        back_request_arrival(j).wait_recv()
        return carry

    lax.fori_loop(1, n, told, 0)
    share(core).start()
    x_t[...] = x_acc[...].astype(BF16)

    xf = x_acc[...]
    scale = lax.rsqrt(jnp.mean(xf * xf, axis=0, keepdims=True) + EPSILON)
    a = (xf * scale * g1_col).astype(BF16)
    a_t[...] = a
    out = dot_nn(wqkv_t[...], a)
    qkv_t[0:hd, :] = out[:hd].astype(BF16) * jnp.array(1.0 / math.sqrt(DH), BF16)
    qkv_t[hd:, :] = out[hd:].astype(BF16)
    kv[...] = dot_nn(a.T, wqkv[:, hd:]).astype(BF16)

    rows = [slice(p * 2 * DH, (p + 1) * 2 * DH) for p in range(pairs)]
    krows = [slice(hd + p * 2 * DH, hd + (p + 1) * 2 * DH) for p in range(pairs)]
    vrows = [slice(2 * hd + p * 2 * DH, 2 * hd + (p + 1) * 2 * DH) for p in range(pairs)]
    jobs = [(i, p) for i in range(group) for p in range(pairs)]

    def members(g):
        return [pl.ds(pl.multiple_of((g * group + i) * length, length), length) for i in range(group)]

    def attend(g, carry):
        parts = members(g)
        key_id = lax.broadcasted_iota(jnp.int32, (length, 2 * length), 0)
        visible = [key_id < lens[0, g * group + i] for i in range(group)]
        scores = [
            dot_nn(kv[parts[i], rows[p]], split_pair(qkv_t[rows[p], parts[i]])) for i, p in jobs
        ]
        probs = []
        for (i, p), score in zip(jobs, scores):
            score = jnp.where(visible[i], score + bias[p], -1000000000.0)
            expo = jnp.exp(score - jnp.max(score, axis=0, keepdims=True))
            prob = expo * (1.0 / jnp.sum(expo, axis=0, keepdims=True))
            p_s[g * group + i, p] = prob
            probs.append(prob.astype(BF16))
        for (i, p), prob in zip(jobs, probs):
            mixed = dot_nn(qkv_t[vrows[p], parts[i]], prob)
            o_t[rows[p], parts[i]] = jnp.concatenate(
                [mixed[:DH, :length], mixed[DH:, length:]], axis=0
            ).astype(BF16)
        return carry

    lax.fori_loop(0, seqs // group, attend, 0)

    m = x_t[...].astype(F32) + dot_nn(wo_t[...], o_t[...])
    scale = lax.rsqrt(jnp.mean(m * m, axis=0, keepdims=True) + EPSILON)
    z = m * scale
    normed = (z * g2_col).astype(BF16)
    c_t[...] = normed
    value, slope = gelu_parts(dot_nn(win_t[...], normed))
    act = value.astype(BF16)
    act_t[...] = act
    du = (dot_nn(wout[...], dy_t[...]) * slope).astype(BF16)
    du_t[...] = du
    y = m + dot_nn(wout_t[...], act)
    for s in range(seqs):
        y_out[s] = y[:, s * length : (s + 1) * length].T.astype(BF16)
    flushes = [
        pltpu.make_async_copy(src, dst, out_sem.at[k])
        for k, (src, dst) in enumerate(
            (
                (y_out, y_far), (ig_out, ig_far), (asked_out, asked_far), (early_tot, early_far),
                (late_tot, late_far), (small_tot, small_far),
            )
        )
    ]
    flushes[0].start()
    dc = dot_nn(win[...], du)
    gain_two = dc * z
    gain_two = sum(gain_two[:, s * length : (s + 1) * length] for s in range(seqs))
    small_tot[1:2, :] = jnp.sum(gain_two.T, axis=0, keepdims=True)
    e = dc * g2_col
    dm = dy_t[...].astype(F32) + scale * (e - z * jnp.mean(e * z, axis=0, keepdims=True))
    dm_t[...] = dm
    dmb = dm.astype(BF16)
    dmb_t[...] = dmb
    do_t[...] = dot_nn(wo[...], dmb).astype(BF16)

    for k in range(ff // width):
        at = slice(k * width, (k + 1) * width)
        early[at, :] = dot_nt(c_t[...], du_t[at, :]).astype(BF16)
    early[ff : 2 * ff, :] = dot_nt(act_t[...], dy_t[...]).astype(BF16)
    if early.shape[0] > 2 * ff:
        early[2 * ff :, :] = jnp.zeros((early.shape[0] - 2 * ff, width), BF16)
    early_sum.start()

    def attend_back(g):
        parts = members(g)
        do2s = [split_pair(do_t[rows[p], parts[i]]) for i, p in jobs]
        dprobs = [dot_nn(kv[parts[i], krows[p]], do2) for (i, p), do2 in zip(jobs, do2s)]
        lows = []
        for (i, p), dprob in zip(jobs, dprobs):
            prob = p_s[g * group + i, p]
            ds = prob * (dprob - jnp.sum(dprob * prob, axis=0, keepdims=True))
            dsum[p] += ds
            lows.append(ds.astype(BF16))
        for (i, p), do2 in zip(jobs, do2s):
            prob = p_s[g * group + i, p].astype(BF16)
            dqkv_t[vrows[p], parts[i]] = dot_nt(do2, prob).astype(BF16)
        for (i, p), low in zip(jobs, lows):
            q2 = split_pair(qkv_t[rows[p], parts[i]])
            dqkv_t[krows[p], parts[i]] = dot_nt(q2, low).astype(BF16)
        for (i, p), low in zip(jobs, lows):
            dq = dot_nn(qkv_t[krows[p], parts[i]], low) * (1.0 / math.sqrt(DH))
            dqkv_t[rows[p], parts[i]] = jnp.concatenate(
                [dq[:DH, :length], dq[DH:, length:]], axis=0
            ).astype(BF16)

    groups = seqs // group

    def back_loop(g, carry):
        attend_back(g)

        @pl.when(g == 0)
        def _():
            early_sum.core_to_lo()

        return carry

    lax.fori_loop(0, groups, back_loop, 0)

    xf = x_t[...].astype(F32)
    scale = lax.rsqrt(jnp.mean(xf * xf, axis=0, keepdims=True) + EPSILON)
    z = xf * scale
    da = dot_nn(wqkv[...], dqkv_t[...])
    gain_one = da * z
    gain_one = sum(gain_one[:, s * length : (s + 1) * length] for s in range(seqs))
    e = da * g1_col
    ig = dm_t[...] + scale * (e - z * jnp.mean(e * z, axis=0, keepdims=True))
    igb_t[...] = ig.astype(BF16)

    def grad_copy(j):
        back = lax.rem(n - j, n)
        return remote(
            slots.at[slot_block(j)], inc.at[core, slot_block(back)],
            grad_send.at[j], grad_recv.at[back], peer(j),
        )

    def grad_arrival(j):
        return remote(
            slots.at[slot_block(j)], inc.at[core, slot_block(j)],
            grad_send.at[j], grad_recv.at[j], peer(j),
        )

    def forward(j, which):
        ref = inc.at[which, slot_block(j)]
        return remote(ref, ref, fwd_send.at[j], fwd_recv.at[j], {"dp": 1 - core})

    def to_slots(k, carry):
        first = pl.multiple_of(k * wide_slots, wide_slots)
        slots[pl.ds(first, wide_slots), :] = dot_nt(
            hot_slots(back_pos[...], first, wide_slots), igb_t[...]
        ).astype(BF16)

        def go(j, inner):
            grad_copy(j).start()
            return inner

        owners = wide_slots // cap
        lax.fori_loop(jnp.maximum(k * owners, 1), (k + 1) * owners, go, 0)
        return carry

    steps = slots.shape[0] // wide_slots

    def send_rows(first, last):
        lax.fori_loop(first * steps // 8, last * steps // 8, to_slots, 0)

    for k in range(3 * hd // width):
        at = slice(k * width, (k + 1) * width)
        late[at, :] = dot_nt(a_t[...], dqkv_t[at, :]).astype(BF16)
    late[3 * hd : 4 * hd, :] = dot_nt(o_t[...], dmb_t[...]).astype(BF16)
    if late.shape[0] > 4 * hd:
        late[4 * hd :, :] = jnp.zeros((late.shape[0] - 4 * hd, width), BF16)
    late_sum.start()

    def pass_on(step, carry):
        j = n - 1 - step
        grad_arrival(j).wait_recv()
        forward(j, core).start()
        return carry

    late_sum.core_to_lo()
    early_sum.lo_to_hi()
    send_rows(0, 3)
    keep = pltpu.make_async_copy(slots.at[slot_block(0)], inc.at[core, slot_block(0)], smem_sem)
    keep.start()
    remote(
        slots.at[slot_block(0)], inc.at[core, slot_block(0)], fwd_send.at[0], fwd_recv.at[0],
        {"dp": 1 - core},
    ).start()
    def bias_back(r, carry):
        part = pl.ds(pl.multiple_of(r * 8, 8), 8)
        bt = buck_t[part, :]
        grads = [dsum[h // 2, part, (h % 2) * length : (h % 2 + 1) * length] for h in range(heads)]
        for b in range(bucket_count):
            here = bt == float(b)
            for h in range(heads):
                b_acc[h, b] += jnp.where(here, grads[h], 0.0)
        return carry

    lax.fori_loop(0, length // 8, bias_back, 0)
    small_parts = [jnp.sum(gain_one.T, axis=0, keepdims=True), small_tot[1:2, :]]
    for h in range(heads):
        by_bucket = jnp.sum(b_acc[h], axis=1)
        row = jnp.sum(by_bucket.T, axis=0, keepdims=True)
        small_parts.append(
            jnp.concatenate([row, jnp.zeros((1, LANES - bucket_count), F32)], axis=1)
        )
    small_sum.start(jnp.concatenate(small_parts, axis=0))
    late_sum.lo_to_hi()
    small_sum.core_to_lo()
    early_sum.hi_to_gather()
    late_sum.hi_to_gather()
    small_sum.lo_to_hi()
    send_rows(3, 6)
    early_sum.gather_to_lo()
    late_sum.gather_to_lo()
    send_rows(6, 8)
    for s in range(seqs):
        ig_out[s] = ig[:, s * length : (s + 1) * length].T
    flushes[1].start()
    early_sum.gather_to_core()
    late_sum.gather_to_core()
    lax.fori_loop(0, 15, pass_on, 0)
    small_sum.finish()
    flushes[5].start()
    early_sum.finish()
    flushes[3].start()
    late_sum.finish()
    flushes[4].start()
    share(core).wait_send()
    share(1 - core).wait_recv()
    flushes[2].start()
    keep.wait()

    def rows_in(j, carry):
        forward(j, 1 - core).wait_recv()
        forward(j, core).wait_send()
        return carry

    lax.fori_loop(0, n, rows_in, 0)

    def sent(j, carry):
        request(j).wait_send()
        back_request(j).wait_send()
        row_copy(j).wait_send()
        grad_copy(j).wait_send()
        return carry

    lax.fori_loop(1, n, sent, 0)
    for flush in flushes:
        flush.wait()


def step_kernel(n, lo, cap, used, sizes, *refs):
    parts, at = [], 0
    for size in sizes:
        parts.append(refs[at : at + size])
        at += size
    step_body(n, lo, cap, used, *parts)


def scatter_body(
    n, cap, used, asked_far, counts, inc, early, late, small, y_in, ig_in,
    y_out, ig_out, grad, g1, wq, wk, wv, wo, bias, g2, win, wout,
    acc, wide, zero, inc_v, y_v, ig_v, early_v, late_v, wq_v, wk_v, wv_v, wo_v, win_v, wout_v,
    out_sem, in_sem, pass_sem, asked, asked_sem,
):
    rows_dev, width = grad.shape
    chunk = zero.shape[0]
    domain_rows = used // 3
    per_domain = domain_rows // chunk
    slots = n * cap
    hd = wq.shape[1]
    ff = win.shape[1]
    loads = [
        pltpu.make_async_copy(src, dst, in_sem.at[k])
        for k, (src, dst) in enumerate(
            ((inc, inc_v), (early, early_v), (late, late_v), (y_in, y_v), (ig_in, ig_v))
        )
    ]
    ask = pltpu.make_async_copy(asked_far, asked, asked_sem)
    ask.start()
    loads[0].start()
    zero[...] = jnp.zeros_like(zero)

    def chunk_at(k):
        return pl.ds(pl.multiple_of(k * chunk, chunk), chunk)

    def clear_copy(k):
        return pltpu.make_async_copy(zero, grad.at[chunk_at(k)], out_sem.at[k])

    def out_copy(k):
        return pltpu.make_async_copy(acc.at[chunk_at(k)], grad.at[chunk_at(k)], out_sem.at[k])

    def in_use(k):
        return (k % per_domain) * chunk < counts[k // per_domain]

    def spare(k, carry):
        clear_copy(k).start()
        return carry

    def prepare(k, carry):
        @pl.when(in_use(k))
        def _():
            def clear(r, inner):
                at = pl.multiple_of(k * chunk + r * 256, 256)
                acc[pl.ds(at, 256), :] = jnp.zeros((256, width), F32)
                return inner

            lax.fori_loop(0, chunk // 256, clear, 0)

        return carry

    lax.fori_loop(0, used // chunk, prepare, 0)
    loads[0].wait()
    for load in loads[1:]:
        load.start()
    lax.fori_loop(used // chunk, rows_dev // chunk, spare, 0)

    def unused(k, carry):
        @pl.when(jnp.logical_not(in_use(k)))
        def _():
            clear_copy(k).start()

        return carry

    lax.fori_loop(0, used // chunk, unused, 0)

    def widen(r, carry):
        at = pl.ds(pl.multiple_of(r * 256, 256), 256)
        wide[at, :] = inc_v[at, :].astype(F32)
        return carry

    lax.fori_loop(0, 2 * slots // 256, widen, 0)

    def source(k, carry):
        base = k * 2 * LANES

        def eight(g, inner):
            first = g * 8
            ats = [asked[base + first + r] for r in range(8)]
            sums = [
                acc[pl.ds(ats[r], 1), :] + wide[pl.ds(k * cap + first + r, 1), :] for r in range(8)
            ]
            for r in range(8):
                acc[pl.ds(ats[r], 1), :] = sums[r]
            return inner

        lax.fori_loop(0, (asked[base + LANES] + 7) // 8, eight, 0)
        return carry

    ask.wait()
    lax.fori_loop(0, 2 * n, source, 0)

    def write(k, carry):
        @pl.when(in_use(k))
        def _():
            out_copy(k).start()

        return carry

    lax.fori_loop(0, used // chunk, write, 0)

    passes = []

    def hand_on(src, dst):
        passes.append(pltpu.make_async_copy(src, dst, pass_sem.at[len(passes)]))
        passes[-1].start()

    for load in loads[1:]:
        load.wait()
    hand_on(y_v, y_out)
    hand_on(ig_v, ig_out)
    for i, (value, out) in enumerate(((wq_v, wq), (wk_v, wk), (wv_v, wv))):
        for k in range(hd // width):
            at = i * hd + k * width
            value[:, k * width : (k + 1) * width] = late_v[at : at + width, :].astype(F32)
        hand_on(value, out)
    wo_v[...] = late_v[3 * hd : 4 * hd, :].astype(F32)
    hand_on(wo_v, wo)
    for k in range(ff // width):
        at = slice(k * width, (k + 1) * width)
        win_v[:, at] = early_v[at, :].astype(F32)
    hand_on(win_v, win)
    wout_v[...] = early_v[ff : 2 * ff, :].astype(F32)
    hand_on(wout_v, wout)
    g1[...] = small[0:1, :]
    g2[...] = small[1:2, :]
    heads, buckets = bias.shape
    bias[...] = small[2 : 2 + heads, 0:buckets]

    def finish(k, carry):
        clear_copy(k).wait()
        return carry

    lax.fori_loop(0, rows_dev // chunk, finish, 0)
    for copy in passes:
        copy.wait()


def on_device(
    hashed_ids, owners, domain_tags, user_counts, lengths, buckets, table, gain_one,
    query_weight_matrix, key_weight_matrix, value_weight_matrix, attention_output_weight,
    bias_table, gain_two, feedforward_input_weight, feedforward_output_weight, cotangent,
):
    n = lax.axis_size("emb")
    seqs, length = hashed_ids.shape
    tokens = seqs * length
    rows_dev, width = table.shape
    used = 3 * (rows_dev // 4)
    cap = max(2, 2 * tokens // n)
    hd = query_weight_matrix.shape[1]
    ff = feedforward_input_weight.shape[1]
    heads = hd // DH
    pairs = heads // 2
    bucket_count = bias_table.shape[0]
    slots = n * cap
    lo = 2 ** ((n.bit_length()) // 2)
    unit = 2 * n * 16
    early_rows = -(-2 * ff // unit) * unit
    late_rows = -(-4 * hd // unit) * unit
    vmem = pl.BlockSpec(memory_space=pltpu.VMEM)
    smem = pl.BlockSpec(memory_space=pltpu.SMEM)
    anywhere = pl.BlockSpec(memory_space=pl.ANY)
    dma = pltpu.SemaphoreType.DMA
    shape = jax.ShapeDtypeStruct

    operands = (
        hashed_ids, owners.reshape(seqs, length), domain_tags, user_counts, lengths, bias_table.T,
        buckets, gain_one.reshape(1, width), gain_two.reshape(1, width), table, cotangent,
        query_weight_matrix, key_weight_matrix, value_weight_matrix, attention_output_weight,
        feedforward_input_weight, feedforward_output_weight,
    )
    results = (
        shape((seqs, length, width), BF16),
        shape((seqs, length, width), F32),
        shape((2, slots, width), BF16),
        shape((2, n, 2, LANES), jnp.int32),
        shape((early_rows, width), BF16),
        shape((late_rows, width), BF16),
        shape((8, LANES), F32),
    )
    lookup_scratch = [
        pltpu.VMEM((n, 1, LANES), jnp.int32),
        pltpu.VMEM((n, 1, LANES), jnp.int32),
        pltpu.SMEM((n, 1, LANES), jnp.int32),
        pltpu.VMEM((used, width), BF16),
        pltpu.VMEM((rows_dev, width), F32),
        pltpu.VMEM((cap, width), F32),
        pltpu.VMEM((slots, width), BF16),
        pltpu.VMEM((slots, width), BF16),
        pltpu.VMEM((width, tokens), F32),
        pltpu.VMEM((seqs, length), jnp.int32),
        pltpu.VMEM((slots, width), BF16),
        pltpu.VMEM((early_rows, width), BF16),
        pltpu.VMEM((late_rows, width), BF16),
        pltpu.VMEM((seqs, length), jnp.int32),
        pltpu.VMEM((n, 2, LANES), jnp.int32),
        dma((n,)), dma((n,)),
        dma((n,)), dma((n,)), dma((n,)), dma((n,)), dma((2,)), dma((6,)), dma,
        dma((n,)), dma((n,)), dma((n,)), dma((n,)),
    ]
    block_scratch = [
        pltpu.VMEM((3 * hd, width), BF16),
        pltpu.VMEM((width, 3 * hd), BF16),
        pltpu.VMEM((width, hd), BF16),
        pltpu.VMEM((ff, width), BF16),
        pltpu.VMEM((width, ff), BF16),
        pltpu.VMEM((length, length), F32),
        pltpu.VMEM((pairs, length, 2 * length), F32),
        pltpu.VMEM((width, tokens), BF16),
        pltpu.VMEM((width, tokens), BF16),
        pltpu.VMEM((3 * hd, tokens), BF16),
        pltpu.VMEM((tokens, 2 * hd), BF16),
        pltpu.VMEM((seqs, pairs, length, 2 * length), F32),
        pltpu.VMEM((hd, tokens), BF16),
        pltpu.VMEM((width, tokens), BF16),
        pltpu.VMEM((ff, tokens), BF16),
        pltpu.VMEM((ff, tokens), BF16),
        pltpu.VMEM((width, tokens), BF16),
        pltpu.VMEM((width, tokens), F32),
        pltpu.VMEM((width, tokens), BF16),
        pltpu.VMEM((hd, tokens), BF16),
        pltpu.VMEM((3 * hd, tokens), BF16),
        pltpu.VMEM((pairs, length, 2 * length), F32),
        pltpu.VMEM((width, tokens), BF16),
        pltpu.VMEM((heads, bucket_count, 8, length), F32),
        pltpu.VMEM((seqs, length, width), BF16),
        pltpu.VMEM((width, hd), BF16),
        pltpu.VMEM((width, hd), BF16),
        pltpu.VMEM((width, hd), BF16),
        pltpu.VMEM((hd, width), BF16),
        pltpu.VMEM((width, ff), BF16),
        pltpu.VMEM((ff, width), BF16),
        dma((11,)),
        pltpu.VMEM((seqs, length), jnp.int32),
        pltpu.VMEM((seqs, length), jnp.int32),
        pltpu.SMEM((seqs,), jnp.int32),
        pltpu.SMEM((user_counts.shape[0],), jnp.int32),
        pltpu.SMEM(lengths.shape, jnp.int32),
        pltpu.SMEM((heads, bucket_count), F32),
        pltpu.VMEM((length, length), jnp.int32),
        pltpu.VMEM((1, width), F32),
        pltpu.VMEM((1, width), F32),
        dma((5,)),
    ]
    block_scratch += [pltpu.VMEM(results[k].shape, results[k].dtype) for k in (0, 1, 3, 4, 5, 6)]
    block_scratch += [dma((6,))]
    early_scratch = Reducer.scratch(n, lo, early_rows)
    late_scratch = Reducer.scratch(n, lo, late_rows)
    small_scratch = SmallReducer.scratch(n, lo)
    scratch = [lookup_scratch, block_scratch, early_scratch, late_scratch, small_scratch]
    sizes = [len(operands), len(results)] + [len(part) for part in scratch]
    y, ig, incoming, asked, early_total, late_total, small_total = pl.pallas_call(
        functools.partial(step_kernel, n, lo, cap, used, sizes),
        out_shape=results,
        in_specs=[anywhere] * len(operands),
        out_specs=(anywhere,) * len(results),
        scratch_shapes=sum(scratch, []),
        compiler_params=pltpu.CompilerParams(
            collective_id=0, has_side_effects=True, vmem_limit_bytes=VMEM_LIMIT
        ),
        name="step",
    )(*operands)

    chunk = math.gcd(1024, used // 3)
    output, input_grad, table_grad, g1, gq, gk, gv, go, gb, g2, gin, gout = pl.pallas_call(
        functools.partial(scatter_body, n, cap, used),
        out_shape=(
            shape((seqs, length, width), BF16),
            shape((seqs, length, width), F32),
            shape((rows_dev, width), F32),
            shape((1, width), F32),
            shape((width, hd), F32),
            shape((width, hd), F32),
            shape((width, hd), F32),
            shape((hd, width), F32),
            shape((heads, bucket_count), F32),
            shape((1, width), F32),
            shape((width, ff), F32),
            shape((ff, width), F32),
        ),
        in_specs=[anywhere, smem, anywhere, anywhere, anywhere, vmem, anywhere, anywhere],
        out_specs=(anywhere,) * 3 + (vmem,) + (anywhere,) * 4 + (vmem,) * 2 + (anywhere,) * 2,
        scratch_shapes=[
            pltpu.VMEM((used + 8, width), F32),
            pltpu.VMEM((2 * slots, width), F32),
            pltpu.VMEM((chunk, width), F32),
            pltpu.VMEM((2 * slots, width), BF16),
            pltpu.VMEM((seqs, length, width), BF16),
            pltpu.VMEM((seqs, length, width), F32),
            pltpu.VMEM((early_rows, width), BF16),
            pltpu.VMEM((late_rows, width), BF16),
            pltpu.VMEM((width, hd), F32),
            pltpu.VMEM((width, hd), F32),
            pltpu.VMEM((width, hd), F32),
            pltpu.VMEM((hd, width), F32),
            pltpu.VMEM((width, ff), F32),
            pltpu.VMEM((ff, width), F32),
            dma((rows_dev // chunk,)), dma((5,)), dma((8,)),
            pltpu.SMEM((2 * n * 2 * LANES,), jnp.int32), dma,
        ],
        compiler_params=pltpu.CompilerParams(vmem_limit_bytes=VMEM_LIMIT),
        name="scatter",
    )(
        asked.reshape(-1), user_counts, incoming.reshape(2 * slots, width), early_total, late_total,
        small_total, y, ig,
    )
    return (
        output, input_grad, table_grad, g1.reshape(width), gq, gk, gv, go, gb.T, g2.reshape(width),
        gin, gout,
    )


def solution(mesh):
    split = ("emb", "dp")
    return jax.shard_map(
        on_device,
        mesh=mesh,
        in_specs=(
            P(split, None), P(split, None, None), P(split), P(), P(split, None), P(),
            P("emb", None), P(), P(), P(), P(), P(), P(), P(), P(), P(), P(split, None, None),
        ),
        out_specs=(
            P(split, None, None), P(split, None, None), P("emb", None), P(), P(), P(), P(), P(),
            P(), P(), P(), P(),
        ),
        check_vma=False,
    )
```

```python
import functools
import math

import jax
import jax.numpy as jnp
from jax import lax
from jax.experimental import pallas as pl
from jax.experimental.pallas import tpu as pltpu
from jax.sharding import PartitionSpec as P

DH = 64
LANES = 128
EPSILON = 1e-06
MESH = pl.DeviceIdType.MESH
F32 = jnp.float32
BF16 = jnp.bfloat16
VMEM_LIMIT = 60 * 1024 * 1024


def dot_nn(a, b):
    return lax.dot_general(a, b, (((1,), (0,)), ((), ())), preferred_element_type=F32)


def dot_nt(a, b):
    return lax.dot_general(a, b, (((1,), (1,)), ((), ())), preferred_element_type=F32)


def dot_tn(a, b):
    return lax.dot_general(a, b, (((0,), (0,)), ((), ())), preferred_element_type=F32)


def hot_slots(pos, first, count):
    rows = lax.broadcasted_iota(jnp.int32, (count, LANES), 0) + first
    parts = [
        jnp.where(rows == pos[s : s + 1, :], 1.0, 0.0).astype(BF16) for s in range(pos.shape[0])
    ]
    return jnp.concatenate(parts, axis=1)


def remote(src, dst, send_sem, recv_sem, device):
    return pltpu.make_async_remote_copy(
        src_ref=src, dst_ref=dst, send_sem=send_sem, recv_sem=recv_sem,
        device_id=device, device_id_type=MESH,
    )


def gelu_parts(u):
    k0 = math.sqrt(2.0 / math.pi)
    k1 = k0 * 0.044715
    square = u * u
    half = 0.5 * jnp.tanh(u * (k1 * square + k0)) + 0.5
    value = u * half
    slope = half + (2.0 * value) * (1.0 - half) * (3.0 * k1 * square + k0)
    return value, slope


def split_pair(both):
    zero = jnp.zeros((DH, LANES), both.dtype)
    left = jnp.concatenate([both[:DH], zero], axis=0)
    right = jnp.concatenate([zero, both[DH:]], axis=0)
    return jnp.concatenate([left, right], axis=1)


class Reducer:
    def __init__(self, n, lo, me, core, part, total, bufs):
        self.n, self.lo, self.hi, self.core = n, lo, n // lo, core
        self.my_hi, self.my_lo = me // lo, lax.rem(me, lo)
        self.part, self.total = part, total
        (
            self.core_buf, self.half, self.lo_buf, self.quarter, self.hi_buf, self.core_sem,
            self.lo_sem, self.hi_sem, self.gh_sem, self.gl_sem, self.gc_sem,
        ) = bufs
        self.half_rows, self.lo_rows = self.half.shape[0], self.quarter.shape[0]
        self.hi_rows = self.hi_buf.shape[1]

    @staticmethod
    def scratch(n, lo, rows):
        hi, dma, width = n // lo, pltpu.SemaphoreType.DMA, LANES
        return [
            pltpu.VMEM((rows // 2, width), BF16),
            pltpu.VMEM((rows // 2, width), BF16),
            pltpu.VMEM((lo, rows // 2 // lo, width), BF16),
            pltpu.VMEM((rows // 2 // lo, width), BF16),
            pltpu.VMEM((hi, rows // 2 // n, width), BF16),
            dma((2,)), dma((2, lo)), dma((2, hi)), dma((2, hi)), dma((2, lo)), dma((2, lo)),
        ]

    def lo_device(self, k):
        return {"emb": self.my_hi * self.lo + self.lo_peer(k)}

    def hi_device(self, k):
        return {"emb": self.hi_peer(k) * self.lo + self.my_lo}

    def lo_peer(self, k):
        return lax.rem(self.my_lo + k, self.lo)

    def hi_peer(self, k):
        return lax.rem(self.my_hi + k, self.hi)

    def swap(self):
        at = pl.ds(pl.multiple_of((1 - self.core) * self.half_rows, self.half_rows), self.half_rows)
        return remote(
            self.part.at[at], self.core_buf, self.core_sem.at[0], self.core_sem.at[1],
            {"dp": 1 - self.core},
        )

    def lo_copy(self, k):
        at = pl.ds(pl.multiple_of(self.lo_peer(k) * self.lo_rows, self.lo_rows), self.lo_rows)
        return remote(
            self.half.at[at], self.lo_buf.at[self.lo - k],
            self.lo_sem.at[0, k], self.lo_sem.at[1, self.lo - k], self.lo_device(k),
        )

    def lo_arrival(self, k):
        return remote(
            self.quarter, self.lo_buf.at[k],
            self.lo_sem.at[0, k], self.lo_sem.at[1, k], self.lo_device(k),
        )

    def hi_copy(self, k):
        at = pl.ds(pl.multiple_of(self.hi_peer(k) * self.hi_rows, self.hi_rows), self.hi_rows)
        return remote(
            self.quarter.at[at], self.hi_buf.at[self.hi - k],
            self.hi_sem.at[0, k], self.hi_sem.at[1, self.hi - k], self.hi_device(k),
        )

    def hi_arrival(self, k):
        return remote(
            self.hi_buf.at[k], self.hi_buf.at[k],
            self.hi_sem.at[0, k], self.hi_sem.at[1, k], self.hi_device(k),
        )

    def piece(self, h):
        at = self.core * self.half_rows + self.my_lo * self.lo_rows + h * self.hi_rows
        return self.total.at[pl.ds(pl.multiple_of(at, self.hi_rows), self.hi_rows)]

    def block(self, core, low):
        at = core * self.half_rows + low * self.lo_rows
        return self.total.at[pl.ds(pl.multiple_of(at, self.lo_rows), self.lo_rows)]

    def gather_hi(self, k):
        mine = self.piece(self.my_hi)
        return remote(
            mine, mine, self.gh_sem.at[0, k], self.gh_sem.at[1, self.hi - k], self.hi_device(k)
        )

    def gather_hi_arrival(self, k):
        other = self.piece(self.hi_peer(k))
        return remote(other, other, self.gh_sem.at[0, k], self.gh_sem.at[1, k], self.hi_device(k))

    def gather_lo(self, k):
        mine = self.block(self.core, self.my_lo)
        return remote(
            mine, mine, self.gl_sem.at[0, k], self.gl_sem.at[1, self.lo - k], self.lo_device(k)
        )

    def gather_lo_arrival(self, k):
        other = self.block(self.core, self.lo_peer(k))
        return remote(other, other, self.gl_sem.at[0, k], self.gl_sem.at[1, k], self.lo_device(k))

    def gather_core(self, low):
        mine = self.block(self.core, low)
        return remote(
            mine, mine, self.gc_sem.at[0, low], self.gc_sem.at[1, low], {"dp": 1 - self.core}
        )

    def gather_core_arrival(self, low):
        other = self.block(1 - self.core, low)
        return remote(
            other, other, self.gc_sem.at[0, low], self.gc_sem.at[1, low], {"dp": 1 - self.core}
        )

    def start(self):
        self.swap().start()

    def core_to_lo(self):
        self.swap().wait()
        step = self.hi_rows

        def add(r, carry):
            at = pl.multiple_of(r * step, step)
            own = self.part[pl.ds(pl.multiple_of(self.core * self.half_rows + at, step), step), :]
            other = self.core_buf[pl.ds(at, step), :]
            self.half[pl.ds(at, step), :] = (own.astype(F32) + other.astype(F32)).astype(BF16)
            return carry

        lax.fori_loop(0, self.half_rows // step, add, 0)
        for k in range(1, self.lo):
            self.lo_copy(k).start()

    def lo_to_hi(self):
        for k in range(1, self.lo):
            self.lo_arrival(k).wait_recv()
        step = self.hi_rows

        def add(r, carry):
            at = pl.multiple_of(r * step, step)
            mine = pl.ds(pl.multiple_of(self.my_lo * self.lo_rows + at, step), step)
            total = self.half[mine, :].astype(F32)
            for k in range(1, self.lo):
                total = total + self.lo_buf[k, pl.ds(at, step), :].astype(F32)
            self.quarter[pl.ds(at, step), :] = total.astype(BF16)
            return carry

        lax.fori_loop(0, self.lo_rows // step, add, 0)
        for k in range(1, self.hi):
            self.hi_copy(k).start()

    def hi_to_gather(self):
        for k in range(1, self.hi):
            self.hi_arrival(k).wait_recv()
        mine = pl.ds(pl.multiple_of(self.my_hi * self.hi_rows, self.hi_rows), self.hi_rows)
        total = self.quarter[mine, :].astype(F32)
        for k in range(1, self.hi):
            total = total + self.hi_buf[k].astype(F32)
        self.piece(self.my_hi)[...] = total.astype(BF16)
        for k in range(1, self.hi):
            self.gather_hi(k).start()

    def gather_to_lo(self):
        for k in range(1, self.hi):
            self.gather_hi_arrival(k).wait_recv()
        for k in range(1, self.lo):
            self.gather_lo(k).start()
        self.gather_core(self.my_lo).start()

    def gather_to_core(self):
        for k in range(1, self.lo):
            self.gather_lo_arrival(k).wait_recv()
            self.gather_core(self.lo_peer(k)).start()

    def finish(self):
        for low in range(self.lo):
            self.gather_core_arrival(low).wait_recv()
        for k in range(1, self.lo):
            self.lo_copy(k).wait_send()
            self.gather_lo(k).wait_send()
        for k in range(1, self.hi):
            self.hi_copy(k).wait_send()
            self.gather_hi(k).wait_send()
        for low in range(self.lo):
            self.gather_core(low).wait_send()


class SmallReducer:
    def __init__(self, n, lo, me, core, total, bufs):
        self.lo, self.hi, self.core = lo, n // lo, core
        self.my_hi, self.my_lo = me // lo, lax.rem(me, lo)
        self.total = total
        self.a, self.b, self.c, self.a_sem, self.b_sem, self.c_sem = bufs

    @staticmethod
    def scratch(n, lo):
        hi, dma = n // lo, pltpu.SemaphoreType.DMA
        return [
            pltpu.VMEM((2, 8, LANES), F32),
            pltpu.VMEM((lo, 8, LANES), F32),
            pltpu.VMEM((hi, 8, LANES), F32),
            dma((2,)), dma((2, lo)), dma((2, hi)),
        ]

    def swap(self, slot):
        ref = self.a.at[slot]
        return remote(ref, ref, self.a_sem.at[0], self.a_sem.at[1], {"dp": 1 - self.core})

    def lo_copy(self, k, slot, come):
        device = {"emb": self.my_hi * self.lo + lax.rem(self.my_lo + k, self.lo)}
        ref = self.b.at[slot]
        return remote(ref, ref, self.b_sem.at[0, k], self.b_sem.at[1, come], device)

    def hi_copy(self, k, slot, come):
        device = {"emb": lax.rem(self.my_hi + k, self.hi) * self.lo + self.my_lo}
        ref = self.c.at[slot]
        return remote(ref, ref, self.c_sem.at[0, k], self.c_sem.at[1, come], device)

    def start(self, value):
        self.a[self.core] = value
        self.swap(self.core).start()

    def core_to_lo(self):
        self.swap(self.core).wait_send()
        self.swap(1 - self.core).wait_recv()
        self.b[self.my_lo] = self.a[0] + self.a[1]
        for k in range(1, self.lo):
            self.lo_copy(k, self.my_lo, self.lo - k).start()

    def lo_to_hi(self):
        for k in range(1, self.lo):
            self.lo_copy(k, lax.rem(self.my_lo + k, self.lo), k).wait_recv()
        total = self.b[0]
        for k in range(1, self.lo):
            total = total + self.b[k]
        self.c[self.my_hi] = total
        for k in range(1, self.hi):
            self.hi_copy(k, self.my_hi, self.hi - k).start()

    def finish(self):
        for k in range(1, self.hi):
            self.hi_copy(k, lax.rem(self.my_hi + k, self.hi), k).wait_recv()
        total = self.c[0]
        for k in range(1, self.hi):
            total = total + self.c[k]
        self.total[...] = total
        for k in range(1, self.lo):
            self.lo_copy(k, self.my_lo, self.lo - k).wait_send()
        for k in range(1, self.hi):
            self.hi_copy(k, self.my_hi, self.hi - k).wait_send()


def step_body(
    n, lo, cap, gcap, used, refs_in, refs_out, lookup_refs, block_refs, early_refs, late_refs, small_refs,
):
    (
        ids_far, own_far, tags_far, counts_far, lens_far, btab_far, buckets_far, g1_far, g2_far,
        table, *far,
    ) = refs_in
    y_far, ig_far, inc, asked_far, early_far, late_far, small_far, over, excess = refs_out
    (
        req, asked_v, asked_s, tab_low, tab, gbuf, send, recv, x_acc, pos_ref, slots, early, late,
        back_pos, back_req, back_send, back_recv,
        req_send, req_recv, row_send, row_recv, pair_sem, tab_sem, smem_sem,
        grad_send, grad_recv, fwd_send, fwd_recv,
    ) = lookup_refs
    (
        wqkv_t, wqkv, wo_t, win_t, wout_t, buck_t, bias, x_t, a_t, qkv_t, kv, p_s, o_t, c_t, act_t,
        du_t, dy_t, dm_t, dmb_t, do_t, dqkv_t, dsum, igb_t, b_acc,
        cot, wq, wk, wv, wo, win, wout, near_sem,
        ids, own, tags, counts, lens, btab, buckets, g1, g2, first_sem,
        y_out, ig_out, asked_out, early_tot, late_tot, small_tot, out_sem,
    ) = block_refs
    near = (cot, wq, wk, wv, wo, win, wout, btab, buckets, g1, g2)
    far = tuple(far) + (btab_far, buckets_far, g1_far, g2_far)
    me = lax.axis_index("emb")
    core = lax.axis_index("dp")
    seqs, length = ids.shape
    width = cot.shape[2]
    tokens = seqs * length
    hd, ff = wq.shape[1], win.shape[1]
    heads = hd // DH
    pairs = heads // 2
    bucket_count = btab.shape[1]
    domain_rows = used // 3
    row_limit = 4 * domain_rows
    pieces = tab_sem.shape[0]
    piece = used // pieces
    group = 4
    owners_at_once = max(1, 256 // cap)
    wide_slots = owners_at_once * gcap
    ocap = cap - gcap
    early_sum = Reducer(n, lo, me, core, early, early_tot, early_refs)
    late_sum = Reducer(n, lo, me, core, late, late_tot, late_refs)
    small_sum = SmallReducer(n, lo, me, core, small_tot, small_refs)

    barrier = pltpu.get_barrier_semaphore()

    def peer(j):
        return {"emb": lax.rem(me + j, n)}

    def greet(k, carry):
        pl.semaphore_signal(barrier, inc=1, device_id=peer(k), device_id_type=MESH)
        return carry

    lax.fori_loop(1, n, greet, 0)
    pl.semaphore_signal(barrier, inc=1, device_id={"dp": 1 - core}, device_id_type=MESH)
    first = [
        pltpu.make_async_copy(src, dst, first_sem.at[k])
        for k, (src, dst) in enumerate(
            (
                (ids_far, ids), (own_far, own), (tags_far, tags), (counts_far, counts),
                (lens_far, lens),
            )
        )
    ]
    for fetch in first:
        fetch.start()

    def table_copy(c):
        part = pl.ds(c * piece, piece)
        return pltpu.make_async_copy(table.at[part], tab_low.at[part], tab_sem.at[c])

    for c in range(pieces):
        table_copy(c).start()
    fetches = [
        pltpu.make_async_copy(src, dst, near_sem.at[k])
        for k, (src, dst) in enumerate(zip(far, near))
    ]
    for fetch in fetches:
        fetch.start()

    for fetch in first:
        fetch.wait()

    row_id = lax.broadcasted_iota(jnp.int32, (seqs, length), 0)
    lane_id = lax.broadcasted_iota(jnp.int32, (seqs, length), 1)
    count_of = jnp.ones((seqs, length), F32)
    tag_of = jnp.zeros((seqs, length), jnp.int32)
    len_of = jnp.zeros((seqs, length), jnp.int32)
    for s in range(seqs):
        tag = tags[s]
        count_of = jnp.where(row_id == s, counts[tag].astype(F32), count_of)
        tag_of = jnp.where(row_id == s, tag, tag_of)
        len_of = jnp.where(row_id == s, lens[0, s], len_of)
    code = ids[...].astype(F32)
    turns = jnp.floor((code + 0.5) / jnp.maximum(count_of, 1.0))
    local = tag_of * domain_rows + (code - turns * count_of).astype(jnp.int32)
    live = lane_id < len_of
    rel = own[...] - me
    rel = jnp.where(rel < 0, rel + n, rel)

    owner_id = lax.broadcasted_iota(jnp.int32, (n, length), 0)
    hots = [jnp.where(owner_id == rel[s : s + 1, :], 1.0, 0.0) for s in range(seqs)]
    before = (
        lax.broadcasted_iota(jnp.int32, (length, length), 0)
        < lax.broadcasted_iota(jnp.int32, (length, length), 1)
    )
    earlier = jnp.where(before, 1.0, 0.0).astype(BF16)
    prefix = dot_nn(jnp.concatenate(hots, axis=0).astype(BF16), earlier)
    running = jnp.zeros((n, 1), F32)
    ranks = []
    for s in range(seqs):
        ranks.append(
            jnp.sum(hots[s] * (prefix[s * n : s * n + n] + running), axis=0, keepdims=True)
        )
        running = running + jnp.sum(hots[s], axis=1, keepdims=True)
    rank = jnp.concatenate(ranks, axis=0).astype(jnp.int32)
    pos_ref[...] = rel * cap + rank

    low = (local & 255).astype(F32)
    high = lax.shift_right_logical(local, 8).astype(F32)
    slot_id = lax.broadcasted_iota(jnp.int32, (LANES, length), 0)
    asking = jnp.zeros((2 * n, LANES), F32)
    for s in range(seqs):
        hot = hots[s]
        values = jnp.concatenate([hot * high[s : s + 1, :], hot * low[s : s + 1, :]], axis=0)
        slot_hot = jnp.where(slot_id == rank[s : s + 1, :], 1.0, 0.0).astype(BF16)
        asking = asking + dot_nt(values.astype(BF16), slot_hot)
    wanted = (asking[:n] * 256.0 + asking[n:]).astype(jnp.int32)
    for j in range(n):
        req[j] = wanted[j : j + 1, :]

    pl.semaphore_wait(barrier, n)

    def request(j):
        back = lax.rem(n - j, n)
        return remote(req.at[j], asked_v.at[back], req_send.at[j], req_recv.at[back], peer(j))

    def request_arrival(j):
        return remote(req.at[j], asked_v.at[j], req_send.at[j], req_recv.at[j], peer(j))

    def ask(j, carry):
        request(j).start()
        return carry

    lax.fori_loop(1, n, ask, 0)
    asked_v[0] = req[0]

    for c in range(pieces):
        table_copy(c).wait()

        def widen(r, carry):
            part = pl.ds(pl.multiple_of(c * piece + r * 256, 256), 256)
            tab[part, :] = tab_low[part, :].astype(F32)
            return carry

        lax.fori_loop(0, piece // 256, widen, 0)

    def all_asked(j, carry):
        request_arrival(j).wait_recv()
        return carry

    lax.fori_loop(1, n, all_asked, 0)
    to_scalar = pltpu.make_async_copy(asked_v, asked_s, smem_sem)
    to_scalar.start()
    to_scalar.wait()

    def slot_block(j):
        return pl.ds(pl.multiple_of(j * cap, cap), cap)

    def row_copy(j):
        back = lax.rem(n - j, n)
        return remote(
            send.at[slot_block(j)], recv.at[slot_block(back)],
            row_send.at[j], row_recv.at[back], peer(j),
        )

    def row_arrival(j):
        at = slot_block(j)
        return remote(send.at[at], recv.at[at], row_send.at[j], row_recv.at[j], peer(j))

    def gather(j):
        def some(c, carry):
            for r in range(16):
                at = asked_s[j, 0, c * 16 + r] & (row_limit - 1)
                gbuf[pl.ds(c * 16 + r, 1), :] = tab[pl.ds(at, 1), :]
            return carry

        lax.fori_loop(0, cap // 16, some, 0)
        return gbuf[...].astype(BF16)

    def pair_at(step):
        half = (step + 1) // 2
        return jnp.where(lax.rem(step, 2) == 1, n // 4 - half, n // 4 + half)

    def serve(step, carry):
        def one(j, inner):
            send[slot_block(j), :] = gather(j)
            row_copy(j).start()
            return inner

        last = n - 2 * pair_at(step)
        return lax.fori_loop(last - 1, jnp.minimum(last + 1, n), one, carry)

    lax.fori_loop(0, n // 2, serve, 0)
    recv[0:cap, :] = gather(0)

    key = jnp.where(live, (rel * row_limit + local).astype(F32), -1.0)
    key_cols = [
        jnp.broadcast_to(key[s : s + 1, :], (length, length)).T for s in range(seqs)
    ]
    fresh = []
    for s in range(seqs):
        seen = jnp.where(before & (key_cols[s] == key[s : s + 1, :]), 1.0, 0.0)
        for e in range(s):
            seen = jnp.maximum(seen, jnp.where(key_cols[e] == key[s : s + 1, :], 1.0, 0.0))
        fresh.append(1.0 - jnp.max(seen, axis=0, keepdims=True))
    fresh = [jnp.where(live[s : s + 1, :], fresh[s], 0.0) for s in range(seqs)]
    news = [hots[s] * fresh[s] for s in range(seqs)]
    prefix = dot_nn(jnp.concatenate(news, axis=0).astype(BF16), earlier)
    running = jnp.zeros((n, 1), F32)
    firsts = []
    for s in range(seqs):
        firsts.append(
            jnp.sum(news[s] * (prefix[s * n : s * n + n] + running), axis=0, keepdims=True)
        )
        running = running + jnp.sum(news[s], axis=1, keepdims=True)
    first_cols = [
        jnp.broadcast_to(firsts[s] * fresh[s] + fresh[s], (length, length)).T for s in range(seqs)
    ]
    found = []
    for s in range(seqs):
        at = jnp.zeros((length, length), F32)
        for e in range(s + 1):
            at = jnp.maximum(at, jnp.where(key_cols[e] == key[s : s + 1, :], first_cols[e], 0.0))
        found.append(jnp.max(at, axis=0, keepdims=True))
    found = jnp.concatenate(found, axis=0).astype(jnp.int32) - 1
    back_at = rel * gcap + found
    if ocap:
        back_at = jnp.where(found < gcap, back_at, n * gcap + rel * ocap + found - gcap)
    back_pos[...] = jnp.where(live, back_at, -1)
    below = used - local
    low = (below & 255).astype(F32)
    high = lax.shift_right_logical(below, 8).astype(F32)
    asking = jnp.zeros((2 * n, LANES), F32)
    for s in range(seqs):
        values = jnp.concatenate(
            [news[s] * high[s : s + 1, :], news[s] * low[s : s + 1, :]], axis=0
        )
        slot_hot = jnp.where(slot_id == firsts[s].astype(jnp.int32), 1.0, 0.0).astype(BF16)
        asking = asking + dot_nt(values.astype(BF16), slot_hot)
    wanted = used - (asking[:n] * 256.0 + asking[n:]).astype(jnp.int32)
    lane = lax.broadcasted_iota(jnp.int32, (n, LANES), 1)
    largest = jnp.max(running, axis=0, keepdims=True)
    limits = jnp.where(lane == 0, running, largest).astype(jnp.int32)
    for j in range(n):
        back_req[j, 0:1] = wanted[j : j + 1, :]
        back_req[j, 1:2] = limits[j : j + 1, :]
    asked_out[core, 0] = back_req[0]

    def back_request(j):
        back = lax.rem(n - j, n)
        return remote(
            back_req.at[j], asked_out.at[core, back], back_send.at[j], back_recv.at[back], peer(j)
        )

    def back_request_arrival(j):
        return remote(
            back_req.at[j], asked_out.at[core, j], back_send.at[j], back_recv.at[j], peer(j)
        )

    def tell(j, carry):
        back_request(j).start()
        return carry

    lax.fori_loop(1, n, tell, 0)

    def share(which):
        ref = asked_out.at[which]
        return remote(ref, ref, pair_sem.at[0], pair_sem.at[1], {"dp": 1 - core})

    for fetch in fetches:
        fetch.wait()
    for part, w in enumerate((wq, wk, wv)):
        wqkv[:, part * hd : (part + 1) * hd] = w[...]
        wqkv_t[part * hd : (part + 1) * hd, :] = w[...].T
    wo_t[...] = wo[...].T
    win_t[...] = win[...].T
    wout_t[...] = wout[...].T
    buck_t[...] = buckets[...].astype(F32).T
    g1_col = jnp.broadcast_to(g1[...], (8, width)).T[:, 0:1]
    g2_col = jnp.broadcast_to(g2[...], (8, width)).T[:, 0:1]
    dsum[...] = jnp.zeros_like(dsum)
    b_acc[...] = jnp.zeros_like(b_acc)

    def bias_rows(r, carry):
        part = pl.ds(pl.multiple_of(r * 8, 8), 8)
        bt = buck_t[part, :]
        rows = [jnp.zeros((8, length), F32) for _ in range(heads)]
        for b in range(bucket_count):
            here = bt == float(b)
            rows = [jnp.where(here, btab[h, b], rows[h]) for h in range(heads)]
        for p in range(pairs):
            bias[p, part, :] = jnp.concatenate(rows[2 * p : 2 * p + 2], axis=1)
        return carry

    lax.fori_loop(0, length // 8, bias_rows, 0)

    def load_dy(s, carry):
        part = pl.ds(pl.multiple_of(s * length, length), length)
        alive = lax.broadcasted_iota(jnp.int32, (width, length), 1) < lens[0, s]
        dy_t[:, part] = jnp.where(alive, cot[s].astype(F32).T, 0.0).astype(BF16)
        return carry

    lax.fori_loop(0, seqs, load_dy, 0)

    def place(step, carry):
        pair = pair_at(step)

        def ready(j, inner):
            row_arrival(j).wait_recv()
            return inner

        lax.fori_loop(jnp.maximum(2 * pair, 1), 2 * pair + 2, ready, 0)
        first = pl.multiple_of(pair * 2 * cap, 2 * cap)
        hot = hot_slots(pos_ref[...], first, 2 * cap)
        got = dot_tn(recv[pl.ds(first, 2 * cap), :], hot)

        @pl.when(step == 0)
        def _():
            x_acc[...] = got

        @pl.when(step > 0)
        def _():
            x_acc[...] += got

        return carry

    lax.fori_loop(0, n // 2, place, 0)

    def told(j, carry):
        back_request_arrival(j).wait_recv()
        return carry

    lax.fori_loop(1, n, told, 0)
    share(core).start()
    x_t[...] = x_acc[...].astype(BF16)

    xf = x_acc[...]
    scale = lax.rsqrt(jnp.mean(xf * xf, axis=0, keepdims=True) + EPSILON)
    a = (xf * scale * g1_col).astype(BF16)
    a_t[...] = a
    out = dot_nn(wqkv_t[...], a)
    qkv_t[0:hd, :] = out[:hd].astype(BF16) * jnp.array(1.0 / math.sqrt(DH), BF16)
    qkv_t[hd:, :] = out[hd:].astype(BF16)
    kv[...] = dot_nn(a.T, wqkv[:, hd:]).astype(BF16)

    rows = [slice(p * 2 * DH, (p + 1) * 2 * DH) for p in range(pairs)]
    krows = [slice(hd + p * 2 * DH, hd + (p + 1) * 2 * DH) for p in range(pairs)]
    vrows = [slice(2 * hd + p * 2 * DH, 2 * hd + (p + 1) * 2 * DH) for p in range(pairs)]
    jobs = [(i, p) for i in range(group) for p in range(pairs)]

    def members(g):
        return [pl.ds(pl.multiple_of((g * group + i) * length, length), length) for i in range(group)]

    def attend(g, carry):
        parts = members(g)
        key_id = lax.broadcasted_iota(jnp.int32, (length, 2 * length), 0)
        visible = [key_id < lens[0, g * group + i] for i in range(group)]
        scores = [
            dot_nn(kv[parts[i], rows[p]], split_pair(qkv_t[rows[p], parts[i]])) for i, p in jobs
        ]
        probs = []
        for (i, p), score in zip(jobs, scores):
            score = jnp.where(visible[i], score + bias[p], -1000000000.0)
            expo = jnp.exp(score - jnp.max(score, axis=0, keepdims=True))
            prob = expo * (1.0 / jnp.sum(expo, axis=0, keepdims=True))
            p_s[g * group + i, p] = prob
            probs.append(prob.astype(BF16))
        for (i, p), prob in zip(jobs, probs):
            mixed = dot_nn(qkv_t[vrows[p], parts[i]], prob)
            o_t[rows[p], parts[i]] = jnp.concatenate(
                [mixed[:DH, :length], mixed[DH:, length:]], axis=0
            ).astype(BF16)
        return carry

    lax.fori_loop(0, seqs // group, attend, 0)

    m = x_t[...].astype(F32) + dot_nn(wo_t[...], o_t[...])
    scale = lax.rsqrt(jnp.mean(m * m, axis=0, keepdims=True) + EPSILON)
    z = m * scale
    normed = (z * g2_col).astype(BF16)
    c_t[...] = normed
    value, slope = gelu_parts(dot_nn(win_t[...], normed))
    act = value.astype(BF16)
    act_t[...] = act
    du = (dot_nn(wout[...], dy_t[...]) * slope).astype(BF16)
    du_t[...] = du
    y = m + dot_nn(wout_t[...], act)
    for s in range(seqs):
        y_out[s] = y[:, s * length : (s + 1) * length].T.astype(BF16)
    flushes = [
        pltpu.make_async_copy(src, dst, out_sem.at[k])
        for k, (src, dst) in enumerate(
            (
                (y_out, y_far), (ig_out, ig_far), (asked_out, asked_far), (early_tot, early_far),
                (late_tot, late_far), (small_tot, small_far),
            )
        )
    ]
    flushes[0].start()
    dc = dot_nn(win[...], du)
    gain_two = dc * z
    gain_two = sum(gain_two[:, s * length : (s + 1) * length] for s in range(seqs))
    small_tot[1:2, :] = jnp.sum(gain_two.T, axis=0, keepdims=True)
    e = dc * g2_col
    dm = dy_t[...].astype(F32) + scale * (e - z * jnp.mean(e * z, axis=0, keepdims=True))
    dm_t[...] = dm
    dmb = dm.astype(BF16)
    dmb_t[...] = dmb
    do_t[...] = dot_nn(wo[...], dmb).astype(BF16)

    for k in range(ff // width):
        at = slice(k * width, (k + 1) * width)
        early[at, :] = dot_nt(c_t[...], du_t[at, :]).astype(BF16)
    early[ff : 2 * ff, :] = dot_nt(act_t[...], dy_t[...]).astype(BF16)
    if early.shape[0] > 2 * ff:
        early[2 * ff :, :] = jnp.zeros((early.shape[0] - 2 * ff, width), BF16)
    early_sum.start()

    def attend_back(g):
        parts = members(g)
        do2s = [split_pair(do_t[rows[p], parts[i]]) for i, p in jobs]
        dprobs = [dot_nn(kv[parts[i], krows[p]], do2) for (i, p), do2 in zip(jobs, do2s)]
        lows = []
        for (i, p), dprob in zip(jobs, dprobs):
            prob = p_s[g * group + i, p]
            ds = prob * (dprob - jnp.sum(dprob * prob, axis=0, keepdims=True))
            dsum[p] += ds
            lows.append(ds.astype(BF16))
        for (i, p), do2 in zip(jobs, do2s):
            prob = p_s[g * group + i, p].astype(BF16)
            dqkv_t[vrows[p], parts[i]] = dot_nt(do2, prob).astype(BF16)
        for (i, p), low in zip(jobs, lows):
            q2 = split_pair(qkv_t[rows[p], parts[i]])
            dqkv_t[krows[p], parts[i]] = dot_nt(q2, low).astype(BF16)
        for (i, p), low in zip(jobs, lows):
            dq = dot_nn(qkv_t[krows[p], parts[i]], low) * (1.0 / math.sqrt(DH))
            dqkv_t[rows[p], parts[i]] = jnp.concatenate(
                [dq[:DH, :length], dq[DH:, length:]], axis=0
            ).astype(BF16)

    groups = seqs // group

    def back_loop(g, carry):
        attend_back(g)

        @pl.when(g == 0)
        def _():
            early_sum.core_to_lo()

        return carry

    lax.fori_loop(0, groups, back_loop, 0)

    xf = x_t[...].astype(F32)
    scale = lax.rsqrt(jnp.mean(xf * xf, axis=0, keepdims=True) + EPSILON)
    z = xf * scale
    da = dot_nn(wqkv[...], dqkv_t[...])
    gain_one = da * z
    gain_one = sum(gain_one[:, s * length : (s + 1) * length] for s in range(seqs))
    e = da * g1_col
    ig = dm_t[...] + scale * (e - z * jnp.mean(e * z, axis=0, keepdims=True))
    igb_t[...] = ig.astype(BF16)

    def grad_block(j):
        return pl.ds(pl.multiple_of(j * gcap, gcap), gcap)

    def grad_copy(j):
        back = lax.rem(n - j, n)
        return remote(
            slots.at[grad_block(j)], inc.at[core, grad_block(back)],
            grad_send.at[j], grad_recv.at[back], peer(j),
        )

    def grad_arrival(j):
        return remote(
            slots.at[grad_block(j)], inc.at[core, grad_block(j)],
            grad_send.at[j], grad_recv.at[j], peer(j),
        )

    def forward(j, which):
        ref = inc.at[which, grad_block(j)]
        return remote(ref, ref, fwd_send.at[j], fwd_recv.at[j], {"dp": 1 - core})

    def to_slots(k, carry):
        first = pl.multiple_of(k * wide_slots, wide_slots)
        slots[pl.ds(first, wide_slots), :] = dot_nt(
            hot_slots(back_pos[...], first, wide_slots), igb_t[...]
        ).astype(BF16)

        def go(j, inner):
            grad_copy(j).start()
            return inner

        owners = owners_at_once
        lax.fori_loop(jnp.maximum(k * owners, 1), (k + 1) * owners, go, 0)
        return carry

    steps = n // owners_at_once

    def send_rows(first, last):
        lax.fori_loop(first * steps // 8, last * steps // 8, to_slots, 0)

    for k in range(3 * hd // width):
        at = slice(k * width, (k + 1) * width)
        late[at, :] = dot_nt(a_t[...], dqkv_t[at, :]).astype(BF16)
    late[3 * hd : 4 * hd, :] = dot_nt(o_t[...], dmb_t[...]).astype(BF16)
    if late.shape[0] > 4 * hd:
        late[4 * hd :, :] = jnp.zeros((late.shape[0] - 4 * hd, width), BF16)
    late_sum.start()

    def pass_on(step, carry):
        j = n - 1 - step
        grad_arrival(j).wait_recv()
        forward(j, core).start()
        return carry

    late_sum.core_to_lo()
    early_sum.lo_to_hi()
    send_rows(0, 3)
    keep = pltpu.make_async_copy(slots.at[grad_block(0)], inc.at[core, grad_block(0)], smem_sem)
    keep.start()
    remote(
        slots.at[grad_block(0)], inc.at[core, grad_block(0)], fwd_send.at[0], fwd_recv.at[0],
        {"dp": 1 - core},
    ).start()
    def bias_back(r, carry):
        part = pl.ds(pl.multiple_of(r * 8, 8), 8)
        bt = buck_t[part, :]
        grads = [dsum[h // 2, part, (h % 2) * length : (h % 2 + 1) * length] for h in range(heads)]
        for b in range(bucket_count):
            here = bt == float(b)
            for h in range(heads):
                b_acc[h, b] += jnp.where(here, grads[h], 0.0)
        return carry

    lax.fori_loop(0, length // 8, bias_back, 0)
    small_parts = [jnp.sum(gain_one.T, axis=0, keepdims=True), small_tot[1:2, :]]
    for h in range(heads):
        by_bucket = jnp.sum(b_acc[h], axis=1)
        row = jnp.sum(by_bucket.T, axis=0, keepdims=True)
        small_parts.append(
            jnp.concatenate([row, jnp.zeros((1, LANES - bucket_count), F32)], axis=1)
        )
    small_sum.start(jnp.concatenate(small_parts, axis=0))
    late_sum.lo_to_hi()
    small_sum.core_to_lo()
    early_sum.hi_to_gather()
    late_sum.hi_to_gather()
    small_sum.lo_to_hi()
    send_rows(3, 6)
    early_sum.gather_to_lo()
    late_sum.gather_to_lo()
    send_rows(6, 8)
    for s in range(seqs):
        ig_out[s] = ig[:, s * length : (s + 1) * length].T
    flushes[1].start()
    if ocap:
        for k in range(n * ocap // 256):
            first = n * gcap + k * 256
            slots[pl.ds(first, 256), :] = dot_nt(
                hot_slots(back_pos[...], first, 256), igb_t[...]
            ).astype(BF16)
        over_rows = pl.ds(0, n * ocap)
        spill = pltpu.make_async_copy(
            slots.at[pl.ds(n * gcap, n * ocap)], over.at[over_rows], smem_sem
        )
        keep.wait()
        spill.start()
    early_sum.gather_to_core()
    late_sum.gather_to_core()
    lax.fori_loop(0, 15, pass_on, 0)
    small_sum.finish()
    flushes[5].start()
    early_sum.finish()
    flushes[3].start()
    late_sum.finish()
    flushes[4].start()
    share(core).wait_send()
    share(1 - core).wait_recv()
    flushes[2].start()
    if ocap:
        spill.wait()
        most = jnp.zeros((1, LANES), F32)

        def peak(j, most):
            return jnp.maximum(
                most, jnp.maximum(asked_out[0, j, 1:2], asked_out[1, j, 1:2]).astype(F32)
            )

        most = lax.fori_loop(0, n, peak, most)
        excess[0, 0] = jnp.max(most).astype(jnp.int32)
    else:
        keep.wait()
        excess[0, 0] = 0

    def rows_in(j, carry):
        forward(j, 1 - core).wait_recv()
        forward(j, core).wait_send()
        return carry

    lax.fori_loop(0, n, rows_in, 0)

    def sent(j, carry):
        request(j).wait_send()
        back_request(j).wait_send()
        row_copy(j).wait_send()
        grad_copy(j).wait_send()
        return carry

    lax.fori_loop(1, n, sent, 0)
    for flush in flushes:
        flush.wait()


def step_kernel(n, lo, cap, gcap, used, sizes, *refs):
    parts, at = [], 0
    for size in sizes:
        parts.append(refs[at : at + size])
        at += size
    step_body(n, lo, cap, gcap, used, *parts)


def rest_body(n, rows, mine, out, send_sem, recv_sem, fwd_send, fwd_recv, self_sem):
    me = lax.axis_index("emb")
    core = lax.axis_index("dp")
    barrier = pltpu.get_barrier_semaphore()

    def peer(j):
        return {"emb": lax.rem(me + j, n)}

    def greet(k, carry):
        pl.semaphore_signal(barrier, inc=1, device_id=peer(k), device_id_type=MESH)
        return carry

    lax.fori_loop(1, n, greet, 0)
    pl.semaphore_signal(barrier, inc=1, device_id={"dp": 1 - core}, device_id_type=MESH)
    pl.semaphore_wait(barrier, n)

    def block(j):
        return pl.ds(pl.multiple_of(j * rows, rows), rows)

    def landed(which, j):
        return out.at[pl.ds(pl.multiple_of((which * n + j) * rows, rows), rows)]

    def copy(j):
        back = lax.rem(n - j, n)
        return remote(
            mine.at[block(j)], landed(core, back), send_sem.at[j], recv_sem.at[back], peer(j)
        )

    def arrival(j):
        return remote(mine.at[block(j)], landed(core, j), send_sem.at[j], recv_sem.at[j], peer(j))

    def forward(j, which):
        ref = landed(which, j)
        return remote(ref, ref, fwd_send.at[j], fwd_recv.at[j], {"dp": 1 - core})

    def start(j, carry):
        copy(j).start()
        return carry

    lax.fori_loop(1, n, start, 0)
    keep = pltpu.make_async_copy(mine.at[block(0)], landed(core, 0), self_sem)
    keep.start()
    keep.wait()
    forward(0, core).start()

    def pass_on(j, carry):
        arrival(j).wait_recv()
        forward(j, core).start()
        return carry

    lax.fori_loop(1, n, pass_on, 0)

    def finish(j, carry):
        forward(j, core).wait_send()
        forward(j, 1 - core).wait_recv()
        return carry

    lax.fori_loop(0, n, finish, 0)

    def sent(j, carry):
        copy(j).wait_send()
        return carry

    lax.fori_loop(1, n, sent, 0)


def exchange_rest(n, rows, over):
    dma = pltpu.SemaphoreType.DMA
    anywhere = pl.BlockSpec(memory_space=pl.ANY)
    return pl.pallas_call(
        functools.partial(rest_body, n, rows),
        out_shape=jax.ShapeDtypeStruct(over.shape, over.dtype),
        in_specs=[anywhere],
        out_specs=anywhere,
        scratch_shapes=[dma((n,)), dma((n,)), dma((n,)), dma((n,)), dma],
        compiler_params=pltpu.CompilerParams(collective_id=1, has_side_effects=True),
        name="rest",
    )(over)


def scatter_body(
    n, cap, rest, used, asked_far, counts, inc, over, early, late, small, y_in, ig_in,
    y_out, ig_out, grad, g1, wq, wk, wv, wo, bias, g2, win, wout,
    acc, wide, zero, inc_v, over_v, y_v, ig_v, early_v, late_v, wq_v, wk_v, wv_v, wo_v, win_v, wout_v,
    out_sem, in_sem, pass_sem, asked, asked_sem, spare_rows,
):
    rows_dev, width = grad.shape
    chunk = zero.shape[0]
    domain_rows = used // 3
    per_domain = domain_rows // chunk
    slots = n * cap
    hd = wq.shape[1]
    ff = win.shape[1]
    loads = [
        pltpu.make_async_copy(src, dst, in_sem.at[k])
        for k, (src, dst) in enumerate(
            (
                (inc, inc_v), (over, over_v), (early, early_v), (late, late_v), (y_in, y_v),
                (ig_in, ig_v),
            )
        )
    ]
    ask = pltpu.make_async_copy(asked_far, asked, asked_sem)
    ask.start()
    loads[0].start()
    zero[...] = jnp.zeros_like(zero)

    def chunk_at(k):
        return pl.ds(pl.multiple_of(k * chunk, chunk), chunk)

    def clear_copy(k):
        return pltpu.make_async_copy(zero, grad.at[chunk_at(k)], out_sem.at[k])

    def out_copy(k):
        return pltpu.make_async_copy(acc.at[chunk_at(k)], grad.at[chunk_at(k)], out_sem.at[k])

    def in_use(k):
        return (k % per_domain) * chunk < counts[k // per_domain]

    def spare(k, carry):
        clear_copy(k).start()
        return carry

    def prepare(k, carry):
        @pl.when(in_use(k))
        def _():
            def clear(r, inner):
                at = pl.multiple_of(k * chunk + r * 256, 256)
                acc[pl.ds(at, 256), :] = jnp.zeros((256, width), F32)
                return inner

            lax.fori_loop(0, chunk // 256, clear, 0)

        return carry

    lax.fori_loop(0, used // chunk, prepare, 0)
    loads[0].wait()
    for load in loads[1:]:
        load.start()
    loads[1].wait()
    lax.fori_loop(used // chunk, rows_dev // chunk, spare, 0)

    def unused(k, carry):
        @pl.when(jnp.logical_not(in_use(k)))
        def _():
            clear_copy(k).start()

        return carry

    lax.fori_loop(0, used // chunk, unused, 0)

    def widen(r, carry):
        at = pl.ds(pl.multiple_of(r * 256, 256), 256)
        wide[at, :] = inc_v[at, :].astype(F32)
        return carry

    lax.fori_loop(0, 2 * slots // 256, widen, 0)

    def source(k, carry):
        base = k * 2 * LANES

        def eight(g, inner):
            first = g * 8
            ats = [asked[base + first + r] for r in range(8)]
            sums = [
                acc[pl.ds(ats[r], 1), :] + wide[pl.ds(k * cap + first + r, 1), :] for r in range(8)
            ]
            for r in range(8):
                acc[pl.ds(ats[r], 1), :] = sums[r]
            return inner

        count = asked[base + LANES]
        lax.fori_loop(0, (jnp.minimum(count, cap) + 7) // 8, eight, 0)
        if rest:
            def more(g, inner):
                first = g * 8
                ats = [asked[base + cap + first + r] for r in range(8)]
                rows = [
                    over_v[pl.ds(pl.multiple_of(k * rest + first // 16 * 16, 16), 16), :]
                ][0].astype(F32)
                spare_rows[...] = rows
                sums = [
                    acc[pl.ds(ats[r], 1), :] + spare_rows[pl.ds(first % 16 + r, 1), :]
                    for r in range(8)
                ]
                for r in range(8):
                    acc[pl.ds(ats[r], 1), :] = sums[r]
                return inner

            lax.fori_loop(0, (jnp.maximum(count - cap, 0) + 7) // 8, more, 0)
        return carry

    ask.wait()
    lax.fori_loop(0, 2 * n, source, 0)

    def write(k, carry):
        @pl.when(in_use(k))
        def _():
            out_copy(k).start()

        return carry

    lax.fori_loop(0, used // chunk, write, 0)

    passes = []

    def hand_on(src, dst):
        passes.append(pltpu.make_async_copy(src, dst, pass_sem.at[len(passes)]))
        passes[-1].start()

    for load in loads[2:]:
        load.wait()
    hand_on(y_v, y_out)
    hand_on(ig_v, ig_out)
    for i, (value, out) in enumerate(((wq_v, wq), (wk_v, wk), (wv_v, wv))):
        for k in range(hd // width):
            at = i * hd + k * width
            value[:, k * width : (k + 1) * width] = late_v[at : at + width, :].astype(F32)
        hand_on(value, out)
    wo_v[...] = late_v[3 * hd : 4 * hd, :].astype(F32)
    hand_on(wo_v, wo)
    for k in range(ff // width):
        at = slice(k * width, (k + 1) * width)
        win_v[:, at] = early_v[at, :].astype(F32)
    hand_on(win_v, win)
    wout_v[...] = early_v[ff : 2 * ff, :].astype(F32)
    hand_on(wout_v, wout)
    g1[...] = small[0:1, :]
    g2[...] = small[1:2, :]
    heads, buckets = bias.shape
    bias[...] = small[2 : 2 + heads, 0:buckets]

    def finish(k, carry):
        clear_copy(k).wait()
        return carry

    lax.fori_loop(0, rows_dev // chunk, finish, 0)
    for copy in passes:
        copy.wait()


def on_device(
    hashed_ids, owners, domain_tags, user_counts, lengths, buckets, table, gain_one,
    query_weight_matrix, key_weight_matrix, value_weight_matrix, attention_output_weight,
    bias_table, gain_two, feedforward_input_weight, feedforward_output_weight, cotangent,
):
    n = lax.axis_size("emb")
    seqs, length = hashed_ids.shape
    tokens = seqs * length
    rows_dev, width = table.shape
    used = 3 * (rows_dev // 4)
    cap = max(2, 2 * tokens // n)
    hd = query_weight_matrix.shape[1]
    ff = feedforward_input_weight.shape[1]
    heads = hd // DH
    pairs = heads // 2
    bucket_count = bias_table.shape[0]
    slots = n * cap
    gcap = max(16, 3 * cap // 4 // 16 * 16)
    ocap = cap - gcap
    lo = 2 ** ((n.bit_length()) // 2)
    unit = 2 * n * 16
    early_rows = -(-2 * ff // unit) * unit
    late_rows = -(-4 * hd // unit) * unit
    vmem = pl.BlockSpec(memory_space=pltpu.VMEM)
    smem = pl.BlockSpec(memory_space=pltpu.SMEM)
    anywhere = pl.BlockSpec(memory_space=pl.ANY)
    dma = pltpu.SemaphoreType.DMA
    shape = jax.ShapeDtypeStruct

    operands = (
        hashed_ids, owners.reshape(seqs, length), domain_tags, user_counts, lengths, bias_table.T,
        buckets, gain_one.reshape(1, width), gain_two.reshape(1, width), table, cotangent,
        query_weight_matrix, key_weight_matrix, value_weight_matrix, attention_output_weight,
        feedforward_input_weight, feedforward_output_weight,
    )
    results = (
        shape((seqs, length, width), BF16),
        shape((seqs, length, width), F32),
        shape((2, n * gcap, width), BF16),
        shape((2, n, 2, LANES), jnp.int32),
        shape((early_rows, width), BF16),
        shape((late_rows, width), BF16),
        shape((8, LANES), F32),
        shape((2 * n * max(ocap, 16), width), BF16),
        shape((1, 1), jnp.int32),
    )
    lookup_scratch = [
        pltpu.VMEM((n, 1, LANES), jnp.int32),
        pltpu.VMEM((n, 1, LANES), jnp.int32),
        pltpu.SMEM((n, 1, LANES), jnp.int32),
        pltpu.VMEM((used, width), BF16),
        pltpu.VMEM((rows_dev, width), F32),
        pltpu.VMEM((cap, width), F32),
        pltpu.VMEM((slots, width), BF16),
        pltpu.VMEM((slots, width), BF16),
        pltpu.VMEM((width, tokens), F32),
        pltpu.VMEM((seqs, length), jnp.int32),
        pltpu.VMEM((slots, width), BF16),
        pltpu.VMEM((early_rows, width), BF16),
        pltpu.VMEM((late_rows, width), BF16),
        pltpu.VMEM((seqs, length), jnp.int32),
        pltpu.VMEM((n, 2, LANES), jnp.int32),
        dma((n,)), dma((n,)),
        dma((n,)), dma((n,)), dma((n,)), dma((n,)), dma((2,)), dma((6,)), dma,
        dma((n,)), dma((n,)), dma((n,)), dma((n,)),
    ]
    block_scratch = [
        pltpu.VMEM((3 * hd, width), BF16),
        pltpu.VMEM((width, 3 * hd), BF16),
        pltpu.VMEM((width, hd), BF16),
        pltpu.VMEM((ff, width), BF16),
        pltpu.VMEM((width, ff), BF16),
        pltpu.VMEM((length, length), F32),
        pltpu.VMEM((pairs, length, 2 * length), F32),
        pltpu.VMEM((width, tokens), BF16),
        pltpu.VMEM((width, tokens), BF16),
        pltpu.VMEM((3 * hd, tokens), BF16),
        pltpu.VMEM((tokens, 2 * hd), BF16),
        pltpu.VMEM((seqs, pairs, length, 2 * length), F32),
        pltpu.VMEM((hd, tokens), BF16),
        pltpu.VMEM((width, tokens), BF16),
        pltpu.VMEM((ff, tokens), BF16),
        pltpu.VMEM((ff, tokens), BF16),
        pltpu.VMEM((width, tokens), BF16),
        pltpu.VMEM((width, tokens), F32),
        pltpu.VMEM((width, tokens), BF16),
        pltpu.VMEM((hd, tokens), BF16),
        pltpu.VMEM((3 * hd, tokens), BF16),
        pltpu.VMEM((pairs, length, 2 * length), F32),
        pltpu.VMEM((width, tokens), BF16),
        pltpu.VMEM((heads, bucket_count, 8, length), F32),
        pltpu.VMEM((seqs, length, width), BF16),
        pltpu.VMEM((width, hd), BF16),
        pltpu.VMEM((width, hd), BF16),
        pltpu.VMEM((width, hd), BF16),
        pltpu.VMEM((hd, width), BF16),
        pltpu.VMEM((width, ff), BF16),
        pltpu.VMEM((ff, width), BF16),
        dma((11,)),
        pltpu.VMEM((seqs, length), jnp.int32),
        pltpu.VMEM((seqs, length), jnp.int32),
        pltpu.SMEM((seqs,), jnp.int32),
        pltpu.SMEM((user_counts.shape[0],), jnp.int32),
        pltpu.SMEM(lengths.shape, jnp.int32),
        pltpu.SMEM((heads, bucket_count), F32),
        pltpu.VMEM((length, length), jnp.int32),
        pltpu.VMEM((1, width), F32),
        pltpu.VMEM((1, width), F32),
        dma((5,)),
    ]
    block_scratch += [pltpu.VMEM(results[k].shape, results[k].dtype) for k in (0, 1, 3, 4, 5, 6)]
    block_scratch += [dma((6,))]
    early_scratch = Reducer.scratch(n, lo, early_rows)
    late_scratch = Reducer.scratch(n, lo, late_rows)
    small_scratch = SmallReducer.scratch(n, lo)
    scratch = [lookup_scratch, block_scratch, early_scratch, late_scratch, small_scratch]
    sizes = [len(operands), len(results)] + [len(part) for part in scratch]
    y, ig, incoming, asked, early_total, late_total, small_total, over, excess = pl.pallas_call(
        functools.partial(step_kernel, n, lo, cap, gcap, used, sizes),
        out_shape=results,
        in_specs=[anywhere] * len(operands),
        out_specs=(anywhere,) * (len(results) - 1) + (smem,),
        scratch_shapes=sum(scratch, []),
        compiler_params=pltpu.CompilerParams(
            collective_id=0, has_side_effects=True, vmem_limit_bytes=VMEM_LIMIT
        ),
        name="step",
    )(*operands)

    if ocap:
        over = lax.cond(
            excess[0, 0] > gcap, functools.partial(exchange_rest, n, ocap), lambda rows: rows, over
        )

    chunk = math.gcd(1024, used // 3)
    output, input_grad, table_grad, g1, gq, gk, gv, go, gb, g2, gin, gout = pl.pallas_call(
        functools.partial(scatter_body, n, gcap, ocap, used),
        out_shape=(
            shape((seqs, length, width), BF16),
            shape((seqs, length, width), F32),
            shape((rows_dev, width), F32),
            shape((1, width), F32),
            shape((width, hd), F32),
            shape((width, hd), F32),
            shape((width, hd), F32),
            shape((hd, width), F32),
            shape((heads, bucket_count), F32),
            shape((1, width), F32),
            shape((width, ff), F32),
            shape((ff, width), F32),
        ),
        in_specs=[anywhere, smem, anywhere, anywhere, anywhere, anywhere, vmem, anywhere, anywhere],
        out_specs=(anywhere,) * 3 + (vmem,) + (anywhere,) * 4 + (vmem,) * 2 + (anywhere,) * 2,
        scratch_shapes=[
            pltpu.VMEM((used + 8, width), F32),
            pltpu.VMEM((2 * n * gcap, width), F32),
            pltpu.VMEM((chunk, width), F32),
            pltpu.VMEM((2 * n * gcap, width), BF16),
            pltpu.VMEM(over.shape, BF16),
            pltpu.VMEM((seqs, length, width), BF16),
            pltpu.VMEM((seqs, length, width), F32),
            pltpu.VMEM((early_rows, width), BF16),
            pltpu.VMEM((late_rows, width), BF16),
            pltpu.VMEM((width, hd), F32),
            pltpu.VMEM((width, hd), F32),
            pltpu.VMEM((width, hd), F32),
            pltpu.VMEM((hd, width), F32),
            pltpu.VMEM((width, ff), F32),
            pltpu.VMEM((ff, width), F32),
            dma((rows_dev // chunk,)), dma((6,)), dma((8,)),
            pltpu.SMEM((2 * n * 2 * LANES,), jnp.int32), dma, pltpu.VMEM((16, width), F32),
        ],
        compiler_params=pltpu.CompilerParams(vmem_limit_bytes=VMEM_LIMIT),
        name="scatter",
    )(
        asked.reshape(-1), user_counts, incoming.reshape(2 * n * gcap, width), over, early_total,
        late_total, small_total, y, ig,
    )
    return (
        output, input_grad, table_grad, g1.reshape(width), gq, gk, gv, go, gb.T, g2.reshape(width),
        gin, gout,
    )


def solution(mesh):
    split = ("emb", "dp")
    return jax.shard_map(
        on_device,
        mesh=mesh,
        in_specs=(
            P(split, None), P(split, None, None), P(split), P(), P(split, None), P(),
            P("emb", None), P(), P(), P(), P(), P(), P(), P(), P(), P(), P(split, None, None),
        ),
        out_specs=(
            P(split, None, None), P(split, None, None), P("emb", None), P(), P(), P(), P(), P(),
            P(), P(), P(), P(),
        ),
        check_vma=False,
    )
```

```python
import functools
import math

import jax
import jax.numpy as jnp
from jax import lax
from jax.experimental import pallas as pl
from jax.experimental.pallas import tpu as pltpu
from jax.sharding import PartitionSpec as P

DH = 64
LANES = 128
EPSILON = 1e-06
MESH = pl.DeviceIdType.MESH
F32 = jnp.float32
BF16 = jnp.bfloat16
VMEM_LIMIT = 61 * 1024 * 1024


def dot_nn(a, b):
    return lax.dot_general(a, b, (((1,), (0,)), ((), ())), preferred_element_type=F32)


def dot_nt(a, b):
    return lax.dot_general(a, b, (((1,), (1,)), ((), ())), preferred_element_type=F32)


def dot_tn(a, b):
    return lax.dot_general(a, b, (((0,), (0,)), ((), ())), preferred_element_type=F32)


def hot_slots(pos, first, count):
    rows = lax.broadcasted_iota(jnp.int32, (count, LANES), 0) + first
    parts = [
        jnp.where(rows == pos[s : s + 1, :], 1.0, 0.0).astype(BF16) for s in range(pos.shape[0])
    ]
    return jnp.concatenate(parts, axis=1)


def remote(src, dst, send_sem, recv_sem, device):
    return pltpu.make_async_remote_copy(
        src_ref=src, dst_ref=dst, send_sem=send_sem, recv_sem=recv_sem,
        device_id=device, device_id_type=MESH,
    )


def gelu_parts(u):
    k0 = math.sqrt(2.0 / math.pi)
    k1 = k0 * 0.044715
    square = u * u
    half = 0.5 * jnp.tanh(u * (k1 * square + k0)) + 0.5
    value = u * half
    slope = half + (2.0 * value) * (1.0 - half) * (3.0 * k1 * square + k0)
    return value, slope


def split_pair(both):
    zero = jnp.zeros((DH, LANES), both.dtype)
    left = jnp.concatenate([both[:DH], zero], axis=0)
    right = jnp.concatenate([zero, both[DH:]], axis=0)
    return jnp.concatenate([left, right], axis=1)


class Reducer:
    def __init__(self, n, lo, me, core, part, total, bufs):
        self.n, self.lo, self.hi, self.core = n, lo, n // lo, core
        self.my_hi, self.my_lo = me // lo, lax.rem(me, lo)
        self.part, self.total = part, total
        (
            self.core_buf, self.half, self.lo_buf, self.quarter, self.hi_buf, self.core_sem,
            self.lo_sem, self.hi_sem, self.gh_sem, self.gl_sem, self.gc_sem,
        ) = bufs
        self.half_rows, self.lo_rows = self.half.shape[0], self.quarter.shape[0]
        self.hi_rows = self.hi_buf.shape[1]

    @staticmethod
    def scratch(n, lo, rows):
        hi, dma, width = n // lo, pltpu.SemaphoreType.DMA, LANES
        return [
            pltpu.VMEM((rows // 2, width), BF16),
            pltpu.VMEM((rows // 2, width), BF16),
            pltpu.VMEM((lo, rows // 2 // lo, width), BF16),
            pltpu.VMEM((rows // 2 // lo, width), BF16),
            pltpu.VMEM((hi, rows // 2 // n, width), BF16),
            dma((2,)), dma((2, lo)), dma((2, hi)), dma((2, hi)), dma((2, lo)), dma((2, lo)),
        ]

    def lo_device(self, k):
        return {"emb": self.my_hi * self.lo + self.lo_peer(k)}

    def hi_device(self, k):
        return {"emb": self.hi_peer(k) * self.lo + self.my_lo}

    def lo_peer(self, k):
        return lax.rem(self.my_lo + k, self.lo)

    def hi_peer(self, k):
        return lax.rem(self.my_hi + k, self.hi)

    def swap(self):
        at = pl.ds(pl.multiple_of((1 - self.core) * self.half_rows, self.half_rows), self.half_rows)
        return remote(
            self.part.at[at], self.core_buf, self.core_sem.at[0], self.core_sem.at[1],
            {"dp": 1 - self.core},
        )

    def lo_copy(self, k):
        at = pl.ds(pl.multiple_of(self.lo_peer(k) * self.lo_rows, self.lo_rows), self.lo_rows)
        return remote(
            self.half.at[at], self.lo_buf.at[self.lo - k],
            self.lo_sem.at[0, k], self.lo_sem.at[1, self.lo - k], self.lo_device(k),
        )

    def lo_arrival(self, k):
        return remote(
            self.quarter, self.lo_buf.at[k],
            self.lo_sem.at[0, k], self.lo_sem.at[1, k], self.lo_device(k),
        )

    def hi_copy(self, k):
        at = pl.ds(pl.multiple_of(self.hi_peer(k) * self.hi_rows, self.hi_rows), self.hi_rows)
        return remote(
            self.quarter.at[at], self.hi_buf.at[self.hi - k],
            self.hi_sem.at[0, k], self.hi_sem.at[1, self.hi - k], self.hi_device(k),
        )

    def hi_arrival(self, k):
        return remote(
            self.hi_buf.at[k], self.hi_buf.at[k],
            self.hi_sem.at[0, k], self.hi_sem.at[1, k], self.hi_device(k),
        )

    def piece(self, h):
        at = self.core * self.half_rows + self.my_lo * self.lo_rows + h * self.hi_rows
        return self.total.at[pl.ds(pl.multiple_of(at, self.hi_rows), self.hi_rows)]

    def block(self, core, low):
        at = core * self.half_rows + low * self.lo_rows
        return self.total.at[pl.ds(pl.multiple_of(at, self.lo_rows), self.lo_rows)]

    def gather_hi(self, k):
        mine = self.piece(self.my_hi)
        return remote(
            mine, mine, self.gh_sem.at[0, k], self.gh_sem.at[1, self.hi - k], self.hi_device(k)
        )

    def gather_hi_arrival(self, k):
        other = self.piece(self.hi_peer(k))
        return remote(other, other, self.gh_sem.at[0, k], self.gh_sem.at[1, k], self.hi_device(k))

    def gather_lo(self, k):
        mine = self.block(self.core, self.my_lo)
        return remote(
            mine, mine, self.gl_sem.at[0, k], self.gl_sem.at[1, self.lo - k], self.lo_device(k)
        )

    def gather_lo_arrival(self, k):
        other = self.block(self.core, self.lo_peer(k))
        return remote(other, other, self.gl_sem.at[0, k], self.gl_sem.at[1, k], self.lo_device(k))

    def gather_core(self, low):
        mine = self.block(self.core, low)
        return remote(
            mine, mine, self.gc_sem.at[0, low], self.gc_sem.at[1, low], {"dp": 1 - self.core}
        )

    def gather_core_arrival(self, low):
        other = self.block(1 - self.core, low)
        return remote(
            other, other, self.gc_sem.at[0, low], self.gc_sem.at[1, low], {"dp": 1 - self.core}
        )

    def start(self):
        self.swap().start()

    def core_to_lo(self):
        self.swap().wait()
        step = self.hi_rows

        def add(r, carry):
            at = pl.multiple_of(r * step, step)
            own = self.part[pl.ds(pl.multiple_of(self.core * self.half_rows + at, step), step), :]
            other = self.core_buf[pl.ds(at, step), :]
            self.half[pl.ds(at, step), :] = (own.astype(F32) + other.astype(F32)).astype(BF16)
            return carry

        lax.fori_loop(0, self.half_rows // step, add, 0)
        for k in range(1, self.lo):
            self.lo_copy(k).start()

    def lo_to_hi(self):
        for k in range(1, self.lo):
            self.lo_arrival(k).wait_recv()
        step = self.hi_rows

        def add(r, carry):
            at = pl.multiple_of(r * step, step)
            mine = pl.ds(pl.multiple_of(self.my_lo * self.lo_rows + at, step), step)
            total = self.half[mine, :].astype(F32)
            for k in range(1, self.lo):
                total = total + self.lo_buf[k, pl.ds(at, step), :].astype(F32)
            self.quarter[pl.ds(at, step), :] = total.astype(BF16)
            return carry

        lax.fori_loop(0, self.lo_rows // step, add, 0)
        for k in range(1, self.hi):
            self.hi_copy(k).start()

    def hi_to_gather(self):
        for k in range(1, self.hi):
            self.hi_arrival(k).wait_recv()
        mine = pl.ds(pl.multiple_of(self.my_hi * self.hi_rows, self.hi_rows), self.hi_rows)
        total = self.quarter[mine, :].astype(F32)
        for k in range(1, self.hi):
            total = total + self.hi_buf[k].astype(F32)
        self.piece(self.my_hi)[...] = total.astype(BF16)
        for k in range(1, self.hi):
            self.gather_hi(k).start()

    def gather_to_lo(self):
        for k in range(1, self.hi):
            self.gather_hi_arrival(k).wait_recv()
        for k in range(1, self.lo):
            self.gather_lo(k).start()
        self.gather_core(self.my_lo).start()

    def gather_to_core(self):
        for k in range(1, self.lo):
            self.gather_lo_arrival(k).wait_recv()
            self.gather_core(self.lo_peer(k)).start()

    def finish(self):
        for low in range(self.lo):
            self.gather_core_arrival(low).wait_recv()
        for k in range(1, self.lo):
            self.lo_copy(k).wait_send()
            self.gather_lo(k).wait_send()
        for k in range(1, self.hi):
            self.hi_copy(k).wait_send()
            self.gather_hi(k).wait_send()
        for low in range(self.lo):
            self.gather_core(low).wait_send()


class SmallReducer:
    def __init__(self, n, lo, me, core, total, bufs):
        self.lo, self.hi, self.core = lo, n // lo, core
        self.my_hi, self.my_lo = me // lo, lax.rem(me, lo)
        self.total = total
        self.a, self.b, self.c, self.a_sem, self.b_sem, self.c_sem = bufs

    @staticmethod
    def scratch(n, lo):
        hi, dma = n // lo, pltpu.SemaphoreType.DMA
        return [
            pltpu.VMEM((2, 8, LANES), F32),
            pltpu.VMEM((lo, 8, LANES), F32),
            pltpu.VMEM((hi, 8, LANES), F32),
            dma((2,)), dma((2, lo)), dma((2, hi)),
        ]

    def swap(self, slot):
        ref = self.a.at[slot]
        return remote(ref, ref, self.a_sem.at[0], self.a_sem.at[1], {"dp": 1 - self.core})

    def lo_copy(self, k, slot, come):
        device = {"emb": self.my_hi * self.lo + lax.rem(self.my_lo + k, self.lo)}
        ref = self.b.at[slot]
        return remote(ref, ref, self.b_sem.at[0, k], self.b_sem.at[1, come], device)

    def hi_copy(self, k, slot, come):
        device = {"emb": lax.rem(self.my_hi + k, self.hi) * self.lo + self.my_lo}
        ref = self.c.at[slot]
        return remote(ref, ref, self.c_sem.at[0, k], self.c_sem.at[1, come], device)

    def start(self, value):
        self.a[self.core] = value
        self.swap(self.core).start()

    def core_to_lo(self):
        self.swap(self.core).wait_send()
        self.swap(1 - self.core).wait_recv()
        self.b[self.my_lo] = self.a[0] + self.a[1]
        for k in range(1, self.lo):
            self.lo_copy(k, self.my_lo, self.lo - k).start()

    def lo_to_hi(self):
        for k in range(1, self.lo):
            self.lo_copy(k, lax.rem(self.my_lo + k, self.lo), k).wait_recv()
        total = self.b[0]
        for k in range(1, self.lo):
            total = total + self.b[k]
        self.c[self.my_hi] = total
        for k in range(1, self.hi):
            self.hi_copy(k, self.my_hi, self.hi - k).start()

    def finish(self):
        for k in range(1, self.hi):
            self.hi_copy(k, lax.rem(self.my_hi + k, self.hi), k).wait_recv()
        total = self.c[0]
        for k in range(1, self.hi):
            total = total + self.c[k]
        self.total[...] = total
        for k in range(1, self.lo):
            self.lo_copy(k, self.my_lo, self.lo - k).wait_send()
        for k in range(1, self.hi):
            self.hi_copy(k, self.my_hi, self.hi - k).wait_send()


def step_body(
    n, lo, cap, gcap, used, refs_in, refs_out, lookup_refs, block_refs, early_refs, late_refs, small_refs,
):
    (
        ids_far, own_far, tags_far, counts_far, lens_far, btab_far, buckets_far, g1_far, g2_far,
        table, *far,
    ) = refs_in
    y_far, ig_far, inc, asked_far, early_far, late_far, small_far, over, excess = refs_out
    (
        req, asked_v, asked_s, tab_low, tab, gbuf, send, recv, x_acc, pos_ref, slots, early, late,
        back_pos, back_req, back_send, back_recv,
        req_send, req_recv, row_send, row_recv, pair_sem, tab_sem, smem_sem,
        grad_send, grad_recv, fwd_send, fwd_recv,
    ) = lookup_refs
    (
        wqkv_t, wqkv, wo_t, win_t, wout_t, buck_t, bias, x_t, a_t, qkv_t, kv, p_s, o_t, c_t, act_t,
        du_t, dy_t, dm_t, dmb_t, do_t, dqkv_t, dsum, igb_t, b_acc,
        cot, wq, wk, wv, wo, win, wout, near_sem,
        ids, own, tags, counts, lens, btab, buckets, g1, g2, first_sem,
        y_out, ig_out, asked_out, early_tot, late_tot, small_tot, out_sem,
    ) = block_refs
    near = (cot, wq, wk, wv, wo, win, wout, btab, buckets, g1, g2)
    far = tuple(far) + (btab_far, buckets_far, g1_far, g2_far)
    me = lax.axis_index("emb")
    core = lax.axis_index("dp")
    seqs, length = ids.shape
    width = cot.shape[2]
    tokens = seqs * length
    hd, ff = wq.shape[1], win.shape[1]
    heads = hd // DH
    pairs = heads // 2
    bucket_count = btab.shape[1]
    domain_rows = used // 3
    row_limit = 4 * domain_rows
    pieces = tab_sem.shape[0]
    piece = used // pieces
    group = 4
    owners_at_once = max(1, 256 // cap)
    wide_slots = owners_at_once * gcap
    ocap = cap - gcap
    early_sum = Reducer(n, lo, me, core, early, early_tot, early_refs)
    late_sum = Reducer(n, lo, me, core, late, late_tot, late_refs)
    small_sum = SmallReducer(n, lo, me, core, small_tot, small_refs)

    barrier = pltpu.get_barrier_semaphore()

    def peer(j):
        return {"emb": lax.rem(me + j, n)}

    def greet(k, carry):
        pl.semaphore_signal(barrier, inc=1, device_id=peer(k), device_id_type=MESH)
        return carry

    lax.fori_loop(1, n, greet, 0)
    pl.semaphore_signal(barrier, inc=1, device_id={"dp": 1 - core}, device_id_type=MESH)
    first = [
        pltpu.make_async_copy(src, dst, first_sem.at[k])
        for k, (src, dst) in enumerate(
            (
                (ids_far, ids), (own_far, own), (tags_far, tags), (counts_far, counts),
                (lens_far, lens),
            )
        )
    ]
    for fetch in first:
        fetch.start()

    def table_copy(c):
        part = pl.ds(c * piece, piece)
        return pltpu.make_async_copy(table.at[part], tab_low.at[part], tab_sem.at[c])

    for c in range(pieces):
        table_copy(c).start()
    fetches = [
        pltpu.make_async_copy(src, dst, near_sem.at[k])
        for k, (src, dst) in enumerate(zip(far, near))
    ]
    for fetch in fetches:
        fetch.start()

    for fetch in first:
        fetch.wait()

    row_id = lax.broadcasted_iota(jnp.int32, (seqs, length), 0)
    lane_id = lax.broadcasted_iota(jnp.int32, (seqs, length), 1)
    count_of = jnp.ones((seqs, length), F32)
    tag_of = jnp.zeros((seqs, length), jnp.int32)
    len_of = jnp.zeros((seqs, length), jnp.int32)
    for s in range(seqs):
        tag = tags[s]
        count_of = jnp.where(row_id == s, counts[tag].astype(F32), count_of)
        tag_of = jnp.where(row_id == s, tag, tag_of)
        len_of = jnp.where(row_id == s, lens[0, s], len_of)
    code = ids[...].astype(F32)
    turns = jnp.floor((code + 0.5) / jnp.maximum(count_of, 1.0))
    local = tag_of * domain_rows + (code - turns * count_of).astype(jnp.int32)
    live = lane_id < len_of
    rel = own[...] - me
    rel = jnp.where(rel < 0, rel + n, rel)

    owner_id = lax.broadcasted_iota(jnp.int32, (n, length), 0)
    hots = [jnp.where(owner_id == rel[s : s + 1, :], 1.0, 0.0) for s in range(seqs)]
    before = (
        lax.broadcasted_iota(jnp.int32, (length, length), 0)
        < lax.broadcasted_iota(jnp.int32, (length, length), 1)
    )
    earlier = jnp.where(before, 1.0, 0.0).astype(BF16)
    prefix = dot_nn(jnp.concatenate(hots, axis=0).astype(BF16), earlier)
    running = jnp.zeros((n, 1), F32)
    ranks = []
    for s in range(seqs):
        ranks.append(
            jnp.sum(hots[s] * (prefix[s * n : s * n + n] + running), axis=0, keepdims=True)
        )
        running = running + jnp.sum(hots[s], axis=1, keepdims=True)
    rank = jnp.concatenate(ranks, axis=0).astype(jnp.int32)
    pos_ref[...] = rel * cap + rank

    low = (local & 255).astype(F32)
    high = lax.shift_right_logical(local, 8).astype(F32)
    slot_id = lax.broadcasted_iota(jnp.int32, (LANES, length), 0)
    asking = jnp.zeros((2 * n, LANES), F32)
    for s in range(seqs):
        hot = hots[s]
        values = jnp.concatenate([hot * high[s : s + 1, :], hot * low[s : s + 1, :]], axis=0)
        slot_hot = jnp.where(slot_id == rank[s : s + 1, :], 1.0, 0.0).astype(BF16)
        asking = asking + dot_nt(values.astype(BF16), slot_hot)
    wanted = (asking[:n] * 256.0 + asking[n:]).astype(jnp.int32)
    for j in range(n):
        req[j] = wanted[j : j + 1, :]

    pl.semaphore_wait(barrier, n)

    def request(j):
        back = lax.rem(n - j, n)
        return remote(req.at[j], asked_v.at[back], req_send.at[j], req_recv.at[back], peer(j))

    def request_arrival(j):
        return remote(req.at[j], asked_v.at[j], req_send.at[j], req_recv.at[j], peer(j))

    def ask(j, carry):
        request(j).start()
        return carry

    lax.fori_loop(1, n, ask, 0)
    asked_v[0] = req[0]

    for c in range(pieces):
        table_copy(c).wait()

        def widen(r, carry):
            part = pl.ds(pl.multiple_of(c * piece + r * 256, 256), 256)
            tab[part, :] = tab_low[part, :].astype(F32)
            return carry

        lax.fori_loop(0, piece // 256, widen, 0)

    def all_asked(j, carry):
        request_arrival(j).wait_recv()
        return carry

    lax.fori_loop(1, n, all_asked, 0)
    to_scalar = pltpu.make_async_copy(asked_v, asked_s, smem_sem)
    to_scalar.start()
    to_scalar.wait()

    def slot_block(j):
        return pl.ds(pl.multiple_of(j * cap, cap), cap)

    def row_copy(j):
        back = lax.rem(n - j, n)
        return remote(
            send.at[slot_block(j)], recv.at[slot_block(back)],
            row_send.at[j], row_recv.at[back], peer(j),
        )

    def row_arrival(j):
        at = slot_block(j)
        return remote(send.at[at], recv.at[at], row_send.at[j], row_recv.at[j], peer(j))

    def gather(j):
        def some(c, carry):
            for r in range(16):
                at = asked_s[j, 0, c * 16 + r] & (row_limit - 1)
                gbuf[pl.ds(c * 16 + r, 1), :] = tab[pl.ds(at, 1), :]
            return carry

        lax.fori_loop(0, cap // 16, some, 0)
        return gbuf[...].astype(BF16)

    def pair_at(step):
        half = (step + 1) // 2
        return jnp.where(lax.rem(step, 2) == 1, n // 4 - half, n // 4 + half)

    def serve(step, carry):
        def one(j, inner):
            send[slot_block(j), :] = gather(j)
            row_copy(j).start()
            return inner

        last = n - 2 * pair_at(step)
        return lax.fori_loop(last - 1, jnp.minimum(last + 1, n), one, carry)

    lax.fori_loop(0, n // 2, serve, 0)
    recv[0:cap, :] = gather(0)

    key = jnp.where(live, (rel * row_limit + local).astype(F32), -1.0)
    key_cols = [
        jnp.broadcast_to(key[s : s + 1, :], (length, length)).T for s in range(seqs)
    ]
    fresh = []
    for s in range(seqs):
        seen = jnp.where(before & (key_cols[s] == key[s : s + 1, :]), 1.0, 0.0)
        for e in range(s):
            seen = jnp.maximum(seen, jnp.where(key_cols[e] == key[s : s + 1, :], 1.0, 0.0))
        fresh.append(1.0 - jnp.max(seen, axis=0, keepdims=True))
    fresh = [jnp.where(live[s : s + 1, :], fresh[s], 0.0) for s in range(seqs)]
    news = [hots[s] * fresh[s] for s in range(seqs)]
    prefix = dot_nn(jnp.concatenate(news, axis=0).astype(BF16), earlier)
    running = jnp.zeros((n, 1), F32)
    firsts = []
    for s in range(seqs):
        firsts.append(
            jnp.sum(news[s] * (prefix[s * n : s * n + n] + running), axis=0, keepdims=True)
        )
        running = running + jnp.sum(news[s], axis=1, keepdims=True)
    first_cols = [
        jnp.broadcast_to(firsts[s] * fresh[s] + fresh[s], (length, length)).T for s in range(seqs)
    ]
    found = []
    for s in range(seqs):
        at = jnp.zeros((length, length), F32)
        for e in range(s + 1):
            at = jnp.maximum(at, jnp.where(key_cols[e] == key[s : s + 1, :], first_cols[e], 0.0))
        found.append(jnp.max(at, axis=0, keepdims=True))
    found = jnp.concatenate(found, axis=0).astype(jnp.int32) - 1
    back_at = rel * gcap + found
    if ocap:
        back_at = jnp.where(found < gcap, back_at, n * gcap + rel * ocap + found - gcap)
    back_pos[...] = jnp.where(live, back_at, -1)
    below = used - local
    low = (below & 255).astype(F32)
    high = lax.shift_right_logical(below, 8).astype(F32)
    asking = jnp.zeros((2 * n, LANES), F32)
    for s in range(seqs):
        values = jnp.concatenate(
            [news[s] * high[s : s + 1, :], news[s] * low[s : s + 1, :]], axis=0
        )
        slot_hot = jnp.where(slot_id == firsts[s].astype(jnp.int32), 1.0, 0.0).astype(BF16)
        asking = asking + dot_nt(values.astype(BF16), slot_hot)
    wanted = used - (asking[:n] * 256.0 + asking[n:]).astype(jnp.int32)
    lane = lax.broadcasted_iota(jnp.int32, (n, LANES), 1)
    largest = jnp.max(running, axis=0, keepdims=True)
    limits = jnp.where(lane == 0, running, largest).astype(jnp.int32)
    for j in range(n):
        back_req[j, 0:1] = wanted[j : j + 1, :]
        back_req[j, 1:2] = limits[j : j + 1, :]
    asked_out[core, 0] = back_req[0]

    def back_request(j):
        back = lax.rem(n - j, n)
        return remote(
            back_req.at[j], asked_out.at[core, back], back_send.at[j], back_recv.at[back], peer(j)
        )

    def back_request_arrival(j):
        return remote(
            back_req.at[j], asked_out.at[core, j], back_send.at[j], back_recv.at[j], peer(j)
        )

    def tell(j, carry):
        back_request(j).start()
        return carry

    lax.fori_loop(1, n, tell, 0)

    def share(which):
        ref = asked_out.at[which]
        return remote(ref, ref, pair_sem.at[0], pair_sem.at[1], {"dp": 1 - core})

    for fetch in fetches:
        fetch.wait()
    for part, w in enumerate((wq, wk, wv)):
        wqkv[:, part * hd : (part + 1) * hd] = w[...]
        wqkv_t[part * hd : (part + 1) * hd, :] = w[...].T
    wo_t[...] = wo[...].T
    win_t[...] = win[...].T
    wout_t[...] = wout[...].T
    buck_t[...] = buckets[...].astype(F32).T
    g1_col = jnp.broadcast_to(g1[...], (8, width)).T[:, 0:1]
    g2_col = jnp.broadcast_to(g2[...], (8, width)).T[:, 0:1]
    dsum[...] = jnp.zeros_like(dsum)
    b_acc[...] = jnp.zeros_like(b_acc)

    def bias_rows(r, carry):
        part = pl.ds(pl.multiple_of(r * 8, 8), 8)
        bt = buck_t[part, :]
        rows = [jnp.zeros((8, length), F32) for _ in range(heads)]
        for b in range(bucket_count):
            here = bt == float(b)
            rows = [jnp.where(here, btab[h, b], rows[h]) for h in range(heads)]
        for p in range(pairs):
            bias[p, part, :] = jnp.concatenate(rows[2 * p : 2 * p + 2], axis=1)
        return carry

    lax.fori_loop(0, length // 8, bias_rows, 0)

    def load_dy(s, carry):
        part = pl.ds(pl.multiple_of(s * length, length), length)
        alive = lax.broadcasted_iota(jnp.int32, (width, length), 1) < lens[0, s]
        dy_t[:, part] = jnp.where(alive, cot[s].astype(F32).T, 0.0).astype(BF16)
        return carry

    lax.fori_loop(0, seqs, load_dy, 0)

    def place(step, carry):
        pair = pair_at(step)

        def ready(j, inner):
            row_arrival(j).wait_recv()
            return inner

        lax.fori_loop(jnp.maximum(2 * pair, 1), 2 * pair + 2, ready, 0)
        first = pl.multiple_of(pair * 2 * cap, 2 * cap)
        hot = hot_slots(pos_ref[...], first, 2 * cap)
        got = dot_tn(recv[pl.ds(first, 2 * cap), :], hot)

        @pl.when(step == 0)
        def _():
            x_acc[...] = got

        @pl.when(step > 0)
        def _():
            x_acc[...] += got

        return carry

    lax.fori_loop(0, n // 2, place, 0)

    def told(j, carry):
        back_request_arrival(j).wait_recv()
        return carry

    lax.fori_loop(1, n, told, 0)
    share(core).start()
    x_t[...] = x_acc[...].astype(BF16)

    xf = x_acc[...]
    scale = lax.rsqrt(jnp.mean(xf * xf, axis=0, keepdims=True) + EPSILON)
    a = (xf * scale * g1_col).astype(BF16)
    a_t[...] = a
    out = dot_nn(wqkv_t[...], a)
    qkv_t[0:hd, :] = out[:hd].astype(BF16) * jnp.array(1.0 / math.sqrt(DH), BF16)
    qkv_t[hd:, :] = out[hd:].astype(BF16)
    kv[...] = dot_nn(a.T, wqkv[:, hd:]).astype(BF16)

    rows = [slice(p * 2 * DH, (p + 1) * 2 * DH) for p in range(pairs)]
    krows = [slice(hd + p * 2 * DH, hd + (p + 1) * 2 * DH) for p in range(pairs)]
    vrows = [slice(2 * hd + p * 2 * DH, 2 * hd + (p + 1) * 2 * DH) for p in range(pairs)]
    jobs = [(i, p) for i in range(group) for p in range(pairs)]

    def members(g):
        return [pl.ds(pl.multiple_of((g * group + i) * length, length), length) for i in range(group)]

    def attend(g, carry):
        parts = members(g)
        key_id = lax.broadcasted_iota(jnp.int32, (length, 2 * length), 0)
        visible = [key_id < lens[0, g * group + i] for i in range(group)]
        scores = [
            dot_nn(kv[parts[i], rows[p]], split_pair(qkv_t[rows[p], parts[i]])) for i, p in jobs
        ]
        probs = []
        for (i, p), score in zip(jobs, scores):
            score = jnp.where(visible[i], score + bias[p], -1000000000.0)
            expo = jnp.exp(score - jnp.max(score, axis=0, keepdims=True))
            prob = expo * (1.0 / jnp.sum(expo, axis=0, keepdims=True))
            p_s[g * group + i, p] = prob
            probs.append(prob.astype(BF16))
        for (i, p), prob in zip(jobs, probs):
            mixed = dot_nn(qkv_t[vrows[p], parts[i]], prob)
            o_t[rows[p], parts[i]] = jnp.concatenate(
                [mixed[:DH, :length], mixed[DH:, length:]], axis=0
            ).astype(BF16)
        return carry

    lax.fori_loop(0, seqs // group, attend, 0)

    m = x_t[...].astype(F32) + dot_nn(wo_t[...], o_t[...])
    scale = lax.rsqrt(jnp.mean(m * m, axis=0, keepdims=True) + EPSILON)
    z = m * scale
    normed = (z * g2_col).astype(BF16)
    c_t[...] = normed
    value, slope = gelu_parts(dot_nn(win_t[...], normed))
    act = value.astype(BF16)
    act_t[...] = act
    du = (dot_nn(wout[...], dy_t[...]) * slope).astype(BF16)
    du_t[...] = du
    y = m + dot_nn(wout_t[...], act)
    for s in range(seqs):
        y_out[s] = y[:, s * length : (s + 1) * length].T.astype(BF16)
    flushes = [
        pltpu.make_async_copy(src, dst, out_sem.at[k])
        for k, (src, dst) in enumerate(
            (
                (y_out, y_far), (ig_out, ig_far), (asked_out, asked_far), (early_tot, early_far),
                (late_tot, late_far), (small_tot, small_far),
            )
        )
    ]
    flushes[0].start()
    dc = dot_nn(win[...], du)
    gain_two = dc * z
    gain_two = sum(gain_two[:, s * length : (s + 1) * length] for s in range(seqs))
    small_tot[1:2, :] = jnp.sum(gain_two.T, axis=0, keepdims=True)
    e = dc * g2_col
    dm = dy_t[...].astype(F32) + scale * (e - z * jnp.mean(e * z, axis=0, keepdims=True))
    dm_t[...] = dm
    dmb = dm.astype(BF16)
    dmb_t[...] = dmb
    do_t[...] = dot_nn(wo[...], dmb).astype(BF16)

    def in_halves(array, filled, first, second, start):
        if array.shape[0] > filled:
            first()
            second()
            array[filled:, :] = jnp.zeros((array.shape[0] - filled, width), BF16)
            start()
            return
        pl.when(core == 1)(first)
        pl.when(core == 0)(second)
        start()
        pl.when(core == 0)(first)
        pl.when(core == 1)(second)

    for k in range(ff // width):
        at = slice(k * width, (k + 1) * width)
        early[at, :] = dot_nt(c_t[...], du_t[at, :]).astype(BF16)
    early[ff : 2 * ff, :] = dot_nt(act_t[...], dy_t[...]).astype(BF16)
    if early.shape[0] > 2 * ff:
        early[2 * ff :, :] = jnp.zeros((early.shape[0] - 2 * ff, width), BF16)
    early_sum.start()

    def attend_back(g):
        parts = members(g)
        do2s = [split_pair(do_t[rows[p], parts[i]]) for i, p in jobs]
        dprobs = [dot_nn(kv[parts[i], krows[p]], do2) for (i, p), do2 in zip(jobs, do2s)]
        lows = []
        for (i, p), dprob in zip(jobs, dprobs):
            prob = p_s[g * group + i, p]
            ds = prob * (dprob - jnp.sum(dprob * prob, axis=0, keepdims=True))
            dsum[p] += ds
            lows.append(ds.astype(BF16))
        for (i, p), do2 in zip(jobs, do2s):
            prob = p_s[g * group + i, p].astype(BF16)
            dqkv_t[vrows[p], parts[i]] = dot_nt(do2, prob).astype(BF16)
        for (i, p), low in zip(jobs, lows):
            q2 = split_pair(qkv_t[rows[p], parts[i]])
            dqkv_t[krows[p], parts[i]] = dot_nt(q2, low).astype(BF16)
        for (i, p), low in zip(jobs, lows):
            dq = dot_nn(qkv_t[krows[p], parts[i]], low) * (1.0 / math.sqrt(DH))
            dqkv_t[rows[p], parts[i]] = jnp.concatenate(
                [dq[:DH, :length], dq[DH:, length:]], axis=0
            ).astype(BF16)

    groups = seqs // group

    def back_loop(g, carry):
        attend_back(g)

        @pl.when(g == 0)
        def _():
            early_sum.core_to_lo()

        return carry

    lax.fori_loop(0, groups, back_loop, 0)

    xf = x_t[...].astype(F32)
    scale = lax.rsqrt(jnp.mean(xf * xf, axis=0, keepdims=True) + EPSILON)
    z = xf * scale
    da = dot_nn(wqkv[...], dqkv_t[...])
    gain_one = da * z
    gain_one = sum(gain_one[:, s * length : (s + 1) * length] for s in range(seqs))
    e = da * g1_col
    ig = dm_t[...] + scale * (e - z * jnp.mean(e * z, axis=0, keepdims=True))
    igb_t[...] = ig.astype(BF16)

    def grad_block(j):
        return pl.ds(pl.multiple_of(j * gcap, gcap), gcap)

    def grad_copy(j):
        back = lax.rem(n - j, n)
        return remote(
            slots.at[grad_block(j)], inc.at[core, grad_block(back)],
            grad_send.at[j], grad_recv.at[back], peer(j),
        )

    def grad_arrival(j):
        return remote(
            slots.at[grad_block(j)], inc.at[core, grad_block(j)],
            grad_send.at[j], grad_recv.at[j], peer(j),
        )

    def forward(j, which):
        ref = inc.at[which, grad_block(j)]
        return remote(ref, ref, fwd_send.at[j], fwd_recv.at[j], {"dp": 1 - core})

    def to_slots(k, carry):
        first = pl.multiple_of(k * wide_slots, wide_slots)
        slots[pl.ds(first, wide_slots), :] = dot_nt(
            hot_slots(back_pos[...], first, wide_slots), igb_t[...]
        ).astype(BF16)

        def go(j, inner):
            grad_copy(j).start()
            return inner

        owners = owners_at_once
        lax.fori_loop(jnp.maximum(k * owners, 1), (k + 1) * owners, go, 0)
        return carry

    steps = n // owners_at_once

    def send_rows(first, last):
        lax.fori_loop(first * steps // 8, last * steps // 8, to_slots, 0)

    def late_blocks(first, last):
        for k in range(first // width, last // width):
            at = slice(k * width, (k + 1) * width)
            late[at, :] = dot_nt(a_t[...], dqkv_t[at, :]).astype(BF16)

    def late_first():
        late_blocks(0, 2 * hd)

    def late_second():
        late_blocks(2 * hd, 3 * hd)
        late[3 * hd : 4 * hd, :] = dot_nt(o_t[...], dmb_t[...]).astype(BF16)

    in_halves(late, 4 * hd, late_first, late_second, late_sum.start)

    def pass_on(step, carry):
        j = n - 1 - step
        grad_arrival(j).wait_recv()
        forward(j, core).start()
        return carry

    late_sum.core_to_lo()
    early_sum.lo_to_hi()
    send_rows(0, 3)
    keep = pltpu.make_async_copy(slots.at[grad_block(0)], inc.at[core, grad_block(0)], smem_sem)
    keep.start()
    remote(
        slots.at[grad_block(0)], inc.at[core, grad_block(0)], fwd_send.at[0], fwd_recv.at[0],
        {"dp": 1 - core},
    ).start()
    def bias_back(r, carry):
        part = pl.ds(pl.multiple_of(r * 8, 8), 8)
        bt = buck_t[part, :]
        grads = [dsum[h // 2, part, (h % 2) * length : (h % 2 + 1) * length] for h in range(heads)]
        for b in range(bucket_count):
            here = bt == float(b)
            for h in range(heads):
                b_acc[h, b] += jnp.where(here, grads[h], 0.0)
        return carry

    lax.fori_loop(0, length // 8, bias_back, 0)
    small_parts = [jnp.sum(gain_one.T, axis=0, keepdims=True), small_tot[1:2, :]]
    for h in range(heads):
        by_bucket = jnp.sum(b_acc[h], axis=1)
        row = jnp.sum(by_bucket.T, axis=0, keepdims=True)
        small_parts.append(
            jnp.concatenate([row, jnp.zeros((1, LANES - bucket_count), F32)], axis=1)
        )
    small_sum.start(jnp.concatenate(small_parts, axis=0))
    late_sum.lo_to_hi()
    small_sum.core_to_lo()
    early_sum.hi_to_gather()
    late_sum.hi_to_gather()
    small_sum.lo_to_hi()
    send_rows(3, 6)
    early_sum.gather_to_lo()
    late_sum.gather_to_lo()
    send_rows(6, 8)
    for s in range(seqs):
        ig_out[s] = ig[:, s * length : (s + 1) * length].T
    flushes[1].start()
    if ocap:
        for k in range(n * ocap // 256):
            first = n * gcap + k * 256
            slots[pl.ds(first, 256), :] = dot_nt(
                hot_slots(back_pos[...], first, 256), igb_t[...]
            ).astype(BF16)
        over_rows = pl.ds(0, n * ocap)
        spill = pltpu.make_async_copy(
            slots.at[pl.ds(n * gcap, n * ocap)], over.at[over_rows], smem_sem
        )
        keep.wait()
        spill.start()
    early_sum.gather_to_core()
    late_sum.gather_to_core()
    lax.fori_loop(0, 15, pass_on, 0)
    small_sum.finish()
    flushes[5].start()
    early_sum.finish()
    flushes[3].start()
    late_sum.finish()
    flushes[4].start()
    share(core).wait_send()
    share(1 - core).wait_recv()
    flushes[2].start()
    if ocap:
        spill.wait()
        most = jnp.zeros((1, LANES), F32)

        def peak(j, most):
            return jnp.maximum(
                most, jnp.maximum(asked_out[0, j, 1:2], asked_out[1, j, 1:2]).astype(F32)
            )

        most = lax.fori_loop(0, n, peak, most)
        excess[0, 0] = jnp.max(most).astype(jnp.int32)
    else:
        keep.wait()
        excess[0, 0] = 0

    def rows_in(j, carry):
        forward(j, 1 - core).wait_recv()
        forward(j, core).wait_send()
        return carry

    lax.fori_loop(0, n, rows_in, 0)

    def sent(j, carry):
        request(j).wait_send()
        back_request(j).wait_send()
        row_copy(j).wait_send()
        grad_copy(j).wait_send()
        return carry

    lax.fori_loop(1, n, sent, 0)
    for flush in flushes:
        flush.wait()


def step_kernel(n, lo, cap, gcap, used, sizes, *refs):
    parts, at = [], 0
    for size in sizes:
        parts.append(refs[at : at + size])
        at += size
    step_body(n, lo, cap, gcap, used, *parts)


def rest_body(n, rows, mine, out, send_sem, recv_sem, fwd_send, fwd_recv, self_sem):
    me = lax.axis_index("emb")
    core = lax.axis_index("dp")
    barrier = pltpu.get_barrier_semaphore()

    def peer(j):
        return {"emb": lax.rem(me + j, n)}

    def greet(k, carry):
        pl.semaphore_signal(barrier, inc=1, device_id=peer(k), device_id_type=MESH)
        return carry

    lax.fori_loop(1, n, greet, 0)
    pl.semaphore_signal(barrier, inc=1, device_id={"dp": 1 - core}, device_id_type=MESH)
    pl.semaphore_wait(barrier, n)

    def block(j):
        return pl.ds(pl.multiple_of(j * rows, rows), rows)

    def landed(which, j):
        return out.at[pl.ds(pl.multiple_of((which * n + j) * rows, rows), rows)]

    def copy(j):
        back = lax.rem(n - j, n)
        return remote(
            mine.at[block(j)], landed(core, back), send_sem.at[j], recv_sem.at[back], peer(j)
        )

    def arrival(j):
        return remote(mine.at[block(j)], landed(core, j), send_sem.at[j], recv_sem.at[j], peer(j))

    def forward(j, which):
        ref = landed(which, j)
        return remote(ref, ref, fwd_send.at[j], fwd_recv.at[j], {"dp": 1 - core})

    def start(j, carry):
        copy(j).start()
        return carry

    lax.fori_loop(1, n, start, 0)
    keep = pltpu.make_async_copy(mine.at[block(0)], landed(core, 0), self_sem)
    keep.start()
    keep.wait()
    forward(0, core).start()

    def pass_on(j, carry):
        arrival(j).wait_recv()
        forward(j, core).start()
        return carry

    lax.fori_loop(1, n, pass_on, 0)

    def finish(j, carry):
        forward(j, core).wait_send()
        forward(j, 1 - core).wait_recv()
        return carry

    lax.fori_loop(0, n, finish, 0)

    def sent(j, carry):
        copy(j).wait_send()
        return carry

    lax.fori_loop(1, n, sent, 0)


def exchange_rest(n, rows, over):
    dma = pltpu.SemaphoreType.DMA
    anywhere = pl.BlockSpec(memory_space=pl.ANY)
    return pl.pallas_call(
        functools.partial(rest_body, n, rows),
        out_shape=jax.ShapeDtypeStruct(over.shape, over.dtype),
        in_specs=[anywhere],
        out_specs=anywhere,
        scratch_shapes=[dma((n,)), dma((n,)), dma((n,)), dma((n,)), dma],
        compiler_params=pltpu.CompilerParams(collective_id=1, has_side_effects=True),
        name="rest",
    )(over)


def scatter_body(
    n, cap, rest, used, asked_far, counts, inc, over, early, late, small, y_in, ig_in,
    y_out, ig_out, grad, g1, wq, wk, wv, wo, bias, g2, win, wout,
    acc, wide, zero, inc_v, over_v, y_v, ig_v, early_v, late_v, wq_v, wk_v, wv_v, wo_v, win_v, wout_v,
    out_sem, in_sem, pass_sem, asked, asked_sem, spare_rows,
):
    rows_dev, width = grad.shape
    chunk = zero.shape[0]
    domain_rows = used // 3
    per_domain = domain_rows // chunk
    slots = n * cap
    hd = wq.shape[1]
    ff = win.shape[1]
    loads = [
        pltpu.make_async_copy(src, dst, in_sem.at[k])
        for k, (src, dst) in enumerate(
            (
                (inc, inc_v), (over, over_v), (early, early_v), (late, late_v), (y_in, y_v),
                (ig_in, ig_v),
            )
        )
    ]
    ask = pltpu.make_async_copy(asked_far, asked, asked_sem)
    ask.start()
    loads[0].start()
    zero[...] = jnp.zeros_like(zero)

    def chunk_at(k):
        return pl.ds(pl.multiple_of(k * chunk, chunk), chunk)

    def clear_copy(k):
        return pltpu.make_async_copy(zero, grad.at[chunk_at(k)], out_sem.at[k])

    def out_copy(k):
        return pltpu.make_async_copy(acc.at[chunk_at(k)], grad.at[chunk_at(k)], out_sem.at[k])

    def in_use(k):
        return (k % per_domain) * chunk < counts[k // per_domain]

    def spare(k, carry):
        clear_copy(k).start()
        return carry

    def prepare(k, carry):
        @pl.when(in_use(k))
        def _():
            def clear(r, inner):
                at = pl.multiple_of(k * chunk + r * 256, 256)
                acc[pl.ds(at, 256), :] = jnp.zeros((256, width), F32)
                return inner

            lax.fori_loop(0, chunk // 256, clear, 0)

        return carry

    lax.fori_loop(0, used // chunk, prepare, 0)
    loads[0].wait()
    for load in loads[1:]:
        load.start()
    loads[1].wait()
    lax.fori_loop(used // chunk, rows_dev // chunk, spare, 0)

    def unused(k, carry):
        @pl.when(jnp.logical_not(in_use(k)))
        def _():
            clear_copy(k).start()

        return carry

    lax.fori_loop(0, used // chunk, unused, 0)

    def widen(r, carry):
        at = pl.ds(pl.multiple_of(r * 256, 256), 256)
        wide[at, :] = inc_v[at, :].astype(F32)
        return carry

    lax.fori_loop(0, 2 * slots // 256, widen, 0)

    def source(k, carry):
        base = k * 2 * LANES

        def eight(g, inner):
            first = g * 8
            ats = [asked[base + first + r] for r in range(8)]
            sums = [
                acc[pl.ds(ats[r], 1), :] + wide[pl.ds(k * cap + first + r, 1), :] for r in range(8)
            ]
            for r in range(8):
                acc[pl.ds(ats[r], 1), :] = sums[r]
            return inner

        count = asked[base + LANES]
        lax.fori_loop(0, (jnp.minimum(count, cap) + 7) // 8, eight, 0)
        if rest:
            def more(g, inner):
                first = g * 8
                ats = [asked[base + cap + first + r] for r in range(8)]
                rows = [
                    over_v[pl.ds(pl.multiple_of(k * rest + first // 16 * 16, 16), 16), :]
                ][0].astype(F32)
                spare_rows[...] = rows
                sums = [
                    acc[pl.ds(ats[r], 1), :] + spare_rows[pl.ds(first % 16 + r, 1), :]
                    for r in range(8)
                ]
                for r in range(8):
                    acc[pl.ds(ats[r], 1), :] = sums[r]
                return inner

            lax.fori_loop(0, (jnp.maximum(count - cap, 0) + 7) // 8, more, 0)
        return carry

    ask.wait()
    lax.fori_loop(0, 2 * n, source, 0)

    def write(k, carry):
        @pl.when(in_use(k))
        def _():
            out_copy(k).start()

        return carry

    lax.fori_loop(0, used // chunk, write, 0)

    passes = []

    def hand_on(src, dst):
        passes.append(pltpu.make_async_copy(src, dst, pass_sem.at[len(passes)]))
        passes[-1].start()

    for load in loads[2:]:
        load.wait()
    hand_on(y_v, y_out)
    hand_on(ig_v, ig_out)
    for i, (value, out) in enumerate(((wq_v, wq), (wk_v, wk), (wv_v, wv))):
        for k in range(hd // width):
            at = i * hd + k * width
            value[:, k * width : (k + 1) * width] = late_v[at : at + width, :].astype(F32)
        hand_on(value, out)
    wo_v[...] = late_v[3 * hd : 4 * hd, :].astype(F32)
    hand_on(wo_v, wo)
    for k in range(ff // width):
        at = slice(k * width, (k + 1) * width)
        win_v[:, at] = early_v[at, :].astype(F32)
    hand_on(win_v, win)
    wout_v[...] = early_v[ff : 2 * ff, :].astype(F32)
    hand_on(wout_v, wout)
    g1[...] = small[0:1, :]
    g2[...] = small[1:2, :]
    heads, buckets = bias.shape
    bias[...] = small[2 : 2 + heads, 0:buckets]

    def finish(k, carry):
        clear_copy(k).wait()
        return carry

    lax.fori_loop(0, rows_dev // chunk, finish, 0)
    for copy in passes:
        copy.wait()


def on_device(
    hashed_ids, owners, domain_tags, user_counts, lengths, buckets, table, gain_one,
    query_weight_matrix, key_weight_matrix, value_weight_matrix, attention_output_weight,
    bias_table, gain_two, feedforward_input_weight, feedforward_output_weight, cotangent,
):
    n = lax.axis_size("emb")
    seqs, length = hashed_ids.shape
    tokens = seqs * length
    rows_dev, width = table.shape
    used = 3 * (rows_dev // 4)
    cap = max(2, 2 * tokens // n)
    hd = query_weight_matrix.shape[1]
    ff = feedforward_input_weight.shape[1]
    heads = hd // DH
    pairs = heads // 2
    bucket_count = bias_table.shape[0]
    slots = n * cap
    gcap = max(16, 3 * cap // 4 // 16 * 16)
    ocap = cap - gcap
    lo = 2 ** ((n.bit_length()) // 2)
    unit = 2 * n * 16
    early_rows = -(-2 * ff // unit) * unit
    late_rows = -(-4 * hd // unit) * unit
    vmem = pl.BlockSpec(memory_space=pltpu.VMEM)
    smem = pl.BlockSpec(memory_space=pltpu.SMEM)
    anywhere = pl.BlockSpec(memory_space=pl.ANY)
    dma = pltpu.SemaphoreType.DMA
    shape = jax.ShapeDtypeStruct

    operands = (
        hashed_ids, owners.reshape(seqs, length), domain_tags, user_counts, lengths, bias_table.T,
        buckets, gain_one.reshape(1, width), gain_two.reshape(1, width), table, cotangent,
        query_weight_matrix, key_weight_matrix, value_weight_matrix, attention_output_weight,
        feedforward_input_weight, feedforward_output_weight,
    )
    results = (
        shape((seqs, length, width), BF16),
        shape((seqs, length, width), F32),
        shape((2, n * gcap, width), BF16),
        shape((2, n, 2, LANES), jnp.int32),
        shape((early_rows, width), BF16),
        shape((late_rows, width), BF16),
        shape((8, LANES), F32),
        shape((2 * n * max(ocap, 16), width), BF16),
        shape((1, 1), jnp.int32),
    )
    lookup_scratch = [
        pltpu.VMEM((n, 1, LANES), jnp.int32),
        pltpu.VMEM((n, 1, LANES), jnp.int32),
        pltpu.SMEM((n, 1, LANES), jnp.int32),
        pltpu.VMEM((used, width), BF16),
        pltpu.VMEM((rows_dev, width), F32),
        pltpu.VMEM((cap, width), F32),
        pltpu.VMEM((slots, width), BF16),
        pltpu.VMEM((slots, width), BF16),
        pltpu.VMEM((width, tokens), F32),
        pltpu.VMEM((seqs, length), jnp.int32),
        pltpu.VMEM((slots, width), BF16),
        pltpu.VMEM((early_rows, width), BF16),
        pltpu.VMEM((late_rows, width), BF16),
        pltpu.VMEM((seqs, length), jnp.int32),
        pltpu.VMEM((n, 2, LANES), jnp.int32),
        dma((n,)), dma((n,)),
        dma((n,)), dma((n,)), dma((n,)), dma((n,)), dma((2,)), dma((6,)), dma,
        dma((n,)), dma((n,)), dma((n,)), dma((n,)),
    ]
    block_scratch = [
        pltpu.VMEM((3 * hd, width), BF16),
        pltpu.VMEM((width, 3 * hd), BF16),
        pltpu.VMEM((width, hd), BF16),
        pltpu.VMEM((ff, width), BF16),
        pltpu.VMEM((width, ff), BF16),
        pltpu.VMEM((length, length), F32),
        pltpu.VMEM((pairs, length, 2 * length), F32),
        pltpu.VMEM((width, tokens), BF16),
        pltpu.VMEM((width, tokens), BF16),
        pltpu.VMEM((3 * hd, tokens), BF16),
        pltpu.VMEM((tokens, 2 * hd), BF16),
        pltpu.VMEM((seqs, pairs, length, 2 * length), F32),
        pltpu.VMEM((hd, tokens), BF16),
        pltpu.VMEM((width, tokens), BF16),
        pltpu.VMEM((ff, tokens), BF16),
        pltpu.VMEM((ff, tokens), BF16),
        pltpu.VMEM((width, tokens), BF16),
        pltpu.VMEM((width, tokens), F32),
        pltpu.VMEM((width, tokens), BF16),
        pltpu.VMEM((hd, tokens), BF16),
        pltpu.VMEM((3 * hd, tokens), BF16),
        pltpu.VMEM((pairs, length, 2 * length), F32),
        pltpu.VMEM((width, tokens), BF16),
        pltpu.VMEM((heads, bucket_count, 8, length), F32),
        pltpu.VMEM((seqs, length, width), BF16),
        pltpu.VMEM((width, hd), BF16),
        pltpu.VMEM((width, hd), BF16),
        pltpu.VMEM((width, hd), BF16),
        pltpu.VMEM((hd, width), BF16),
        pltpu.VMEM((width, ff), BF16),
        pltpu.VMEM((ff, width), BF16),
        dma((11,)),
        pltpu.VMEM((seqs, length), jnp.int32),
        pltpu.VMEM((seqs, length), jnp.int32),
        pltpu.SMEM((seqs,), jnp.int32),
        pltpu.SMEM((user_counts.shape[0],), jnp.int32),
        pltpu.SMEM(lengths.shape, jnp.int32),
        pltpu.SMEM((heads, bucket_count), F32),
        pltpu.VMEM((length, length), jnp.int32),
        pltpu.VMEM((1, width), F32),
        pltpu.VMEM((1, width), F32),
        dma((5,)),
    ]
    block_scratch += [pltpu.VMEM(results[k].shape, results[k].dtype) for k in (0, 1, 3, 4, 5, 6)]
    block_scratch += [dma((6,))]
    early_scratch = Reducer.scratch(n, lo, early_rows)
    late_scratch = Reducer.scratch(n, lo, late_rows)
    small_scratch = SmallReducer.scratch(n, lo)
    scratch = [lookup_scratch, block_scratch, early_scratch, late_scratch, small_scratch]
    sizes = [len(operands), len(results)] + [len(part) for part in scratch]
    y, ig, incoming, asked, early_total, late_total, small_total, over, excess = pl.pallas_call(
        functools.partial(step_kernel, n, lo, cap, gcap, used, sizes),
        out_shape=results,
        in_specs=[anywhere] * len(operands),
        out_specs=(anywhere,) * (len(results) - 1) + (smem,),
        scratch_shapes=sum(scratch, []),
        compiler_params=pltpu.CompilerParams(
            collective_id=0, has_side_effects=True, vmem_limit_bytes=VMEM_LIMIT
        ),
        name="step",
    )(*operands)

    if ocap:
        over = lax.cond(
            excess[0, 0] > gcap, functools.partial(exchange_rest, n, ocap), lambda rows: rows, over
        )

    chunk = math.gcd(1024, used // 3)
    output, input_grad, table_grad, g1, gq, gk, gv, go, gb, g2, gin, gout = pl.pallas_call(
        functools.partial(scatter_body, n, gcap, ocap, used),
        out_shape=(
            shape((seqs, length, width), BF16),
            shape((seqs, length, width), F32),
            shape((rows_dev, width), F32),
            shape((1, width), F32),
            shape((width, hd), F32),
            shape((width, hd), F32),
            shape((width, hd), F32),
            shape((hd, width), F32),
            shape((heads, bucket_count), F32),
            shape((1, width), F32),
            shape((width, ff), F32),
            shape((ff, width), F32),
        ),
        in_specs=[anywhere, smem, anywhere, anywhere, anywhere, anywhere, vmem, anywhere, anywhere],
        out_specs=(anywhere,) * 3 + (vmem,) + (anywhere,) * 4 + (vmem,) * 2 + (anywhere,) * 2,
        scratch_shapes=[
            pltpu.VMEM((used + 8, width), F32),
            pltpu.VMEM((2 * n * gcap, width), F32),
            pltpu.VMEM((chunk, width), F32),
            pltpu.VMEM((2 * n * gcap, width), BF16),
            pltpu.VMEM(over.shape, BF16),
            pltpu.VMEM((seqs, length, width), BF16),
            pltpu.VMEM((seqs, length, width), F32),
            pltpu.VMEM((early_rows, width), BF16),
            pltpu.VMEM((late_rows, width), BF16),
            pltpu.VMEM((width, hd), F32),
            pltpu.VMEM((width, hd), F32),
            pltpu.VMEM((width, hd), F32),
            pltpu.VMEM((hd, width), F32),
            pltpu.VMEM((width, ff), F32),
            pltpu.VMEM((ff, width), F32),
            dma((rows_dev // chunk,)), dma((6,)), dma((8,)),
            pltpu.SMEM((2 * n * 2 * LANES,), jnp.int32), dma, pltpu.VMEM((16, width), F32),
        ],
        compiler_params=pltpu.CompilerParams(vmem_limit_bytes=VMEM_LIMIT),
        name="scatter",
    )(
        asked.reshape(-1), user_counts, incoming.reshape(2 * n * gcap, width), over, early_total,
        late_total, small_total, y, ig,
    )
    return (
        output, input_grad, table_grad, g1.reshape(width), gq, gk, gv, go, gb.T, g2.reshape(width),
        gin, gout,
    )


def solution(mesh):
    split = ("emb", "dp")
    return jax.shard_map(
        on_device,
        mesh=mesh,
        in_specs=(
            P(split, None), P(split, None, None), P(split), P(), P(split, None), P(),
            P("emb", None), P(), P(), P(), P(), P(), P(), P(), P(), P(), P(split, None, None),
        ),
        out_specs=(
            P(split, None, None), P(split, None, None), P("emb", None), P(), P(), P(), P(), P(),
            P(), P(), P(), P(),
        ),
        check_vma=False,
    )
```

```python
import functools
import math

import jax
import jax.numpy as jnp
from jax import lax
from jax.experimental import pallas as pl
from jax.experimental.pallas import tpu as pltpu
from jax.sharding import PartitionSpec as P

DH = 64
LANES = 128
EPSILON = 1e-06
MESH = pl.DeviceIdType.MESH
F32 = jnp.float32
BF16 = jnp.bfloat16
VMEM_LIMIT = 60 * 1024 * 1024


def dot_nn(a, b):
    return lax.dot_general(a, b, (((1,), (0,)), ((), ())), preferred_element_type=F32)


def dot_nt(a, b):
    return lax.dot_general(a, b, (((1,), (1,)), ((), ())), preferred_element_type=F32)


def dot_tn(a, b):
    return lax.dot_general(a, b, (((0,), (0,)), ((), ())), preferred_element_type=F32)


def hot_slots(pos, first, count):
    rows = lax.broadcasted_iota(jnp.int32, (count, LANES), 0) + first
    parts = [
        jnp.where(rows == pos[s : s + 1, :], 1.0, 0.0).astype(BF16) for s in range(pos.shape[0])
    ]
    return jnp.concatenate(parts, axis=1)


def remote(src, dst, send_sem, recv_sem, device):
    return pltpu.make_async_remote_copy(
        src_ref=src, dst_ref=dst, send_sem=send_sem, recv_sem=recv_sem,
        device_id=device, device_id_type=MESH,
    )


def gelu_parts(u):
    k0 = math.sqrt(2.0 / math.pi)
    k1 = k0 * 0.044715
    square = u * u
    half = 0.5 * jnp.tanh(u * (k1 * square + k0)) + 0.5
    value = u * half
    slope = half + (2.0 * value) * (1.0 - half) * (3.0 * k1 * square + k0)
    return value, slope


def split_pair(both):
    zero = jnp.zeros((DH, LANES), both.dtype)
    left = jnp.concatenate([both[:DH], zero], axis=0)
    right = jnp.concatenate([zero, both[DH:]], axis=0)
    return jnp.concatenate([left, right], axis=1)


class Reducer:
    def __init__(self, n, lo, me, core, part, total, bufs):
        self.n, self.lo, self.hi, self.core = n, lo, n // lo, core
        self.my_hi, self.my_lo = me // lo, lax.rem(me, lo)
        self.part, self.total = part, total
        (
            self.core_buf, self.half, self.lo_buf, self.quarter, self.hi_buf, self.core_sem,
            self.lo_sem, self.hi_sem, self.gh_sem, self.gl_sem, self.gc_sem,
        ) = bufs
        self.half_rows, self.lo_rows = self.half.shape[0], self.quarter.shape[0]
        self.hi_rows = self.hi_buf.shape[1]

    @staticmethod
    def scratch(n, lo, rows):
        hi, dma, width = n // lo, pltpu.SemaphoreType.DMA, LANES
        return [
            pltpu.VMEM((rows // 2, width), BF16),
            pltpu.VMEM((rows // 2, width), BF16),
            pltpu.VMEM((lo, rows // 2 // lo, width), BF16),
            pltpu.VMEM((rows // 2 // lo, width), BF16),
            pltpu.VMEM((hi, rows // 2 // n, width), BF16),
            dma((2,)), dma((2, lo)), dma((2, hi)), dma((2, hi)), dma((2, lo)), dma((2, lo)),
        ]

    def lo_device(self, k):
        return {"emb": self.my_hi * self.lo + self.lo_peer(k)}

    def hi_device(self, k):
        return {"emb": self.hi_peer(k) * self.lo + self.my_lo}

    def lo_peer(self, k):
        return lax.rem(self.my_lo + k, self.lo)

    def hi_peer(self, k):
        return lax.rem(self.my_hi + k, self.hi)

    def swap(self):
        at = pl.ds(pl.multiple_of((1 - self.core) * self.half_rows, self.half_rows), self.half_rows)
        return remote(
            self.part.at[at], self.core_buf, self.core_sem.at[0], self.core_sem.at[1],
            {"dp": 1 - self.core},
        )

    def lo_copy(self, k):
        at = pl.ds(pl.multiple_of(self.lo_peer(k) * self.lo_rows, self.lo_rows), self.lo_rows)
        return remote(
            self.half.at[at], self.lo_buf.at[self.lo - k],
            self.lo_sem.at[0, k], self.lo_sem.at[1, self.lo - k], self.lo_device(k),
        )

    def lo_arrival(self, k):
        return remote(
            self.quarter, self.lo_buf.at[k],
            self.lo_sem.at[0, k], self.lo_sem.at[1, k], self.lo_device(k),
        )

    def hi_copy(self, k):
        at = pl.ds(pl.multiple_of(self.hi_peer(k) * self.hi_rows, self.hi_rows), self.hi_rows)
        return remote(
            self.quarter.at[at], self.hi_buf.at[self.hi - k],
            self.hi_sem.at[0, k], self.hi_sem.at[1, self.hi - k], self.hi_device(k),
        )

    def hi_arrival(self, k):
        return remote(
            self.hi_buf.at[k], self.hi_buf.at[k],
            self.hi_sem.at[0, k], self.hi_sem.at[1, k], self.hi_device(k),
        )

    def piece(self, h):
        at = self.core * self.half_rows + self.my_lo * self.lo_rows + h * self.hi_rows
        return self.total.at[pl.ds(pl.multiple_of(at, self.hi_rows), self.hi_rows)]

    def block(self, core, low):
        at = core * self.half_rows + low * self.lo_rows
        return self.total.at[pl.ds(pl.multiple_of(at, self.lo_rows), self.lo_rows)]

    def gather_hi(self, k):
        mine = self.piece(self.my_hi)
        return remote(
            mine, mine, self.gh_sem.at[0, k], self.gh_sem.at[1, self.hi - k], self.hi_device(k)
        )

    def gather_hi_arrival(self, k):
        other = self.piece(self.hi_peer(k))
        return remote(other, other, self.gh_sem.at[0, k], self.gh_sem.at[1, k], self.hi_device(k))

    def gather_lo(self, k):
        mine = self.block(self.core, self.my_lo)
        return remote(
            mine, mine, self.gl_sem.at[0, k], self.gl_sem.at[1, self.lo - k], self.lo_device(k)
        )

    def gather_lo_arrival(self, k):
        other = self.block(self.core, self.lo_peer(k))
        return remote(other, other, self.gl_sem.at[0, k], self.gl_sem.at[1, k], self.lo_device(k))

    def gather_core(self, low):
        mine = self.block(self.core, low)
        return remote(
            mine, mine, self.gc_sem.at[0, low], self.gc_sem.at[1, low], {"dp": 1 - self.core}
        )

    def gather_core_arrival(self, low):
        other = self.block(1 - self.core, low)
        return remote(
            other, other, self.gc_sem.at[0, low], self.gc_sem.at[1, low], {"dp": 1 - self.core}
        )

    def start(self):
        self.swap().start()

    def core_to_lo(self):
        self.swap().wait()
        step = self.hi_rows

        def add(r, carry):
            at = pl.multiple_of(r * step, step)
            own = self.part[pl.ds(pl.multiple_of(self.core * self.half_rows + at, step), step), :]
            other = self.core_buf[pl.ds(at, step), :]
            self.half[pl.ds(at, step), :] = (own.astype(F32) + other.astype(F32)).astype(BF16)
            return carry

        lax.fori_loop(0, self.half_rows // step, add, 0)
        for k in range(1, self.lo):
            self.lo_copy(k).start()

    def lo_to_hi(self):
        for k in range(1, self.lo):
            self.lo_arrival(k).wait_recv()
        step = self.hi_rows

        def add(r, carry):
            at = pl.multiple_of(r * step, step)
            mine = pl.ds(pl.multiple_of(self.my_lo * self.lo_rows + at, step), step)
            total = self.half[mine, :].astype(F32)
            for k in range(1, self.lo):
                total = total + self.lo_buf[k, pl.ds(at, step), :].astype(F32)
            self.quarter[pl.ds(at, step), :] = total.astype(BF16)
            return carry

        lax.fori_loop(0, self.lo_rows // step, add, 0)
        for k in range(1, self.hi):
            self.hi_copy(k).start()

    def hi_to_gather(self):
        for k in range(1, self.hi):
            self.hi_arrival(k).wait_recv()
        mine = pl.ds(pl.multiple_of(self.my_hi * self.hi_rows, self.hi_rows), self.hi_rows)
        total = self.quarter[mine, :].astype(F32)
        for k in range(1, self.hi):
            total = total + self.hi_buf[k].astype(F32)
        self.piece(self.my_hi)[...] = total.astype(BF16)
        for k in range(1, self.hi):
            self.gather_hi(k).start()

    def gather_to_lo(self):
        for k in range(1, self.hi):
            self.gather_hi_arrival(k).wait_recv()
        for k in range(1, self.lo):
            self.gather_lo(k).start()
        self.gather_core(self.my_lo).start()

    def gather_to_core(self):
        for k in range(1, self.lo):
            self.gather_lo_arrival(k).wait_recv()
            self.gather_core(self.lo_peer(k)).start()

    def finish(self):
        for low in range(self.lo):
            self.gather_core_arrival(low).wait_recv()
        for k in range(1, self.lo):
            self.lo_copy(k).wait_send()
            self.gather_lo(k).wait_send()
        for k in range(1, self.hi):
            self.hi_copy(k).wait_send()
            self.gather_hi(k).wait_send()
        for low in range(self.lo):
            self.gather_core(low).wait_send()


class SmallReducer:
    def __init__(self, n, lo, me, core, total, bufs):
        self.lo, self.hi, self.core = lo, n // lo, core
        self.my_hi, self.my_lo = me // lo, lax.rem(me, lo)
        self.total = total
        self.a, self.b, self.c, self.a_sem, self.b_sem, self.c_sem = bufs

    @staticmethod
    def scratch(n, lo):
        hi, dma = n // lo, pltpu.SemaphoreType.DMA
        return [
            pltpu.VMEM((2, 8, LANES), F32),
            pltpu.VMEM((lo, 8, LANES), F32),
            pltpu.VMEM((hi, 8, LANES), F32),
            dma((2,)), dma((2, lo)), dma((2, hi)),
        ]

    def swap(self, slot):
        ref = self.a.at[slot]
        return remote(ref, ref, self.a_sem.at[0], self.a_sem.at[1], {"dp": 1 - self.core})

    def lo_copy(self, k, slot, come):
        device = {"emb": self.my_hi * self.lo + lax.rem(self.my_lo + k, self.lo)}
        ref = self.b.at[slot]
        return remote(ref, ref, self.b_sem.at[0, k], self.b_sem.at[1, come], device)

    def hi_copy(self, k, slot, come):
        device = {"emb": lax.rem(self.my_hi + k, self.hi) * self.lo + self.my_lo}
        ref = self.c.at[slot]
        return remote(ref, ref, self.c_sem.at[0, k], self.c_sem.at[1, come], device)

    def start(self, value):
        self.a[self.core] = value
        self.swap(self.core).start()

    def core_to_lo(self):
        self.swap(self.core).wait_send()
        self.swap(1 - self.core).wait_recv()
        self.b[self.my_lo] = self.a[0] + self.a[1]
        for k in range(1, self.lo):
            self.lo_copy(k, self.my_lo, self.lo - k).start()

    def lo_to_hi(self):
        for k in range(1, self.lo):
            self.lo_copy(k, lax.rem(self.my_lo + k, self.lo), k).wait_recv()
        total = self.b[0]
        for k in range(1, self.lo):
            total = total + self.b[k]
        self.c[self.my_hi] = total
        for k in range(1, self.hi):
            self.hi_copy(k, self.my_hi, self.hi - k).start()

    def finish(self):
        for k in range(1, self.hi):
            self.hi_copy(k, lax.rem(self.my_hi + k, self.hi), k).wait_recv()
        total = self.c[0]
        for k in range(1, self.hi):
            total = total + self.c[k]
        self.total[...] = total
        for k in range(1, self.lo):
            self.lo_copy(k, self.my_lo, self.lo - k).wait_send()
        for k in range(1, self.hi):
            self.hi_copy(k, self.my_hi, self.hi - k).wait_send()


def step_body(
    n, lo, cap, gcap, used, refs_in, refs_out, lookup_refs, block_refs, early_refs, late_refs, small_refs,
):
    (
        ids_far, own_far, tags_far, counts_far, lens_far, btab_far, buckets_far, g1_far, g2_far,
        table, *far,
    ) = refs_in
    y_far, ig_far, inc, asked_far, early_far, late_far, small_far, over, excess = refs_out
    (
        req, asked_v, asked_s, tab_low, tab, gbuf, send, recv, x_acc, pos_ref, slots, early, late,
        back_pos, back_req, back_send, back_recv,
        req_send, req_recv, row_send, row_recv, pair_sem, tab_sem, smem_sem,
        grad_send, grad_recv, fwd_send, fwd_recv,
    ) = lookup_refs
    (
        wqkv_t, wqkv, wo_t, win_t, wout_t, buck_t, bias, x_t, a_t, qkv_t, kv, p_s, o_t, c_t, act_t,
        du_t, dy_t, dm_t, dmb_t, do_t, dqkv_t, dsum, igb_t, b_acc,
        cot, wq, wk, wv, wo, win, wout, near_sem,
        ids, own, tags, counts, lens, btab, buckets, g1, g2, first_sem,
        y_out, ig_out, asked_out, early_tot, late_tot, small_tot, out_sem,
    ) = block_refs
    near = (cot, wq, wk, wv, wo, win, wout, btab, buckets, g1, g2)
    far = tuple(far) + (btab_far, buckets_far, g1_far, g2_far)
    me = lax.axis_index("emb")
    core = lax.axis_index("dp")
    seqs, length = ids.shape
    width = cot.shape[2]
    tokens = seqs * length
    hd, ff = wq.shape[1], win.shape[1]
    heads = hd // DH
    pairs = heads // 2
    bucket_count = btab.shape[1]
    domain_rows = used // 3
    row_limit = 4 * domain_rows
    pieces = tab_sem.shape[0]
    piece = used // pieces
    group = 4
    owners_at_once = max(1, 256 // cap)
    wide_slots = owners_at_once * gcap
    ocap = cap - gcap
    early_sum = Reducer(n, lo, me, core, early, early_tot, early_refs)
    late_sum = Reducer(n, lo, me, core, late, late_tot, late_refs)
    small_sum = SmallReducer(n, lo, me, core, small_tot, small_refs)

    barrier = pltpu.get_barrier_semaphore()

    def peer(j):
        return {"emb": lax.rem(me + j, n)}

    def greet(k, carry):
        pl.semaphore_signal(barrier, inc=1, device_id=peer(k), device_id_type=MESH)
        return carry

    lax.fori_loop(1, n, greet, 0)
    pl.semaphore_signal(barrier, inc=1, device_id={"dp": 1 - core}, device_id_type=MESH)
    first = [
        pltpu.make_async_copy(src, dst, first_sem.at[k])
        for k, (src, dst) in enumerate(
            (
                (ids_far, ids), (own_far, own), (tags_far, tags), (counts_far, counts),
                (lens_far, lens),
            )
        )
    ]
    for fetch in first:
        fetch.start()

    def table_copy(c):
        part = pl.ds(c * piece, piece)
        return pltpu.make_async_copy(table.at[part], tab_low.at[part], tab_sem.at[c])

    for c in range(pieces):
        table_copy(c).start()
    fetches = [
        pltpu.make_async_copy(src, dst, near_sem.at[k])
        for k, (src, dst) in enumerate(zip(far, near))
    ]
    for fetch in fetches:
        fetch.start()

    for fetch in first:
        fetch.wait()

    row_id = lax.broadcasted_iota(jnp.int32, (seqs, length), 0)
    lane_id = lax.broadcasted_iota(jnp.int32, (seqs, length), 1)
    count_of = jnp.ones((seqs, length), F32)
    tag_of = jnp.zeros((seqs, length), jnp.int32)
    len_of = jnp.zeros((seqs, length), jnp.int32)
    for s in range(seqs):
        tag = tags[s]
        count_of = jnp.where(row_id == s, counts[tag].astype(F32), count_of)
        tag_of = jnp.where(row_id == s, tag, tag_of)
        len_of = jnp.where(row_id == s, lens[0, s], len_of)
    code = ids[...].astype(F32)
    turns = jnp.floor((code + 0.5) / jnp.maximum(count_of, 1.0))
    local = tag_of * domain_rows + (code - turns * count_of).astype(jnp.int32)
    live = lane_id < len_of
    rel = own[...] - me
    rel = jnp.where(rel < 0, rel + n, rel)

    owner_id = lax.broadcasted_iota(jnp.int32, (n, length), 0)
    hots = [jnp.where(owner_id == rel[s : s + 1, :], 1.0, 0.0) for s in range(seqs)]
    before = (
        lax.broadcasted_iota(jnp.int32, (length, length), 0)
        < lax.broadcasted_iota(jnp.int32, (length, length), 1)
    )
    earlier = jnp.where(before, 1.0, 0.0).astype(BF16)
    prefix = dot_nn(jnp.concatenate(hots, axis=0).astype(BF16), earlier)
    running = jnp.zeros((n, 1), F32)
    ranks = []
    for s in range(seqs):
        ranks.append(
            jnp.sum(hots[s] * (prefix[s * n : s * n + n] + running), axis=0, keepdims=True)
        )
        running = running + jnp.sum(hots[s], axis=1, keepdims=True)
    rank = jnp.concatenate(ranks, axis=0).astype(jnp.int32)
    pos_ref[...] = rel * cap + rank

    low = (local & 255).astype(F32)
    high = lax.shift_right_logical(local, 8).astype(F32)
    slot_id = lax.broadcasted_iota(jnp.int32, (LANES, length), 0)
    asking = jnp.zeros((2 * n, LANES), F32)
    for s in range(seqs):
        hot = hots[s]
        values = jnp.concatenate([hot * high[s : s + 1, :], hot * low[s : s + 1, :]], axis=0)
        slot_hot = jnp.where(slot_id == rank[s : s + 1, :], 1.0, 0.0).astype(BF16)
        asking = asking + dot_nt(values.astype(BF16), slot_hot)
    wanted = (asking[:n] * 256.0 + asking[n:]).astype(jnp.int32)
    for j in range(n):
        req[j] = wanted[j : j + 1, :]

    pl.semaphore_wait(barrier, n)

    def request(j):
        back = lax.rem(n - j, n)
        return remote(req.at[j], asked_v.at[back], req_send.at[j], req_recv.at[back], peer(j))

    def request_arrival(j):
        return remote(req.at[j], asked_v.at[j], req_send.at[j], req_recv.at[j], peer(j))

    def ask(j, carry):
        request(j).start()
        return carry

    lax.fori_loop(1, n, ask, 0)
    asked_v[0] = req[0]

    for c in range(pieces):
        table_copy(c).wait()

        def widen(r, carry):
            part = pl.ds(pl.multiple_of(c * piece + r * 256, 256), 256)
            tab[part, :] = tab_low[part, :].astype(F32)
            return carry

        lax.fori_loop(0, piece // 256, widen, 0)

    def all_asked(j, carry):
        request_arrival(j).wait_recv()
        return carry

    lax.fori_loop(1, n, all_asked, 0)
    to_scalar = pltpu.make_async_copy(asked_v, asked_s, smem_sem)
    to_scalar.start()
    to_scalar.wait()

    def slot_block(j):
        return pl.ds(pl.multiple_of(j * cap, cap), cap)

    def row_copy(j):
        back = lax.rem(n - j, n)
        return remote(
            send.at[slot_block(j)], recv.at[slot_block(back)],
            row_send.at[j], row_recv.at[back], peer(j),
        )

    def row_arrival(j):
        at = slot_block(j)
        return remote(send.at[at], recv.at[at], row_send.at[j], row_recv.at[j], peer(j))

    def gather(j):
        def some(c, carry):
            for r in range(16):
                at = asked_s[j, 0, c * 16 + r] & (row_limit - 1)
                gbuf[pl.ds(c * 16 + r, 1), :] = tab[pl.ds(at, 1), :]
            return carry

        lax.fori_loop(0, cap // 16, some, 0)
        return gbuf[...].astype(BF16)

    def pair_at(step):
        half = (step + 1) // 2
        return jnp.where(lax.rem(step, 2) == 1, n // 4 - half, n // 4 + half)

    def serve(step, carry):
        def one(j, inner):
            send[slot_block(j), :] = gather(j)
            row_copy(j).start()
            return inner

        last = n - 2 * pair_at(step)
        return lax.fori_loop(last - 1, jnp.minimum(last + 1, n), one, carry)

    lax.fori_loop(0, n // 2, serve, 0)
    recv[0:cap, :] = gather(0)

    key = jnp.where(live, (rel * row_limit + local).astype(F32), -1.0)
    key_cols = [
        jnp.broadcast_to(key[s : s + 1, :], (length, length)).T for s in range(seqs)
    ]
    fresh = []
    for s in range(seqs):
        seen = jnp.where(before & (key_cols[s] == key[s : s + 1, :]), 1.0, 0.0)
        for e in range(s):
            seen = jnp.maximum(seen, jnp.where(key_cols[e] == key[s : s + 1, :], 1.0, 0.0))
        fresh.append(1.0 - jnp.max(seen, axis=0, keepdims=True))
    fresh = [jnp.where(live[s : s + 1, :], fresh[s], 0.0) for s in range(seqs)]
    news = [hots[s] * fresh[s] for s in range(seqs)]
    prefix = dot_nn(jnp.concatenate(news, axis=0).astype(BF16), earlier)
    running = jnp.zeros((n, 1), F32)
    firsts = []
    for s in range(seqs):
        firsts.append(
            jnp.sum(news[s] * (prefix[s * n : s * n + n] + running), axis=0, keepdims=True)
        )
        running = running + jnp.sum(news[s], axis=1, keepdims=True)
    first_cols = [
        jnp.broadcast_to(firsts[s] * fresh[s] + fresh[s], (length, length)).T for s in range(seqs)
    ]
    found = []
    for s in range(seqs):
        at = jnp.zeros((length, length), F32)
        for e in range(s + 1):
            at = jnp.maximum(at, jnp.where(key_cols[e] == key[s : s + 1, :], first_cols[e], 0.0))
        found.append(jnp.max(at, axis=0, keepdims=True))
    found = jnp.concatenate(found, axis=0).astype(jnp.int32) - 1
    back_at = rel * gcap + found
    if ocap:
        back_at = jnp.where(found < gcap, back_at, n * gcap + rel * ocap + found - gcap)
    back_pos[...] = jnp.where(live, back_at, -1)
    below = used - local
    low = (below & 255).astype(F32)
    high = lax.shift_right_logical(below, 8).astype(F32)
    asking = jnp.zeros((2 * n, LANES), F32)
    for s in range(seqs):
        values = jnp.concatenate(
            [news[s] * high[s : s + 1, :], news[s] * low[s : s + 1, :]], axis=0
        )
        slot_hot = jnp.where(slot_id == firsts[s].astype(jnp.int32), 1.0, 0.0).astype(BF16)
        asking = asking + dot_nt(values.astype(BF16), slot_hot)
    wanted = used - (asking[:n] * 256.0 + asking[n:]).astype(jnp.int32)
    lane = lax.broadcasted_iota(jnp.int32, (n, LANES), 1)
    largest = jnp.max(running, axis=0, keepdims=True)
    limits = jnp.where(lane == 0, running, largest).astype(jnp.int32)
    for j in range(n):
        back_req[j, 0:1] = wanted[j : j + 1, :]
        back_req[j, 1:2] = limits[j : j + 1, :]
    asked_out[core, 0] = back_req[0]

    def back_request(j):
        back = lax.rem(n - j, n)
        return remote(
            back_req.at[j], asked_out.at[core, back], back_send.at[j], back_recv.at[back], peer(j)
        )

    def back_request_arrival(j):
        return remote(
            back_req.at[j], asked_out.at[core, j], back_send.at[j], back_recv.at[j], peer(j)
        )

    def tell(j, carry):
        back_request(j).start()
        return carry

    lax.fori_loop(1, n, tell, 0)

    def share(which):
        ref = asked_out.at[which]
        return remote(ref, ref, pair_sem.at[0], pair_sem.at[1], {"dp": 1 - core})

    for fetch in fetches:
        fetch.wait()
    for part, w in enumerate((wq, wk, wv)):
        wqkv[:, part * hd : (part + 1) * hd] = w[...]
        wqkv_t[part * hd : (part + 1) * hd, :] = w[...].T
    wo_t[...] = wo[...].T
    win_t[...] = win[...].T
    wout_t[...] = wout[...].T
    buck_t[...] = buckets[...].astype(F32).T
    g1_col = jnp.broadcast_to(g1[...], (8, width)).T[:, 0:1]
    g2_col = jnp.broadcast_to(g2[...], (8, width)).T[:, 0:1]
    dsum[...] = jnp.zeros_like(dsum)
    b_acc[...] = jnp.zeros_like(b_acc)

    def bias_rows(r, carry):
        part = pl.ds(pl.multiple_of(r * 8, 8), 8)
        bt = buck_t[part, :]
        rows = [jnp.zeros((8, length), F32) for _ in range(heads)]
        for b in range(bucket_count):
            here = bt == float(b)
            rows = [jnp.where(here, btab[h, b], rows[h]) for h in range(heads)]
        for p in range(pairs):
            bias[p, part, :] = jnp.concatenate(rows[2 * p : 2 * p + 2], axis=1)
        return carry

    lax.fori_loop(0, length // 8, bias_rows, 0)

    def load_dy(s, carry):
        part = pl.ds(pl.multiple_of(s * length, length), length)
        alive = lax.broadcasted_iota(jnp.int32, (width, length), 1) < lens[0, s]
        dy_t[:, part] = jnp.where(alive, cot[s].astype(F32).T, 0.0).astype(BF16)
        return carry

    lax.fori_loop(0, seqs, load_dy, 0)

    def place(step, carry):
        pair = pair_at(step)

        def ready(j, inner):
            row_arrival(j).wait_recv()
            return inner

        lax.fori_loop(jnp.maximum(2 * pair, 1), 2 * pair + 2, ready, 0)
        first = pl.multiple_of(pair * 2 * cap, 2 * cap)
        hot = hot_slots(pos_ref[...], first, 2 * cap)
        got = dot_tn(recv[pl.ds(first, 2 * cap), :], hot)

        @pl.when(step == 0)
        def _():
            x_acc[...] = got

        @pl.when(step > 0)
        def _():
            x_acc[...] += got

        return carry

    lax.fori_loop(0, n // 2, place, 0)

    x_t[...] = x_acc[...].astype(BF16)

    xf = x_acc[...]
    scale = lax.rsqrt(jnp.mean(xf * xf, axis=0, keepdims=True) + EPSILON)
    a = (xf * scale * g1_col).astype(BF16)
    a_t[...] = a
    out = dot_nn(wqkv_t[...], a)
    qkv_t[0:hd, :] = out[:hd].astype(BF16) * jnp.array(1.0 / math.sqrt(DH), BF16)
    qkv_t[hd:, :] = out[hd:].astype(BF16)
    kv[...] = dot_nn(a.T, wqkv[:, hd:]).astype(BF16)

    rows = [slice(p * 2 * DH, (p + 1) * 2 * DH) for p in range(pairs)]
    krows = [slice(hd + p * 2 * DH, hd + (p + 1) * 2 * DH) for p in range(pairs)]
    vrows = [slice(2 * hd + p * 2 * DH, 2 * hd + (p + 1) * 2 * DH) for p in range(pairs)]
    jobs = [(i, p) for i in range(group) for p in range(pairs)]

    def members(g):
        return [pl.ds(pl.multiple_of((g * group + i) * length, length), length) for i in range(group)]

    def attend(g, carry):
        parts = members(g)
        key_id = lax.broadcasted_iota(jnp.int32, (length, 2 * length), 0)
        visible = [key_id < lens[0, g * group + i] for i in range(group)]
        scores = [
            dot_nn(kv[parts[i], rows[p]], split_pair(qkv_t[rows[p], parts[i]])) for i, p in jobs
        ]
        probs = []
        for (i, p), score in zip(jobs, scores):
            score = jnp.where(visible[i], score + bias[p], -1000000000.0)
            expo = jnp.exp(score - jnp.max(score, axis=0, keepdims=True))
            prob = expo * (1.0 / jnp.sum(expo, axis=0, keepdims=True))
            p_s[g * group + i, p] = prob
            probs.append(prob.astype(BF16))
        for (i, p), prob in zip(jobs, probs):
            mixed = dot_nn(qkv_t[vrows[p], parts[i]], prob)
            o_t[rows[p], parts[i]] = jnp.concatenate(
                [mixed[:DH, :length], mixed[DH:, length:]], axis=0
            ).astype(BF16)
        return carry

    lax.fori_loop(0, seqs // group, attend, 0)

    def told(j, carry):
        back_request_arrival(j).wait_recv()
        return carry

    lax.fori_loop(1, n, told, 0)
    share(core).start()

    m = x_t[...].astype(F32) + dot_nn(wo_t[...], o_t[...])
    scale = lax.rsqrt(jnp.mean(m * m, axis=0, keepdims=True) + EPSILON)
    z = m * scale
    normed = (z * g2_col).astype(BF16)
    c_t[...] = normed
    value, slope = gelu_parts(dot_nn(win_t[...], normed))
    act = value.astype(BF16)
    act_t[...] = act
    du = (dot_nn(wout[...], dy_t[...]) * slope).astype(BF16)
    du_t[...] = du
    y = m + dot_nn(wout_t[...], act)
    for s in range(seqs):
        y_out[s] = y[:, s * length : (s + 1) * length].T.astype(BF16)
    flushes = [
        pltpu.make_async_copy(src, dst, out_sem.at[k])
        for k, (src, dst) in enumerate(
            (
                (y_out, y_far), (ig_out, ig_far), (asked_out, asked_far), (early_tot, early_far),
                (late_tot, late_far), (small_tot, small_far),
            )
        )
    ]
    flushes[0].start()
    dc = dot_nn(win[...], du)
    gain_two = dc * z
    gain_two = sum(gain_two[:, s * length : (s + 1) * length] for s in range(seqs))
    small_tot[1:2, :] = jnp.sum(gain_two.T, axis=0, keepdims=True)
    e = dc * g2_col
    dm = dy_t[...].astype(F32) + scale * (e - z * jnp.mean(e * z, axis=0, keepdims=True))
    dm_t[...] = dm
    dmb = dm.astype(BF16)
    dmb_t[...] = dmb
    do_t[...] = dot_nn(wo[...], dmb).astype(BF16)

    for k in range(ff // width):
        at = slice(k * width, (k + 1) * width)
        early[at, :] = dot_nt(c_t[...], du_t[at, :]).astype(BF16)
    early[ff : 2 * ff, :] = dot_nt(act_t[...], dy_t[...]).astype(BF16)
    if early.shape[0] > 2 * ff:
        early[2 * ff :, :] = jnp.zeros((early.shape[0] - 2 * ff, width), BF16)
    early_sum.start()

    def attend_back(g):
        parts = members(g)
        do2s = [split_pair(do_t[rows[p], parts[i]]) for i, p in jobs]
        dprobs = [dot_nn(kv[parts[i], krows[p]], do2) for (i, p), do2 in zip(jobs, do2s)]
        lows = []
        for (i, p), dprob in zip(jobs, dprobs):
            prob = p_s[g * group + i, p]
            ds = prob * (dprob - jnp.sum(dprob * prob, axis=0, keepdims=True))
            dsum[p] += ds
            lows.append(ds.astype(BF16))
        for (i, p), do2 in zip(jobs, do2s):
            prob = p_s[g * group + i, p].astype(BF16)
            dqkv_t[vrows[p], parts[i]] = dot_nt(do2, prob).astype(BF16)
        for (i, p), low in zip(jobs, lows):
            q2 = split_pair(qkv_t[rows[p], parts[i]])
            dqkv_t[krows[p], parts[i]] = dot_nt(q2, low).astype(BF16)
        for (i, p), low in zip(jobs, lows):
            dq = dot_nn(qkv_t[krows[p], parts[i]], low) * (1.0 / math.sqrt(DH))
            dqkv_t[rows[p], parts[i]] = jnp.concatenate(
                [dq[:DH, :length], dq[DH:, length:]], axis=0
            ).astype(BF16)

    groups = seqs // group

    def back_loop(g, carry):
        attend_back(g)

        @pl.when(g == 0)
        def _():
            early_sum.core_to_lo()

        return carry

    lax.fori_loop(0, groups, back_loop, 0)

    xf = x_t[...].astype(F32)
    scale = lax.rsqrt(jnp.mean(xf * xf, axis=0, keepdims=True) + EPSILON)
    z = xf * scale
    da = dot_nn(wqkv[...], dqkv_t[...])
    gain_one = da * z
    gain_one = sum(gain_one[:, s * length : (s + 1) * length] for s in range(seqs))
    e = da * g1_col
    ig = dm_t[...] + scale * (e - z * jnp.mean(e * z, axis=0, keepdims=True))
    igb_t[...] = ig.astype(BF16)

    def grad_block(j):
        return pl.ds(pl.multiple_of(j * gcap, gcap), gcap)

    def grad_copy(j):
        back = lax.rem(n - j, n)
        return remote(
            slots.at[grad_block(j)], inc.at[core, grad_block(back)],
            grad_send.at[j], grad_recv.at[back], peer(j),
        )

    def grad_arrival(j):
        return remote(
            slots.at[grad_block(j)], inc.at[core, grad_block(j)],
            grad_send.at[j], grad_recv.at[j], peer(j),
        )

    def forward(j, which):
        ref = inc.at[which, grad_block(j)]
        return remote(ref, ref, fwd_send.at[j], fwd_recv.at[j], {"dp": 1 - core})

    def to_slots(k, carry):
        first = pl.multiple_of(k * wide_slots, wide_slots)
        slots[pl.ds(first, wide_slots), :] = dot_nt(
            hot_slots(back_pos[...], first, wide_slots), igb_t[...]
        ).astype(BF16)

        def go(j, inner):
            grad_copy(j).start()
            return inner

        owners = owners_at_once
        lax.fori_loop(jnp.maximum(k * owners, 1), (k + 1) * owners, go, 0)
        return carry

    steps = n // owners_at_once

    def send_rows(first, last):
        lax.fori_loop(first * steps // 8, last * steps // 8, to_slots, 0)

    for k in range(3 * hd // width):
        at = slice(k * width, (k + 1) * width)
        late[at, :] = dot_nt(a_t[...], dqkv_t[at, :]).astype(BF16)
    late[3 * hd : 4 * hd, :] = dot_nt(o_t[...], dmb_t[...]).astype(BF16)
    if late.shape[0] > 4 * hd:
        late[4 * hd :, :] = jnp.zeros((late.shape[0] - 4 * hd, width), BF16)
    late_sum.start()

    def pass_on(step, carry):
        j = n - 1 - step
        grad_arrival(j).wait_recv()
        forward(j, core).start()
        return carry

    late_sum.core_to_lo()
    early_sum.lo_to_hi()
    send_rows(0, 3)
    keep = pltpu.make_async_copy(slots.at[grad_block(0)], inc.at[core, grad_block(0)], smem_sem)
    keep.start()
    remote(
        slots.at[grad_block(0)], inc.at[core, grad_block(0)], fwd_send.at[0], fwd_recv.at[0],
        {"dp": 1 - core},
    ).start()
    def bias_back(r, carry):
        part = pl.ds(pl.multiple_of(r * 8, 8), 8)
        bt = buck_t[part, :]
        grads = [dsum[h // 2, part, (h % 2) * length : (h % 2 + 1) * length] for h in range(heads)]
        for b in range(bucket_count):
            here = bt == float(b)
            for h in range(heads):
                b_acc[h, b] += jnp.where(here, grads[h], 0.0)
        return carry

    lax.fori_loop(0, length // 8, bias_back, 0)
    small_parts = [jnp.sum(gain_one.T, axis=0, keepdims=True), small_tot[1:2, :]]
    for h in range(heads):
        by_bucket = jnp.sum(b_acc[h], axis=1)
        row = jnp.sum(by_bucket.T, axis=0, keepdims=True)
        small_parts.append(
            jnp.concatenate([row, jnp.zeros((1, LANES - bucket_count), F32)], axis=1)
        )
    small_sum.start(jnp.concatenate(small_parts, axis=0))
    late_sum.lo_to_hi()
    small_sum.core_to_lo()
    early_sum.hi_to_gather()
    late_sum.hi_to_gather()
    small_sum.lo_to_hi()
    send_rows(3, 6)
    early_sum.gather_to_lo()
    late_sum.gather_to_lo()
    send_rows(6, 8)
    for s in range(seqs):
        ig_out[s] = ig[:, s * length : (s + 1) * length].T
    flushes[1].start()
    if ocap:
        for k in range(n * ocap // 256):
            first = n * gcap + k * 256
            slots[pl.ds(first, 256), :] = dot_nt(
                hot_slots(back_pos[...], first, 256), igb_t[...]
            ).astype(BF16)
        over_rows = pl.ds(0, n * ocap)
        spill = pltpu.make_async_copy(
            slots.at[pl.ds(n * gcap, n * ocap)], over.at[over_rows], smem_sem
        )
        keep.wait()
        spill.start()
    early_sum.gather_to_core()
    late_sum.gather_to_core()
    lax.fori_loop(0, 15, pass_on, 0)
    small_sum.finish()
    flushes[5].start()
    early_sum.finish()
    flushes[3].start()
    late_sum.finish()
    flushes[4].start()
    share(core).wait_send()
    share(1 - core).wait_recv()
    flushes[2].start()
    if ocap:
        spill.wait()
        most = jnp.zeros((1, LANES), F32)

        def peak(j, most):
            return jnp.maximum(
                most, jnp.maximum(asked_out[0, j, 1:2], asked_out[1, j, 1:2]).astype(F32)
            )

        most = lax.fori_loop(0, n, peak, most)
        excess[0, 0] = jnp.max(most).astype(jnp.int32)
    else:
        keep.wait()
        excess[0, 0] = 0

    def rows_in(j, carry):
        forward(j, 1 - core).wait_recv()
        forward(j, core).wait_send()
        return carry

    lax.fori_loop(0, n, rows_in, 0)

    def sent(j, carry):
        request(j).wait_send()
        back_request(j).wait_send()
        row_copy(j).wait_send()
        grad_copy(j).wait_send()
        return carry

    lax.fori_loop(1, n, sent, 0)
    for flush in flushes:
        flush.wait()


def step_kernel(n, lo, cap, gcap, used, sizes, *refs):
    parts, at = [], 0
    for size in sizes:
        parts.append(refs[at : at + size])
        at += size
    step_body(n, lo, cap, gcap, used, *parts)


def rest_body(n, rows, mine, out, send_sem, recv_sem, fwd_send, fwd_recv, self_sem):
    me = lax.axis_index("emb")
    core = lax.axis_index("dp")
    barrier = pltpu.get_barrier_semaphore()

    def peer(j):
        return {"emb": lax.rem(me + j, n)}

    def greet(k, carry):
        pl.semaphore_signal(barrier, inc=1, device_id=peer(k), device_id_type=MESH)
        return carry

    lax.fori_loop(1, n, greet, 0)
    pl.semaphore_signal(barrier, inc=1, device_id={"dp": 1 - core}, device_id_type=MESH)
    pl.semaphore_wait(barrier, n)

    def block(j):
        return pl.ds(pl.multiple_of(j * rows, rows), rows)

    def landed(which, j):
        return out.at[pl.ds(pl.multiple_of((which * n + j) * rows, rows), rows)]

    def copy(j):
        back = lax.rem(n - j, n)
        return remote(
            mine.at[block(j)], landed(core, back), send_sem.at[j], recv_sem.at[back], peer(j)
        )

    def arrival(j):
        return remote(mine.at[block(j)], landed(core, j), send_sem.at[j], recv_sem.at[j], peer(j))

    def forward(j, which):
        ref = landed(which, j)
        return remote(ref, ref, fwd_send.at[j], fwd_recv.at[j], {"dp": 1 - core})

    def start(j, carry):
        copy(j).start()
        return carry

    lax.fori_loop(1, n, start, 0)
    keep = pltpu.make_async_copy(mine.at[block(0)], landed(core, 0), self_sem)
    keep.start()
    keep.wait()
    forward(0, core).start()

    def pass_on(j, carry):
        arrival(j).wait_recv()
        forward(j, core).start()
        return carry

    lax.fori_loop(1, n, pass_on, 0)

    def finish(j, carry):
        forward(j, core).wait_send()
        forward(j, 1 - core).wait_recv()
        return carry

    lax.fori_loop(0, n, finish, 0)

    def sent(j, carry):
        copy(j).wait_send()
        return carry

    lax.fori_loop(1, n, sent, 0)


def exchange_rest(n, rows, over):
    dma = pltpu.SemaphoreType.DMA
    anywhere = pl.BlockSpec(memory_space=pl.ANY)
    return pl.pallas_call(
        functools.partial(rest_body, n, rows),
        out_shape=jax.ShapeDtypeStruct(over.shape, over.dtype),
        in_specs=[anywhere],
        out_specs=anywhere,
        scratch_shapes=[dma((n,)), dma((n,)), dma((n,)), dma((n,)), dma],
        compiler_params=pltpu.CompilerParams(collective_id=1, has_side_effects=True),
        name="rest",
    )(over)


def scatter_body(
    n, cap, rest, used, asked_far, counts, inc, over, early, late, small, y_in, ig_in,
    y_out, ig_out, grad, g1, wq, wk, wv, wo, bias, g2, win, wout,
    acc, wide, zero, inc_v, over_v, y_v, ig_v, early_v, late_v, wq_v, wk_v, wv_v, wo_v, win_v, wout_v,
    out_sem, in_sem, pass_sem, asked, asked_sem, spare_rows,
):
    rows_dev, width = grad.shape
    chunk = zero.shape[0]
    domain_rows = used // 3
    per_domain = domain_rows // chunk
    slots = n * cap
    hd = wq.shape[1]
    ff = win.shape[1]
    loads = [
        pltpu.make_async_copy(src, dst, in_sem.at[k])
        for k, (src, dst) in enumerate(
            (
                (inc, inc_v), (over, over_v), (early, early_v), (late, late_v), (y_in, y_v),
                (ig_in, ig_v),
            )
        )
    ]
    ask = pltpu.make_async_copy(asked_far, asked, asked_sem)
    ask.start()
    loads[0].start()
    zero[...] = jnp.zeros_like(zero)

    def chunk_at(k):
        return pl.ds(pl.multiple_of(k * chunk, chunk), chunk)

    def clear_copy(k):
        return pltpu.make_async_copy(zero, grad.at[chunk_at(k)], out_sem.at[k])

    def out_copy(k):
        return pltpu.make_async_copy(acc.at[chunk_at(k)], grad.at[chunk_at(k)], out_sem.at[k])

    def in_use(k):
        return (k % per_domain) * chunk < counts[k // per_domain]

    def spare(k, carry):
        clear_copy(k).start()
        return carry

    def prepare(k, carry):
        @pl.when(in_use(k))
        def _():
            def clear(r, inner):
                at = pl.multiple_of(k * chunk + r * 256, 256)
                acc[pl.ds(at, 256), :] = jnp.zeros((256, width), F32)
                return inner

            lax.fori_loop(0, chunk // 256, clear, 0)

        return carry

    lax.fori_loop(0, used // chunk, prepare, 0)
    loads[0].wait()
    for load in loads[1:]:
        load.start()
    loads[1].wait()
    lax.fori_loop(used // chunk, rows_dev // chunk, spare, 0)

    def unused(k, carry):
        @pl.when(jnp.logical_not(in_use(k)))
        def _():
            clear_copy(k).start()

        return carry

    lax.fori_loop(0, used // chunk, unused, 0)

    def widen(r, carry):
        at = pl.ds(pl.multiple_of(r * 256, 256), 256)
        wide[at, :] = inc_v[at, :].astype(F32)
        return carry

    lax.fori_loop(0, 2 * slots // 256, widen, 0)

    def source(k, carry):
        base = k * 2 * LANES

        def eight(g, inner):
            first = g * 8
            ats = [asked[base + first + r] for r in range(8)]
            sums = [
                acc[pl.ds(ats[r], 1), :] + wide[pl.ds(k * cap + first + r, 1), :] for r in range(8)
            ]
            for r in range(8):
                acc[pl.ds(ats[r], 1), :] = sums[r]
            return inner

        count = asked[base + LANES]
        lax.fori_loop(0, (jnp.minimum(count, cap) + 7) // 8, eight, 0)
        if rest:
            def more(g, inner):
                first = g * 8
                ats = [asked[base + cap + first + r] for r in range(8)]
                rows = [
                    over_v[pl.ds(pl.multiple_of(k * rest + first // 16 * 16, 16), 16), :]
                ][0].astype(F32)
                spare_rows[...] = rows
                sums = [
                    acc[pl.ds(ats[r], 1), :] + spare_rows[pl.ds(first % 16 + r, 1), :]
                    for r in range(8)
                ]
                for r in range(8):
                    acc[pl.ds(ats[r], 1), :] = sums[r]
                return inner

            lax.fori_loop(0, (jnp.maximum(count - cap, 0) + 7) // 8, more, 0)
        return carry

    ask.wait()
    lax.fori_loop(0, 2 * n, source, 0)

    def write(k, carry):
        @pl.when(in_use(k))
        def _():
            out_copy(k).start()

        return carry

    lax.fori_loop(0, used // chunk, write, 0)

    passes = []

    def hand_on(src, dst):
        passes.append(pltpu.make_async_copy(src, dst, pass_sem.at[len(passes)]))
        passes[-1].start()

    for load in loads[2:]:
        load.wait()
    hand_on(y_v, y_out)
    hand_on(ig_v, ig_out)
    for i, (value, out) in enumerate(((wq_v, wq), (wk_v, wk), (wv_v, wv))):
        for k in range(hd // width):
            at = i * hd + k * width
            value[:, k * width : (k + 1) * width] = late_v[at : at + width, :].astype(F32)
        hand_on(value, out)
    wo_v[...] = late_v[3 * hd : 4 * hd, :].astype(F32)
    hand_on(wo_v, wo)
    for k in range(ff // width):
        at = slice(k * width, (k + 1) * width)
        win_v[:, at] = early_v[at, :].astype(F32)
    hand_on(win_v, win)
    wout_v[...] = early_v[ff : 2 * ff, :].astype(F32)
    hand_on(wout_v, wout)
    g1[...] = small[0:1, :]
    g2[...] = small[1:2, :]
    heads, buckets = bias.shape
    bias[...] = small[2 : 2 + heads, 0:buckets]

    def finish(k, carry):
        clear_copy(k).wait()
        return carry

    lax.fori_loop(0, rows_dev // chunk, finish, 0)
    for copy in passes:
        copy.wait()


def on_device(
    hashed_ids, owners, domain_tags, user_counts, lengths, buckets, table, gain_one,
    query_weight_matrix, key_weight_matrix, value_weight_matrix, attention_output_weight,
    bias_table, gain_two, feedforward_input_weight, feedforward_output_weight, cotangent,
):
    n = lax.axis_size("emb")
    seqs, length = hashed_ids.shape
    tokens = seqs * length
    rows_dev, width = table.shape
    used = 3 * (rows_dev // 4)
    cap = max(2, 2 * tokens // n)
    hd = query_weight_matrix.shape[1]
    ff = feedforward_input_weight.shape[1]
    heads = hd // DH
    pairs = heads // 2
    bucket_count = bias_table.shape[0]
    slots = n * cap
    gcap = max(16, 3 * cap // 4 // 16 * 16)
    ocap = cap - gcap
    lo = 2 ** ((n.bit_length()) // 2)
    unit = 2 * n * 16
    early_rows = -(-2 * ff // unit) * unit
    late_rows = -(-4 * hd // unit) * unit
    vmem = pl.BlockSpec(memory_space=pltpu.VMEM)
    smem = pl.BlockSpec(memory_space=pltpu.SMEM)
    anywhere = pl.BlockSpec(memory_space=pl.ANY)
    dma = pltpu.SemaphoreType.DMA
    shape = jax.ShapeDtypeStruct

    operands = (
        hashed_ids, owners.reshape(seqs, length), domain_tags, user_counts, lengths, bias_table.T,
        buckets, gain_one.reshape(1, width), gain_two.reshape(1, width), table, cotangent,
        query_weight_matrix, key_weight_matrix, value_weight_matrix, attention_output_weight,
        feedforward_input_weight, feedforward_output_weight,
    )
    results = (
        shape((seqs, length, width), BF16),
        shape((seqs, length, width), F32),
        shape((2, n * gcap, width), BF16),
        shape((2, n, 2, LANES), jnp.int32),
        shape((early_rows, width), BF16),
        shape((late_rows, width), BF16),
        shape((8, LANES), F32),
        shape((2 * n * max(ocap, 16), width), BF16),
        shape((1, 1), jnp.int32),
    )
    lookup_scratch = [
        pltpu.VMEM((n, 1, LANES), jnp.int32),
        pltpu.VMEM((n, 1, LANES), jnp.int32),
        pltpu.SMEM((n, 1, LANES), jnp.int32),
        pltpu.VMEM((used, width), BF16),
        pltpu.VMEM((rows_dev, width), F32),
        pltpu.VMEM((cap, width), F32),
        pltpu.VMEM((slots, width), BF16),
        pltpu.VMEM((slots, width), BF16),
        pltpu.VMEM((width, tokens), F32),
        pltpu.VMEM((seqs, length), jnp.int32),
        pltpu.VMEM((slots, width), BF16),
        pltpu.VMEM((early_rows, width), BF16),
        pltpu.VMEM((late_rows, width), BF16),
        pltpu.VMEM((seqs, length), jnp.int32),
        pltpu.VMEM((n, 2, LANES), jnp.int32),
        dma((n,)), dma((n,)),
        dma((n,)), dma((n,)), dma((n,)), dma((n,)), dma((2,)), dma((6,)), dma,
        dma((n,)), dma((n,)), dma((n,)), dma((n,)),
    ]
    block_scratch = [
        pltpu.VMEM((3 * hd, width), BF16),
        pltpu.VMEM((width, 3 * hd), BF16),
        pltpu.VMEM((width, hd), BF16),
        pltpu.VMEM((ff, width), BF16),
        pltpu.VMEM((width, ff), BF16),
        pltpu.VMEM((length, length), F32),
        pltpu.VMEM((pairs, length, 2 * length), F32),
        pltpu.VMEM((width, tokens), BF16),
        pltpu.VMEM((width, tokens), BF16),
        pltpu.VMEM((3 * hd, tokens), BF16),
        pltpu.VMEM((tokens, 2 * hd), BF16),
        pltpu.VMEM((seqs, pairs, length, 2 * length), F32),
        pltpu.VMEM((hd, tokens), BF16),
        pltpu.VMEM((width, tokens), BF16),
        pltpu.VMEM((ff, tokens), BF16),
        pltpu.VMEM((ff, tokens), BF16),
        pltpu.VMEM((width, tokens), BF16),
        pltpu.VMEM((width, tokens), F32),
        pltpu.VMEM((width, tokens), BF16),
        pltpu.VMEM((hd, tokens), BF16),
        pltpu.VMEM((3 * hd, tokens), BF16),
        pltpu.VMEM((pairs, length, 2 * length), F32),
        pltpu.VMEM((width, tokens), BF16),
        pltpu.VMEM((heads, bucket_count, 8, length), F32),
        pltpu.VMEM((seqs, length, width), BF16),
        pltpu.VMEM((width, hd), BF16),
        pltpu.VMEM((width, hd), BF16),
        pltpu.VMEM((width, hd), BF16),
        pltpu.VMEM((hd, width), BF16),
        pltpu.VMEM((width, ff), BF16),
        pltpu.VMEM((ff, width), BF16),
        dma((11,)),
        pltpu.VMEM((seqs, length), jnp.int32),
        pltpu.VMEM((seqs, length), jnp.int32),
        pltpu.SMEM((seqs,), jnp.int32),
        pltpu.SMEM((user_counts.shape[0],), jnp.int32),
        pltpu.SMEM(lengths.shape, jnp.int32),
        pltpu.SMEM((heads, bucket_count), F32),
        pltpu.VMEM((length, length), jnp.int32),
        pltpu.VMEM((1, width), F32),
        pltpu.VMEM((1, width), F32),
        dma((5,)),
    ]
    block_scratch += [pltpu.VMEM(results[k].shape, results[k].dtype) for k in (0, 1, 3, 4, 5, 6)]
    block_scratch += [dma((6,))]
    early_scratch = Reducer.scratch(n, lo, early_rows)
    late_scratch = Reducer.scratch(n, lo, late_rows)
    small_scratch = SmallReducer.scratch(n, lo)
    scratch = [lookup_scratch, block_scratch, early_scratch, late_scratch, small_scratch]
    sizes = [len(operands), len(results)] + [len(part) for part in scratch]
    y, ig, incoming, asked, early_total, late_total, small_total, over, excess = pl.pallas_call(
        functools.partial(step_kernel, n, lo, cap, gcap, used, sizes),
        out_shape=results,
        in_specs=[anywhere] * len(operands),
        out_specs=(anywhere,) * (len(results) - 1) + (smem,),
        scratch_shapes=sum(scratch, []),
        compiler_params=pltpu.CompilerParams(
            collective_id=0, has_side_effects=True, vmem_limit_bytes=VMEM_LIMIT
        ),
        name="step",
    )(*operands)

    if ocap:
        over = lax.cond(
            excess[0, 0] > gcap, functools.partial(exchange_rest, n, ocap), lambda rows: rows, over
        )

    chunk = math.gcd(1024, used // 3)
    output, input_grad, table_grad, g1, gq, gk, gv, go, gb, g2, gin, gout = pl.pallas_call(
        functools.partial(scatter_body, n, gcap, ocap, used),
        out_shape=(
            shape((seqs, length, width), BF16),
            shape((seqs, length, width), F32),
            shape((rows_dev, width), F32),
            shape((1, width), F32),
            shape((width, hd), F32),
            shape((width, hd), F32),
            shape((width, hd), F32),
            shape((hd, width), F32),
            shape((heads, bucket_count), F32),
            shape((1, width), F32),
            shape((width, ff), F32),
            shape((ff, width), F32),
        ),
        in_specs=[anywhere, smem, anywhere, anywhere, anywhere, anywhere, vmem, anywhere, anywhere],
        out_specs=(anywhere,) * 3 + (vmem,) + (anywhere,) * 4 + (vmem,) * 2 + (anywhere,) * 2,
        scratch_shapes=[
            pltpu.VMEM((used + 8, width), F32),
            pltpu.VMEM((2 * n * gcap, width), F32),
            pltpu.VMEM((chunk, width), F32),
            pltpu.VMEM((2 * n * gcap, width), BF16),
            pltpu.VMEM(over.shape, BF16),
            pltpu.VMEM((seqs, length, width), BF16),
            pltpu.VMEM((seqs, length, width), F32),
            pltpu.VMEM((early_rows, width), BF16),
            pltpu.VMEM((late_rows, width), BF16),
            pltpu.VMEM((width, hd), F32),
            pltpu.VMEM((width, hd), F32),
            pltpu.VMEM((width, hd), F32),
            pltpu.VMEM((hd, width), F32),
            pltpu.VMEM((width, ff), F32),
            pltpu.VMEM((ff, width), F32),
            dma((rows_dev // chunk,)), dma((6,)), dma((8,)),
            pltpu.SMEM((2 * n * 2 * LANES,), jnp.int32), dma, pltpu.VMEM((16, width), F32),
        ],
        compiler_params=pltpu.CompilerParams(vmem_limit_bytes=VMEM_LIMIT),
        name="scatter",
    )(
        asked.reshape(-1), user_counts, incoming.reshape(2 * n * gcap, width), over, early_total,
        late_total, small_total, y, ig,
    )
    return (
        output, input_grad, table_grad, g1.reshape(width), gq, gk, gv, go, gb.T, g2.reshape(width),
        gin, gout,
    )


def solution(mesh):
    split = ("emb", "dp")
    return jax.shard_map(
        on_device,
        mesh=mesh,
        in_specs=(
            P(split, None), P(split, None, None), P(split), P(), P(split, None), P(),
            P("emb", None), P(), P(), P(), P(), P(), P(), P(), P(), P(), P(split, None, None),
        ),
        out_specs=(
            P(split, None, None), P(split, None, None), P("emb", None), P(), P(), P(), P(), P(),
            P(), P(), P(), P(),
        ),
        check_vma=False,
    )
```
